32 devices in a mesh: groups: 2 (over y), lon: 4 (over z), lat: 2 (over x), sub: 2 (over core).
Axes of the slice: x: 2, y: 2, z: 4, core: 2. Of those that a mesh axis runs over, the one named last changes fastest.
Arguments:
- grid_latent: bfloat16 [16384, 512], P(('groups', 'lon', 'lat', 'sub')), parts along dimension 0, may hold values from -6 to 6
- mesh_latent: bfloat16 [8192, 512], P(('groups', 'lon', 'lat', 'sub')), parts along dimension 0, may hold values from -6 to 6
- cotangent: bfloat16 [8192, 512], P(('groups', 'lon', 'lat', 'sub')), parts along dimension 0, may hold values from -6 to 6
- embed_weight: bfloat16 [512, 512], replicated, may hold values from -0.25 to 0.25
- merge_weight: bfloat16 [512, 512], replicated, may hold values from -0.125 to 0.125
- send_weight: bfloat16 [2, 512, 512], replicated, may hold values from -0.25 to 0.25
- recv_weight: bfloat16 [2, 512, 512], replicated, may hold values from -0.25 to 0.25
- update_weight: bfloat16 [2, 512, 512], replicated, may hold values from -0.109375 to 0.109375
- target_row: int32 [16384], P(('groups', 'lon', 'lat', 'sub')), parts along dimension 0, may hold values from 0 to 255
- send_rows: int32 [32, 6, 16], P(('groups', 'lon', 'lat', 'sub')), parts along dimension 0, may hold values from 0 to 512, as said below
- incoming_rows: int32 [32, 6, 16], P(('groups', 'lon', 'lat', 'sub')), parts along dimension 0, may hold values from 0 to 256, as said below
- border_mesh_rows: int32 [32, 6, 8], P(('groups', 'lon', 'lat', 'sub')), parts along dimension 0, may hold values from 0 to 255
- mesh_senders: int32 [8192, 6], P(('groups', 'lon', 'lat', 'sub')), parts along dimension 0, may hold values from 0 to 303, as said below
Outputs:
- mesh_out: bfloat16 [8192, 512], P(('groups', 'lon', 'lat', 'sub')), parts along dimension 0
- grid_grad: bfloat16 [16384, 512], P(('groups', 'lon', 'lat', 'sub')), parts along dimension 0
- embed_grad: float32 [1024, 512], P(('groups', 'lon', 'lat', 'sub')), parts along dimension 0
- merge_grad: float32 [1024, 512], P(('groups', 'lon', 'lat', 'sub')), parts along dimension 0
- send_grad: float32 [4, 512, 512], P('groups', ('lon', 'lat', 'sub')), parts along dimension 0
- recv_grad: float32 [4, 512, 512], P('groups', ('lon', 'lat', 'sub')), parts along dimension 0
- update_grad: float32 [4, 512, 512], P('groups', ('lon', 'lat', 'sub')), parts along dimension 0
The draws below stay inside these ranges and needn't reach their ends.
There are 2 independent parts, one for each index of `groups`. The reference program is written for one: setup_inputs(seed, part) draws one part's arguments, and reference() takes and returns one part's arrays. A program takes and returns all parts, laid end to end along the dimension named above; an argument that names none is the same for every part. Nothing has to cross between parts.
Inputs may be any that keep to these rules, and one draw needn't show every extreme that they name: `send_rows`: an entry 512 marks an empty place. In each partition's block the named rows are distinct and each slot's used places come first; slot d % 4 of partition d is empty, every other slot holds 1 or more rows, and one slot of each partition holds all 16. An entry 256 marks an empty place; incoming_rows[d, s, k] < 256 exactly where send_rows[peer(d, s), back(d, s), k] < 512. `mesh_senders`: A partition's table is its own 256 rows followed by 48 received boundary rows, slot after slot; the rows of the partition's own slot d % 4 are never named, and every other received row is the sender of exactly one edge of that partition.
All inputs are finite; a program needn't handle non-finite values.
Results may differ from the reference program's by a relative error of at most 0.02.
Values may be sent and summed in bfloat16 or wider, within the bound.
No kernel may reach another device: no remote copies, remote signals or barrier semaphores. Data moves between devices by JAX's collectives and lax.ppermute only.
A program may use at most 128 MiB of HBM per device.

```python
import jax
import jax.numpy as jnp
from jax import lax

C = 512
GRID_PER_PART = 512
MESH_PER_PART = 256
DEG = 6
LAYERS = 2
COL = 4
NEIGHBOUR_SLOTS = 6
PART_COUNT = 16
BORDER_ROWS = 8
GRID_SEND_LIMIT = 16
GRID = 8192
MESH = 4096
N_LON = 4
N_LAT = 2
N_SUB = 2


def traffic_plan(key):
    row_counts = jax.random.randint(jax.random.fold_in(key, 101), (PART_COUNT, NEIGHBOUR_SLOTS), max(1, GRID_SEND_LIMIT // 4), GRID_SEND_LIMIT + 1)
    occupied_flags = jax.random.randint(jax.random.fold_in(key, 102), (PART_COUNT,), 0, NEIGHBOUR_SLOTS - 1)
    column = jnp.arange(PART_COUNT, dtype=jnp.int32) % COL
    occupied_flags = occupied_flags + (occupied_flags >= column).astype(jnp.int32)
    neighbour_slot_index = jnp.arange(NEIGHBOUR_SLOTS, dtype=jnp.int32)[None, :]
    row_counts = jnp.where(neighbour_slot_index == occupied_flags[:, None], GRID_SEND_LIMIT, row_counts)
    row_counts = jnp.where(neighbour_slot_index == column[:, None], 0, row_counts)
    return row_counts.astype(jnp.int32)


def draw_send_rows(key, part):
    row_counts = traffic_plan(key)
    key = jax.random.fold_in(key, 7)
    block_random_keys = jax.random.split(key, PART_COUNT)

    def single_block(block_random_key):
        return jax.random.permutation(block_random_key, GRID_PER_PART)[:NEIGHBOUR_SLOTS * GRID_SEND_LIMIT].astype(jnp.int32)
    sorted_order = jax.vmap(single_block)(block_random_keys).reshape(PART_COUNT, NEIGHBOUR_SLOTS, GRID_SEND_LIMIT)
    places = jnp.arange(GRID_SEND_LIMIT, dtype=jnp.int32)[None, None, :]
    return jnp.where(places < row_counts[:, :, None], sorted_order, GRID_PER_PART).astype(jnp.int32)


def draw_incoming_rows(key, part):
    row_counts = traffic_plan(key)
    key = jax.random.fold_in(key, 8)
    chosen_rows = jax.random.randint(key, (PART_COUNT, NEIGHBOUR_SLOTS, GRID_SEND_LIMIT), 0, MESH_PER_PART)
    lon_count = PART_COUNT // COL
    part_ids = jnp.arange(PART_COUNT, dtype=jnp.int32)[:, None]
    neighbour_slot_index = jnp.arange(NEIGHBOUR_SLOTS, dtype=jnp.int32)[None, :]
    lon_index = part_ids // COL
    column = part_ids % COL
    left = (lon_index - 1 + lon_count) % lon_count * COL + column
    right = (lon_index + 1) % lon_count * COL + column
    peers = jnp.where(neighbour_slot_index < COL, lon_index * COL + neighbour_slot_index, jnp.where(neighbour_slot_index == COL, left, right))
    backs = jnp.where(neighbour_slot_index < COL, column, jnp.where(neighbour_slot_index == COL, COL + 1, COL))
    arrived = row_counts[peers, backs]
    places = jnp.arange(GRID_SEND_LIMIT, dtype=jnp.int32)[None, None, :]
    return jnp.where(places < arrived[:, :, None], chosen_rows, MESH_PER_PART).astype(jnp.int32)


def draw_mesh_senders(key, part):
    key = jax.random.fold_in(key, 11)
    edges = MESH_PER_PART * DEG
    foreign_rows = (NEIGHBOUR_SLOTS - 1) * BORDER_ROWS

    def single_block(block_random_key, part_id):
        first, second = jax.random.split(block_random_key)
        sorted_order = jax.random.permutation(first, edges).astype(jnp.int32)
        local = jax.random.randint(second, (edges,), 0, MESH_PER_PART)
        raw_slot = sorted_order // BORDER_ROWS
        slot = raw_slot + (raw_slot >= part_id % COL).astype(jnp.int32)
        named = MESH_PER_PART + slot * BORDER_ROWS + sorted_order % BORDER_ROWS
        chosen = jnp.where(sorted_order < foreign_rows, named, local)
        return chosen.reshape(MESH_PER_PART, DEG)
    block_random_keys = jax.random.split(key, PART_COUNT)
    part_ids = jnp.arange(PART_COUNT, dtype=jnp.int32)
    return jax.vmap(single_block)(block_random_keys, part_ids).reshape(MESH_PER_PART * PART_COUNT, DEG).astype(jnp.int32)


def place_ends(entries, key, smallest, high):
    longest = entries.shape.index(max(entries.shape))
    spots = []
    for shift in (0, 1):
        where = [jax.random.randint(jax.random.fold_in(key, axis), (), 0, length) for axis, length in enumerate(entries.shape)]
        where[longest] = (where[longest] + shift) % entries.shape[longest]
        spots.append(tuple(where))
    return entries.at[spots[0]].set(smallest).at[spots[1]].set(high)


def block_scale(key, extent, shards, smallest, largest):
    gain = 1.0
    for axis_at, blocks in shards:
        heights = jax.random.uniform(jax.random.fold_in(jax.random.fold_in(key, 6), axis_at), (blocks,), jnp.float32, smallest / len(shards), largest / len(shards))
        gain = gain * jnp.repeat(jnp.exp(heights), extent[axis_at] // blocks).reshape((-1,) + (1,) * (len(extent) - 1 - axis_at))
    return gain


def bell_draw(stream_key, dims, scale, reach, shards=(), kind=jnp.bfloat16):
    drawn = jax.random.normal(stream_key, dims, jnp.float32) * scale
    if len(shards) > 0:
        drawn = block_scale(stream_key, dims, shards, -0.22, 0.18) * drawn
    return jnp.clip(drawn, min=-reach, max=reach).astype(kind)


def setup_inputs(seed: int = 0, part: int = 0) -> dict:
    splits = jax.random.split(jax.random.key(seed), 14)
    part_splits = jax.random.split(jax.random.fold_in(splits[13], part), 14)
    return {
        "grid_latent": bell_draw(part_splits[0], (GRID, C), 1.0, 6.0, ((0, 16),)),
        "mesh_latent": bell_draw(part_splits[1], (MESH, C), 1.0, 6.0, ((0, 16),)),
        "cotangent": bell_draw(part_splits[2], (MESH, C), 1.0, 6.0, ((0, 16),)),
        "embed_weight": bell_draw(splits[3], (C, C), C ** -0.5, 0.25),
        "merge_weight": bell_draw(splits[4], (C, C), (4 * C) ** -0.5, 0.125),
        "send_weight": bell_draw(splits[5], (LAYERS, C, C), C ** -0.5, 0.25),
        "recv_weight": bell_draw(splits[6], (LAYERS, C, C), C ** -0.5, 0.25),
        "update_weight": bell_draw(splits[7], (LAYERS, C, C), (DEG * C) ** -0.5, 0.109375),
        "target_row": place_ends(jax.random.randint(part_splits[8], (GRID,), 0, MESH_PER_PART), jax.random.fold_in(part_splits[8], 1), 0, MESH_PER_PART - 1).astype(jnp.int32),
        "send_rows": draw_send_rows(jax.random.fold_in(jax.random.fold_in(splits[13], part), 71), part),
        "incoming_rows": draw_incoming_rows(jax.random.fold_in(jax.random.fold_in(splits[13], part), 71), part),
        "border_mesh_rows": place_ends(jax.random.randint(part_splits[11], (PART_COUNT, NEIGHBOUR_SLOTS, BORDER_ROWS), 0, MESH_PER_PART), jax.random.fold_in(part_splits[11], 1), 0, MESH_PER_PART - 1).astype(jnp.int32),
        "mesh_senders": draw_mesh_senders(jax.random.fold_in(jax.random.fold_in(splits[13], part), 71), part),
    }


def silu_slope(value):
    sig = jax.nn.sigmoid(value)
    return sig * (1.0 + value * (1.0 - sig))


def slot_peer(part_ids, neighbour_slot_index):
    column_count = N_LAT * N_SUB
    lon_index = part_ids // column_count
    column = part_ids % column_count
    left = ((lon_index - 1 + N_LON) % N_LON) * column_count + column
    right = ((lon_index + 1) % N_LON) * column_count + column
    inside = lon_index * column_count + neighbour_slot_index
    return jnp.where(neighbour_slot_index < column_count, inside, jnp.where(neighbour_slot_index == column_count, left, right)).astype(jnp.int32)


def slot_back(part_ids, neighbour_slot_index):
    column_count = N_LAT * N_SUB
    column = part_ids % column_count
    return jnp.where(neighbour_slot_index < column_count, column, jnp.where(neighbour_slot_index == column_count, column_count + 1, column_count)).astype(jnp.int32)


def layer_forward(state, weight_send, weight_recv, weight_update, sources):
    sent = jnp.dot(state, weight_send, preferred_element_type=jnp.float32).astype(jnp.bfloat16)
    recv = jnp.dot(state, weight_recv, preferred_element_type=jnp.float32)
    total = jnp.zeros(recv.shape, jnp.float32)
    for edge in range(DEG):
        total = total + jax.nn.silu(sent[sources[:, edge]].astype(jnp.float32) + recv)
    summed = total.astype(jnp.bfloat16)
    result = (state.astype(jnp.float32) + jnp.dot(summed, weight_update, preferred_element_type=jnp.float32)).astype(jnp.bfloat16)
    return result, (state, sent, recv, summed)


def layer_backward(grad_out, saved, weight_send, weight_recv, weight_update, sources):
    state, sent, recv, summed = saved
    total_nodes = state.shape[0]
    grad_update = jnp.dot(summed.T, grad_out, preferred_element_type=jnp.float32)
    grad_sum = jnp.dot(grad_out, weight_update.T, preferred_element_type=jnp.float32).astype(jnp.bfloat16)
    grad_recv = jnp.zeros(recv.shape, jnp.float32)
    grad_sent = jnp.zeros(recv.shape, jnp.float32)
    for edge in range(DEG):
        pre = sent[sources[:, edge]].astype(jnp.float32) + recv
        edge_grad = grad_sum.astype(jnp.float32) * silu_slope(pre)
        grad_recv = grad_recv + edge_grad
        grad_sent = grad_sent + jax.ops.segment_sum(edge_grad, sources[:, edge], total_nodes)
    recv_low = grad_recv.astype(jnp.bfloat16)
    sent_low = grad_sent.astype(jnp.bfloat16)
    grad_wsend = jnp.dot(state.T, sent_low, preferred_element_type=jnp.float32)
    grad_wrecv = jnp.dot(state.T, recv_low, preferred_element_type=jnp.float32)
    grad_in = grad_out.astype(jnp.float32) + jnp.dot(recv_low, weight_recv.T, preferred_element_type=jnp.float32)
    grad_in = (grad_in + jnp.dot(sent_low, weight_send.T, preferred_element_type=jnp.float32)).astype(jnp.bfloat16)
    return grad_in, grad_wsend, grad_wrecv, grad_update


def reference(grid_latent, mesh_latent, cotangent, embed_weight, merge_weight, send_weight, recv_weight, update_weight, target_row, send_rows, incoming_rows, border_mesh_rows, mesh_senders):
    parts = N_LON * N_LAT * N_SUB
    slot_total = N_LAT * N_SUB + 2
    total_nodes = parts * MESH_PER_PART
    grid_nodes = parts * GRID_PER_PART
    capacity = send_rows.shape[2]

    grid_owner = (jnp.arange(grid_nodes, dtype=jnp.int32) // GRID_PER_PART).astype(jnp.int32)
    target = (grid_owner * MESH_PER_PART + target_row).astype(jnp.int32)
    part_ids = jnp.arange(parts, dtype=jnp.int32)[:, None, None]
    neighbour_slot_index = jnp.arange(slot_total, dtype=jnp.int32)[None, :, None]
    place_ids = jnp.arange(capacity, dtype=jnp.int32)[None, None, :]
    peers = slot_peer(part_ids, neighbour_slot_index)
    backs = slot_back(part_ids, neighbour_slot_index)
    far_rows = incoming_rows[peers, backs, place_ids]
    far_target = (peers * MESH_PER_PART + far_rows).astype(jnp.int32)
    valid = send_rows < GRID_PER_PART
    grid_index = jnp.where(valid, part_ids * GRID_PER_PART + send_rows, grid_nodes).astype(jnp.int32)
    target = target.at[grid_index.reshape(-1)].set(far_target.reshape(-1), mode="drop").astype(jnp.int32)

    owner = (jnp.arange(total_nodes, dtype=jnp.int32) // MESH_PER_PART).astype(jnp.int32)[:, None]
    offset = jnp.maximum(mesh_senders - MESH_PER_PART, 0).astype(jnp.int32)
    slot = (offset // BORDER_ROWS).astype(jnp.int32)
    within = (offset % BORDER_ROWS).astype(jnp.int32)
    peer = slot_peer(owner, slot)
    back = slot_back(owner, slot)
    foreign_rows = peer * MESH_PER_PART + border_mesh_rows[peer, back, within]
    local = owner * MESH_PER_PART + mesh_senders
    sources = jnp.where(mesh_senders < MESH_PER_PART, local, foreign_rows).astype(jnp.int32)

    pre0 = jnp.dot(grid_latent, embed_weight, preferred_element_type=jnp.float32)
    message = jax.nn.silu(pre0).astype(jnp.bfloat16)
    message = lax.optimization_barrier(message)
    gathered = jax.ops.segment_sum(message.astype(jnp.float32), target, total_nodes)
    merged = gathered.astype(jnp.bfloat16)
    state = (mesh_latent.astype(jnp.float32) + jnp.dot(merged, merge_weight, preferred_element_type=jnp.float32)).astype(jnp.bfloat16)

    saved = []
    for layer in range(LAYERS):
        state, keep = layer_forward(state, send_weight[layer], recv_weight[layer], update_weight[layer], sources)
        saved.append(keep)
    mesh_out = state

    grad = cotangent
    send_list, recv_list, update_list = [], [], []
    for layer in reversed(range(LAYERS)):
        grad, grad_s, grad_r, grad_u = layer_backward(grad, saved[layer], send_weight[layer], recv_weight[layer], update_weight[layer], sources)
        send_list.insert(0, grad_s)
        recv_list.insert(0, grad_r)
        update_list.insert(0, grad_u)

    merge_grad = jnp.dot(merged.T, grad, preferred_element_type=jnp.float32)
    grad_merged = jnp.dot(grad, merge_weight.T, preferred_element_type=jnp.float32).astype(jnp.bfloat16)
    grad_pre = (grad_merged[target].astype(jnp.float32) * silu_slope(pre0)).astype(jnp.bfloat16)
    embed_grad = jnp.dot(grid_latent.T, grad_pre, preferred_element_type=jnp.float32)
    grid_grad = jnp.dot(grad_pre, embed_weight.T, preferred_element_type=jnp.float32).astype(jnp.bfloat16)
    return (mesh_out, grid_grad, embed_grad, merge_grad, jnp.stack(send_list), jnp.stack(recv_list), jnp.stack(update_list))
```

```python
import jax
import jax.numpy as jnp
from jax import lax
from jax.sharding import PartitionSpec as P


def extended_2(block, sides, width):
    for axis, dim in sides:
        count = lax.axis_size(axis)
        forward = [(i, i + 1) for i in range(count - 1)]
        forward.append((count - 1, 0))
        backward = [(target, source) for source, target in forward]
        low = lax.ppermute(
            lax.slice_in_dim(block, block.shape[dim] - width, None, axis=dim), axis, forward
        )
        high = lax.ppermute(lax.slice_in_dim(block, 0, width, axis=dim), axis, backward)
        block = jnp.concatenate([low, block, high], axis=dim)
    return block


def silu_slope(value):
    sig = jax.nn.sigmoid(value)
    return sig * (1.0 + value * (1.0 - sig))


def spread_grid(payload):
    column_count = lax.axis_size(("lat", "sub"))
    column = payload[:column_count]
    arrived = lax.all_to_all(column, ("lat", "sub"), split_axis=0, concat_axis=0, tiled=True)
    extended = extended_2(payload[column_count:], (("lon", 0),), 1)
    return jnp.concatenate([arrived, extended[0:1], extended[3:4]], axis=0)


def return_grid(payload):
    column_count = lax.axis_size(("lat", "sub"))
    column = payload[:column_count]
    arrived = lax.all_to_all(column, ("lat", "sub"), split_axis=0, concat_axis=0, tiled=True)
    extended = extended_2(payload[column_count:], (("lon", 0),), 1)
    return jnp.concatenate([arrived, extended[0:1], extended[3:4]], axis=0)


def spread_mesh(payload):
    column_count = lax.axis_size(("lat", "sub"))
    arrived = lax.all_to_all(
        payload[:column_count], ("lat", "sub"), split_axis=0, concat_axis=0, tiled=True
    )
    extended = extended_2(payload[column_count:], (("lon", 0),), 1)
    return jnp.concatenate([arrived, extended[0:1], extended[3:4]], axis=0)


def return_mesh(payload):
    column_count = lax.axis_size(("lat", "sub"))
    arrived = lax.all_to_all(
        payload[:column_count].astype(jnp.bfloat16),
        ("lat", "sub"),
        split_axis=0,
        concat_axis=0,
        tiled=True,
    ).astype(jnp.float32)
    extended = extended_2(payload[column_count:].astype(jnp.bfloat16), (("lon", 0),), 1).astype(
        jnp.float32
    )
    return jnp.concatenate([arrived, extended[0:1], extended[3:4]], axis=0)


def scatter_weights(partials):
    lon, lat, sub = (lax.axis_size(axis) for axis in ("lon", "lat", "sub"))
    rows, width = partials[0].shape
    depth = rows // (lon * lat * sub)
    blocks = [
        part.astype(jnp.bfloat16).reshape(lon, lat, sub, depth, width).transpose(2, 1, 0, 3, 4)
        for part in partials
    ]
    block = jnp.concatenate(blocks, axis=3)
    for axis in ("sub", "lat", "lon"):
        block = lax.psum_scatter(block, axis, scatter_dimension=0, tiled=False)
    block = block.astype(jnp.float32)
    return [block[i * depth : (i + 1) * depth] for i in range(len(partials))]


def layer_forward(state, weight_send, weight_recv, weight_update, bounds, senders):
    width = state.shape[1]
    sent = jnp.dot(state, weight_send, preferred_element_type=jnp.float32).astype(jnp.bfloat16)
    incoming = spread_mesh(sent[bounds])
    recv = jnp.dot(state, weight_recv, preferred_element_type=jnp.float32)
    table = jnp.concatenate([sent, incoming.reshape(-1, width)], axis=0)
    pre_edge = table[senders].astype(jnp.float32) + recv[:, None, :]
    summed = jnp.sum(jax.nn.silu(pre_edge), axis=1).astype(jnp.bfloat16)
    result = (
        state.astype(jnp.float32)
        + jnp.dot(summed, weight_update, preferred_element_type=jnp.float32)
    ).astype(jnp.bfloat16)
    return (result, (state, table, recv, summed))


def layer_backward(grad_out, saved, weight_send, weight_recv, weight_update, bounds, senders):
    state, table, recv, summed = saved
    node_count, width = state.shape
    slot_count, depth = bounds.shape
    grad_sum = jnp.dot(grad_out, weight_update.T, preferred_element_type=jnp.float32).astype(
        jnp.bfloat16
    )
    pre_edge = table[senders].astype(jnp.float32) + recv[:, None, :]
    edge_grad = grad_sum.astype(jnp.float32)[:, None, :] * silu_slope(pre_edge)
    recv_low = jnp.sum(edge_grad, axis=1).astype(jnp.bfloat16)
    table_grad = jax.ops.segment_sum(
        edge_grad.reshape(-1, width), senders.reshape(-1), node_count + slot_count * depth
    )
    returned = return_mesh(table_grad[node_count:].reshape(slot_count, depth, width))
    grad_sent = table_grad[:node_count] + jax.ops.segment_sum(
        returned.reshape(-1, width), bounds.reshape(-1), node_count
    )
    sent_low = grad_sent.astype(jnp.bfloat16)
    partials = (
        jnp.dot(state.T, sent_low, preferred_element_type=jnp.float32),
        jnp.dot(state.T, recv_low, preferred_element_type=jnp.float32),
        jnp.dot(summed.T, grad_out, preferred_element_type=jnp.float32),
    )
    grad_in = grad_out.astype(jnp.float32) + jnp.dot(
        recv_low, weight_recv.T, preferred_element_type=jnp.float32
    )
    grad_in = (
        grad_in + jnp.dot(sent_low, weight_send.T, preferred_element_type=jnp.float32)
    ).astype(jnp.bfloat16)
    return (grad_in, partials)


def body(
    grid_latent,
    mesh_latent,
    cotangent,
    embed_weight,
    merge_weight,
    send_weight,
    recv_weight,
    update_weight,
    target_row,
    send_rows,
    incoming_rows,
    border_mesh_rows,
    mesh_senders,
):
    chosen_rows, width = grid_latent.shape
    node_count = mesh_latent.shape[0]
    layer_count = send_weight.shape[0]
    sends = send_rows[0]
    arrivals = incoming_rows[0]
    bounds = border_mesh_rows[0]
    flat_sends = sends.reshape(-1)
    kept = jnp.ones((chosen_rows + 1,), jnp.bool_).at[flat_sends].set(False)[:chosen_rows]
    local_labels = jnp.where(kept, target_row, node_count)
    pre_grid = jnp.dot(grid_latent, embed_weight, preferred_element_type=jnp.float32)
    message = jax.nn.silu(pre_grid).astype(jnp.bfloat16)
    padded_message = jnp.concatenate([message, jnp.zeros((1, width), jnp.bfloat16)], axis=0)
    arrived = spread_grid(padded_message[sends])
    all_labels = jnp.concatenate([local_labels, arrivals.reshape(-1)], axis=0)
    all_values = jnp.concatenate([message, arrived.reshape(-1, width)], axis=0).astype(jnp.float32)
    gathered = jax.ops.segment_sum(all_values, all_labels, node_count + 1)[:node_count]
    merged = gathered.astype(jnp.bfloat16)
    state = (
        mesh_latent.astype(jnp.float32)
        + jnp.dot(merged, merge_weight, preferred_element_type=jnp.float32)
    ).astype(jnp.bfloat16)
    saved = []
    for layer in range(layer_count):
        state, keep = layer_forward(
            state,
            send_weight[layer],
            recv_weight[layer],
            update_weight[layer],
            bounds,
            mesh_senders,
        )
        saved.append(keep)
    grad = cotangent
    send_list, recv_list, update_list = ([], [], [])
    for layer in reversed(range(layer_count)):
        grad, partials = layer_backward(
            grad,
            saved[layer],
            send_weight[layer],
            recv_weight[layer],
            update_weight[layer],
            bounds,
            mesh_senders,
        )
        partials = scatter_weights(partials)
        send_list.insert(0, partials[0])
        recv_list.insert(0, partials[1])
        update_list.insert(0, partials[2])
    merge_partial = jnp.dot(merged.T, grad, preferred_element_type=jnp.float32)
    grad_merged = jnp.dot(grad, merge_weight.T, preferred_element_type=jnp.float32).astype(
        jnp.bfloat16
    )
    padded_grad = jnp.concatenate([grad_merged, jnp.zeros((1, width), jnp.bfloat16)], axis=0)
    replies = return_grid(padded_grad[arrivals])
    local_grad = jnp.concatenate(
        [padded_grad[local_labels], jnp.zeros((1, width), jnp.bfloat16)], axis=0
    )
    grid_back = local_grad.at[flat_sends].set(replies.reshape(-1, width))[:chosen_rows]
    grad_pre = (grid_back.astype(jnp.float32) * silu_slope(pre_grid)).astype(jnp.bfloat16)
    embed_partial = jnp.dot(grid_latent.T, grad_pre, preferred_element_type=jnp.float32)
    grid_grad = jnp.dot(grad_pre, embed_weight.T, preferred_element_type=jnp.float32).astype(
        jnp.bfloat16
    )
    embed_grad, merge_grad = scatter_weights((embed_partial, merge_partial))
    send_grad = jnp.stack(send_list)
    recv_grad = jnp.stack(recv_list)
    update_grad = jnp.stack(update_list)
    return (state, grid_grad, embed_grad, merge_grad, send_grad, recv_grad, update_grad)


def solution(mesh):
    in_specs = (
        P(("groups", "lon", "lat", "sub"), None),
        P(("groups", "lon", "lat", "sub"), None),
        P(("groups", "lon", "lat", "sub"), None),
        P(),
        P(),
        P(),
        P(),
        P(),
        P(("groups", "lon", "lat", "sub")),
        P(("groups", "lon", "lat", "sub"), None, None),
        P(("groups", "lon", "lat", "sub"), None, None),
        P(("groups", "lon", "lat", "sub"), None, None),
        P(("groups", "lon", "lat", "sub"), None),
    )
    out_specs = (
        P(("groups", "lon", "lat", "sub"), None),
        P(("groups", "lon", "lat", "sub"), None),
        P(("groups", "lon", "lat", "sub"), None),
        P(("groups", "lon", "lat", "sub"), None),
        P("groups", ("lon", "lat", "sub"), None),
        P("groups", ("lon", "lat", "sub"), None),
        P("groups", ("lon", "lat", "sub"), None),
    )
    return jax.shard_map(body, mesh=mesh, in_specs=in_specs, out_specs=out_specs, check_vma=False)
```

```python
import itertools

import jax
import jax.numpy as jnp
from jax import lax
from jax.experimental import pallas as pl
from jax.experimental.pallas import tpu as pltpu
from jax.sharding import PartitionSpec as P

BF = jnp.bfloat16
F32 = jnp.float32
NN = (((1,), (0,)), ((), ()))
NT = (((1,), (1,)), ((), ()))
TN = (((0,), (0,)), ((), ()))
BORDER = 8
GROUP = ("lon", "lat", "sub")
COLUMN = ("lat", "sub")


def dot(a, b, dims=NN):
    return lax.dot_general(a, b, dims, preferred_element_type=F32)


def low(value):
    return value.astype(BF)


def sigmoid(value):
    return 0.5 * jnp.tanh(0.5 * value) + 0.5


def silu(value):
    return value * sigmoid(value)


def silu_both(value):
    sig = sigmoid(value)
    act = value * sig
    return act, sig + act * (1.0 - sig)


def silu_slope(value):
    return silu_both(value)[1]


def iota(rows, columns, dim):
    return lax.broadcasted_iota(jnp.int32, (rows, columns), dim)


def hot(mask):
    return jnp.where(mask, 1.0, 0.0)


def pieces(value, slots, starts, sizes):
    step = value.shape[0] // slots
    found = []
    for start, size in zip(starts, sizes):
        found.append(
            jnp.concatenate(
                [value[s * step + start : s * step + start + size] for s in range(slots)], axis=0
            )
        )
    return found


def braid(parts, slots):
    rows = []
    for s in range(slots):
        for part in parts:
            size = part.shape[0] // slots
            rows.append(part[s * size : (s + 1) * size])
    return jnp.concatenate(rows, axis=0)


def receivers(senders_t, nodes, halo):
    found = jnp.zeros((halo, nodes), F32)
    ids = iota(halo, nodes, 0) + nodes
    for j in range(senders_t.shape[0]):
        found = found + hot(senders_t[j : j + 1, :] == ids)
    return found


def receivers_t(senders, halo):
    nodes, degree = senders.shape
    found = jnp.zeros((nodes, halo), F32)
    ids = iota(nodes, halo, 1) + nodes
    for j in range(degree):
        found = found + hot(senders[:, j : j + 1] == ids)
    return found


def store_blocks(ref, at, value, dims, order):
    value = low(value)
    rows = value.shape[0]
    depth = rows // (dims[0] * dims[1] * dims[2])
    if depth % 16:
        ref[at] = value
        return
    for place in itertools.product(*(range(size) for size in dims)):
        block = (place[0] * dims[1] + place[1]) * dims[2] + place[2]
        spot = 0
        for axis in order:
            spot = spot * dims[axis] + place[axis]
        ref[spot, at * depth : (at + 1) * depth, :] = value[block * depth : (block + 1) * depth]


def blocks_shape(count, rows, width, dims):
    total = dims[0] * dims[1] * dims[2]
    depth = rows // total
    if depth % 16:
        return jax.ShapeDtypeStruct((count, rows, width), BF)
    return jax.ShapeDtypeStruct((total, count * depth, width), BF)


def arrange(blocks, rows, dims, order):
    total = dims[0] * dims[1] * dims[2]
    depth = rows // total
    if depth % 16:
        count, _, width = blocks.shape
        blocks = blocks.reshape((count,) + dims + (depth, width))
        blocks = blocks.transpose(tuple(axis + 1 for axis in order) + (0, 4, 5))
        blocks = blocks.reshape(total, count * depth, width)
    return blocks


def scatter_sum(blocks, stages):
    for at, axes in enumerate(stages):
        size = lax.axis_size(axes)
        blocks = blocks.reshape((size, blocks.shape[0] // size) + blocks.shape[1:])
        moved = lax.all_to_all(blocks, axes, split_axis=0, concat_axis=0, tiled=True)
        total = moved[0].astype(F32)
        for i in range(1, size):
            total = total + moved[i].astype(F32)
        blocks = total if at == len(stages) - 1 else low(total)
    return blocks[0]


def call(kernel, name, outs, args, flops):
    size = sum(a.size * a.dtype.itemsize for a in (*args, *outs))
    return pl.pallas_call(
        kernel,
        out_shape=list(outs),
        in_specs=[pl.BlockSpec(memory_space=pltpu.VMEM)] * len(args),
        out_specs=[pl.BlockSpec(memory_space=pltpu.VMEM)] * len(outs),
        compiler_params=pltpu.CompilerParams(vmem_limit_bytes=48 * 1024 * 1024),
        cost_estimate=pl.CostEstimate(flops=flops, bytes_accessed=size, transcendentals=0),
        name=name,
    )(*args)


def exchange(payload):
    column = lax.axis_size(COLUMN)
    count = lax.axis_size("lon")
    forward = [(i, (i + 1) % count) for i in range(count)]
    backward = [(target, source) for source, target in forward]
    from_right = lax.ppermute(payload[column], "lon", backward)
    from_left = lax.ppermute(payload[column + 1], "lon", forward)
    arrived = lax.all_to_all(payload[:column], COLUMN, split_axis=0, concat_axis=0, tiled=True)
    return jnp.concatenate([arrived, from_left[None], from_right[None]], axis=0)


def shape(*dims, dtype=BF):
    return jax.ShapeDtypeStruct(dims, dtype)


def first_payload(sends_ref, senders_t_ref, grid_ref, cot_ref, out_ref):
    taken = sends_ref.shape[0]
    chosen, nodes = grid_ref.shape[0], cot_ref.shape[0]
    slots = taken // 16
    rows = dot(low(hot(sends_ref[...] == iota(taken, chosen, 1))), grid_ref[...])
    back = low(receivers(senders_t_ref[...], nodes, slots * BORDER))
    out_ref[...] = low(braid([rows, dot(back, cot_ref[...])], slots))


def embed_local(grid_ref, weight_ref, target_ref, sends_ref, sum_ref, slope_ref):
    chosen = grid_ref.shape[0]
    nodes = sum_ref.shape[0]
    taken = sends_ref.shape[0]
    pre = dot(grid_ref[...], weight_ref[...])
    act, slope = silu_both(pre)
    slope_ref[...] = low(slope)
    sent = jnp.max(hot(sends_ref[...] == iota(taken, chosen, 1)), axis=0, keepdims=True)
    label = jnp.where(sent > 0.0, nodes, target_ref[...])
    sum_ref[...] = dot(low(hot(label == iota(nodes, chosen, 0))), low(act))


def merge_nodes(
    slots, arr_ref, incoming_ref, embed_ref, local_ref, mesh_ref, weight_ref, bounds_ref,
    senders_t_ref, merged_ref, state_ref, pay_ref, slope_ref, lat_ref,
):
    nodes = mesh_ref.shape[0]
    taken = incoming_ref.shape[1]
    halo = slots * BORDER
    (lat,) = pieces(arr_ref[...].astype(F32), slots, (0,), (16,))
    lat = low(lat)
    lat_ref[...] = lat
    act, slope = silu_both(dot(lat, embed_ref[...]))
    slope_ref[...] = low(slope)
    place = low(hot(incoming_ref[...] == iota(nodes, taken, 0)))
    merged = low(local_ref[...] + dot(place, low(act)))
    merged_ref[...] = merged
    state = low(mesh_ref[...].astype(F32) + dot(merged, weight_ref[...]))
    state_ref[...] = state
    border = hot(bounds_ref[...] == iota(halo, nodes, 1))
    back = receivers(senders_t_ref[...], nodes, halo)
    pick = low(braid([border, back], slots))
    rows = pieces(dot(pick, state), slots, (0, BORDER), (BORDER, BORDER))
    pay_ref[...] = low(braid([*rows, dot(low(border), merged)], slots))


def local_edges(senders, sent, recv, each):
    nodes, degree = senders.shape
    total = jnp.zeros(recv.shape, F32)
    ids = iota(nodes, nodes, 1)
    for j in range(degree):
        named = senders[:, j : j + 1]
        act, slope = silu_both(dot(low(hot(named == ids)), sent) + recv)
        keep = hot(named < nodes)
        total = total + act * keep
        each(j, slope * keep)
    return total


def forward_local(
    state_ref, send_ref, recv_ref, senders_ref, senders_t_ref, bounds_ref,
    total_ref, slope_ref, recv_n_ref, sent_b_ref,
):
    state = state_ref[...]
    nodes = state.shape[0]
    halo = bounds_ref.shape[0]
    sent = low(dot(state, send_ref[...]))
    recv = dot(state, recv_ref[...])

    def keep(j, slope):
        slope_ref[j] = low(slope)

    total_ref[...] = local_edges(senders_ref[...], sent, recv, keep)
    back = low(receivers(senders_t_ref[...], nodes, halo))
    recv_n_ref[...] = dot(low(dot(back, state)), recv_ref[...])
    sent_b_ref[...] = low(dot(low(hot(bounds_ref[...] == iota(halo, nodes, 1))), sent))


def forward_halo(
    slots, arr_ref, recv_n_ref, total_ref, state_ref, send_ref, update_ref, senders_ref,
    senders_t_ref, bounds_ref, summed_ref, out_ref, pay_ref,
):
    nodes = state_ref.shape[0]
    halo = slots * BORDER
    (rows,) = pieces(arr_ref[...].astype(F32), slots, (0,), (BORDER,))
    pre = low(dot(low(rows), send_ref[...])).astype(F32) + recv_n_ref[...]
    place = low(receivers_t(senders_ref[...], halo))
    summed = low(total_ref[...] + dot(place, low(silu(pre))))
    summed_ref[...] = summed
    state = low(state_ref[...].astype(F32) + dot(summed, update_ref[...]))
    out_ref[...] = state
    border = hot(bounds_ref[...] == iota(halo, nodes, 1))
    back = receivers(senders_t_ref[...], nodes, halo)
    pay_ref[...] = low(dot(low(braid([border, back], slots)), state))


def turn_local(
    slots, state_ref, send_ref, recv_ref, update_ref, cot_ref, arr1_ref, arr2_ref, recv_n0_ref,
    sent_b0_ref, send0_ref, recv0_ref, senders_ref, senders_t_ref, bounds_ref,
    total_ref, grecv_ref, gsent_ref, recv_n_ref, sent_b_ref, gsum_n_ref, gsum_r_ref,
    slope_k_ref, slope_r_ref, rows_ref, merged_ref,
):
    halo = slots * BORDER
    rows0, back0, merged0 = pieces(
        arr2_ref[...].astype(F32), slots, (0, BORDER, 2 * BORDER), (BORDER,) * 3
    )
    rows_ref[...] = low(rows0)
    merged_ref[...] = low(merged0)
    pre = low(dot(low(rows0), send0_ref[...])).astype(F32) + recv_n0_ref[...]
    slope_k_ref[...] = low(silu_slope(pre))
    pre = sent_b0_ref[...].astype(F32) + dot(low(back0), recv0_ref[...])
    slope_r_ref[...] = low(silu_slope(pre))
    state = state_ref[...]
    nodes = state.shape[0]
    sent = low(dot(state, send_ref[...]))
    recv = dot(state, recv_ref[...])
    gsum = low(dot(cot_ref[...], update_ref[...], NT))
    grad = gsum.astype(F32)
    grecv_ref[...] = jnp.zeros(grecv_ref.shape, F32)
    gsent_ref[...] = jnp.zeros(gsent_ref.shape, F32)

    def back_edge(j, slope):
        gpre = grad * slope
        grecv_ref[...] += gpre
        place = low(hot(senders_t_ref[j : j + 1, :] == iota(nodes, nodes, 0)))
        gsent_ref[...] += dot(place, low(gpre))

    total_ref[...] = local_edges(senders_ref[...], sent, recv, back_edge)
    back = low(receivers(senders_t_ref[...], nodes, halo))
    recv_n_ref[...] = dot(low(dot(back, state)), recv_ref[...])
    sent_b_ref[...] = low(dot(low(hot(bounds_ref[...] == iota(halo, nodes, 1))), sent))
    gsum_n_ref[...] = low(dot(back, gsum))
    (cot_r,) = pieces(arr1_ref[...].astype(F32), slots, (16,), (BORDER,))
    gsum_r_ref[...] = low(dot(low(cot_r), update_ref[...], NT))


def turn_halo(
    slots, arr_ref, recv_n_ref, sent_b_ref, gsum_n_ref, gsum_r_ref, total_ref, grecv_ref,
    gsent_ref, cot_ref, send_ref, recv_ref, senders_ref, senders_t_ref, bounds_ref,
    summed_ref, grecv_out_ref, gsent_out_ref, gin_ref, pay_ref,
):
    nodes = cot_ref.shape[0]
    halo = slots * BORDER
    rows, back = pieces(arr_ref[...].astype(F32), slots, (0, BORDER), (BORDER,) * 2)
    pre = low(dot(low(rows), send_ref[...])).astype(F32) + recv_n_ref[...]
    act, slope = silu_both(pre)
    place = low(receivers_t(senders_ref[...], halo))
    gpre = low(gsum_n_ref[...].astype(F32) * slope)
    grecv = low(grecv_ref[...] + dot(place, gpre))
    pre = sent_b_ref[...].astype(F32) + dot(low(back), recv_ref[...])
    gpre = low(gsum_r_ref[...].astype(F32) * silu_slope(pre))
    border = low(hot(bounds_ref[...] == iota(nodes, halo, 0)))
    gsent = low(gsent_ref[...] + dot(border, gpre))
    gin = cot_ref[...].astype(F32) + dot(grecv, recv_ref[...], NT) + dot(gsent, send_ref[...], NT)
    gin = low(gin)
    gin_ref[...] = gin
    pay_ref[...] = low(dot(low(receivers(senders_t_ref[...], nodes, halo)), gin))
    summed_ref[...] = low(total_ref[...] + dot(place, low(act)))
    grecv_out_ref[...] = grecv
    gsent_out_ref[...] = gsent


def last_weights(
    dims, order, state_ref, summed_ref, cot_ref, grecv_ref, gsent_ref, update_ref, out_ref, mesh_ref
):
    state, summed = state_ref[...], summed_ref[...]
    store_blocks(out_ref, 0, dot(state, gsent_ref[...], TN), dims, order)
    store_blocks(out_ref, 1, dot(state, grecv_ref[...], TN), dims, order)
    store_blocks(out_ref, 2, dot(summed, cot_ref[...], TN), dims, order)
    mesh_ref[...] = low(state.astype(F32) + dot(summed, update_ref[...]))


def back_local(
    dims, order, gin_ref, slope_ref, slope_k_ref, send_ref, recv_ref, update_ref, senders_ref,
    senders_t_ref, state_ref, rows_ref, summed_ref, merged_ref, merged_r_ref,
    part_ref, out_ref,
):
    nodes = gin_ref.shape[0]
    halo = slope_k_ref.shape[0]
    gin = gin_ref[...]
    gsum = low(dot(gin, update_ref[...], NT))
    grad = gsum.astype(F32)
    place = low(receivers_t(senders_ref[...], halo))
    back = low(receivers(senders_t_ref[...], nodes, halo))
    gpre_k = low(dot(back, gsum) * slope_k_ref[...].astype(F32))
    grecv = dot(place, gpre_k)
    gsent = jnp.zeros(grad.shape, F32)
    for j in range(senders_t_ref.shape[0]):
        gpre = grad * slope_ref[j].astype(F32)
        grecv = grecv + gpre
        spread = low(hot(senders_t_ref[j : j + 1, :] == iota(nodes, nodes, 0)))
        gsent = gsent + dot(spread, low(gpre))
    grecv, gsent = low(grecv), low(gsent)
    part = gin.astype(F32) + dot(grecv, recv_ref[...], NT) + dot(gsent, send_ref[...], NT)
    part_ref[...] = part
    state, merged = state_ref[...], merged_ref[...]
    grad_send = dot(state, gsent, TN) + dot(rows_ref[...], gpre_k, TN)
    store_blocks(out_ref, 0, grad_send, dims, order)
    store_blocks(out_ref, 1, dot(state, grecv, TN), dims, order)
    store_blocks(out_ref, 2, dot(summed_ref[...], gin, TN), dims, order)
    far = low(dot(gpre_k, send_ref[...], NT))
    grad_merge = dot(merged, low(part), TN) + dot(merged_r_ref[...], far, TN)
    store_blocks(out_ref, 3, grad_merge, dims, order)


def embed_back(
    dims, order, arr_ref, slope_r_ref, part_ref, update_ref, send_ref, merge_ref, bounds_ref,
    target_ref, sends_ref, incoming_ref, slope_g_ref, slope_a_ref, grid_ref, lat_ref,
    out_ref, gpre_ref, gpre_a_ref,
):
    nodes = part_ref.shape[0]
    halo = arr_ref.shape[0]
    chosen = grid_ref.shape[0]
    taken = sends_ref.shape[0]
    gsum = low(dot(arr_ref[...], update_ref[...], NT)).astype(F32)
    gpre = low(gsum * slope_r_ref[...].astype(F32))
    border = low(hot(bounds_ref[...] == iota(nodes, halo, 0)))
    gin = low(part_ref[...] + dot(low(dot(border, gpre)), send_ref[...], NT))
    gmerged = low(dot(gin, merge_ref[...], NT))
    sent = jnp.max(hot(sends_ref[...] == iota(taken, chosen, 1)), axis=0, keepdims=True)
    label = jnp.where(sent > 0.0, nodes, target_ref[...])
    pick = low(hot(label == iota(nodes, chosen, 0)))
    gpre_g = low(dot(pick, gmerged, TN) * slope_g_ref[...].astype(F32))
    place = low(hot(incoming_ref[...] == iota(nodes, taken, 0)))
    gpre_a = low(dot(place, gmerged, TN) * slope_a_ref[...].astype(F32))
    grad = dot(grid_ref[...], gpre_g, TN) + dot(lat_ref[...], gpre_a, TN)
    store_blocks(out_ref, 0, grad, dims, order)
    gpre_ref[...] = gpre_g
    gpre_a_ref[...] = gpre_a


def grid_rows(gpre_ref, weight_ref, out_ref):
    out_ref[...] = low(dot(gpre_ref[...], weight_ref[...], NT))


def grid_place(gpre_ref, weight_ref, sends_ref, arr_ref, out_ref):
    chosen = gpre_ref.shape[0]
    taken = sends_ref.shape[1]
    local = dot(gpre_ref[...], weight_ref[...], NT)
    place = low(hot(sends_ref[...] == iota(chosen, taken, 0)))
    out_ref[...] = low(local + dot(place, arr_ref[...]))


def body(
    dims, stages, order,
    grid_latent, mesh_latent, cotangent, embed_weight, merge_weight, send_weight, recv_weight,
    update_weight, target_row, send_rows, incoming_rows, border_mesh_rows, mesh_senders,
):
    chosen, width = grid_latent.shape
    nodes, degree = mesh_senders.shape
    slots, capacity = send_rows.shape[1:]
    halo = slots * BORDER
    taken = slots * capacity
    sends_col = send_rows.reshape(taken, 1)
    sends_row = send_rows.reshape(1, taken)
    incoming = incoming_rows.reshape(1, taken)
    bounds_col = border_mesh_rows.reshape(halo, 1)
    bounds_row = border_mesh_rows.reshape(1, halo)
    targets = target_row.reshape(1, chosen)
    senders_t = mesh_senders.T
    unit = 2 * nodes * width * width

    send0, send1 = send_weight[0], send_weight[1]
    recv0, recv1 = recv_weight[0], recv_weight[1]
    update0, update1 = update_weight[0], update_weight[1]

    (pay1,) = call(
        first_payload, "first_payload", [shape(slots * 24, width)],
        (sends_col, senders_t, grid_latent, cotangent), flops=unit // 2,
    )
    arr1 = exchange(pay1.reshape(slots, 24, width)).reshape(slots * 24, width)
    local, slope_g = call(
        embed_local, "embed_local", [shape(nodes, width, dtype=F32), shape(chosen, width)],
        (grid_latent, embed_weight, targets, sends_col), flops=3 * unit,
    )
    merged, state0, pay2, slope_a, lat_a = call(
        lambda *refs: merge_nodes(slots, *refs), "merge_nodes",
        [shape(nodes, width), shape(nodes, width), shape(slots * 24, width),
         shape(taken, width), shape(taken, width)],
        (arr1, incoming, embed_weight, local, mesh_latent, merge_weight, bounds_col, senders_t),
        flops=2 * unit,
    )
    arr2 = exchange(pay2.reshape(slots, 24, width)).reshape(slots * 24, width)
    total0, slope0, recv_n0, sent_b0 = call(
        forward_local, "forward_local",
        [shape(nodes, width, dtype=F32), shape(degree, nodes, width),
         shape(halo, width, dtype=F32), shape(halo, width)],
        (state0, send0, recv0, mesh_senders, senders_t, bounds_col),
        flops=6 * unit,
    )
    summed0, state1, pay3 = call(
        lambda *refs: forward_halo(slots, *refs), "forward_halo",
        [shape(nodes, width), shape(nodes, width), shape(slots * 16, width)],
        (arr2, recv_n0, total0, state0, send0, update0, mesh_senders, senders_t,
         bounds_col),
        flops=2 * unit,
    )
    arr3 = exchange(pay3.reshape(slots, 16, width)).reshape(slots * 16, width)
    (total1, grecv_l, gsent_l, recv_n1, sent_b1, gsum_n1, gsum_r1, slope_k0, slope_r0, rows0,
     merged_r) = call(
        lambda *refs: turn_local(slots, *refs), "turn_local",
        [shape(nodes, width, dtype=F32), shape(nodes, width, dtype=F32),
         shape(nodes, width, dtype=F32), shape(halo, width, dtype=F32), shape(halo, width),
         shape(halo, width), shape(halo, width), shape(halo, width), shape(halo, width),
         shape(halo, width), shape(halo, width)],
        (state1, send1, recv1, update1, cotangent, arr1, arr2, recv_n0, sent_b0,
         send0, recv0, mesh_senders, senders_t, bounds_col),
        flops=10 * unit,
    )
    summed1, grecv1, gsent1, gin1, pay4 = call(
        lambda *refs: turn_halo(slots, *refs), "turn_halo",
        [shape(nodes, width)] * 4 + [shape(halo, width)],
        (arr3, recv_n1, sent_b1, gsum_n1, gsum_r1, total1, grecv_l, gsent_l, cotangent,
         send1, recv1, mesh_senders, senders_t, bounds_row),
        flops=3 * unit,
    )
    arr4 = exchange(pay4.reshape(slots, BORDER, width)).reshape(halo, width)
    blocks1, mesh_out = call(
        lambda *refs: last_weights(dims, order, *refs), "last_weights",
        [blocks_shape(3, width, width, dims), shape(nodes, width)],
        (state1, summed1, cotangent, grecv1, gsent1, update1),
        flops=4 * unit,
    )
    part0, blocks0 = call(
        lambda *refs: back_local(dims, order, *refs), "back_local",
        [shape(nodes, width, dtype=F32), blocks_shape(4, width, width, dims)],
        (gin1, slope0, slope_k0, send0, recv0, update0, mesh_senders, senders_t,
         state0, rows0, summed0, merged, merged_r),
        flops=10 * unit,
    )
    blocks_e, gpre_g, gpre_a = call(
        lambda *refs: embed_back(dims, order, *refs), "embed_back",
        [blocks_shape(1, width, width, dims), shape(chosen, width), shape(taken, width)],
        (arr4, slope_r0, part0, update0, send0, merge_weight, bounds_row, targets,
         sends_col, incoming, slope_g, slope_a, grid_latent, lat_a),
        flops=6 * unit,
    )
    (back_rows,) = call(
        grid_rows, "grid_rows", [shape(taken, width)], (gpre_a, embed_weight), flops=unit // 2
    )
    arr5 = exchange(back_rows.reshape(slots, capacity, width)).reshape(taken, width)
    (grid_grad,) = call(
        grid_place, "grid_place", [shape(chosen, width)],
        (gpre_g, embed_weight, sends_row, arr5), flops=3 * unit,
    )
    sum1 = scatter_sum(arrange(blocks1, width, dims, order), stages)
    sum0 = scatter_sum(arrange(blocks0, width, dims, order), stages)
    embed_grad = scatter_sum(arrange(blocks_e, width, dims, order), stages)
    depth = embed_grad.shape[0]
    send_grad, recv_grad, update_grad = (
        jnp.stack([sum0[i * depth : (i + 1) * depth], sum1[i * depth : (i + 1) * depth]])
        for i in range(3)
    )
    merge_grad = sum0[3 * depth :]
    return (mesh_out, grid_grad, embed_grad, merge_grad, send_grad, recv_grad, update_grad)


def solution(mesh):
    split = ("groups", "lon", "lat", "sub")
    dims = tuple(mesh.shape[axis] for axis in GROUP)
    stages = (COLUMN, ("lon",))
    order = tuple(GROUP.index(axis) for axes in stages for axis in axes)
    rows = P(split, None)
    whole = P("groups", GROUP, None)
    in_specs = (
        rows, rows, rows, P(), P(), P(), P(), P(), P(split), P(split, None, None),
        P(split, None, None), P(split, None, None), rows,
    )
    out_specs = (rows, rows, rows, rows, whole, whole, whole)
    return jax.shard_map(
        lambda *args: body(dims, stages, order, *args),
        mesh=mesh, in_specs=in_specs, out_specs=out_specs, check_vma=False,
    )
```

```python
import jax
import jax.numpy as jnp
from jax import lax
from jax.experimental import pallas as pl
from jax.experimental.pallas import tpu as pltpu
from jax.sharding import PartitionSpec as P

BF = jnp.bfloat16
F32 = jnp.float32
NN = (((1,), (0,)), ((), ()))
NT = (((1,), (1,)), ((), ()))
TN = (((0,), (0,)), ((), ()))
BORDER = 8
GROUP = ("lon", "lat", "sub")
COLUMN = ("lat", "sub")


def dot(a, b, dims=NN):
    return lax.dot_general(a, b, dims, preferred_element_type=F32)


def low(value):
    return value.astype(BF)


def sigmoid(value):
    return 0.5 * jnp.tanh(0.5 * value) + 0.5


def silu(value):
    return value * sigmoid(value)


def silu_both(value):
    sig = sigmoid(value)
    act = value * sig
    return act, sig + act * (1.0 - sig)


def silu_slope(value):
    return silu_both(value)[1]


def iota(rows, columns, dim):
    return lax.broadcasted_iota(jnp.int32, (rows, columns), dim)


def hot(mask):
    return jnp.where(mask, 1.0, 0.0)


def pieces(value, slots, starts, sizes):
    step = value.shape[0] // slots
    found = []
    for start, size in zip(starts, sizes):
        found.append(
            jnp.concatenate(
                [value[s * step + start : s * step + start + size] for s in range(slots)], axis=0
            )
        )
    return found


def braid(parts, slots):
    rows = []
    for s in range(slots):
        for part in parts:
            size = part.shape[0] // slots
            rows.append(part[s * size : (s + 1) * size])
    return jnp.concatenate(rows, axis=0)


def receivers(senders_t, nodes, halo):
    found = jnp.zeros((halo, nodes), F32)
    ids = iota(halo, nodes, 0) + nodes
    for j in range(senders_t.shape[0]):
        found = found + hot(senders_t[j : j + 1, :] == ids)
    return found


def receivers_t(senders, halo):
    nodes, degree = senders.shape
    found = jnp.zeros((nodes, halo), F32)
    ids = iota(nodes, halo, 1) + nodes
    for j in range(degree):
        found = found + hot(senders[:, j : j + 1] == ids)
    return found


def block_spot(block, dims, halving):
    lon, lat, sub = dims
    if halving:
        spot = 0
        for bit in range((lon * lat * sub - 1).bit_length()):
            spot = 2 * spot + (block >> bit) % 2
        return spot
    return (block % sub * lat + block // sub % lat) * lon + block // (lat * sub)


def store_blocks(ref, at, value, dims, halving):
    value = low(value)
    rows = value.shape[0]
    total = dims[0] * dims[1] * dims[2]
    depth = rows // total
    if depth % 16:
        ref[at] = value
        return
    for block in range(total):
        spot = block_spot(block, dims, halving)
        part = value[block * depth : (block + 1) * depth]
        if halving:
            half = total // 2
            start = spot % half * (ref.shape[1] // half) + at * depth
            ref[spot // half, start : start + depth, :] = part
        else:
            ref[spot, at * depth : (at + 1) * depth, :] = part


def fine(rows, dims):
    return (rows // (dims[0] * dims[1] * dims[2])) % 16 == 0


def blocks_shape(count, rows, width, dims):
    total = dims[0] * dims[1] * dims[2]
    if fine(rows, dims):
        return jax.ShapeDtypeStruct((total, count * rows // total, width), BF)
    return jax.ShapeDtypeStruct((count, rows, width), BF)


def scatter_offload(blocks, rows, dims):
    lon, lat, sub = dims
    if not fine(rows, dims):
        count, _, width = blocks.shape
        depth = rows // (lon * lat * sub)
        blocks = blocks.reshape(count, lon, lat, sub, depth, width)
        blocks = blocks.transpose(3, 2, 1, 0, 4, 5)
    blocks = blocks.reshape(sub, lat, lon, -1, blocks.shape[-1])
    for axis in ("sub", "lat", "lon"):
        blocks = lax.psum_scatter(blocks, axis, scatter_dimension=0, tiled=False)
    return blocks


def swap(block, bit, dims):
    total = dims[0] * dims[1] * dims[2]
    return lax.ppermute(block, GROUP, [(i, i ^ (1 << bit)) for i in range(total)])


def call(kernel, name, outs, args, flops, me=None, scratch=()):
    size = sum(a.size * a.dtype.itemsize for a in (*args, *outs))
    in_specs = [pl.BlockSpec(memory_space=pltpu.VMEM)] * len(args)
    if me is not None:
        args = (me, *args)
        in_specs = [pl.BlockSpec(memory_space=pltpu.SMEM)] + in_specs
    return pl.pallas_call(
        kernel,
        out_shape=list(outs),
        in_specs=in_specs,
        out_specs=[pl.BlockSpec(memory_space=pltpu.VMEM)] * len(outs),
        scratch_shapes=list(scratch),
        compiler_params=pltpu.CompilerParams(vmem_limit_bytes=16 * 1024 * 1024),
        cost_estimate=pl.CostEstimate(flops=flops, bytes_accessed=size, transcendentals=0),
        name=name,
    )(*args)


def exchange(parts, dims):
    column = dims[1] * dims[2]
    count = dims[0]
    forward = [(i, (i + 1) % count) for i in range(count)]
    backward = [(target, source) for source, target in forward]
    arrived = [
        lax.ppermute(parts[r - 1], COLUMN, [(i, i ^ r) for i in range(column)])
        for r in range(1, column)
    ]
    to_left, to_right = parts[column - 1 :]
    from_right = lax.ppermute(to_left, "lon", backward)
    from_left = lax.ppermute(to_right, "lon", forward)
    return (*arrived, from_left, from_right)


def slot_of(me, at, column):
    return jnp.bitwise_xor(me, at + 1) if at + 1 < column else at + 1


def spread(me, value, buf, refs):
    column = len(refs) - 1
    rows = refs[0].shape[0]
    buf[...] = value
    for at, ref in enumerate(refs):
        start = pl.multiple_of(slot_of(me, at, column) * rows, 8)
        ref[...] = low(buf[pl.ds(start, rows), :])


def collect(me, refs, buf):
    column = len(refs) - 1
    rows = refs[0].shape[0]
    buf[pl.ds(pl.multiple_of(me * rows, 8), rows), :] = jnp.zeros((rows, buf.shape[1]), F32)
    for at, ref in enumerate(refs):
        start = pl.multiple_of(slot_of(me, at, column) * rows, 8)
        buf[pl.ds(start, rows), :] = ref[...].astype(F32)
    return buf[...]


def shape(*dims, dtype=BF):
    return jax.ShapeDtypeStruct(dims, dtype)


def first_payload(me_ref, sends_ref, senders_t_ref, grid_ref, cot_ref, *rest):
    *out_refs, buf = rest
    taken = sends_ref.shape[0]
    chosen, nodes = grid_ref.shape[0], cot_ref.shape[0]
    slots = taken // 16
    rows = dot(low(hot(sends_ref[...] == iota(taken, chosen, 1))), grid_ref[...])
    back = low(receivers(senders_t_ref[...], nodes, slots * BORDER))
    spread(me_ref[0], braid([rows, dot(back, cot_ref[...])], slots), buf, out_refs)


def embed_local(grid_ref, weight_ref, target_ref, sends_ref, sum_ref, slope_ref):
    chosen = grid_ref.shape[0]
    nodes = sum_ref.shape[0]
    taken = sends_ref.shape[0]
    pre = dot(grid_ref[...], weight_ref[...])
    act, slope = silu_both(pre)
    slope_ref[...] = low(slope)
    sent = jnp.max(hot(sends_ref[...] == iota(taken, chosen, 1)), axis=0, keepdims=True)
    label = jnp.where(sent > 0.0, nodes, target_ref[...])
    sum_ref[...] = dot(low(hot(label == iota(nodes, chosen, 0))), low(act))


def merge_nodes(slots, me_ref, *refs):
    arr_refs, refs = refs[: slots - 1], refs[slots - 1 :]
    (incoming_ref, embed_ref, local_ref, mesh_ref, weight_ref, bounds_ref, senders_t_ref,
     merged_ref, state_ref, slope_ref, lat_ref, cot_ref, *pay_refs, buf) = refs
    me = me_ref[0]
    nodes = mesh_ref.shape[0]
    taken = incoming_ref.shape[1]
    halo = slots * BORDER
    lat, cot = pieces(collect(me, arr_refs, buf), slots, (0, 16), (16, BORDER))
    cot_ref[...] = low(cot)
    lat = low(lat)
    lat_ref[...] = lat
    act, slope = silu_both(dot(lat, embed_ref[...]))
    slope_ref[...] = low(slope)
    place = low(hot(incoming_ref[...] == iota(nodes, taken, 0)))
    merged = low(local_ref[...] + dot(place, low(act)))
    merged_ref[...] = merged
    state = low(mesh_ref[...].astype(F32) + dot(merged, weight_ref[...]))
    state_ref[...] = state
    border = hot(bounds_ref[...] == iota(halo, nodes, 1))
    back = receivers(senders_t_ref[...], nodes, halo)
    pick = low(braid([border, back], slots))
    rows = pieces(dot(pick, state), slots, (0, BORDER), (BORDER, BORDER))
    spread(me, braid([*rows, dot(low(border), merged)], slots), buf, pay_refs)


def local_edges(senders, sent, recv, each):
    nodes, degree = senders.shape
    total = jnp.zeros(recv.shape, F32)
    ids = iota(nodes, nodes, 1)
    for j in range(degree):
        named = senders[:, j : j + 1]
        act, slope = silu_both(dot(low(hot(named == ids)), sent) + recv)
        keep = hot(named < nodes)
        total = total + act * keep
        each(j, slope * keep)
    return total


def forward_local(
    state_ref, send_ref, recv_ref, senders_ref, senders_t_ref, bounds_ref,
    total_ref, slope_ref, recv_n_ref, sent_b_ref,
):
    state = state_ref[...]
    nodes = state.shape[0]
    halo = bounds_ref.shape[0]
    sent = low(dot(state, send_ref[...]))
    recv = dot(state, recv_ref[...])

    def keep(j, slope):
        slope_ref[j] = low(slope)

    total_ref[...] = local_edges(senders_ref[...], sent, recv, keep)
    back = low(receivers(senders_t_ref[...], nodes, halo))
    recv_n_ref[...] = dot(low(dot(back, state)), recv_ref[...])
    sent_b_ref[...] = low(dot(low(hot(bounds_ref[...] == iota(halo, nodes, 1))), sent))


def forward_halo(slots, me_ref, *refs):
    arr_refs, refs = refs[: slots - 1], refs[slots - 1 :]
    (recv_n_ref, total_ref, state_ref, send_ref, update_ref, senders_ref, senders_t_ref,
     bounds_ref, summed_ref, out_ref, pre_ref, rows_ref, back_ref, merged_ref, *pay_refs, buf,
     out_buf) = refs
    me = me_ref[0]
    nodes = state_ref.shape[0]
    halo = slots * BORDER
    rows, back, merged = pieces(
        collect(me, arr_refs, buf), slots, (0, BORDER, 2 * BORDER), (BORDER,) * 3
    )
    rows_ref[...], back_ref[...], merged_ref[...] = low(rows), low(back), low(merged)
    pre = low(dot(low(rows), send_ref[...])).astype(F32) + recv_n_ref[...]
    pre_ref[...] = pre
    place = low(receivers_t(senders_ref[...], halo))
    summed = low(total_ref[...] + dot(place, low(silu(pre))))
    summed_ref[...] = summed
    state = low(state_ref[...].astype(F32) + dot(summed, update_ref[...]))
    out_ref[...] = state
    border = hot(bounds_ref[...] == iota(halo, nodes, 1))
    back = receivers(senders_t_ref[...], nodes, halo)
    spread(me, dot(low(braid([border, back], slots)), state), out_buf, pay_refs)


def turn_local(
    slots, state_ref, send_ref, recv_ref, update_ref, cot_ref, cot_r_ref, pre_ref, back0_ref,
    sent_b0_ref, recv0_ref, senders_ref, senders_t_ref, bounds_ref,
    total_ref, grecv_ref, gsent_ref, recv_n_ref, sent_b_ref, gsum_n_ref, gsum_r_ref,
    slope_k_ref, slope_r_ref,
):
    halo = slots * BORDER
    slope_k_ref[...] = low(silu_slope(pre_ref[...]))
    pre = sent_b0_ref[...].astype(F32) + dot(back0_ref[...], recv0_ref[...])
    slope_r_ref[...] = low(silu_slope(pre))
    state = state_ref[...]
    nodes = state.shape[0]
    sent = low(dot(state, send_ref[...]))
    recv = dot(state, recv_ref[...])
    gsum = low(dot(cot_ref[...], update_ref[...], NT))
    grad = gsum.astype(F32)
    grecv_ref[...] = jnp.zeros(grecv_ref.shape, F32)
    gsent_ref[...] = jnp.zeros(gsent_ref.shape, F32)

    def back_edge(j, slope):
        gpre = grad * slope
        grecv_ref[...] += gpre
        place = low(hot(senders_t_ref[j : j + 1, :] == iota(nodes, nodes, 0)))
        gsent_ref[...] += dot(place, low(gpre))

    total_ref[...] = local_edges(senders_ref[...], sent, recv, back_edge)
    back = low(receivers(senders_t_ref[...], nodes, halo))
    recv_n_ref[...] = dot(low(dot(back, state)), recv_ref[...])
    sent_b_ref[...] = low(dot(low(hot(bounds_ref[...] == iota(halo, nodes, 1))), sent))
    gsum_n_ref[...] = low(dot(back, gsum))
    gsum_r_ref[...] = low(dot(cot_r_ref[...], update_ref[...], NT))


def turn_halo(slots, me_ref, *refs):
    arr_refs, refs = refs[: slots - 1], refs[slots - 1 :]
    (recv_n_ref, sent_b_ref, gsum_n_ref, gsum_r_ref, total_ref, grecv_ref, gsent_ref, cot_ref,
     send_ref, recv_ref, senders_ref, senders_t_ref, bounds_ref, summed_ref, grecv_out_ref,
     gsent_out_ref, gin_ref, *pay_refs, buf, out_buf) = refs
    me = me_ref[0]
    nodes = cot_ref.shape[0]
    halo = slots * BORDER
    rows, back = pieces(collect(me, arr_refs, buf), slots, (0, BORDER), (BORDER,) * 2)
    pre = low(dot(low(rows), send_ref[...])).astype(F32) + recv_n_ref[...]
    act, slope = silu_both(pre)
    place = low(receivers_t(senders_ref[...], halo))
    gpre = low(gsum_n_ref[...].astype(F32) * slope)
    grecv = low(grecv_ref[...] + dot(place, gpre))
    pre = sent_b_ref[...].astype(F32) + dot(low(back), recv_ref[...])
    gpre = low(gsum_r_ref[...].astype(F32) * silu_slope(pre))
    border = low(hot(bounds_ref[...] == iota(nodes, halo, 0)))
    gsent = low(gsent_ref[...] + dot(border, gpre))
    gin = cot_ref[...].astype(F32) + dot(grecv, recv_ref[...], NT) + dot(gsent, send_ref[...], NT)
    gin = low(gin)
    gin_ref[...] = gin
    spread(me, dot(low(receivers(senders_t_ref[...], nodes, halo)), gin), out_buf, pay_refs)
    summed_ref[...] = low(total_ref[...] + dot(place, low(act)))
    grecv_out_ref[...] = grecv
    gsent_out_ref[...] = gsent


def last_weights(
    dims, state_ref, summed_ref, cot_ref, grecv_ref, gsent_ref, update_ref, out_ref, mesh_ref
):
    state, summed = state_ref[...], summed_ref[...]
    store_blocks(out_ref, 0, dot(state, gsent_ref[...], TN), dims, False)
    store_blocks(out_ref, 1, dot(state, grecv_ref[...], TN), dims, False)
    store_blocks(out_ref, 2, dot(summed, cot_ref[...], TN), dims, False)
    mesh_ref[...] = low(state.astype(F32) + dot(summed, update_ref[...]))


def back_local(
    dims, gin_ref, slope_ref, slope_k_ref, send_ref, recv_ref, update_ref, senders_ref,
    senders_t_ref, part_ref, gpre_out_ref, grecv_out_ref, gsent_out_ref,
):
    nodes = gin_ref.shape[0]
    halo = slope_k_ref.shape[0]
    gin = gin_ref[...]
    gsum = low(dot(gin, update_ref[...], NT))
    grad = gsum.astype(F32)
    place = low(receivers_t(senders_ref[...], halo))
    back = low(receivers(senders_t_ref[...], nodes, halo))
    gpre_k = low(dot(back, gsum) * slope_k_ref[...].astype(F32))
    grecv = dot(place, gpre_k)
    gsent = jnp.zeros(grad.shape, F32)
    for j in range(senders_t_ref.shape[0]):
        gpre = grad * slope_ref[j].astype(F32)
        grecv = grecv + gpre
        target = low(hot(senders_t_ref[j : j + 1, :] == iota(nodes, nodes, 0)))
        gsent = gsent + dot(target, low(gpre))
    grecv, gsent = low(grecv), low(gsent)
    part = gin.astype(F32) + dot(grecv, recv_ref[...], NT) + dot(gsent, send_ref[...], NT)
    part_ref[...] = part
    gpre_out_ref[...], grecv_out_ref[...], gsent_out_ref[...] = gpre_k, grecv, gsent


def embed_back(slots, dims, me_ref, *refs):
    arr_refs, refs = refs[: slots - 1], refs[slots - 1 :]
    (slope_r_ref, part_ref, update_ref, send_ref, merge_ref, bounds_ref, target_ref, sends_ref,
     incoming_ref, slope_g_ref, slope_a_ref, grid_ref, lat_ref, embed_ref, state_ref, rows_ref,
     gpre_k_ref, gsent_ref, grecv_ref, summed_ref, gin1_ref, merged_ref, merged_r_ref,
     gpre_ref, keep_ref, give_ref, *pay_refs, buf, out_buf, blocks) = refs
    me = me_ref[0]
    nodes = part_ref.shape[0]
    halo = slots * BORDER
    chosen = grid_ref.shape[0]
    taken = sends_ref.shape[0]
    gsum = low(dot(low(collect(me, arr_refs, buf)), update_ref[...], NT)).astype(F32)
    gpre = low(gsum * slope_r_ref[...].astype(F32))
    border = low(hot(bounds_ref[...] == iota(nodes, halo, 0)))
    gsent_r = low(dot(border, gpre))
    gin = low(part_ref[...] + dot(gsent_r, send_ref[...], NT))
    gmerged = low(dot(gin, merge_ref[...], NT))
    place = low(hot(incoming_ref[...] == iota(nodes, taken, 0)))
    gpre_a = low(dot(place, gmerged, TN) * slope_a_ref[...].astype(F32))
    spread(me, dot(gpre_a, embed_ref[...], NT), out_buf, pay_refs)
    sent = jnp.max(hot(sends_ref[...] == iota(taken, chosen, 1)), axis=0, keepdims=True)
    label = jnp.where(sent > 0.0, nodes, target_ref[...])
    pick = low(hot(label == iota(nodes, chosen, 0)))
    gpre_g = low(dot(pick, gmerged, TN) * slope_g_ref[...].astype(F32))
    gpre_ref[...] = gpre_g
    state = state_ref[...]
    grad_embed = dot(grid_ref[...], gpre_g, TN) + dot(lat_ref[...], gpre_a, TN)
    store_blocks(blocks, 0, grad_embed, dims, True)
    store_blocks(blocks, 1, dot(merged_ref[...], gin, TN), dims, True)
    grad_send = dot(state, gsent_ref[...], TN) + dot(rows_ref[...], gpre_k_ref[...], TN)
    store_blocks(blocks, 2, grad_send, dims, True)
    store_blocks(blocks, 3, dot(state, grecv_ref[...], TN), dims, True)
    store_blocks(blocks, 4, dot(summed_ref[...], gin1_ref[...], TN), dims, True)
    if not fine(grid_ref.shape[1], dims):
        keep_ref[...] = blocks[...]
        return
    mine = me_ref[1] % 2
    keep_ref[...] = blocks[mine]
    give_ref[...] = blocks[1 - mine]


def halve(bit, me_ref, keep_ref, arr_ref, keep_out, give_out):
    half = keep_ref.shape[0] // 2
    mine = jnp.bitwise_and(jnp.right_shift(me_ref[1], bit), 1)
    for out, side in ((keep_out, mine), (give_out, 1 - mine)):
        rows = pl.ds(pl.multiple_of(side * half, 16), half)
        out[...] = low(keep_ref[rows, :].astype(F32) + arr_ref[rows, :].astype(F32))


def finish(
    keep_ref, arr_ref, last_ref, embed_ref, merge_ref, send_ref, recv_ref, update_ref
):
    total = keep_ref[...].astype(F32) + arr_ref[...].astype(F32)
    depth = embed_ref.shape[0]
    embed_ref[...] = total[:depth]
    merge_ref[...] = total[depth : 2 * depth]
    for at, ref in enumerate((send_ref, recv_ref, update_ref)):
        ref[0] = total[(at + 2) * depth : (at + 3) * depth]
        ref[1] = last_ref[at * depth : (at + 1) * depth, :].astype(F32)


def grid_place(slots, me_ref, *refs):
    arr_refs, refs = refs[: slots - 1], refs[slots - 1 :]
    gpre_ref, weight_ref, sends_ref, out_ref, buf = refs
    chosen = gpre_ref.shape[0]
    taken = sends_ref.shape[1]
    local = dot(gpre_ref[...], weight_ref[...], NT)
    place = low(hot(sends_ref[...] == iota(chosen, taken, 0)))
    out_ref[...] = low(local + dot(place, low(collect(me_ref[0], arr_refs, buf))))


def body(
    dims,
    grid_latent, mesh_latent, cotangent, embed_weight, merge_weight, send_weight, recv_weight,
    update_weight, target_row, send_rows, incoming_rows, border_mesh_rows, mesh_senders,
):
    chosen, width = grid_latent.shape
    nodes, degree = mesh_senders.shape
    slots, capacity = send_rows.shape[1:]
    peers = slots - 1
    halo = slots * BORDER
    taken = slots * capacity
    sends_col = send_rows.reshape(taken, 1)
    sends_row = send_rows.reshape(1, taken)
    incoming = incoming_rows.reshape(1, taken)
    bounds_col = border_mesh_rows.reshape(halo, 1)
    bounds_row = border_mesh_rows.reshape(1, halo)
    targets = target_row.reshape(1, chosen)
    senders_t = mesh_senders.T
    send0, send1 = send_weight[0], send_weight[1]
    recv0, recv1 = recv_weight[0], recv_weight[1]
    update0, update1 = update_weight[0], update_weight[1]
    me = jnp.stack([lax.axis_index(COLUMN), lax.axis_index(GROUP)]).astype(jnp.int32)
    unit = 2 * nodes * width * width

    def buffer(rows):
        return pltpu.VMEM((slots * rows, width), F32)

    pay1 = call(
        first_payload, "first_payload", [shape(24, width)] * peers,
        (sends_col, senders_t, grid_latent, cotangent), flops=unit // 2, me=me,
        scratch=[buffer(24)],
    )
    arr1 = exchange(pay1, dims)
    local, slope_g = call(
        embed_local, "embed_local", [shape(nodes, width, dtype=F32), shape(chosen, width)],
        (grid_latent, embed_weight, targets, sends_col), flops=3 * unit,
    )
    merged, state0, slope_a, lat_a, cot_r, *pay2 = call(
        lambda *refs: merge_nodes(slots, *refs), "merge_nodes",
        [shape(nodes, width), shape(nodes, width), shape(taken, width), shape(taken, width),
         shape(halo, width)] + [shape(24, width)] * peers,
        (*arr1, incoming, embed_weight, local, mesh_latent, merge_weight, bounds_col, senders_t),
        flops=2 * unit, me=me, scratch=[buffer(24)],
    )
    arr2 = exchange(pay2, dims)
    total0, slope0, recv_n0, sent_b0 = call(
        forward_local, "forward_local",
        [shape(nodes, width, dtype=F32), shape(degree, nodes, width),
         shape(halo, width, dtype=F32), shape(halo, width)],
        (state0, send0, recv0, mesh_senders, senders_t, bounds_col), flops=6 * unit,
    )
    summed0, state1, pre0, rows0, back0, merged_r, *pay3 = call(
        lambda *refs: forward_halo(slots, *refs), "forward_halo",
        [shape(nodes, width), shape(nodes, width), shape(halo, width, dtype=F32)]
        + [shape(halo, width)] * 3 + [shape(16, width)] * peers,
        (*arr2, recv_n0, total0, state0, send0, update0, mesh_senders, senders_t, bounds_col),
        flops=2 * unit, me=me, scratch=[buffer(24), buffer(16)],
    )
    arr3 = exchange(pay3, dims)
    (total1, grecv_l, gsent_l, recv_n1, sent_b1, gsum_n1, gsum_r1, slope_k0, slope_r0) = call(
        lambda *refs: turn_local(slots, *refs), "turn_local",
        [shape(nodes, width, dtype=F32)] * 3 + [shape(halo, width, dtype=F32)]
        + [shape(halo, width)] * 5,
        (state1, send1, recv1, update1, cotangent, cot_r, pre0, back0, sent_b0, recv0,
         mesh_senders, senders_t, bounds_col),
        flops=10 * unit,
    )
    summed1, grecv1, gsent1, gin1, *pay4 = call(
        lambda *refs: turn_halo(slots, *refs), "turn_halo",
        [shape(nodes, width)] * 4 + [shape(BORDER, width)] * peers,
        (*arr3, recv_n1, sent_b1, gsum_n1, gsum_r1, total1, grecv_l, gsent_l, cotangent,
         send1, recv1, mesh_senders, senders_t, bounds_row),
        flops=3 * unit, me=me, scratch=[buffer(16), buffer(BORDER)],
    )
    arr4 = exchange(pay4, dims)
    blocks1, mesh_out = call(
        lambda *refs: last_weights(dims, *refs), "last_weights",
        [blocks_shape(3, width, width, dims), shape(nodes, width)],
        (state1, summed1, cotangent, grecv1, gsent1, update1), flops=4 * unit,
    )
    sum1 = scatter_offload(blocks1, width, dims)
    part0, gpre_k, grecv0, gsent0 = call(
        lambda *refs: back_local(dims, *refs), "back_local",
        [shape(nodes, width, dtype=F32), shape(halo, width), shape(nodes, width),
         shape(nodes, width)],
        (gin1, slope0, slope_k0, send0, recv0, update0, mesh_senders, senders_t),
        flops=6 * unit,
    )
    total = dims[0] * dims[1] * dims[2]
    depth = width // total
    if fine(width, dims):
        scratch = pltpu.VMEM((2, total // 2 * 5 * depth, width), BF)
        given = [shape(total // 2 * 5 * depth, width)] * 2
    else:
        scratch = pltpu.VMEM((5, width, width), BF)
        given = [shape(5, width, width), shape(16, width)]
    gpre_g, keep, give, *pay5 = call(
        lambda *refs: embed_back(slots, dims, *refs), "embed_back",
        [shape(chosen, width), *given] + [shape(capacity, width)] * peers,
        (*arr4, slope_r0, part0, update0, send0, merge_weight, bounds_row, targets,
         sends_col, incoming, slope_g, slope_a, grid_latent, lat_a, embed_weight, state0, rows0,
         gpre_k, gsent0, grecv0, summed0, gin1, merged, merged_r),
        flops=10 * unit, me=me, scratch=[buffer(BORDER), buffer(capacity), scratch],
    )
    arr5 = exchange(pay5, dims)
    (grid_grad,) = call(
        lambda *refs: grid_place(slots, *refs), "grid_place", [shape(chosen, width)],
        (*arr5, gpre_g, embed_weight, sends_row), flops=3 * unit, me=me,
        scratch=[buffer(capacity)],
    )
    if not fine(width, dims):
        sum0 = scatter_offload(keep, width, dims).astype(F32)
        sum1 = sum1.astype(F32)
        parts = [sum0[i * depth : (i + 1) * depth] for i in range(5)]
        stacked = [
            jnp.stack([parts[i + 2], sum1[i * depth : (i + 1) * depth]]) for i in range(3)
        ]
        return (mesh_out, grid_grad, parts[0], parts[1], *stacked)
    bits = (total - 1).bit_length()
    arrived = swap(give, 0, dims)
    for bit in range(1, bits):
        rows = keep.shape[0] // 2
        keep, give = call(
            lambda *refs: halve(bit, *refs), "halve", [shape(rows, width)] * 2, (keep, arrived),
            flops=4 * rows * width, me=me,
        )
        arrived = swap(give, bit, dims)
    grads = call(
        finish, "finish",
        [shape(depth, width, dtype=F32)] * 2 + [shape(2, depth, width, dtype=F32)] * 3,
        (keep, arrived, sum1), flops=5 * depth * width,
    )
    return (mesh_out, grid_grad, *grads)


def solution(mesh):
    split = ("groups", "lon", "lat", "sub")
    dims = tuple(mesh.shape[axis] for axis in GROUP)
    rows = P(split, None)
    whole = P("groups", GROUP, None)
    in_specs = (
        rows, rows, rows, P(), P(), P(), P(), P(), P(split), P(split, None, None),
        P(split, None, None), P(split, None, None), rows,
    )
    out_specs = (rows, rows, rows, rows, whole, whole, whole)
    return jax.shard_map(
        lambda *args: body(dims, *args),
        mesh=mesh, in_specs=in_specs, out_specs=out_specs, check_vma=False,
    )
```

```python
import jax
import jax.numpy as jnp
from jax import lax
from jax.experimental import pallas as pl
from jax.experimental.pallas import tpu as pltpu
from jax.sharding import PartitionSpec as P

BF = jnp.bfloat16
F32 = jnp.float32
I32 = jnp.int32
NN = (((1,), (0,)), ((), ()))
NT = (((1,), (1,)), ((), ()))
TN = (((0,), (0,)), ((), ()))
BORDER = 8
GROUP = ("lon", "lat", "sub")
COLUMN = ("lat", "sub")


def dot(a, b, dims=NN):
    return lax.dot_general(a, b, dims, preferred_element_type=F32)


def low(value):
    return value.astype(BF)


def sigmoid(value):
    return 0.5 * jnp.tanh(0.5 * value) + 0.5


def silu(value):
    return value * sigmoid(value)


def silu_both(value):
    sig = sigmoid(value)
    act = value * sig
    return act, sig + act * (1.0 - sig)


def silu_slope(value):
    return silu_both(value)[1]


def iota(rows, columns, dim):
    return lax.broadcasted_iota(I32, (rows, columns), dim)


def hot(mask):
    return jnp.where(mask, 1.0, 0.0)


def slot_of(at, column, me, odd):
    far = jnp.where(at == column - 1, column + 1 - odd, column + odd)
    return jnp.where(at < column - 1, jnp.bitwise_xor(at + 1, me), far)


def as_column(values, wide, column, me, odd):
    slots = values.shape[0]
    count = (slots - 1) * wide
    row = iota(count, slots, 0)
    pick = low(hot(slot_of(row // wide, column, me, odd) == iota(count, slots, 1)))
    found = 16.0 * dot(pick, low((values // 16).astype(F32)))
    found = found + dot(pick, low((values % 16).astype(F32)))
    keep = iota(count, wide, 0) % wide == iota(count, wide, 1)
    return jnp.sum(jnp.where(keep, found, 0.0), axis=1, keepdims=True).astype(I32)


def as_row(values, wide, column, me, odd):
    slots = values.shape[0]
    count = (slots - 1) * wide
    pick = low(hot(iota(wide, count, 1) % wide == iota(wide, count, 0)))
    found = 16.0 * dot(low((values // 16).astype(F32)), pick)
    found = found + dot(low((values % 16).astype(F32)), pick)
    at = iota(slots, count, 1) // wide
    keep = slot_of(at, column, me, odd) == iota(slots, count, 0)
    return jnp.sum(jnp.where(keep, found, 0.0), axis=0, keepdims=True).astype(I32)


def split_parts(refs, starts, sizes):
    values = [ref[...].astype(F32) for ref in refs]
    return [
        jnp.concatenate([value[start : start + size] for value in values], axis=0)
        for start, size in zip(starts, sizes)
    ]


def store_parts(refs, parts):
    peers = len(refs)
    for at, ref in enumerate(refs):
        rows = []
        for part in parts:
            size = part.shape[0] // peers
            rows.append(part[at * size : (at + 1) * size])
        ref[...] = low(rows[0] if len(rows) == 1 else jnp.concatenate(rows, axis=0))


def receivers(senders_t, halo):
    degree, nodes = senders_t.shape
    found = jnp.zeros((halo, nodes), F32)
    ids = iota(halo, nodes, 0) + nodes
    for j in range(degree):
        found = found + hot(senders_t[j : j + 1, :] == ids)
    return found


def receivers_t(senders, degree, halo):
    nodes = senders.shape[0]
    found = jnp.zeros((nodes, halo), F32)
    ids = iota(nodes, halo, 1) + nodes
    for j in range(degree):
        found = found + hot(senders[:, j : j + 1] == ids)
    return found


def fine(rows, dims):
    return (rows // (dims[0] * dims[1] * dims[2])) % 16 == 0


def reverse_bits(block, bits):
    spot = 0
    for bit in range(bits):
        spot = 2 * spot + (block >> bit) % 2
    return spot


def store_blocks(keep_ref, give_ref, at, count, value, dims, bits_ref):
    value = low(value)
    rows = value.shape[0]
    total = dims[0] * dims[1] * dims[2]
    depth = rows // total
    if not fine(rows, dims):
        keep_ref[at] = value
        return
    bits = (total - 1).bit_length()
    upper = bits_ref[0:1, 2:3] == 1
    for block in range(0, total, 2):
        start = reverse_bits(block, bits) * count * depth + at * depth
        first = value[block * depth : (block + 1) * depth].astype(F32)
        second = value[(block + 1) * depth : (block + 2) * depth].astype(F32)
        keep_ref[start : start + depth, :] = low(jnp.where(upper, second, first))
        give_ref[start : start + depth, :] = low(jnp.where(upper, first, second))


def blocks_shapes(count, rows, width, dims):
    if fine(rows, dims):
        return [jax.ShapeDtypeStruct((count * rows // 2, width), BF)] * 2
    return [jax.ShapeDtypeStruct((count, rows, width), BF), jax.ShapeDtypeStruct((16, width), BF)]


def halve(bit, bits_ref, keep_ref, arr_ref, keep_out, give_out):
    half = keep_ref.shape[0] // 2
    upper = bits_ref[0:1, 2 + bit : 3 + bit] == 1
    first = keep_ref[:half, :].astype(F32) + arr_ref[:half, :].astype(F32)
    second = keep_ref[half:, :].astype(F32) + arr_ref[half:, :].astype(F32)
    keep_out[...] = low(jnp.where(upper, second, first))
    give_out[...] = low(jnp.where(upper, first, second))


def swap(block, bit, dims):
    total = dims[0] * dims[1] * dims[2]
    return lax.ppermute(block, GROUP, [(i, i ^ (1 << bit)) for i in range(total)])


def scatter_halving(keep, give, place, dims):
    width = keep.shape[1]
    bits = (dims[0] * dims[1] * dims[2] - 1).bit_length()
    arrived = swap(give, 0, dims)
    for bit in range(1, bits):
        rows = keep.shape[0] // 2
        keep, give = call(
            lambda *refs: halve(bit, *refs), "halve", [shape(rows, width)] * 2,
            (place, keep, arrived), flops=4 * rows * width,
        )
        arrived = swap(give, bit, dims)
    return keep, arrived


def scatter_plain(blocks, dims):
    lon, lat, sub = dims
    count, rows, width = blocks.shape
    depth = rows // (lon * lat * sub)
    blocks = blocks.reshape(count, lon, lat, sub, depth, width)
    blocks = blocks.transpose(3, 2, 1, 0, 4, 5)
    for axis in ("sub", "lat", "lon"):
        blocks = lax.psum_scatter(blocks, axis, scatter_dimension=0, tiled=False)
    return blocks.astype(F32)


def call(kernel, name, outs, args, flops):
    size = sum(a.size * a.dtype.itemsize for a in (*args, *outs))
    return pl.pallas_call(
        kernel,
        out_shape=list(outs),
        in_specs=[pl.BlockSpec(memory_space=pltpu.VMEM)] * len(args),
        out_specs=[pl.BlockSpec(memory_space=pltpu.VMEM)] * len(outs),
        compiler_params=pltpu.CompilerParams(vmem_limit_bytes=16 * 1024 * 1024),
        cost_estimate=pl.CostEstimate(flops=flops, bytes_accessed=size, transcendentals=0),
        name=name,
    )(*args)


def exchange(parts, dims):
    column = dims[1] * dims[2]
    count = dims[0]
    arrived = [
        lax.ppermute(parts[r - 1], COLUMN, [(i, i ^ r) for i in range(column)])
        for r in range(1, column)
    ]
    near = lax.ppermute(parts[column - 1], "lon", [(i, i ^ 1) for i in range(count)])
    other = [(i, (i - 1 + 2 * (i % 2)) % count) for i in range(count)]
    far = lax.ppermute(parts[column], "lon", other)
    return (*arrived, near, far)


def shape(*dims, dtype=BF):
    return jax.ShapeDtypeStruct(dims, dtype)


def first_payload(column, capacity, ints_ref, grid_ref, sends_ref, *pay_refs):
    chosen = grid_ref.shape[0]
    ints = ints_ref[...]
    base = 2 * capacity + BORDER
    me, odd = ints[0:1, base : base + 1], ints[0:1, base + 1 : base + 2]
    sends = as_column(ints[:, :capacity], capacity, column, me, odd)
    sends_ref[...] = sends
    rows = dot(low(hot(sends == iota(sends.shape[0], chosen, 1))), grid_ref[...])
    store_parts(pay_refs, [rows])


def embed_local(
    column, capacity, ints_ref, senders_ref, grid_ref, weight_ref, target_ref, sends_ref,
    sum_ref, slope_ref, sends_row_ref, incoming_ref, bounds_ref, bounds_row_ref, senders_t_ref,
    senders_out_ref, place_ref,
):
    chosen = grid_ref.shape[0]
    nodes = sum_ref.shape[0]
    taken = sends_ref.shape[0]
    act, slope = silu_both(dot(grid_ref[...], weight_ref[...]))
    slope_ref[...] = low(slope)
    sent = jnp.max(hot(sends_ref[...] == iota(taken, chosen, 1)), axis=0, keepdims=True)
    label = jnp.where(sent > 0.0, nodes, target_ref[...])
    sum_ref[...] = dot(low(hot(label == iota(nodes, chosen, 0))), low(act))
    ints = ints_ref[...]
    base = 2 * capacity + BORDER
    place_ref[...] = ints[:, base:]
    me, odd = ints[0:1, base : base + 1], ints[0:1, base + 1 : base + 2]
    sends, incoming = ints[:, :capacity], ints[:, capacity : 2 * capacity]
    bounds = ints[:, 2 * capacity : base]
    sends_row_ref[...] = as_row(sends, capacity, column, me, odd)
    incoming_ref[...] = as_row(incoming, capacity, column, me, odd)
    bounds_ref[...] = as_column(bounds, BORDER, column, me, odd)
    bounds_row_ref[...] = as_row(bounds, BORDER, column, me, odd)
    senders = senders_ref[...]
    degree = senders.shape[0]
    offset = senders - nodes
    slot = offset // BORDER
    far = jnp.where(slot == column, column - odd, column - 1 + odd)
    at = jnp.where(slot < column, jnp.bitwise_xor(slot, me) - 1, far)
    senders = jnp.where(offset < 0, senders, nodes + at * BORDER + offset % BORDER)
    senders_t_ref[...] = senders
    filler = jnp.zeros((8 - degree, nodes), I32)
    senders_out_ref[...] = jnp.concatenate([senders, filler], axis=0).T


def merge_nodes(peers, *refs):
    arr_refs, refs = refs[:peers], refs[peers:]
    (incoming_ref, embed_ref, local_ref, mesh_ref, weight_ref, bounds_ref, senders_t_ref, cot_ref,
     merged_ref, state_ref, slope_ref, lat_ref, *pay_refs) = refs
    nodes = mesh_ref.shape[0]
    taken = incoming_ref.shape[1]
    halo = peers * BORDER
    lat = jnp.concatenate([ref[...] for ref in arr_refs], axis=0)
    lat_ref[...] = lat
    act, slope = silu_both(dot(lat, embed_ref[...]))
    slope_ref[...] = low(slope)
    place = low(hot(incoming_ref[...] == iota(nodes, taken, 0)))
    merged = low(local_ref[...] + dot(place, low(act)))
    merged_ref[...] = merged
    state = low(mesh_ref[...].astype(F32) + dot(merged, weight_ref[...]))
    state_ref[...] = state
    border = low(hot(bounds_ref[...] == iota(halo, nodes, 1)))
    back = low(receivers(senders_t_ref[...], halo))
    store_parts(
        pay_refs,
        [dot(border, state), dot(back, state), dot(border, merged), dot(back, cot_ref[...])],
    )


def local_edges(senders, degree, sent, recv, each):
    nodes = senders.shape[0]
    total = jnp.zeros(recv.shape, F32)
    ids = iota(nodes, nodes, 1)
    for j in range(degree):
        named = senders[:, j : j + 1]
        act, slope = silu_both(dot(low(hot(named == ids)), sent) + recv)
        keep = hot(named < nodes)
        total = total + act * keep
        each(j, slope * keep)
    return total


def forward_local(
    state_ref, send_ref, recv_ref, senders_ref, senders_t_ref, bounds_ref,
    total_ref, slope_ref, recv_n_ref, sent_b_ref,
):
    state = state_ref[...]
    nodes = state.shape[0]
    halo = bounds_ref.shape[0]
    sent = low(dot(state, send_ref[0]))
    recv = dot(state, recv_ref[0])

    def keep(j, slope):
        slope_ref[j] = low(slope)

    total_ref[...] = local_edges(senders_ref[...], senders_t_ref.shape[0], sent, recv, keep)
    back = low(receivers(senders_t_ref[...], halo))
    recv_n_ref[...] = dot(low(dot(back, state)), recv_ref[0])
    sent_b_ref[...] = low(dot(low(hot(bounds_ref[...] == iota(halo, nodes, 1))), sent))


def forward_halo(peers, *refs):
    arr_refs, refs = refs[:peers], refs[peers:]
    (recv_n_ref, total_ref, state_ref, send_ref, update_ref, senders_ref, senders_t_ref,
     bounds_ref, summed_ref, out_ref, pre_ref, rows_ref, back_ref, merged_ref, cot_ref,
     *pay_refs) = refs
    nodes = state_ref.shape[0]
    degree = senders_t_ref.shape[0]
    halo = peers * BORDER
    rows, back, merged, cot = split_parts(
        arr_refs, (0, BORDER, 2 * BORDER, 3 * BORDER), (BORDER,) * 4
    )
    rows_ref[...], back_ref[...] = low(rows), low(back)
    merged_ref[...], cot_ref[...] = low(merged), low(cot)
    pre = low(dot(low(rows), send_ref[0])).astype(F32) + recv_n_ref[...]
    pre_ref[...] = pre
    place = low(receivers_t(senders_ref[...], degree, halo))
    summed = low(total_ref[...] + dot(place, low(silu(pre))))
    summed_ref[...] = summed
    state = low(state_ref[...].astype(F32) + dot(summed, update_ref[0]))
    out_ref[...] = state
    border = low(hot(bounds_ref[...] == iota(halo, nodes, 1)))
    back = low(receivers(senders_t_ref[...], halo))
    store_parts(pay_refs, [dot(border, state), dot(back, state)])


def turn_local(
    state_ref, send_ref, recv_ref, update_ref, cot_ref, cot_r_ref, pre_ref, back0_ref,
    sent_b0_ref, senders_ref, senders_t_ref, bounds_ref,
    total_ref, grecv_ref, gsent_ref, recv_n_ref, sent_b_ref, gsum_n_ref, gsum_r_ref,
    slope_k_ref, slope_r_ref,
):
    halo = bounds_ref.shape[0]
    slope_k_ref[...] = low(silu_slope(pre_ref[...]))
    pre = sent_b0_ref[...].astype(F32) + dot(back0_ref[...], recv_ref[0])
    slope_r_ref[...] = low(silu_slope(pre))
    state = state_ref[...]
    nodes = state.shape[0]
    sent = low(dot(state, send_ref[1]))
    recv = dot(state, recv_ref[1])
    gsum = low(dot(cot_ref[...], update_ref[1], NT))
    grad = gsum.astype(F32)
    grecv_ref[...] = jnp.zeros(grecv_ref.shape, F32)
    gsent_ref[...] = jnp.zeros(gsent_ref.shape, F32)

    def back_edge(j, slope):
        gpre = grad * slope
        grecv_ref[...] += gpre
        target = low(hot(senders_t_ref[j : j + 1, :] == iota(nodes, nodes, 0)))
        gsent_ref[...] += dot(target, low(gpre))

    degree = senders_t_ref.shape[0]
    total_ref[...] = local_edges(senders_ref[...], degree, sent, recv, back_edge)
    back = low(receivers(senders_t_ref[...], halo))
    recv_n_ref[...] = dot(low(dot(back, state)), recv_ref[1])
    sent_b_ref[...] = low(dot(low(hot(bounds_ref[...] == iota(halo, nodes, 1))), sent))
    gsum_n_ref[...] = low(dot(back, gsum))
    gsum_r_ref[...] = low(dot(cot_r_ref[...], update_ref[1], NT))


def turn_halo(peers, *refs):
    arr_refs, refs = refs[:peers], refs[peers:]
    (recv_n_ref, sent_b_ref, gsum_n_ref, gsum_r_ref, total_ref, grecv_ref, gsent_ref, cot_ref,
     send_ref, recv_ref, senders_ref, senders_t_ref, bounds_ref, summed_ref, grecv_out_ref,
     gsent_out_ref, gin_ref, *pay_refs) = refs
    nodes = cot_ref.shape[0]
    degree = senders_t_ref.shape[0]
    halo = peers * BORDER
    rows, back = split_parts(arr_refs, (0, BORDER), (BORDER,) * 2)
    pre = low(dot(low(rows), send_ref[1])).astype(F32) + recv_n_ref[...]
    act, slope = silu_both(pre)
    place = low(receivers_t(senders_ref[...], degree, halo))
    gpre = low(gsum_n_ref[...].astype(F32) * slope)
    grecv = low(grecv_ref[...] + dot(place, gpre))
    pre = sent_b_ref[...].astype(F32) + dot(low(back), recv_ref[1])
    gpre = low(gsum_r_ref[...].astype(F32) * silu_slope(pre))
    border = low(hot(bounds_ref[...] == iota(nodes, halo, 0)))
    gsent = low(gsent_ref[...] + dot(border, gpre))
    gin = cot_ref[...].astype(F32) + dot(grecv, recv_ref[1], NT) + dot(gsent, send_ref[1], NT)
    gin = low(gin)
    gin_ref[...] = gin
    store_parts(pay_refs, [dot(low(receivers(senders_t_ref[...], halo)), gin)])
    summed_ref[...] = low(total_ref[...] + dot(place, low(act)))
    grecv_out_ref[...] = grecv
    gsent_out_ref[...] = gsent


def last_weights(
    dims, place_ref, state_ref, summed_ref, cot_ref, grecv_ref, gsent_ref, update_ref,
    keep_ref, give_ref, mesh_ref,
):
    state, summed = state_ref[...], summed_ref[...]

    def store(at, value):
        store_blocks(keep_ref, give_ref, at, 3, value, dims, place_ref)

    store(0, dot(state, gsent_ref[...], TN))
    store(1, dot(state, grecv_ref[...], TN))
    store(2, dot(summed, cot_ref[...], TN))
    mesh_ref[...] = low(state.astype(F32) + dot(summed, update_ref[1]))


def back_local(
    dims, place_ref, gin_ref, slope_ref, slope_k_ref, send_ref, recv_ref, update_ref, senders_ref,
    senders_t_ref, state_ref, rows_ref, summed_ref, merged_ref, merged_r_ref,
    part_ref, keep_ref, give_ref,
):
    nodes = gin_ref.shape[0]
    halo = slope_k_ref.shape[0]
    degree = senders_t_ref.shape[0]
    gin = gin_ref[...]
    gsum = low(dot(gin, update_ref[0], NT))
    grad = gsum.astype(F32)
    place = low(receivers_t(senders_ref[...], degree, halo))
    back = low(receivers(senders_t_ref[...], halo))
    gpre_k = low(dot(back, gsum) * slope_k_ref[...].astype(F32))
    grecv = dot(place, gpre_k)
    gsent = jnp.zeros(grad.shape, F32)
    for j in range(degree):
        gpre = grad * slope_ref[j].astype(F32)
        grecv = grecv + gpre
        target = low(hot(senders_t_ref[j : j + 1, :] == iota(nodes, nodes, 0)))
        gsent = gsent + dot(target, low(gpre))
    grecv, gsent = low(grecv), low(gsent)
    part = gin.astype(F32) + dot(grecv, recv_ref[0], NT) + dot(gsent, send_ref[0], NT)
    part_ref[...] = part
    state = state_ref[...]

    def store(at, value):
        store_blocks(keep_ref, give_ref, at, 4, value, dims, place_ref)

    store(0, dot(state, gsent, TN) + dot(rows_ref[...], gpre_k, TN))
    store(1, dot(state, grecv, TN))
    store(2, dot(summed_ref[...], gin, TN))
    far = low(dot(gpre_k, send_ref[0], NT))
    store(3, dot(merged_ref[...], low(part), TN) + dot(merged_r_ref[...], far, TN))


def embed_back(peers, dims, *refs):
    arr_refs, refs = refs[:peers], refs[peers:]
    (place_ref, slope_r_ref, part_ref, update_ref, send_ref, merge_ref, bounds_ref, target_ref,
     sends_ref, incoming_ref, slope_g_ref, slope_a_ref, grid_ref, lat_ref, embed_ref,
     gpre_ref, keep_ref, give_ref, *pay_refs) = refs
    nodes = part_ref.shape[0]
    halo = peers * BORDER
    chosen = grid_ref.shape[0]
    taken = sends_ref.shape[0]
    (arrived,) = split_parts(arr_refs, (0,), (BORDER,))
    gsum = low(dot(low(arrived), update_ref[0], NT)).astype(F32)
    gpre = low(gsum * slope_r_ref[...].astype(F32))
    border = low(hot(bounds_ref[...] == iota(nodes, halo, 0)))
    gsent = low(dot(border, gpre))
    gin = low(part_ref[...] + dot(gsent, send_ref[0], NT))
    gmerged = low(dot(gin, merge_ref[...], NT))
    place = low(hot(incoming_ref[...] == iota(nodes, taken, 0)))
    gpre_a = low(dot(place, gmerged, TN) * slope_a_ref[...].astype(F32))
    sent = jnp.max(hot(sends_ref[...] == iota(taken, chosen, 1)), axis=0, keepdims=True)
    label = jnp.where(sent > 0.0, nodes, target_ref[...])
    pick = low(hot(label == iota(nodes, chosen, 0)))
    gpre_g = low(dot(pick, gmerged, TN) * slope_g_ref[...].astype(F32))
    gpre_ref[...] = gpre_g
    grad = dot(grid_ref[...], gpre_g, TN) + dot(lat_ref[...], gpre_a, TN)
    store_blocks(keep_ref, give_ref, 0, 1, grad, dims, place_ref)
    store_parts(pay_refs, [dot(gpre_a, embed_ref[...], NT)])


def grid_place(peers, *refs):
    arr_refs, refs = refs[:peers], refs[peers:]
    gpre_ref, weight_ref, sends_ref, out_ref = refs
    chosen = gpre_ref.shape[0]
    taken = sends_ref.shape[1]
    local = dot(gpre_ref[...], weight_ref[...], NT)
    place = low(hot(sends_ref[...] == iota(chosen, taken, 0)))
    rows = jnp.concatenate([ref[...] for ref in arr_refs], axis=0)
    out_ref[...] = low(local + dot(place, rows))


def finish(
    keep1_ref, arr1_ref, keep0_ref, arr0_ref, keep_e_ref, arr_e_ref,
    embed_ref, merge_ref, send_ref, recv_ref, update_ref,
):
    last = keep1_ref[...].astype(F32) + arr1_ref[...].astype(F32)
    first = keep0_ref[...].astype(F32) + arr0_ref[...].astype(F32)
    embed_ref[...] = keep_e_ref[...].astype(F32) + arr_e_ref[...].astype(F32)
    depth = embed_ref.shape[0]
    for at, ref in enumerate((send_ref, recv_ref, update_ref)):
        ref[0] = first[at * depth : (at + 1) * depth]
        ref[1] = last[at * depth : (at + 1) * depth]
    merge_ref[...] = first[3 * depth :]


def body(
    dims,
    grid_latent, mesh_latent, cotangent, embed_weight, merge_weight, send_weight, recv_weight,
    update_weight, target_row, send_rows, incoming_rows, border_mesh_rows, mesh_senders,
):
    chosen, width = grid_latent.shape
    nodes, degree = mesh_senders.shape
    slots, capacity = send_rows.shape[1:]
    column = dims[1] * dims[2]
    peers = slots - 1
    halo = peers * BORDER
    taken = peers * capacity
    total = dims[0] * dims[1] * dims[2]
    bits = (total - 1).bit_length()
    spot = lax.axis_index(GROUP)
    place = [lax.axis_index(COLUMN), lax.axis_index("lon") % 2]
    place += [(spot >> bit) % 2 for bit in range(bits)]
    place = jnp.broadcast_to(jnp.stack(place).astype(I32)[None], (slots, 2 + bits))
    ints = jnp.concatenate([send_rows[0], incoming_rows[0], border_mesh_rows[0], place], axis=1)
    targets = target_row.reshape(1, chosen)
    unit = 2 * nodes * width * width

    sends, *pay1 = call(
        lambda *refs: first_payload(column, capacity, *refs), "first_payload",
        [shape(taken, 1, dtype=I32)] + [shape(capacity, width)] * peers,
        (ints, grid_latent), flops=unit // 2,
    )
    arr1 = exchange(pay1, dims)
    (local, slope_g, sends_row, incoming, bounds, bounds_row, senders_t, senders, place) = call(
        lambda *refs: embed_local(column, capacity, *refs), "embed_local",
        [shape(nodes, width, dtype=F32), shape(chosen, width), shape(1, taken, dtype=I32),
         shape(1, taken, dtype=I32), shape(halo, 1, dtype=I32), shape(1, halo, dtype=I32),
         shape(degree, nodes, dtype=I32), shape(nodes, 8, dtype=I32),
         shape(slots, 2 + bits, dtype=I32)],
        (ints, mesh_senders.T, grid_latent, embed_weight, targets, sends), flops=3 * unit,
    )
    merged, state0, slope_a, lat_a, *pay2 = call(
        lambda *refs: merge_nodes(peers, *refs), "merge_nodes",
        [shape(nodes, width), shape(nodes, width), shape(taken, width), shape(taken, width)]
        + [shape(4 * BORDER, width)] * peers,
        (*arr1, incoming, embed_weight, local, mesh_latent, merge_weight, bounds, senders_t,
         cotangent),
        flops=2 * unit,
    )
    arr2 = exchange(pay2, dims)
    total0, slope0, recv_n0, sent_b0 = call(
        forward_local, "forward_local",
        [shape(nodes, width, dtype=F32), shape(degree, nodes, width),
         shape(halo, width, dtype=F32), shape(halo, width)],
        (state0, send_weight, recv_weight, senders, senders_t, bounds), flops=6 * unit,
    )
    summed0, state1, pre0, rows0, back0, merged_r, cot_r, *pay3 = call(
        lambda *refs: forward_halo(peers, *refs), "forward_halo",
        [shape(nodes, width), shape(nodes, width), shape(halo, width, dtype=F32)]
        + [shape(halo, width)] * 4 + [shape(2 * BORDER, width)] * peers,
        (*arr2, recv_n0, total0, state0, send_weight, update_weight, senders, senders_t, bounds),
        flops=2 * unit,
    )
    arr3 = exchange(pay3, dims)
    (total1, grecv_l, gsent_l, recv_n1, sent_b1, gsum_n1, gsum_r1, slope_k0, slope_r0) = call(
        turn_local, "turn_local",
        [shape(nodes, width, dtype=F32)] * 3 + [shape(halo, width, dtype=F32)]
        + [shape(halo, width)] * 5,
        (state1, send_weight, recv_weight, update_weight, cotangent, cot_r, pre0, back0, sent_b0,
         senders, senders_t, bounds),
        flops=10 * unit,
    )
    summed1, grecv1, gsent1, gin1, *pay4 = call(
        lambda *refs: turn_halo(peers, *refs), "turn_halo",
        [shape(nodes, width)] * 4 + [shape(BORDER, width)] * peers,
        (*arr3, recv_n1, sent_b1, gsum_n1, gsum_r1, total1, grecv_l, gsent_l, cotangent,
         send_weight, recv_weight, senders, senders_t, bounds_row),
        flops=3 * unit,
    )
    arr4 = exchange(pay4, dims)
    keep1, give1, mesh_out = call(
        lambda *refs: last_weights(dims, *refs), "last_weights",
        blocks_shapes(3, width, width, dims) + [shape(nodes, width)],
        (place, state1, summed1, cotangent, grecv1, gsent1, update_weight), flops=4 * unit,
    )
    part0, keep0, give0 = call(
        lambda *refs: back_local(dims, *refs), "back_local",
        [shape(nodes, width, dtype=F32)] + blocks_shapes(4, width, width, dims),
        (place, gin1, slope0, slope_k0, send_weight, recv_weight, update_weight, senders,
         senders_t, state0, rows0, summed0, merged, merged_r),
        flops=10 * unit,
    )
    gpre_g, keep_e, give_e, *pay5 = call(
        lambda *refs: embed_back(peers, dims, *refs), "embed_back",
        [shape(chosen, width)] + blocks_shapes(1, width, width, dims)
        + [shape(capacity, width)] * peers,
        (*arr4, place, slope_r0, part0, update_weight, send_weight, merge_weight, bounds_row,
         targets, sends, incoming, slope_g, slope_a, grid_latent, lat_a, embed_weight),
        flops=6 * unit,
    )
    arr5 = exchange(pay5, dims)
    (grid_grad,) = call(
        lambda *refs: grid_place(peers, *refs), "grid_place", [shape(chosen, width)],
        (*arr5, gpre_g, embed_weight, sends_row), flops=3 * unit,
    )
    depth = width // total
    if not fine(width, dims):
        last, first, embed = (scatter_plain(blocks, dims) for blocks in (keep1, keep0, keep_e))
        grads = [jnp.stack([first[i], last[i]]) for i in range(3)]
        return (mesh_out, grid_grad, embed[0], first[3], *grads)
    grads = call(
        finish, "finish",
        [shape(depth, width, dtype=F32)] * 2 + [shape(2, depth, width, dtype=F32)] * 3,
        (*scatter_halving(keep1, give1, place, dims), *scatter_halving(keep0, give0, place, dims),
         *scatter_halving(keep_e, give_e, place, dims)),
        flops=8 * depth * width,
    )
    return (mesh_out, grid_grad, *grads)


def solution(mesh):
    split = ("groups", "lon", "lat", "sub")
    dims = tuple(mesh.shape[axis] for axis in GROUP)
    rows = P(split, None)
    whole = P("groups", GROUP, None)
    in_specs = (
        rows, rows, rows, P(), P(), P(), P(), P(), P(split), P(split, None, None),
        P(split, None, None), P(split, None, None), rows,
    )
    out_specs = (rows, rows, rows, rows, whole, whole, whole)
    return jax.shard_map(
        lambda *args: body(dims, *args),
        mesh=mesh, in_specs=in_specs, out_specs=out_specs, check_vma=False,
    )
```

```python
import jax
import jax.numpy as jnp
from jax import lax
from jax.experimental import pallas as pl
from jax.experimental.pallas import tpu as pltpu
from jax.sharding import PartitionSpec as P

BF = jnp.bfloat16
F32 = jnp.float32
I32 = jnp.int32
NN = (((1,), (0,)), ((), ()))
NT = (((1,), (1,)), ((), ()))
TN = (((0,), (0,)), ((), ()))
BORDER = 8
GROUP = ("lon", "lat", "sub")
COLUMN = ("lat", "sub")


def dot(a, b, dims=NN):
    return lax.dot_general(a, b, dims, preferred_element_type=F32)


def low(value):
    return value.astype(BF)


def sigmoid(value):
    return 0.5 * jnp.tanh(0.5 * value) + 0.5


def silu(value):
    return value * sigmoid(value)


def silu_both(value):
    sig = sigmoid(value)
    act = value * sig
    return act, sig + act * (1.0 - sig)


def silu_slope(value):
    return silu_both(value)[1]


def iota(rows, columns, dim):
    return lax.broadcasted_iota(I32, (rows, columns), dim)


def hot(mask):
    return jnp.where(mask, 1.0, 0.0)


def slot_of(at, column, me, odd):
    far = jnp.where(at == column - 1, column + 1 - odd, column + odd)
    return jnp.where(at < column - 1, jnp.bitwise_xor(at + 1, me), far)


def as_column(values, wide, column, me, odd):
    slots = values.shape[0]
    count = (slots - 1) * wide
    row = iota(count, slots, 0)
    pick = low(hot(slot_of(row // wide, column, me, odd) == iota(count, slots, 1)))
    found = 16.0 * dot(pick, low((values // 16).astype(F32)))
    found = found + dot(pick, low((values % 16).astype(F32)))
    keep = iota(count, wide, 0) % wide == iota(count, wide, 1)
    return jnp.sum(jnp.where(keep, found, 0.0), axis=1, keepdims=True).astype(I32)


def as_row(values, wide, column, me, odd):
    slots = values.shape[0]
    count = (slots - 1) * wide
    pick = low(hot(iota(wide, count, 1) % wide == iota(wide, count, 0)))
    found = 16.0 * dot(low((values // 16).astype(F32)), pick)
    found = found + dot(low((values % 16).astype(F32)), pick)
    at = iota(slots, count, 1) // wide
    keep = slot_of(at, column, me, odd) == iota(slots, count, 0)
    return jnp.sum(jnp.where(keep, found, 0.0), axis=0, keepdims=True).astype(I32)


def split_parts(refs, starts, sizes):
    values = [ref[...].astype(F32) for ref in refs]
    return [
        jnp.concatenate([value[start : start + size] for value in values], axis=0)
        for start, size in zip(starts, sizes)
    ]


def store_parts(refs, parts):
    peers = len(refs)
    for at, ref in enumerate(refs):
        rows = []
        for part in parts:
            size = part.shape[0] // peers
            rows.append(part[at * size : (at + 1) * size])
        ref[...] = low(rows[0] if len(rows) == 1 else jnp.concatenate(rows, axis=0))


def receivers(senders_t, halo):
    degree, nodes = senders_t.shape
    found = jnp.zeros((halo, nodes), F32)
    ids = iota(halo, nodes, 0) + nodes
    for j in range(degree):
        found = found + hot(senders_t[j : j + 1, :] == ids)
    return found


def receivers_t(senders, degree, halo):
    nodes = senders.shape[0]
    found = jnp.zeros((nodes, halo), F32)
    ids = iota(nodes, halo, 1) + nodes
    for j in range(degree):
        found = found + hot(senders[:, j : j + 1] == ids)
    return found


def fine(rows, dims):
    return (rows // (dims[0] * dims[1] * dims[2])) % 16 == 0


def reverse_bits(block, bits):
    spot = 0
    for bit in range(bits):
        spot = 2 * spot + (block >> bit) % 2
    return spot


def store_blocks(keep_ref, give_ref, at, count, value, dims, bits_ref):
    value = low(value)
    rows = value.shape[0]
    total = dims[0] * dims[1] * dims[2]
    depth = rows // total
    if not fine(rows, dims):
        keep_ref[at] = value
        return
    bits = (total - 1).bit_length()
    upper = bits_ref[0:1, 2:3] == 1
    for block in range(0, total, 2):
        start = reverse_bits(block, bits) * count * depth + at * depth
        first = value[block * depth : (block + 1) * depth].astype(F32)
        second = value[(block + 1) * depth : (block + 2) * depth].astype(F32)
        keep_ref[start : start + depth, :] = low(jnp.where(upper, second, first))
        give_ref[start : start + depth, :] = low(jnp.where(upper, first, second))


def blocks_shapes(count, rows, width, dims):
    if fine(rows, dims):
        return [jax.ShapeDtypeStruct((count * rows // 2, width), BF)] * 2
    return [jax.ShapeDtypeStruct((count, rows, width), BF), jax.ShapeDtypeStruct((16, width), BF)]


def halve(bit, bits_ref, keep_ref, arr_ref, keep_out, give_out):
    half = keep_ref.shape[0] // 2
    upper = bits_ref[0:1, 2 + bit : 3 + bit] == 1
    first = keep_ref[:half, :].astype(F32) + arr_ref[:half, :].astype(F32)
    second = keep_ref[half:, :].astype(F32) + arr_ref[half:, :].astype(F32)
    keep_out[...] = low(jnp.where(upper, second, first))
    give_out[...] = low(jnp.where(upper, first, second))


def swap(block, bit, dims):
    total = dims[0] * dims[1] * dims[2]
    return lax.ppermute(block, GROUP, [(i, i ^ (1 << bit)) for i in range(total)])


def scatter_halving(keep, give, place, dims):
    width = keep.shape[1]
    bits = (dims[0] * dims[1] * dims[2] - 1).bit_length()
    arrived = swap(give, 0, dims)
    for bit in range(1, bits):
        rows = keep.shape[0] // 2
        keep, give = call(
            lambda *refs: halve(bit, *refs), "halve", [shape(rows, width)] * 2,
            (place, keep, arrived), flops=4 * rows * width,
        )
        arrived = swap(give, bit, dims)
    return keep, arrived


def scatter_plain(blocks, dims):
    lon, lat, sub = dims
    count, rows, width = blocks.shape
    depth = rows // (lon * lat * sub)
    blocks = blocks.reshape(count, lon, lat, sub, depth, width)
    blocks = blocks.transpose(3, 2, 1, 0, 4, 5)
    for axis in ("sub", "lat", "lon"):
        blocks = lax.psum_scatter(blocks, axis, scatter_dimension=0, tiled=False)
    return blocks.astype(F32)


def call(kernel, name, outs, args, flops, loads=(), scratch=()):
    size = sum(a.size * a.dtype.itemsize for a in (*args, *outs, *loads))
    args = (*(pltpu.with_memory_space_constraint(a, pltpu.HBM) for a in loads), *args)
    scratch = list(scratch)
    if loads:
        scratch.append(pltpu.SemaphoreType.DMA((len(loads),)))
    in_specs = [pl.BlockSpec(memory_space=pltpu.HBM)] * len(loads)
    in_specs += [pl.BlockSpec(memory_space=pltpu.VMEM)] * (len(args) - len(loads))
    return pl.pallas_call(
        kernel,
        out_shape=[shape(*a.shape, dtype=a.dtype) for a in loads] + list(outs),
        in_specs=in_specs,
        out_specs=[pl.BlockSpec(memory_space=pltpu.VMEM)] * (len(outs) + len(loads)),
        scratch_shapes=scratch,
        compiler_params=pltpu.CompilerParams(vmem_limit_bytes=16 * 1024 * 1024),
        cost_estimate=pl.CostEstimate(flops=flops, bytes_accessed=size, transcendentals=0),
        name=name,
    )(*args)


def exchange(parts, dims):
    column = dims[1] * dims[2]
    count = dims[0]
    other = [(i, (i - 1 + 2 * (i % 2)) % count) for i in range(count)]
    far = lax.ppermute(parts[column], "lon", other)
    near = lax.ppermute(parts[column - 1], "lon", [(i, i ^ 1) for i in range(count)])
    arrived = [
        lax.ppermute(parts[r - 1], COLUMN, [(i, i ^ r) for i in range(column)])
        for r in range(column - 1, 0, -1)
    ]
    return (*arrived[::-1], near, far)


def shape(*dims, dtype=BF):
    return jax.ShapeDtypeStruct(dims, dtype)


def start_loads(sources, targets, sems):
    copies = [
        pltpu.make_async_copy(source, target, sems.at[at])
        for at, (source, target) in enumerate(zip(sources, targets))
    ]
    for copy in copies:
        copy.start()
    return copies


def first_payload(
    column, capacity, grid_far, embed_far, target_far, senders_far, ints_ref,
    grid_ref, embed_ref, target_ref, senders_ref, sends_ref, *rest
):
    *pay_refs, sems = rest
    grid_load, *loads = start_loads(
        (grid_far, embed_far, target_far, senders_far),
        (grid_ref, embed_ref, target_ref, senders_ref), sems,
    )
    chosen = grid_ref.shape[0]
    ints = ints_ref[...]
    base = 2 * capacity + BORDER
    me, odd = ints[0:1, base : base + 1], ints[0:1, base + 1 : base + 2]
    sends = as_column(ints[:, :capacity], capacity, column, me, odd)
    sends_ref[...] = sends
    pick = low(hot(sends == iota(sends.shape[0], chosen, 1)))
    grid_load.wait()
    store_parts(pay_refs, [dot(pick, grid_ref[...])])
    for load in loads:
        load.wait()


def embed_local(
    column, capacity, mesh_far, merge_far, cot_far, ints_ref, senders_ref, grid_ref, weight_ref,
    target_ref, sends_ref, mesh_ref, merge_ref, cot_ref,
    sum_ref, slope_ref, sends_row_ref, incoming_ref, bounds_ref, bounds_row_ref, senders_t_ref,
    senders_out_ref, place_ref, sems,
):
    loads = start_loads((mesh_far, merge_far, cot_far), (mesh_ref, merge_ref, cot_ref), sems)
    chosen = grid_ref.shape[0]
    nodes = sum_ref.shape[0]
    taken = sends_ref.shape[0]
    act, slope = silu_both(dot(grid_ref[...], weight_ref[...]))
    slope_ref[...] = low(slope)
    sent = jnp.max(hot(sends_ref[...] == iota(taken, chosen, 1)), axis=0, keepdims=True)
    label = jnp.where(sent > 0.0, nodes, target_ref[...])
    sum_ref[...] = dot(low(hot(label == iota(nodes, chosen, 0))), low(act))
    ints = ints_ref[...]
    base = 2 * capacity + BORDER
    place_ref[...] = ints[:, base:]
    me, odd = ints[0:1, base : base + 1], ints[0:1, base + 1 : base + 2]
    sends, incoming = ints[:, :capacity], ints[:, capacity : 2 * capacity]
    bounds = ints[:, 2 * capacity : base]
    sends_row_ref[...] = as_row(sends, capacity, column, me, odd)
    incoming_ref[...] = as_row(incoming, capacity, column, me, odd)
    bounds_ref[...] = as_column(bounds, BORDER, column, me, odd)
    bounds_row_ref[...] = as_row(bounds, BORDER, column, me, odd)
    senders = senders_ref[...]
    degree = senders.shape[0]
    offset = senders - nodes
    slot = offset // BORDER
    far = jnp.where(slot == column, column - odd, column - 1 + odd)
    at = jnp.where(slot < column, jnp.bitwise_xor(slot, me) - 1, far)
    senders = jnp.where(offset < 0, senders, nodes + at * BORDER + offset % BORDER)
    senders_t_ref[...] = senders
    filler = jnp.zeros((8 - degree, nodes), I32)
    senders_out_ref[...] = jnp.concatenate([senders, filler], axis=0).T
    for load in loads:
        load.wait()


def merge_nodes(peers, *refs):
    arr_refs, refs = refs[:peers], refs[peers:]
    (incoming_ref, embed_ref, local_ref, mesh_ref, weight_ref, bounds_ref, senders_t_ref, cot_ref,
     merged_ref, state_ref, slope_ref, lat_ref, *pay_refs) = refs
    nodes = mesh_ref.shape[0]
    taken = incoming_ref.shape[1]
    halo = peers * BORDER
    lat = jnp.concatenate([ref[...] for ref in arr_refs], axis=0)
    lat_ref[...] = lat
    act, slope = silu_both(dot(lat, embed_ref[...]))
    slope_ref[...] = low(slope)
    place = low(hot(incoming_ref[...] == iota(nodes, taken, 0)))
    merged = low(local_ref[...] + dot(place, low(act)))
    merged_ref[...] = merged
    state = low(mesh_ref[...].astype(F32) + dot(merged, weight_ref[...]))
    state_ref[...] = state
    border = low(hot(bounds_ref[...] == iota(halo, nodes, 1)))
    back = low(receivers(senders_t_ref[...], halo))
    store_parts(
        pay_refs,
        [dot(border, state), dot(back, state), dot(border, merged), dot(back, cot_ref[...])],
    )


def local_edges(senders, degree, sent, recv, each):
    nodes = senders.shape[0]
    total = None
    ids = iota(nodes, nodes, 1)
    for j in range(degree):
        act, slope = silu_both(dot(low(hot(senders[:, j : j + 1] == ids)), sent) + recv)
        total = act if total is None else total + act
        each(j, slope)
    return total


def edge_targets(senders_t):
    degree, nodes = senders_t.shape
    ids = iota(nodes, nodes, 0)
    return jnp.concatenate(
        [low(hot(senders_t[j : j + 1, :] == ids)) for j in range(degree)], axis=1
    )


def forward_local(
    state_ref, send_ref, recv_ref, senders_ref, senders_t_ref, bounds_ref,
    total_ref, slope_ref, recv_n_ref, sent_b_ref,
):
    state = state_ref[...]
    nodes = state.shape[0]
    halo = bounds_ref.shape[0]
    sent = low(dot(state, send_ref[0]))
    recv = dot(state, recv_ref[0])

    def keep(j, slope):
        slope_ref[j] = low(slope)

    total_ref[...] = local_edges(senders_ref[...], senders_t_ref.shape[0], sent, recv, keep)
    back = low(receivers(senders_t_ref[...], halo))
    recv_n_ref[...] = dot(low(dot(back, state)), recv_ref[0])
    sent_b_ref[...] = low(dot(low(hot(bounds_ref[...] == iota(halo, nodes, 1))), sent))


def forward_halo(peers, *refs):
    arr_refs, refs = refs[:peers], refs[peers:]
    (recv_n_ref, total_ref, state_ref, send_ref, update_ref, senders_ref, senders_t_ref,
     bounds_ref, summed_ref, out_ref, pre_ref, rows_ref, back_ref, merged_ref, cot_ref,
     *pay_refs) = refs
    nodes = state_ref.shape[0]
    degree = senders_t_ref.shape[0]
    halo = peers * BORDER
    rows, back, merged, cot = split_parts(
        arr_refs, (0, BORDER, 2 * BORDER, 3 * BORDER), (BORDER,) * 4
    )
    rows_ref[...], back_ref[...] = low(rows), low(back)
    merged_ref[...], cot_ref[...] = low(merged), low(cot)
    pre = low(dot(low(rows), send_ref[0])).astype(F32) + recv_n_ref[...]
    pre_ref[...] = pre
    place = low(receivers_t(senders_ref[...], degree, halo))
    extra = silu(pre) - silu(recv_n_ref[...])
    summed = low(total_ref[...] + dot(place, low(extra)))
    summed_ref[...] = summed
    state = low(state_ref[...].astype(F32) + dot(summed, update_ref[0]))
    out_ref[...] = state
    border = low(hot(bounds_ref[...] == iota(halo, nodes, 1)))
    back = low(receivers(senders_t_ref[...], halo))
    store_parts(pay_refs, [dot(border, state), dot(back, state)])


def turn_local(
    state_ref, send_ref, recv_ref, update_ref, cot_ref, cot_r_ref, pre_ref, recv_n0_ref, back0_ref,
    sent_b0_ref, senders_ref, senders_t_ref, bounds_ref,
    total_ref, grecv_ref, gsent_ref, recv_n_ref, sent_b_ref, gsum_n_ref, gsum_r_ref,
    slope_k_ref, slope_d_ref, slope_r_ref, gpre_ref,
):
    halo = bounds_ref.shape[0]
    slope = silu_slope(pre_ref[...])
    slope_k_ref[...] = low(slope)
    slope_d_ref[...] = low(slope - silu_slope(recv_n0_ref[...]))
    pre = sent_b0_ref[...].astype(F32) + dot(back0_ref[...], recv_ref[0])
    slope_r_ref[...] = low(silu_slope(pre))
    state = state_ref[...]
    nodes = state.shape[0]
    sent = low(dot(state, send_ref[1]))
    recv = dot(state, recv_ref[1])
    gsum = low(dot(cot_ref[...], update_ref[1], NT))
    grad = gsum.astype(F32)
    grecv = []

    def back_edge(j, slope):
        gpre = grad * slope
        grecv.append(gpre if j == 0 else grecv[-1] + gpre)
        gpre_ref[j * nodes : (j + 1) * nodes, :] = low(gpre)

    degree = senders_t_ref.shape[0]
    total_ref[...] = local_edges(senders_ref[...], degree, sent, recv, back_edge)
    grecv_ref[...] = grecv[-1]
    gsent_ref[...] = dot(edge_targets(senders_t_ref[...]), gpre_ref[...])
    back = low(receivers(senders_t_ref[...], halo))
    recv_n_ref[...] = dot(low(dot(back, state)), recv_ref[1])
    sent_b_ref[...] = low(dot(low(hot(bounds_ref[...] == iota(halo, nodes, 1))), sent))
    gsum_n_ref[...] = low(dot(back, gsum))
    gsum_r_ref[...] = low(dot(cot_r_ref[...], update_ref[1], NT))


def turn_halo(peers, *refs):
    arr_refs, refs = refs[:peers], refs[peers:]
    (recv_n_ref, sent_b_ref, gsum_n_ref, gsum_r_ref, total_ref, grecv_ref, gsent_ref, cot_ref,
     send_ref, recv_ref, senders_ref, senders_t_ref, bounds_ref, summed_ref, grecv_out_ref,
     gsent_out_ref, gin_ref, *pay_refs) = refs
    nodes = cot_ref.shape[0]
    degree = senders_t_ref.shape[0]
    halo = peers * BORDER
    rows, back = split_parts(arr_refs, (0, BORDER), (BORDER,) * 2)
    pre = low(dot(low(rows), send_ref[1])).astype(F32) + recv_n_ref[...]
    act, slope = silu_both(pre)
    place = low(receivers_t(senders_ref[...], degree, halo))
    base, base_slope = silu_both(recv_n_ref[...])
    gpre = low(gsum_n_ref[...].astype(F32) * (slope - base_slope))
    grecv = low(grecv_ref[...] + dot(place, gpre))
    pre = sent_b_ref[...].astype(F32) + dot(low(back), recv_ref[1])
    gpre = low(gsum_r_ref[...].astype(F32) * silu_slope(pre))
    border = low(hot(bounds_ref[...] == iota(nodes, halo, 0)))
    gsent = low(gsent_ref[...] + dot(border, gpre))
    gin = cot_ref[...].astype(F32) + dot(grecv, recv_ref[1], NT) + dot(gsent, send_ref[1], NT)
    gin = low(gin)
    gin_ref[...] = gin
    store_parts(pay_refs, [dot(low(receivers(senders_t_ref[...], halo)), gin)])
    summed_ref[...] = low(total_ref[...] + dot(place, low(act - base)))
    grecv_out_ref[...] = grecv
    gsent_out_ref[...] = gsent


def last_weights(
    dims, place_ref, state_ref, summed_ref, cot_ref, grecv_ref, gsent_ref, update_ref,
    keep_ref, give_ref, mesh_ref,
):
    state, summed = state_ref[...], summed_ref[...]

    def store(at, value):
        store_blocks(keep_ref, give_ref, at, 3, value, dims, place_ref)

    store(0, dot(state, gsent_ref[...], TN))
    store(1, dot(state, grecv_ref[...], TN))
    store(2, dot(summed, cot_ref[...], TN))
    mesh_ref[...] = low(state.astype(F32) + dot(summed, update_ref[1]))


def back_local(
    dims, place_ref, gin_ref, slope_ref, slope_k_ref, slope_d_ref, send_ref, recv_ref, update_ref,
    senders_ref, senders_t_ref, state_ref, rows_ref, summed_ref, merged_ref, merged_r_ref,
    part_ref, keep_ref, give_ref, gpre_ref,
):
    nodes = gin_ref.shape[0]
    halo = slope_k_ref.shape[0]
    degree = senders_t_ref.shape[0]
    gin = gin_ref[...]
    gsum = low(dot(gin, update_ref[0], NT))
    place = low(receivers_t(senders_ref[...], degree, halo))
    back = low(receivers(senders_t_ref[...], halo))
    gsum_n = low(dot(back, gsum))
    gpre_k = gsum_n * slope_k_ref[...]
    grecv = dot(place, gsum_n * slope_d_ref[...])
    for j in range(degree):
        gpre = gsum * slope_ref[j]
        grecv = grecv + gpre.astype(F32)
        gpre_ref[j * nodes : (j + 1) * nodes, :] = gpre
    gsent = dot(edge_targets(senders_t_ref[...]), gpre_ref[...])
    grecv, gsent = low(grecv), low(gsent)
    part = gin.astype(F32) + dot(grecv, recv_ref[0], NT) + dot(gsent, send_ref[0], NT)
    part_ref[...] = part
    state = state_ref[...]

    def store(at, value):
        store_blocks(keep_ref, give_ref, at, 4, value, dims, place_ref)

    store(0, dot(state, gsent, TN) + dot(rows_ref[...], gpre_k, TN))
    store(1, dot(state, grecv, TN))
    store(2, dot(summed_ref[...], gin, TN))
    far = low(dot(gpre_k, send_ref[0], NT))
    store(3, dot(merged_ref[...], low(part), TN) + dot(merged_r_ref[...], far, TN))


def embed_back(peers, dims, *refs):
    arr_refs, refs = refs[:peers], refs[peers:]
    (place_ref, slope_r_ref, part_ref, update_ref, send_ref, merge_ref, bounds_ref, target_ref,
     sends_ref, incoming_ref, slope_g_ref, slope_a_ref, grid_ref, lat_ref, embed_ref,
     gpre_ref, keep_ref, give_ref, *pay_refs) = refs
    nodes = part_ref.shape[0]
    halo = peers * BORDER
    chosen = grid_ref.shape[0]
    taken = sends_ref.shape[0]
    (arrived,) = split_parts(arr_refs, (0,), (BORDER,))
    gsum = low(dot(low(arrived), update_ref[0], NT)).astype(F32)
    gpre = low(gsum * slope_r_ref[...].astype(F32))
    border = low(hot(bounds_ref[...] == iota(nodes, halo, 0)))
    gsent = low(dot(border, gpre))
    gin = low(part_ref[...] + dot(gsent, send_ref[0], NT))
    gmerged = low(dot(gin, merge_ref[...], NT))
    place = low(hot(incoming_ref[...] == iota(nodes, taken, 0)))
    gpre_a = low(dot(place, gmerged, TN) * slope_a_ref[...].astype(F32))
    sent = jnp.max(hot(sends_ref[...] == iota(taken, chosen, 1)), axis=0, keepdims=True)
    label = jnp.where(sent > 0.0, nodes, target_ref[...])
    pick = low(hot(label == iota(nodes, chosen, 0)))
    gpre_g = low(dot(pick, gmerged, TN) * slope_g_ref[...].astype(F32))
    gpre_ref[...] = gpre_g
    grad = dot(grid_ref[...], gpre_g, TN) + dot(lat_ref[...], gpre_a, TN)
    store_blocks(keep_ref, give_ref, 0, 1, grad, dims, place_ref)
    store_parts(pay_refs, [dot(gpre_a, embed_ref[...], NT)])


def grid_place(peers, *refs):
    arr_refs, refs = refs[:peers], refs[peers:]
    gpre_ref, weight_ref, sends_ref, out_ref = refs
    chosen = gpre_ref.shape[0]
    taken = sends_ref.shape[1]
    local = dot(gpre_ref[...], weight_ref[...], NT)
    place = low(hot(sends_ref[...] == iota(chosen, taken, 0)))
    rows = jnp.concatenate([ref[...] for ref in arr_refs], axis=0)
    out_ref[...] = low(local + dot(place, rows))


def finish(
    keep1_ref, arr1_ref, keep0_ref, arr0_ref, keep_e_ref, arr_e_ref,
    embed_ref, merge_ref, send_ref, recv_ref, update_ref,
):
    last = keep1_ref[...].astype(F32) + arr1_ref[...].astype(F32)
    first = keep0_ref[...].astype(F32) + arr0_ref[...].astype(F32)
    embed_ref[...] = keep_e_ref[...].astype(F32) + arr_e_ref[...].astype(F32)
    depth = embed_ref.shape[0]
    for at, ref in enumerate((send_ref, recv_ref, update_ref)):
        ref[0] = first[at * depth : (at + 1) * depth]
        ref[1] = last[at * depth : (at + 1) * depth]
    merge_ref[...] = first[3 * depth :]


def body(
    dims,
    grid_latent, mesh_latent, cotangent, embed_weight, merge_weight, send_weight, recv_weight,
    update_weight, target_row, send_rows, incoming_rows, border_mesh_rows, mesh_senders,
):
    chosen, width = grid_latent.shape
    nodes, degree = mesh_senders.shape
    slots, capacity = send_rows.shape[1:]
    column = dims[1] * dims[2]
    peers = slots - 1
    halo = peers * BORDER
    taken = peers * capacity
    total = dims[0] * dims[1] * dims[2]
    bits = (total - 1).bit_length()
    spot = lax.axis_index(GROUP)
    place = [lax.axis_index(COLUMN), lax.axis_index("lon") % 2]
    place += [(spot >> bit) % 2 for bit in range(bits)]
    place = jnp.broadcast_to(jnp.stack(place).astype(I32)[None], (slots, 2 + bits))
    ints = jnp.concatenate([send_rows[0], incoming_rows[0], border_mesh_rows[0], place], axis=1)
    unit = 2 * nodes * width * width

    grid, embed, targets, senders_raw, sends, *pay1 = call(
        lambda *refs: first_payload(column, capacity, *refs), "first_payload",
        [shape(taken, 1, dtype=I32)] + [shape(capacity, width)] * peers,
        (ints,), flops=unit // 2,
        loads=(grid_latent, embed_weight, target_row.reshape(1, chosen), mesh_senders.T),
    )
    arr1 = exchange(pay1, dims)
    (mesh, merge, cot, local, slope_g, sends_row, incoming, bounds, bounds_row, senders_t, senders,
     place) = call(
        lambda *refs: embed_local(column, capacity, *refs), "embed_local",
        [shape(nodes, width, dtype=F32), shape(chosen, width), shape(1, taken, dtype=I32),
         shape(1, taken, dtype=I32), shape(halo, 1, dtype=I32), shape(1, halo, dtype=I32),
         shape(degree, nodes, dtype=I32), shape(nodes, 8, dtype=I32),
         shape(slots, 2 + bits, dtype=I32)],
        (ints, senders_raw, grid, embed, targets, sends), flops=3 * unit,
        loads=(mesh_latent, merge_weight, cotangent),
    )
    merged, state0, slope_a, lat_a, *pay2 = call(
        lambda *refs: merge_nodes(peers, *refs), "merge_nodes",
        [shape(nodes, width), shape(nodes, width), shape(taken, width), shape(taken, width)]
        + [shape(4 * BORDER, width)] * peers,
        (*arr1, incoming, embed, local, mesh, merge, bounds, senders_t, cot),
        flops=2 * unit,
    )
    arr2 = exchange(pay2, dims)
    total0, slope0, recv_n0, sent_b0 = call(
        forward_local, "forward_local",
        [shape(nodes, width, dtype=F32), shape(degree, nodes, width),
         shape(halo, width, dtype=F32), shape(halo, width)],
        (state0, send_weight, recv_weight, senders, senders_t, bounds), flops=6 * unit,
    )
    summed0, state1, pre0, rows0, back0, merged_r, cot_r, *pay3 = call(
        lambda *refs: forward_halo(peers, *refs), "forward_halo",
        [shape(nodes, width), shape(nodes, width), shape(halo, width, dtype=F32)]
        + [shape(halo, width)] * 4 + [shape(2 * BORDER, width)] * peers,
        (*arr2, recv_n0, total0, state0, send_weight, update_weight, senders, senders_t, bounds),
        flops=2 * unit,
    )
    arr3 = exchange(pay3, dims)
    (total1, grecv_l, gsent_l, recv_n1, sent_b1, gsum_n1, gsum_r1, slope_k0, slope_d0,
     slope_r0) = call(
        turn_local, "turn_local",
        [shape(nodes, width, dtype=F32)] * 3 + [shape(halo, width, dtype=F32)]
        + [shape(halo, width)] * 6,
        (state1, send_weight, recv_weight, update_weight, cot, cot_r, pre0, recv_n0, back0,
         sent_b0, senders, senders_t, bounds),
        flops=10 * unit, scratch=[pltpu.VMEM((degree * nodes, width), BF)],
    )
    summed1, grecv1, gsent1, gin1, *pay4 = call(
        lambda *refs: turn_halo(peers, *refs), "turn_halo",
        [shape(nodes, width)] * 4 + [shape(BORDER, width)] * peers,
        (*arr3, recv_n1, sent_b1, gsum_n1, gsum_r1, total1, grecv_l, gsent_l, cot,
         send_weight, recv_weight, senders, senders_t, bounds_row),
        flops=3 * unit,
    )
    arr4 = exchange(pay4, dims)
    keep1, give1, mesh_out = call(
        lambda *refs: last_weights(dims, *refs), "last_weights",
        blocks_shapes(3, width, width, dims) + [shape(nodes, width)],
        (place, state1, summed1, cot, grecv1, gsent1, update_weight), flops=4 * unit,
    )
    part0, keep0, give0 = call(
        lambda *refs: back_local(dims, *refs), "back_local",
        [shape(nodes, width, dtype=F32)] + blocks_shapes(4, width, width, dims),
        (place, gin1, slope0, slope_k0, slope_d0, send_weight, recv_weight, update_weight, senders,
         senders_t, state0, rows0, summed0, merged, merged_r),
        flops=10 * unit, scratch=[pltpu.VMEM((degree * nodes, width), BF)],
    )
    give1, give0, *arr4 = lax.optimization_barrier((give1, give0, *arr4))
    gpre_g, keep_e, give_e, *pay5 = call(
        lambda *refs: embed_back(peers, dims, *refs), "embed_back",
        [shape(chosen, width)] + blocks_shapes(1, width, width, dims)
        + [shape(capacity, width)] * peers,
        (*arr4, place, slope_r0, part0, update_weight, send_weight, merge, bounds_row,
         targets, sends, incoming, slope_g, slope_a, grid, lat_a, embed),
        flops=6 * unit,
    )
    arr5 = exchange(pay5, dims)
    (grid_grad,) = call(
        lambda *refs: grid_place(peers, *refs), "grid_place", [shape(chosen, width)],
        (*arr5, gpre_g, embed, sends_row), flops=3 * unit,
    )
    depth = width // total
    if not fine(width, dims):
        last, first, embed = (scatter_plain(blocks, dims) for blocks in (keep1, keep0, keep_e))
        grads = [jnp.stack([first[i], last[i]]) for i in range(3)]
        return (mesh_out, grid_grad, embed[0], first[3], *grads)
    grads = call(
        finish, "finish",
        [shape(depth, width, dtype=F32)] * 2 + [shape(2, depth, width, dtype=F32)] * 3,
        (*scatter_halving(keep1, give1, place, dims), *scatter_halving(keep0, give0, place, dims),
         *scatter_halving(keep_e, give_e, place, dims)),
        flops=8 * depth * width,
    )
    return (mesh_out, grid_grad, *grads)


def solution(mesh):
    split = ("groups", "lon", "lat", "sub")
    dims = tuple(mesh.shape[axis] for axis in GROUP)
    rows = P(split, None)
    whole = P("groups", GROUP, None)
    in_specs = (
        rows, rows, rows, P(), P(), P(), P(), P(), P(split), P(split, None, None),
        P(split, None, None), P(split, None, None), rows,
    )
    out_specs = (rows, rows, rows, rows, whole, whole, whole)
    return jax.shard_map(
        lambda *args: body(dims, *args),
        mesh=mesh, in_specs=in_specs, out_specs=out_specs, check_vma=False,
    )
```

```python
import jax
import jax.numpy as jnp
from jax import lax
from jax.experimental import pallas as pl
from jax.experimental.pallas import tpu as pltpu
from jax.sharding import PartitionSpec as P

BF = jnp.bfloat16
F32 = jnp.float32
I32 = jnp.int32
NN = (((1,), (0,)), ((), ()))
NT = (((1,), (1,)), ((), ()))
TN = (((0,), (0,)), ((), ()))
BORDER = 8
GROUP = ("lon", "lat", "sub")
COLUMN = ("lat", "sub")


def dot(a, b, dims=NN):
    return lax.dot_general(a, b, dims, preferred_element_type=F32)


def low(value):
    return value.astype(BF)


def sigmoid(value):
    return 0.5 * jnp.tanh(0.5 * value) + 0.5


def silu(value):
    return value * sigmoid(value)


def silu_both(value):
    sig = sigmoid(value)
    act = value * sig
    return act, sig + act * (1.0 - sig)


def silu_slope(value):
    return silu_both(value)[1]


def iota(rows, columns, dim):
    return lax.broadcasted_iota(I32, (rows, columns), dim)


def hot(mask):
    return jnp.where(mask, 1.0, 0.0)


def slot_of(at, column, me, odd):
    far = jnp.where(at == column - 1, column + 1 - odd, column + odd)
    return jnp.where(at < column - 1, jnp.bitwise_xor(at + 1, me), far)


def as_column(values, wide, column, me, odd):
    slots = values.shape[0]
    count = (slots - 1) * wide
    row = iota(count, slots, 0)
    pick = low(hot(slot_of(row // wide, column, me, odd) == iota(count, slots, 1)))
    found = 16.0 * dot(pick, low((values // 16).astype(F32)))
    found = found + dot(pick, low((values % 16).astype(F32)))
    keep = iota(count, wide, 0) % wide == iota(count, wide, 1)
    return jnp.sum(jnp.where(keep, found, 0.0), axis=1, keepdims=True).astype(I32)


def as_row(values, wide, column, me, odd):
    slots = values.shape[0]
    count = (slots - 1) * wide
    pick = low(hot(iota(wide, count, 1) % wide == iota(wide, count, 0)))
    found = 16.0 * dot(low((values // 16).astype(F32)), pick)
    found = found + dot(low((values % 16).astype(F32)), pick)
    at = iota(slots, count, 1) // wide
    keep = slot_of(at, column, me, odd) == iota(slots, count, 0)
    return jnp.sum(jnp.where(keep, found, 0.0), axis=0, keepdims=True).astype(I32)


def split_parts(refs, starts, sizes):
    values = [ref[...].astype(F32) for ref in refs]
    return [
        jnp.concatenate([value[start : start + size] for value in values], axis=0)
        for start, size in zip(starts, sizes)
    ]


def store_parts(refs, parts):
    peers = len(refs)
    for at, ref in enumerate(refs):
        rows = []
        for part in parts:
            size = part.shape[0] // peers
            rows.append(part[at * size : (at + 1) * size])
        ref[...] = low(rows[0] if len(rows) == 1 else jnp.concatenate(rows, axis=0))


def receivers(senders_t, halo):
    degree, nodes = senders_t.shape
    found = jnp.zeros((halo, nodes), F32)
    ids = iota(halo, nodes, 0) + nodes
    for j in range(degree):
        found = found + hot(senders_t[j : j + 1, :] == ids)
    return found


def receivers_t(senders, degree, halo):
    nodes = senders.shape[0]
    found = jnp.zeros((nodes, halo), F32)
    ids = iota(nodes, halo, 1) + nodes
    for j in range(degree):
        found = found + hot(senders[:, j : j + 1] == ids)
    return found


def fine(rows, dims):
    return (rows // (dims[0] * dims[1] * dims[2])) % 16 == 0


def reverse_bits(block, bits):
    spot = 0
    for bit in range(bits):
        spot = 2 * spot + (block >> bit) % 2
    return spot


def store_blocks(keep_ref, give_ref, at, count, value, dims, bits_ref):
    value = low(value)
    rows = value.shape[0]
    total = dims[0] * dims[1] * dims[2]
    depth = rows // total
    if not fine(rows, dims):
        keep_ref[at] = value
        return
    bits = (total - 1).bit_length()
    upper = bits_ref[0:1, 2:3] == 1
    for block in range(0, total, 2):
        start = reverse_bits(block, bits) * count * depth + at * depth
        first = value[block * depth : (block + 1) * depth].astype(F32)
        second = value[(block + 1) * depth : (block + 2) * depth].astype(F32)
        keep_ref[start : start + depth, :] = low(jnp.where(upper, second, first))
        give_ref[start : start + depth, :] = low(jnp.where(upper, first, second))


def blocks_shapes(count, rows, width, dims):
    if fine(rows, dims):
        return [jax.ShapeDtypeStruct((count * rows // 2, width), BF)] * 2
    return [jax.ShapeDtypeStruct((count, rows, width), BF), jax.ShapeDtypeStruct((16, width), BF)]


def halve(bit, bits_ref, keep_ref, arr_ref, keep_out, give_out):
    half = keep_ref.shape[0] // 2
    upper = bits_ref[0:1, 2 + bit : 3 + bit] == 1
    first = keep_ref[:half, :].astype(F32) + arr_ref[:half, :].astype(F32)
    second = keep_ref[half:, :].astype(F32) + arr_ref[half:, :].astype(F32)
    keep_out[...] = low(jnp.where(upper, second, first))
    give_out[...] = low(jnp.where(upper, first, second))


def swap(block, bit, dims):
    total = dims[0] * dims[1] * dims[2]
    return lax.ppermute(block, GROUP, [(i, i ^ (1 << bit)) for i in range(total)])


def halve_step(bit, keep, arrived, place):
    rows, width = keep.shape[0] // 2, keep.shape[1]
    return call(
        lambda *refs: halve(bit, *refs), "halve", [shape(rows, width)] * 2,
        (place, keep, arrived), flops=4 * rows * width,
    )


def rest_of_halving(first, keep, give, place, dims):
    bits = (dims[0] * dims[1] * dims[2] - 1).bit_length()
    arrived = swap(give, first, dims)
    for bit in range(first + 1, bits):
        keep, give = halve_step(bit, keep, arrived, place)
        arrived = swap(give, bit, dims)
    return keep, arrived


def halve_carry(bit, bits_ref, keep_ref, arr_ref, *refs):
    *own_refs, keep_out, give_out, here_ref, on_ref = refs
    rows = keep_ref.shape[0]
    half = rows // 2
    size = here_ref.shape[0]
    upper = bits_ref[0:1, 2 + bit : 3 + bit] == 1
    value = arr_ref[...].astype(F32)
    first = keep_ref[:half, :].astype(F32) + value[:half]
    second = keep_ref[half:, :].astype(F32) + value[half:rows]
    keep_out[...] = low(jnp.where(upper, second, first))
    here_ref[...] = low(value[rows : rows + size])
    passed = value[rows + size : rows + 2 * size]
    on_ref[...] = low(passed)
    extra = [ref[...].astype(F32) for ref in own_refs]
    if len(extra) < 2:
        extra.append(passed)
    give_out[...] = low(jnp.concatenate([jnp.where(upper, first, second), *extra], axis=0))


def carry_step(bit, keep, arrived, own, place, capacity):
    rows, width = keep.shape[0] // 2, keep.shape[1]
    return call(
        lambda *refs: halve_carry(bit, *refs), "halve_carry",
        [shape(rows, width), shape(rows + min(len(own) + 1, 2) * capacity, width),
         shape(capacity, width), shape(capacity, width)],
        (place, keep, arrived, *own), flops=4 * rows * width,
    )


def scatter_plain(blocks, dims):
    lon, lat, sub = dims
    count, rows, width = blocks.shape
    depth = rows // (lon * lat * sub)
    blocks = blocks.reshape(count, lon, lat, sub, depth, width)
    blocks = blocks.transpose(3, 2, 1, 0, 4, 5)
    for axis in ("sub", "lat", "lon"):
        blocks = lax.psum_scatter(blocks, axis, scatter_dimension=0, tiled=False)
    return blocks.astype(F32)


def call(kernel, name, outs, args, flops, loads=(), scratch=()):
    size = sum(a.size * a.dtype.itemsize for a in (*args, *outs, *loads))
    args = (*(pltpu.with_memory_space_constraint(a, pltpu.HBM) for a in loads), *args)
    scratch = list(scratch)
    if loads:
        scratch.append(pltpu.SemaphoreType.DMA((len(loads),)))
    in_specs = [pl.BlockSpec(memory_space=pltpu.HBM)] * len(loads)
    in_specs += [pl.BlockSpec(memory_space=pltpu.VMEM)] * (len(args) - len(loads))
    return pl.pallas_call(
        kernel,
        out_shape=[shape(*a.shape, dtype=a.dtype) for a in loads] + list(outs),
        in_specs=in_specs,
        out_specs=[pl.BlockSpec(memory_space=pltpu.VMEM)] * (len(outs) + len(loads)),
        scratch_shapes=scratch,
        compiler_params=pltpu.CompilerParams(vmem_limit_bytes=16 * 1024 * 1024),
        cost_estimate=pl.CostEstimate(flops=flops, bytes_accessed=size, transcendentals=0),
        name=name,
    )(*args)


def exchange(parts, dims):
    column = dims[1] * dims[2]
    count = dims[0]
    other = [(i, (i - 1 + 2 * (i % 2)) % count) for i in range(count)]
    far = lax.ppermute(parts[column], "lon", other)
    near = lax.ppermute(parts[column - 1], "lon", [(i, i ^ 1) for i in range(count)])
    arrived = [
        lax.ppermute(parts[r - 1], COLUMN, [(i, i ^ r) for i in range(column)])
        for r in range(column - 1, 0, -1)
    ]
    return (far, near, *arrived)


def shape(*dims, dtype=BF):
    return jax.ShapeDtypeStruct(dims, dtype)


def start_loads(sources, targets, sems):
    copies = [
        pltpu.make_async_copy(source, target, sems.at[at])
        for at, (source, target) in enumerate(zip(sources, targets))
    ]
    for copy in copies:
        copy.start()
    return copies


def first_payload(
    column, capacity, grid_far, embed_far, target_far, senders_far, ints_ref,
    grid_ref, embed_ref, target_ref, senders_ref, sends_ref, *rest
):
    *pay_refs, sems = rest
    grid_load, *loads = start_loads(
        (grid_far, embed_far, target_far, senders_far),
        (grid_ref, embed_ref, target_ref, senders_ref), sems,
    )
    chosen = grid_ref.shape[0]
    ints = ints_ref[...]
    base = 2 * capacity + BORDER
    me, odd = ints[0:1, base : base + 1], ints[0:1, base + 1 : base + 2]
    sends = as_column(ints[:, :capacity], capacity, column, me, odd)
    sends_ref[...] = sends
    pick = low(hot(sends == iota(sends.shape[0], chosen, 1)))
    grid_load.wait()
    store_parts(pay_refs, [dot(pick, grid_ref[...])])
    for load in loads:
        load.wait()


def embed_local(
    column, capacity, mesh_far, merge_far, cot_far, ints_ref, senders_ref, grid_ref, weight_ref,
    target_ref, sends_ref, mesh_ref, merge_ref, cot_ref,
    sum_ref, slope_ref, sends_row_ref, incoming_ref, bounds_ref, bounds_row_ref, senders_t_ref,
    senders_out_ref, place_ref, sems,
):
    loads = start_loads((mesh_far, merge_far, cot_far), (mesh_ref, merge_ref, cot_ref), sems)
    chosen = grid_ref.shape[0]
    nodes = sum_ref.shape[0]
    taken = sends_ref.shape[0]
    act, slope = silu_both(dot(grid_ref[...], weight_ref[...]))
    slope_ref[...] = low(slope)
    sent = jnp.max(hot(sends_ref[...] == iota(taken, chosen, 1)), axis=0, keepdims=True)
    label = jnp.where(sent > 0.0, nodes, target_ref[...])
    sum_ref[...] = dot(low(hot(label == iota(nodes, chosen, 0))), low(act))
    ints = ints_ref[...]
    base = 2 * capacity + BORDER
    place_ref[...] = ints[:, base:]
    me, odd = ints[0:1, base : base + 1], ints[0:1, base + 1 : base + 2]
    sends, incoming = ints[:, :capacity], ints[:, capacity : 2 * capacity]
    bounds = ints[:, 2 * capacity : base]
    sends_row_ref[...] = as_row(sends, capacity, column, me, odd)
    incoming_ref[...] = as_row(incoming, capacity, column, me, odd)
    bounds_ref[...] = as_column(bounds, BORDER, column, me, odd)
    bounds_row_ref[...] = as_row(bounds, BORDER, column, me, odd)
    senders = senders_ref[...]
    degree = senders.shape[0]
    offset = senders - nodes
    slot = offset // BORDER
    far = jnp.where(slot == column, column - odd, column - 1 + odd)
    at = jnp.where(slot < column, jnp.bitwise_xor(slot, me) - 1, far)
    senders = jnp.where(offset < 0, senders, nodes + at * BORDER + offset % BORDER)
    senders_t_ref[...] = senders
    filler = jnp.zeros((8 - degree, nodes), I32)
    senders_out_ref[...] = jnp.concatenate([senders, filler], axis=0).T
    for load in loads:
        load.wait()


def merge_nodes(peers, *refs):
    arr_refs, refs = refs[:peers][::-1], refs[peers:]
    (incoming_ref, embed_ref, local_ref, mesh_ref, weight_ref, bounds_ref, senders_t_ref, cot_ref,
     merged_ref, state_ref, slope_ref, lat_ref, *pay_refs) = refs
    nodes = mesh_ref.shape[0]
    taken = incoming_ref.shape[1]
    halo = peers * BORDER
    lat = jnp.concatenate([ref[...] for ref in arr_refs], axis=0)
    lat_ref[...] = lat
    act, slope = silu_both(dot(lat, embed_ref[...]))
    slope_ref[...] = low(slope)
    place = low(hot(incoming_ref[...] == iota(nodes, taken, 0)))
    merged = low(local_ref[...] + dot(place, low(act)))
    merged_ref[...] = merged
    state = low(mesh_ref[...].astype(F32) + dot(merged, weight_ref[...]))
    state_ref[...] = state
    border = low(hot(bounds_ref[...] == iota(halo, nodes, 1)))
    back = low(receivers(senders_t_ref[...], halo))
    store_parts(
        pay_refs,
        [dot(border, state), dot(back, state), dot(border, merged), dot(back, cot_ref[...])],
    )


def local_edges(senders, degree, sent, recv, each):
    nodes = senders.shape[0]
    total = None
    ids = iota(nodes, nodes, 1)
    for j in range(degree):
        act, slope = silu_both(dot(low(hot(senders[:, j : j + 1] == ids)), sent) + recv)
        total = act if total is None else total + act
        each(j, slope)
    return total


def edge_targets(senders_t):
    degree, nodes = senders_t.shape
    ids = iota(nodes, nodes, 0)
    return jnp.concatenate(
        [low(hot(senders_t[j : j + 1, :] == ids)) for j in range(degree)], axis=1
    )


def forward_local(
    state_ref, send_ref, recv_ref, senders_ref, senders_t_ref, bounds_ref,
    total_ref, slope_ref, recv_n_ref, sent_b_ref,
):
    state = state_ref[...]
    nodes = state.shape[0]
    halo = bounds_ref.shape[0]
    sent = low(dot(state, send_ref[0]))
    recv = dot(state, recv_ref[0])

    def keep(j, slope):
        slope_ref[j] = low(slope)

    total_ref[...] = local_edges(senders_ref[...], senders_t_ref.shape[0], sent, recv, keep)
    back = low(receivers(senders_t_ref[...], halo))
    recv_n_ref[...] = dot(low(dot(back, state)), recv_ref[0])
    sent_b_ref[...] = low(dot(low(hot(bounds_ref[...] == iota(halo, nodes, 1))), sent))


def forward_halo(peers, *refs):
    arr_refs, refs = refs[:peers][::-1], refs[peers:]
    (recv_n_ref, total_ref, state_ref, send_ref, update_ref, senders_ref, senders_t_ref,
     bounds_ref, summed_ref, out_ref, pre_ref, rows_ref, back_ref, merged_ref, cot_ref,
     *pay_refs) = refs
    nodes = state_ref.shape[0]
    degree = senders_t_ref.shape[0]
    halo = peers * BORDER
    rows, back, merged, cot = split_parts(
        arr_refs, (0, BORDER, 2 * BORDER, 3 * BORDER), (BORDER,) * 4
    )
    rows_ref[...], back_ref[...] = low(rows), low(back)
    merged_ref[...], cot_ref[...] = low(merged), low(cot)
    pre = low(dot(low(rows), send_ref[0])).astype(F32) + recv_n_ref[...]
    pre_ref[...] = pre
    place = low(receivers_t(senders_ref[...], degree, halo))
    extra = silu(pre) - silu(recv_n_ref[...])
    summed = low(total_ref[...] + dot(place, low(extra)))
    summed_ref[...] = summed
    state = low(state_ref[...].astype(F32) + dot(summed, update_ref[0]))
    out_ref[...] = state
    border = low(hot(bounds_ref[...] == iota(halo, nodes, 1)))
    back = low(receivers(senders_t_ref[...], halo))
    store_parts(pay_refs, [dot(border, state), dot(back, state)])


def turn_local(
    state_ref, send_ref, recv_ref, update_ref, cot_ref, cot_r_ref, pre_ref, recv_n0_ref, back0_ref,
    sent_b0_ref, senders_ref, senders_t_ref, bounds_ref,
    total_ref, grecv_ref, gsent_ref, recv_n_ref, sent_b_ref, gsum_n_ref, gsum_r_ref,
    slope_k_ref, slope_d_ref, slope_r_ref, gpre_ref,
):
    halo = bounds_ref.shape[0]
    slope = silu_slope(pre_ref[...])
    slope_k_ref[...] = low(slope)
    slope_d_ref[...] = low(slope - silu_slope(recv_n0_ref[...]))
    pre = sent_b0_ref[...].astype(F32) + dot(back0_ref[...], recv_ref[0])
    slope_r_ref[...] = low(silu_slope(pre))
    state = state_ref[...]
    nodes = state.shape[0]
    sent = low(dot(state, send_ref[1]))
    recv = dot(state, recv_ref[1])
    gsum = low(dot(cot_ref[...], update_ref[1], NT))
    grad = gsum.astype(F32)
    grecv = []

    def back_edge(j, slope):
        gpre = grad * slope
        grecv.append(gpre if j == 0 else grecv[-1] + gpre)
        gpre_ref[j * nodes : (j + 1) * nodes, :] = low(gpre)

    degree = senders_t_ref.shape[0]
    total_ref[...] = local_edges(senders_ref[...], degree, sent, recv, back_edge)
    grecv_ref[...] = grecv[-1]
    gsent_ref[...] = dot(edge_targets(senders_t_ref[...]), gpre_ref[...])
    back = low(receivers(senders_t_ref[...], halo))
    recv_n_ref[...] = dot(low(dot(back, state)), recv_ref[1])
    sent_b_ref[...] = low(dot(low(hot(bounds_ref[...] == iota(halo, nodes, 1))), sent))
    gsum_n_ref[...] = low(dot(back, gsum))
    gsum_r_ref[...] = low(dot(cot_r_ref[...], update_ref[1], NT))


def turn_halo(peers, *refs):
    arr_refs, refs = refs[:peers][::-1], refs[peers:]
    (recv_n_ref, sent_b_ref, gsum_n_ref, gsum_r_ref, total_ref, grecv_ref, gsent_ref, cot_ref,
     send_ref, recv_ref, senders_ref, senders_t_ref, bounds_ref, summed_ref, grecv_out_ref,
     gsent_out_ref, gin_ref, *pay_refs) = refs
    nodes = cot_ref.shape[0]
    degree = senders_t_ref.shape[0]
    halo = peers * BORDER
    rows, back = split_parts(arr_refs, (0, BORDER), (BORDER,) * 2)
    pre = low(dot(low(rows), send_ref[1])).astype(F32) + recv_n_ref[...]
    act, slope = silu_both(pre)
    place = low(receivers_t(senders_ref[...], degree, halo))
    base, base_slope = silu_both(recv_n_ref[...])
    gpre = low(gsum_n_ref[...].astype(F32) * (slope - base_slope))
    grecv = low(grecv_ref[...] + dot(place, gpre))
    pre = sent_b_ref[...].astype(F32) + dot(low(back), recv_ref[1])
    gpre = low(gsum_r_ref[...].astype(F32) * silu_slope(pre))
    border = low(hot(bounds_ref[...] == iota(nodes, halo, 0)))
    gsent = low(gsent_ref[...] + dot(border, gpre))
    gin = cot_ref[...].astype(F32) + dot(grecv, recv_ref[1], NT) + dot(gsent, send_ref[1], NT)
    gin = low(gin)
    gin_ref[...] = gin
    store_parts(pay_refs, [dot(low(receivers(senders_t_ref[...], halo)), gin)])
    summed_ref[...] = low(total_ref[...] + dot(place, low(act - base)))
    grecv_out_ref[...] = grecv
    gsent_out_ref[...] = gsent


def last_weights(
    dims, place_ref, state_ref, summed_ref, cot_ref, grecv_ref, gsent_ref, update_ref,
    keep_ref, give_ref, mesh_ref,
):
    state, summed = state_ref[...], summed_ref[...]

    def store(at, value):
        store_blocks(keep_ref, give_ref, at, 3, value, dims, place_ref)

    store(0, dot(state, gsent_ref[...], TN))
    store(1, dot(state, grecv_ref[...], TN))
    store(2, dot(summed, cot_ref[...], TN))
    mesh_ref[...] = low(state.astype(F32) + dot(summed, update_ref[1]))


def back_local(
    dims, place_ref, gin_ref, slope_ref, slope_k_ref, slope_d_ref, send_ref, recv_ref, update_ref,
    senders_ref, senders_t_ref, state_ref, rows_ref, summed_ref, merged_ref, merged_r_ref,
    after_ref, part_ref, keep_ref, give_ref, keep2_ref, give2_ref, gpre_ref,
):
    nodes = gin_ref.shape[0]
    halo = slope_k_ref.shape[0]
    degree = senders_t_ref.shape[0]
    gin = gin_ref[...]
    gsum = low(dot(gin, update_ref[0], NT))
    place = low(receivers_t(senders_ref[...], degree, halo))
    back = low(receivers(senders_t_ref[...], halo))
    gsum_n = low(dot(back, gsum))
    gpre_k = gsum_n * slope_k_ref[...]
    grecv = dot(place, gsum_n * slope_d_ref[...])
    for j in range(degree):
        gpre = gsum * slope_ref[j]
        grecv = grecv + gpre.astype(F32)
        gpre_ref[j * nodes : (j + 1) * nodes, :] = gpre
    gsent = dot(edge_targets(senders_t_ref[...]), gpre_ref[...])
    grecv, gsent = low(grecv), low(gsent)
    part = gin.astype(F32) + dot(grecv, recv_ref[0], NT) + dot(gsent, send_ref[0], NT)
    part_ref[...] = part
    state = state_ref[...]

    def store(at, value):
        store_blocks(keep_ref, give_ref, at, 2, value, dims, place_ref)

    def store2(at, value):
        store_blocks(keep2_ref, give2_ref, at, 2, value, dims, place_ref)

    store(0, dot(state, gsent, TN) + dot(rows_ref[...], gpre_k, TN))
    store(1, dot(state, grecv, TN))
    store2(0, dot(summed_ref[...], gin, TN))
    far = low(dot(gpre_k, send_ref[0], NT))
    store2(1, dot(merged_ref[...], low(part), TN) + dot(merged_r_ref[...], far, TN))


def embed_back(peers, dims, carry, *refs):
    arr_refs, refs = refs[:peers][::-1], refs[peers:]
    (place_ref, slope_r_ref, part_ref, update_ref, send_ref, merge_ref, bounds_ref, target_ref,
     sends_ref, incoming_ref, slope_g_ref, slope_a_ref, grid_ref, lat_ref, embed_ref,
     gpre_ref, keep_ref, give_ref, *pay_refs) = refs
    nodes = part_ref.shape[0]
    halo = peers * BORDER
    chosen = grid_ref.shape[0]
    taken = sends_ref.shape[0]
    (arrived,) = split_parts(arr_refs, (0,), (BORDER,))
    gsum = low(dot(low(arrived), update_ref[0], NT)).astype(F32)
    gpre = low(gsum * slope_r_ref[...].astype(F32))
    border = low(hot(bounds_ref[...] == iota(nodes, halo, 0)))
    gsent = low(dot(border, gpre))
    gin = low(part_ref[...] + dot(gsent, send_ref[0], NT))
    gmerged = low(dot(gin, merge_ref[...], NT))
    place = low(hot(incoming_ref[...] == iota(nodes, taken, 0)))
    gpre_a = low(dot(place, gmerged, TN) * slope_a_ref[...].astype(F32))
    sent = jnp.max(hot(sends_ref[...] == iota(taken, chosen, 1)), axis=0, keepdims=True)
    label = jnp.where(sent > 0.0, nodes, target_ref[...])
    pick = low(hot(label == iota(nodes, chosen, 0)))
    gpre_g = low(dot(pick, gmerged, TN) * slope_g_ref[...].astype(F32))
    gpre_ref[...] = gpre_g
    grad = dot(grid_ref[...], gpre_g, TN) + dot(lat_ref[...], gpre_a, TN)
    store_blocks(keep_ref, give_ref, 0, 1, grad, dims, place_ref)
    rows = dot(gpre_a, embed_ref[...], NT)
    store_parts(pay_refs, [rows])
    if carry:
        size = taken // peers
        start = keep_ref.shape[0]
        give_ref[start : start + 2 * size, :] = low(
            jnp.concatenate([rows[:size], rows[2 * size : 3 * size]], axis=0)
        )


def grid_place(peers, *refs):
    arr_refs, refs = refs[:peers][::-1], refs[peers:]
    gpre_ref, weight_ref, sends_ref, out_ref = refs
    chosen = gpre_ref.shape[0]
    taken = sends_ref.shape[1]
    local = dot(gpre_ref[...], weight_ref[...], NT)
    place = low(hot(sends_ref[...] == iota(chosen, taken, 0)))
    size = taken // peers
    rows = [ref[...].astype(F32) for ref in arr_refs]
    rows = low(jnp.concatenate([row[row.shape[0] - size :] for row in rows], axis=0))
    out_ref[...] = low(local + dot(place, rows))


def finish(
    keep1_ref, arr1_ref, keep0_ref, arr0_ref, keep2_ref, arr2_ref, keep_e_ref, arr_e_ref,
    embed_ref, merge_ref, send_ref, recv_ref, update_ref,
):
    last = keep1_ref[...].astype(F32) + arr1_ref[...].astype(F32)
    first = keep0_ref[...].astype(F32) + arr0_ref[...].astype(F32)
    second = keep2_ref[...].astype(F32) + arr2_ref[...].astype(F32)
    depth = embed_ref.shape[0]
    embed_ref[...] = keep_e_ref[...].astype(F32) + arr_e_ref[:depth, :].astype(F32)
    for at, ref in enumerate((send_ref, recv_ref, update_ref)):
        ref[1] = last[at * depth : (at + 1) * depth]
    send_ref[0], recv_ref[0], update_ref[0] = first[:depth], first[depth:], second[:depth]
    merge_ref[...] = second[depth:]


def body(
    dims,
    grid_latent, mesh_latent, cotangent, embed_weight, merge_weight, send_weight, recv_weight,
    update_weight, target_row, send_rows, incoming_rows, border_mesh_rows, mesh_senders,
):
    chosen, width = grid_latent.shape
    nodes, degree = mesh_senders.shape
    slots, capacity = send_rows.shape[1:]
    column = dims[1] * dims[2]
    peers = slots - 1
    halo = peers * BORDER
    taken = peers * capacity
    total = dims[0] * dims[1] * dims[2]
    bits = (total - 1).bit_length()
    carry = dims == (4, 2, 2) and fine(width, dims)
    spot = lax.axis_index(GROUP)
    place = [lax.axis_index(COLUMN), lax.axis_index("lon") % 2]
    place += [(spot >> bit) % 2 for bit in range(bits)]
    place = jnp.broadcast_to(jnp.stack(place).astype(I32)[None], (slots, 2 + bits))
    ints = jnp.concatenate([send_rows[0], incoming_rows[0], border_mesh_rows[0], place], axis=1)
    unit = 2 * nodes * width * width

    grid, embed, targets, senders_raw, sends, *pay1 = call(
        lambda *refs: first_payload(column, capacity, *refs), "first_payload",
        [shape(taken, 1, dtype=I32)] + [shape(capacity, width)] * peers,
        (ints,), flops=unit // 2,
        loads=(grid_latent, embed_weight, target_row.reshape(1, chosen), mesh_senders.T),
    )
    arr1 = exchange(pay1, dims)
    (mesh, merge, cot, local, slope_g, sends_row, incoming, bounds, bounds_row, senders_t, senders,
     place) = call(
        lambda *refs: embed_local(column, capacity, *refs), "embed_local",
        [shape(nodes, width, dtype=F32), shape(chosen, width), shape(1, taken, dtype=I32),
         shape(1, taken, dtype=I32), shape(halo, 1, dtype=I32), shape(1, halo, dtype=I32),
         shape(degree, nodes, dtype=I32), shape(nodes, 8, dtype=I32),
         shape(slots, 2 + bits, dtype=I32)],
        (ints, senders_raw, grid, embed, targets, sends), flops=3 * unit,
        loads=(mesh_latent, merge_weight, cotangent),
    )
    merged, state0, slope_a, lat_a, *pay2 = call(
        lambda *refs: merge_nodes(peers, *refs), "merge_nodes",
        [shape(nodes, width), shape(nodes, width), shape(taken, width), shape(taken, width)]
        + [shape(4 * BORDER, width)] * peers,
        (*arr1, incoming, embed, local, mesh, merge, bounds, senders_t, cot),
        flops=2 * unit,
    )
    arr2 = exchange(pay2, dims)
    total0, slope0, recv_n0, sent_b0 = call(
        forward_local, "forward_local",
        [shape(nodes, width, dtype=F32), shape(degree, nodes, width),
         shape(halo, width, dtype=F32), shape(halo, width)],
        (state0, send_weight, recv_weight, senders, senders_t, bounds), flops=6 * unit,
    )
    summed0, state1, pre0, rows0, back0, merged_r, cot_r, *pay3 = call(
        lambda *refs: forward_halo(peers, *refs), "forward_halo",
        [shape(nodes, width), shape(nodes, width), shape(halo, width, dtype=F32)]
        + [shape(halo, width)] * 4 + [shape(2 * BORDER, width)] * peers,
        (*arr2, recv_n0, total0, state0, send_weight, update_weight, senders, senders_t, bounds),
        flops=2 * unit,
    )
    arr3 = exchange(pay3, dims)
    (total1, grecv_l, gsent_l, recv_n1, sent_b1, gsum_n1, gsum_r1, slope_k0, slope_d0,
     slope_r0) = call(
        turn_local, "turn_local",
        [shape(nodes, width, dtype=F32)] * 3 + [shape(halo, width, dtype=F32)]
        + [shape(halo, width)] * 6,
        (state1, send_weight, recv_weight, update_weight, cot, cot_r, pre0, recv_n0, back0,
         sent_b0, senders, senders_t, bounds),
        flops=10 * unit, scratch=[pltpu.VMEM((degree * nodes, width), BF)],
    )
    summed1, grecv1, gsent1, gin1, *pay4 = call(
        lambda *refs: turn_halo(peers, *refs), "turn_halo",
        [shape(nodes, width)] * 4 + [shape(BORDER, width)] * peers,
        (*arr3, recv_n1, sent_b1, gsum_n1, gsum_r1, total1, grecv_l, gsent_l, cot,
         send_weight, recv_weight, senders, senders_t, bounds_row),
        flops=3 * unit,
    )
    arr4 = exchange(pay4, dims)
    keep1, give1, mesh_out = call(
        lambda *refs: last_weights(dims, *refs), "last_weights",
        blocks_shapes(3, width, width, dims) + [shape(nodes, width)],
        (place, state1, summed1, cot, grecv1, gsent1, update_weight), flops=4 * unit,
    )
    part0, keep0, give0, keep2, give2 = call(
        lambda *refs: back_local(dims, *refs), "back_local",
        [shape(nodes, width, dtype=F32)] + blocks_shapes(2, width, width, dims) * 2,
        (place, gin1, slope0, slope_k0, slope_d0, send_weight, recv_weight, update_weight, senders,
         senders_t, state0, rows0, summed0, merged, merged_r, give1),
        flops=10 * unit, scratch=[pltpu.VMEM((degree * nodes, width), BF)],
    )
    split = fine(width, dims)
    if split:
        give1, last = lax.optimization_barrier((give1, arr4[-1]))
        arr4 = (*arr4[:-1], last)
        give0, give2, *arr4 = lax.optimization_barrier((give0, give2, *arr4))
        keep1, give1 = halve_step(1, keep1, swap(give1, 0, dims), place)
        keep1, *arr4 = lax.optimization_barrier((keep1, *arr4))
    shapes = blocks_shapes(1, width, width, dims)
    if carry:
        shapes[1] = shape(shapes[1].shape[0] + 2 * capacity, width)
    gpre_g, keep_e, give_e, *pay5 = call(
        lambda *refs: embed_back(peers, dims, carry, *refs), "embed_back",
        [shape(chosen, width)] + shapes + [shape(capacity, width)] * peers,
        (*arr4, place, slope_r0, part0, update_weight, send_weight, merge, bounds_row,
         targets, sends, incoming, slope_g, slope_a, grid, lat_a, embed),
        flops=6 * unit,
    )
    if carry:
        arrived = swap(give_e, 0, dims)
        keep_e, give_e, from_sub, _ = carry_step(1, keep_e, arrived, (pay5[1],), place, capacity)
    else:
        arr5 = exchange(pay5, dims)
    if split:
        keep0, give0 = halve_step(1, keep0, swap(give0, 0, dims), place)
        keep2, give2 = halve_step(1, keep2, swap(give2, 0, dims), place)
        give0, give2, keep_e = lax.optimization_barrier((give0, give2, keep_e))
    if carry:
        arrived = swap(give_e, 1, dims)
        keep_e, give_e, from_lat, from_diag = carry_step(
            2, keep_e, arrived, pay5[3:], place, capacity
        )
        arrived = swap(give_e, 2, dims)
        keep_e, give_e, from_near, _ = carry_step(3, keep_e, arrived, (), place, capacity)
        arr_e = swap(give_e, 3, dims)
        arr5 = (arr_e, from_near, from_diag, from_lat, from_sub)
    (grid_grad,) = call(
        lambda *refs: grid_place(peers, *refs), "grid_place", [shape(chosen, width)],
        (*arr5, gpre_g, embed, sends_row), flops=3 * unit,
    )
    depth = width // total
    if not split:
        last, first, second, embed = (
            scatter_plain(blocks, dims) for blocks in (keep1, keep0, keep2, keep_e)
        )
        grads = [jnp.stack([a, last[i]]) for i, a in enumerate((first[0], first[1], second[0]))]
        return (mesh_out, grid_grad, embed[0], second[1], *grads)
    if not carry:
        keep_e, arr_e = rest_of_halving(0, keep_e, give_e, place, dims)
    grads = call(
        finish, "finish",
        [shape(depth, width, dtype=F32)] * 2 + [shape(2, depth, width, dtype=F32)] * 3,
        (*rest_of_halving(1, keep1, give1, place, dims),
         *rest_of_halving(1, keep0, give0, place, dims),
         *rest_of_halving(1, keep2, give2, place, dims), keep_e, arr_e),
        flops=8 * depth * width,
    )
    return (mesh_out, grid_grad, *grads)


def solution(mesh):
    split = ("groups", "lon", "lat", "sub")
    dims = tuple(mesh.shape[axis] for axis in GROUP)
    rows = P(split, None)
    whole = P("groups", GROUP, None)
    in_specs = (
        rows, rows, rows, P(), P(), P(), P(), P(), P(split), P(split, None, None),
        P(split, None, None), P(split, None, None), rows,
    )
    out_specs = (rows, rows, rows, rows, whole, whole, whole)
    return jax.shard_map(
        lambda *args: body(dims, *args),
        mesh=mesh, in_specs=in_specs, out_specs=out_specs, check_vma=False,
    )
```

```python
import jax
import jax.numpy as jnp
from jax import lax
from jax.experimental import pallas as pl
from jax.experimental.pallas import tpu as pltpu
from jax.sharding import PartitionSpec as P

BF = jnp.bfloat16
F32 = jnp.float32
I32 = jnp.int32
NN = (((1,), (0,)), ((), ()))
NT = (((1,), (1,)), ((), ()))
TN = (((0,), (0,)), ((), ()))
BORDER = 8
GROUP = ("lon", "lat", "sub")
COLUMN = ("lat", "sub")


def dot(a, b, dims=NN):
    return lax.dot_general(a, b, dims, preferred_element_type=F32)


def low(value):
    return value.astype(BF)


def sigmoid(value):
    return 0.5 * jnp.tanh(0.5 * value) + 0.5


def silu(value):
    return value * sigmoid(value)


def silu_both(value):
    sig = sigmoid(value)
    act = value * sig
    return act, sig + act * (1.0 - sig)


def silu_slope(value):
    return silu_both(value)[1]


def iota(rows, columns, dim):
    return lax.broadcasted_iota(I32, (rows, columns), dim)


def hot(mask):
    return jnp.where(mask, 1.0, 0.0)


def slot_of(at, column, me, odd):
    far = jnp.where(at == column - 1, column + 1 - odd, column + odd)
    return jnp.where(at < column - 1, jnp.bitwise_xor(at + 1, me), far)


def as_column(values, wide, column, me, odd):
    slots = values.shape[0]
    count = (slots - 1) * wide
    row = iota(count, slots, 0)
    pick = low(hot(slot_of(row // wide, column, me, odd) == iota(count, slots, 1)))
    found = 16.0 * dot(pick, low((values // 16).astype(F32)))
    found = found + dot(pick, low((values % 16).astype(F32)))
    keep = iota(count, wide, 0) % wide == iota(count, wide, 1)
    return jnp.sum(jnp.where(keep, found, 0.0), axis=1, keepdims=True).astype(I32)


def as_row(values, wide, column, me, odd):
    slots = values.shape[0]
    count = (slots - 1) * wide
    pick = low(hot(iota(wide, count, 1) % wide == iota(wide, count, 0)))
    found = 16.0 * dot(low((values // 16).astype(F32)), pick)
    found = found + dot(low((values % 16).astype(F32)), pick)
    at = iota(slots, count, 1) // wide
    keep = slot_of(at, column, me, odd) == iota(slots, count, 0)
    return jnp.sum(jnp.where(keep, found, 0.0), axis=0, keepdims=True).astype(I32)


def split_parts(refs, starts, sizes):
    values = [ref[...].astype(F32) for ref in refs]
    return [
        jnp.concatenate([value[start : start + size] for value in values], axis=0)
        for start, size in zip(starts, sizes)
    ]


def store_parts(refs, parts):
    peers = len(refs)
    for at, ref in enumerate(refs):
        rows = []
        for part in parts:
            size = part.shape[0] // peers
            rows.append(part[at * size : (at + 1) * size])
        ref[...] = low(rows[0] if len(rows) == 1 else jnp.concatenate(rows, axis=0))


def receivers(senders_t, halo):
    degree, nodes = senders_t.shape
    found = jnp.zeros((halo, nodes), F32)
    ids = iota(halo, nodes, 0) + nodes
    for j in range(degree):
        found = found + hot(senders_t[j : j + 1, :] == ids)
    return found


def receivers_t(senders, degree, halo):
    nodes = senders.shape[0]
    found = jnp.zeros((nodes, halo), F32)
    ids = iota(nodes, halo, 1) + nodes
    for j in range(degree):
        found = found + hot(senders[:, j : j + 1] == ids)
    return found


def fine(rows, dims):
    return (rows // (dims[0] * dims[1] * dims[2])) % 16 == 0


def reverse_bits(block, bits):
    spot = 0
    for bit in range(bits):
        spot = 2 * spot + (block >> bit) % 2
    return spot


def store_blocks(keep_ref, give_ref, at, count, value, dims, bits_ref):
    value = low(value)
    rows = value.shape[0]
    total = dims[0] * dims[1] * dims[2]
    depth = rows // total
    if not fine(rows, dims):
        keep_ref[at] = value
        return
    bits = (total - 1).bit_length()
    upper = bits_ref[0:1, 2:3] == 1
    for block in range(0, total, 2):
        start = reverse_bits(block, bits) * count * depth + at * depth
        first = value[block * depth : (block + 1) * depth].astype(F32)
        second = value[(block + 1) * depth : (block + 2) * depth].astype(F32)
        keep_ref[start : start + depth, :] = low(jnp.where(upper, second, first))
        give_ref[start : start + depth, :] = low(jnp.where(upper, first, second))


def blocks_shapes(count, rows, width, dims):
    if fine(rows, dims):
        return [jax.ShapeDtypeStruct((count * rows // 2, width), BF)] * 2
    return [jax.ShapeDtypeStruct((count, rows, width), BF), jax.ShapeDtypeStruct((16, width), BF)]


def halve(bit, bits_ref, keep_ref, arr_ref, keep_out, give_out):
    half = keep_ref.shape[0] // 2
    upper = bits_ref[0:1, 2 + bit : 3 + bit] == 1
    first = keep_ref[:half, :].astype(F32) + arr_ref[:half, :].astype(F32)
    second = keep_ref[half:, :].astype(F32) + arr_ref[half:, :].astype(F32)
    keep_out[...] = low(jnp.where(upper, second, first))
    give_out[...] = low(jnp.where(upper, first, second))


def swap(block, bit, dims):
    total = dims[0] * dims[1] * dims[2]
    return lax.ppermute(block, GROUP, [(i, i ^ (1 << bit)) for i in range(total)])


def halve_step(bit, keep, arrived, place):
    rows, width = keep.shape[0] // 2, keep.shape[1]
    return call(
        lambda *refs: halve(bit, *refs), "halve", [shape(rows, width)] * 2,
        (place, keep, arrived), flops=4 * rows * width, size=0,
    )


def rest_of_halving(first, keep, give, place, dims):
    bits = (dims[0] * dims[1] * dims[2] - 1).bit_length()
    arrived = swap(give, first, dims)
    for bit in range(first + 1, bits):
        keep, give = halve_step(bit, keep, arrived, place)
        arrived = swap(give, bit, dims)
    return keep, arrived


def halve_carry(bit, bits_ref, keep_ref, arr_ref, *refs):
    *own_refs, keep_out, give_out, here_ref, on_ref = refs
    rows = keep_ref.shape[0]
    half = rows // 2
    size = here_ref.shape[0]
    upper = bits_ref[0:1, 2 + bit : 3 + bit] == 1
    value = arr_ref[...].astype(F32)
    first = keep_ref[:half, :].astype(F32) + value[:half]
    second = keep_ref[half:, :].astype(F32) + value[half:rows]
    keep_out[...] = low(jnp.where(upper, second, first))
    here_ref[...] = low(value[rows : rows + size])
    passed = value[rows + size : rows + 2 * size]
    on_ref[...] = low(passed)
    extra = [ref[...].astype(F32) for ref in own_refs]
    if len(extra) < 2:
        extra.append(passed)
    give_out[...] = low(jnp.concatenate([jnp.where(upper, first, second), *extra], axis=0))


def carry_step(bit, keep, arrived, own, place, capacity):
    rows, width = keep.shape[0] // 2, keep.shape[1]
    return call(
        lambda *refs: halve_carry(bit, *refs), "halve_carry",
        [shape(rows, width), shape(rows + min(len(own) + 1, 2) * capacity, width),
         shape(capacity, width), shape(capacity, width)],
        (place, keep, arrived, *own), flops=4 * rows * width, size=0,
    )


def scatter_plain(blocks, dims):
    lon, lat, sub = dims
    count, rows, width = blocks.shape
    depth = rows // (lon * lat * sub)
    blocks = blocks.reshape(count, lon, lat, sub, depth, width)
    blocks = blocks.transpose(3, 2, 1, 0, 4, 5)
    for axis in ("sub", "lat", "lon"):
        blocks = lax.psum_scatter(blocks, axis, scatter_dimension=0, tiled=False)
    return blocks.astype(F32)


def call(kernel, name, outs, args, flops, loads=(), scratch=(), size=None):
    if size is None:
        size = sum(a.size * a.dtype.itemsize for a in (*args, *outs, *loads))
    args = (*(pltpu.with_memory_space_constraint(a, pltpu.HBM) for a in loads), *args)
    scratch = list(scratch)
    if loads:
        scratch.append(pltpu.SemaphoreType.DMA((len(loads),)))
    in_specs = [pl.BlockSpec(memory_space=pltpu.HBM)] * len(loads)
    in_specs += [pl.BlockSpec(memory_space=pltpu.VMEM)] * (len(args) - len(loads))
    return pl.pallas_call(
        kernel,
        out_shape=[shape(*a.shape, dtype=a.dtype) for a in loads] + list(outs),
        in_specs=in_specs,
        out_specs=[pl.BlockSpec(memory_space=pltpu.VMEM)] * (len(outs) + len(loads)),
        scratch_shapes=scratch,
        compiler_params=pltpu.CompilerParams(vmem_limit_bytes=16 * 1024 * 1024),
        cost_estimate=pl.CostEstimate(flops=flops, bytes_accessed=size, transcendentals=0),
        name=name,
    )(*args)


def exchange(parts, dims):
    column = dims[1] * dims[2]
    count = dims[0]
    other = [(i, (i - 1 + 2 * (i % 2)) % count) for i in range(count)]
    far = lax.ppermute(parts[column], "lon", other)
    near = lax.ppermute(parts[column - 1], "lon", [(i, i ^ 1) for i in range(count)])
    arrived = [
        lax.ppermute(parts[r - 1], COLUMN, [(i, i ^ r) for i in range(column)])
        for r in range(column - 1, 0, -1)
    ]
    return (far, near, *arrived)


def shape(*dims, dtype=BF):
    return jax.ShapeDtypeStruct(dims, dtype)


def start_loads(sources, targets, sems):
    copies = [
        pltpu.make_async_copy(source, target, sems.at[at])
        for at, (source, target) in enumerate(zip(sources, targets))
    ]
    for copy in copies:
        copy.start()
    return copies


def first_payload(column, capacity, count, *refs):
    sources, ints_ref, targets = refs[:count], refs[count], refs[count + 1 : 2 * count + 1]
    sends_ref, *pay_refs, sems = refs[2 * count + 1 :]
    grid_ref = targets[0]
    grid_load, *loads = start_loads(sources, targets, sems)
    chosen = grid_ref.shape[0]
    ints = ints_ref[...]
    base = 2 * capacity + BORDER
    me, odd = ints[0:1, base : base + 1], ints[0:1, base + 1 : base + 2]
    sends = as_column(ints[:, :capacity], capacity, column, me, odd)
    sends_ref[...] = sends
    pick = low(hot(sends == iota(sends.shape[0], chosen, 1)))
    grid_load.wait()
    store_parts(pay_refs, [dot(pick, grid_ref[...])])
    for load in loads:
        load.wait()


def embed_local(
    column, capacity, ints_ref, senders_ref, grid_ref, weight_ref, target_ref, sends_ref,
    sum_ref, slope_ref, sends_row_ref, incoming_ref, bounds_ref, bounds_row_ref, senders_t_ref,
    senders_out_ref, place_ref,
):
    chosen = grid_ref.shape[0]
    nodes = sum_ref.shape[0]
    taken = sends_ref.shape[0]
    act, slope = silu_both(dot(grid_ref[...], weight_ref[...]))
    slope_ref[...] = low(slope)
    sent = jnp.max(hot(sends_ref[...] == iota(taken, chosen, 1)), axis=0, keepdims=True)
    label = jnp.where(sent > 0.0, nodes, target_ref[...])
    sum_ref[...] = dot(low(hot(label == iota(nodes, chosen, 0))), low(act))
    ints = ints_ref[...]
    base = 2 * capacity + BORDER
    place_ref[...] = ints[:, base:]
    me, odd = ints[0:1, base : base + 1], ints[0:1, base + 1 : base + 2]
    sends, incoming = ints[:, :capacity], ints[:, capacity : 2 * capacity]
    bounds = ints[:, 2 * capacity : base]
    sends_row_ref[...] = as_row(sends, capacity, column, me, odd)
    incoming_ref[...] = as_row(incoming, capacity, column, me, odd)
    bounds_ref[...] = as_column(bounds, BORDER, column, me, odd)
    bounds_row_ref[...] = as_row(bounds, BORDER, column, me, odd)
    senders = senders_ref[...]
    degree = senders.shape[0]
    offset = senders - nodes
    slot = offset // BORDER
    far = jnp.where(slot == column, column - odd, column - 1 + odd)
    at = jnp.where(slot < column, jnp.bitwise_xor(slot, me) - 1, far)
    senders = jnp.where(offset < 0, senders, nodes + at * BORDER + offset % BORDER)
    senders_t_ref[...] = senders
    filler = jnp.zeros((8 - degree, nodes), I32)
    senders_out_ref[...] = jnp.concatenate([senders, filler], axis=0).T


def merge_nodes(peers, *refs):
    arr_refs, refs = refs[:peers][::-1], refs[peers:]
    (incoming_ref, embed_ref, local_ref, mesh_ref, weight_ref, bounds_ref, senders_t_ref, cot_ref,
     merged_ref, state_ref, slope_ref, lat_ref, *pay_refs) = refs
    nodes = mesh_ref.shape[0]
    taken = incoming_ref.shape[1]
    halo = peers * BORDER
    lat = jnp.concatenate([ref[...] for ref in arr_refs], axis=0)
    lat_ref[...] = lat
    act, slope = silu_both(dot(lat, embed_ref[...]))
    slope_ref[...] = low(slope)
    place = low(hot(incoming_ref[...] == iota(nodes, taken, 0)))
    merged = low(local_ref[...] + dot(place, low(act)))
    merged_ref[...] = merged
    state = low(mesh_ref[...].astype(F32) + dot(merged, weight_ref[...]))
    state_ref[...] = state
    border = low(hot(bounds_ref[...] == iota(halo, nodes, 1)))
    back = low(receivers(senders_t_ref[...], halo))
    store_parts(
        pay_refs,
        [dot(border, state), dot(back, state), dot(border, merged), dot(back, cot_ref[...])],
    )


def local_edges(senders, degree, sent, recv, each):
    nodes = senders.shape[0]
    total = None
    ids = iota(nodes, nodes, 1)
    for j in range(degree):
        act, slope = silu_both(dot(low(hot(senders[:, j : j + 1] == ids)), sent) + recv)
        total = act if total is None else total + act
        each(j, slope)
    return total


def edge_targets(senders_t):
    degree, nodes = senders_t.shape
    ids = iota(nodes, nodes, 0)
    return jnp.concatenate(
        [low(hot(senders_t[j : j + 1, :] == ids)) for j in range(degree)], axis=1
    )


def forward_local(
    state_ref, send_ref, recv_ref, senders_ref, senders_t_ref, bounds_ref,
    total_ref, slope_ref, recv_n_ref, sent_b_ref,
):
    state = state_ref[...]
    nodes = state.shape[0]
    halo = bounds_ref.shape[0]
    sent = low(dot(state, send_ref[0]))
    recv = dot(state, recv_ref[0])

    def keep(j, slope):
        slope_ref[j] = low(slope)

    total_ref[...] = local_edges(senders_ref[...], senders_t_ref.shape[0], sent, recv, keep)
    back = low(receivers(senders_t_ref[...], halo))
    recv_n_ref[...] = dot(low(dot(back, state)), recv_ref[0])
    sent_b_ref[...] = low(dot(low(hot(bounds_ref[...] == iota(halo, nodes, 1))), sent))


def forward_halo(peers, *refs):
    arr_refs, refs = refs[:peers][::-1], refs[peers:]
    (recv_n_ref, total_ref, state_ref, send_ref, update_ref, senders_ref, senders_t_ref,
     bounds_ref, summed_ref, out_ref, pre_ref, rows_ref, back_ref, merged_ref, cot_ref,
     *pay_refs) = refs
    nodes = state_ref.shape[0]
    degree = senders_t_ref.shape[0]
    halo = peers * BORDER
    rows, back, merged, cot = split_parts(
        arr_refs, (0, BORDER, 2 * BORDER, 3 * BORDER), (BORDER,) * 4
    )
    rows_ref[...], back_ref[...] = low(rows), low(back)
    merged_ref[...], cot_ref[...] = low(merged), low(cot)
    pre = low(dot(low(rows), send_ref[0])).astype(F32) + recv_n_ref[...]
    pre_ref[...] = pre
    place = low(receivers_t(senders_ref[...], degree, halo))
    extra = silu(pre) - silu(recv_n_ref[...])
    summed = low(total_ref[...] + dot(place, low(extra)))
    summed_ref[...] = summed
    state = low(state_ref[...].astype(F32) + dot(summed, update_ref[0]))
    out_ref[...] = state
    border = low(hot(bounds_ref[...] == iota(halo, nodes, 1)))
    back = low(receivers(senders_t_ref[...], halo))
    store_parts(pay_refs, [dot(border, state), dot(back, state)])


def turn_local(
    state_ref, send_ref, recv_ref, update_ref, cot_ref, cot_r_ref, pre_ref, recv_n0_ref, back0_ref,
    sent_b0_ref, senders_ref, senders_t_ref, bounds_ref,
    total_ref, grecv_ref, gsent_ref, recv_n_ref, sent_b_ref, gsum_n_ref, gsum_r_ref,
    slope_k_ref, slope_d_ref, slope_r_ref, gpre_ref,
):
    halo = bounds_ref.shape[0]
    slope = silu_slope(pre_ref[...])
    slope_k_ref[...] = low(slope)
    slope_d_ref[...] = low(slope - silu_slope(recv_n0_ref[...]))
    pre = sent_b0_ref[...].astype(F32) + dot(back0_ref[...], recv_ref[0])
    slope_r_ref[...] = low(silu_slope(pre))
    state = state_ref[...]
    nodes = state.shape[0]
    sent = low(dot(state, send_ref[1]))
    recv = dot(state, recv_ref[1])
    gsum = low(dot(cot_ref[...], update_ref[1], NT))
    grad = gsum.astype(F32)
    grecv = []

    def back_edge(j, slope):
        gpre = grad * slope
        grecv.append(gpre if j == 0 else grecv[-1] + gpre)
        gpre_ref[j * nodes : (j + 1) * nodes, :] = low(gpre)

    degree = senders_t_ref.shape[0]
    total_ref[...] = local_edges(senders_ref[...], degree, sent, recv, back_edge)
    grecv_ref[...] = grecv[-1]
    gsent_ref[...] = dot(edge_targets(senders_t_ref[...]), gpre_ref[...])
    back = low(receivers(senders_t_ref[...], halo))
    recv_n_ref[...] = dot(low(dot(back, state)), recv_ref[1])
    sent_b_ref[...] = low(dot(low(hot(bounds_ref[...] == iota(halo, nodes, 1))), sent))
    gsum_n_ref[...] = low(dot(back, gsum))
    gsum_r_ref[...] = low(dot(cot_r_ref[...], update_ref[1], NT))


def turn_halo(peers, *refs):
    arr_refs, refs = refs[:peers][::-1], refs[peers:]
    (recv_n_ref, sent_b_ref, gsum_n_ref, gsum_r_ref, total_ref, grecv_ref, gsent_ref, cot_ref,
     send_ref, recv_ref, senders_ref, senders_t_ref, bounds_ref, summed_ref, grecv_out_ref,
     gsent_out_ref, gin_ref, *pay_refs) = refs
    nodes = cot_ref.shape[0]
    degree = senders_t_ref.shape[0]
    halo = peers * BORDER
    rows, back = split_parts(arr_refs, (0, BORDER), (BORDER,) * 2)
    pre = low(dot(low(rows), send_ref[1])).astype(F32) + recv_n_ref[...]
    act, slope = silu_both(pre)
    place = low(receivers_t(senders_ref[...], degree, halo))
    base, base_slope = silu_both(recv_n_ref[...])
    gpre = low(gsum_n_ref[...].astype(F32) * (slope - base_slope))
    grecv = low(grecv_ref[...] + dot(place, gpre))
    pre = sent_b_ref[...].astype(F32) + dot(low(back), recv_ref[1])
    gpre = low(gsum_r_ref[...].astype(F32) * silu_slope(pre))
    border = low(hot(bounds_ref[...] == iota(nodes, halo, 0)))
    gsent = low(gsent_ref[...] + dot(border, gpre))
    gin = cot_ref[...].astype(F32) + dot(grecv, recv_ref[1], NT) + dot(gsent, send_ref[1], NT)
    gin = low(gin)
    gin_ref[...] = gin
    store_parts(pay_refs, [dot(low(receivers(senders_t_ref[...], halo)), gin)])
    summed_ref[...] = low(total_ref[...] + dot(place, low(act - base)))
    grecv_out_ref[...] = grecv
    gsent_out_ref[...] = gsent


def last_weights(
    dims, place_ref, state_ref, summed_ref, cot_ref, grecv_ref, gsent_ref, update_ref,
    keep_ref, give_ref, mesh_ref,
):
    state, summed = state_ref[...], summed_ref[...]

    def store(at, value):
        store_blocks(keep_ref, give_ref, at, 3, value, dims, place_ref)

    store(0, dot(state, gsent_ref[...], TN))
    store(1, dot(state, grecv_ref[...], TN))
    store(2, dot(summed, cot_ref[...], TN))
    mesh_ref[...] = low(state.astype(F32) + dot(summed, update_ref[1]))


def back_local(
    dims, place_ref, gin_ref, slope_ref, slope_k_ref, slope_d_ref, send_ref, recv_ref, update_ref,
    senders_ref, senders_t_ref, state_ref, rows_ref, summed_ref, merged_ref, merged_r_ref,
    after_ref, part_ref, keep_ref, give_ref, keep2_ref, give2_ref, gpre_ref,
):
    nodes = gin_ref.shape[0]
    halo = slope_k_ref.shape[0]
    degree = senders_t_ref.shape[0]
    gin = gin_ref[...]
    gsum = low(dot(gin, update_ref[0], NT))
    place = low(receivers_t(senders_ref[...], degree, halo))
    back = low(receivers(senders_t_ref[...], halo))
    gsum_n = low(dot(back, gsum))
    gpre_k = gsum_n * slope_k_ref[...]
    grecv = dot(place, gsum_n * slope_d_ref[...])
    for j in range(degree):
        gpre = gsum * slope_ref[j]
        grecv = grecv + gpre.astype(F32)
        gpre_ref[j * nodes : (j + 1) * nodes, :] = gpre
    gsent = dot(edge_targets(senders_t_ref[...]), gpre_ref[...])
    grecv, gsent = low(grecv), low(gsent)
    part = gin.astype(F32) + dot(grecv, recv_ref[0], NT) + dot(gsent, send_ref[0], NT)
    part_ref[...] = part
    state = state_ref[...]

    def store(at, value):
        store_blocks(keep_ref, give_ref, at, 2, value, dims, place_ref)

    def store2(at, value):
        store_blocks(keep2_ref, give2_ref, at, 2, value, dims, place_ref)

    store(0, dot(state, gsent, TN) + dot(rows_ref[...], gpre_k, TN))
    store(1, dot(state, grecv, TN))
    store2(0, dot(summed_ref[...], gin, TN))
    far = low(dot(gpre_k, send_ref[0], NT))
    store2(1, dot(merged_ref[...], low(part), TN) + dot(merged_r_ref[...], far, TN))


def embed_back(peers, dims, carry, *refs):
    arr_refs, refs = refs[:peers][::-1], refs[peers:]
    (place_ref, slope_r_ref, part_ref, update_ref, send_ref, merge_ref, bounds_ref, target_ref,
     sends_ref, incoming_ref, slope_g_ref, slope_a_ref, grid_ref, lat_ref, embed_ref,
     gpre_ref, keep_ref, give_ref, *pay_refs) = refs
    nodes = part_ref.shape[0]
    halo = peers * BORDER
    chosen = grid_ref.shape[0]
    taken = sends_ref.shape[0]
    (arrived,) = split_parts(arr_refs, (0,), (BORDER,))
    gsum = low(dot(low(arrived), update_ref[0], NT)).astype(F32)
    gpre = low(gsum * slope_r_ref[...].astype(F32))
    border = low(hot(bounds_ref[...] == iota(nodes, halo, 0)))
    gsent = low(dot(border, gpre))
    gin = low(part_ref[...] + dot(gsent, send_ref[0], NT))
    gmerged = low(dot(gin, merge_ref[...], NT))
    place = low(hot(incoming_ref[...] == iota(nodes, taken, 0)))
    gpre_a = low(dot(place, gmerged, TN) * slope_a_ref[...].astype(F32))
    sent = jnp.max(hot(sends_ref[...] == iota(taken, chosen, 1)), axis=0, keepdims=True)
    label = jnp.where(sent > 0.0, nodes, target_ref[...])
    pick = low(hot(label == iota(nodes, chosen, 0)))
    gpre_g = low(dot(pick, gmerged, TN) * slope_g_ref[...].astype(F32))
    gpre_ref[...] = gpre_g
    grad = dot(grid_ref[...], gpre_g, TN) + dot(lat_ref[...], gpre_a, TN)
    store_blocks(keep_ref, give_ref, 0, 1, grad, dims, place_ref)
    rows = dot(gpre_a, embed_ref[...], NT)
    store_parts(pay_refs, [rows])
    if carry:
        size = taken // peers
        start = keep_ref.shape[0]
        give_ref[start : start + 2 * size, :] = low(
            jnp.concatenate([rows[:size], rows[2 * size : 3 * size]], axis=0)
        )


def grid_place(peers, *refs):
    arr_refs, refs = refs[:peers][::-1], refs[peers:]
    gpre_ref, weight_ref, sends_ref, out_ref = refs
    chosen = gpre_ref.shape[0]
    taken = sends_ref.shape[1]
    local = dot(gpre_ref[...], weight_ref[...], NT)
    place = low(hot(sends_ref[...] == iota(chosen, taken, 0)))
    size = taken // peers
    rows = [ref[...].astype(F32) for ref in arr_refs]
    rows = low(jnp.concatenate([row[row.shape[0] - size :] for row in rows], axis=0))
    out_ref[...] = low(local + dot(place, rows))


def finish(
    keep1_ref, arr1_ref, keep0_ref, arr0_ref, keep2_ref, arr2_ref, keep_e_ref, arr_e_ref,
    embed_ref, merge_ref, send_ref, recv_ref, update_ref,
):
    last = keep1_ref[...].astype(F32) + arr1_ref[...].astype(F32)
    first = keep0_ref[...].astype(F32) + arr0_ref[...].astype(F32)
    second = keep2_ref[...].astype(F32) + arr2_ref[...].astype(F32)
    depth = embed_ref.shape[0]
    embed_ref[...] = keep_e_ref[...].astype(F32) + arr_e_ref[:depth, :].astype(F32)
    for at, ref in enumerate((send_ref, recv_ref, update_ref)):
        ref[1] = last[at * depth : (at + 1) * depth]
    send_ref[0], recv_ref[0], update_ref[0] = first[:depth], first[depth:], second[:depth]
    merge_ref[...] = second[depth:]


def body(
    dims,
    grid_latent, mesh_latent, cotangent, embed_weight, merge_weight, send_weight, recv_weight,
    update_weight, target_row, send_rows, incoming_rows, border_mesh_rows, mesh_senders,
):
    chosen, width = grid_latent.shape
    nodes, degree = mesh_senders.shape
    slots, capacity = send_rows.shape[1:]
    column = dims[1] * dims[2]
    peers = slots - 1
    halo = peers * BORDER
    taken = peers * capacity
    total = dims[0] * dims[1] * dims[2]
    bits = (total - 1).bit_length()
    carry = dims == (4, 2, 2) and fine(width, dims)
    spot = lax.axis_index(GROUP)
    place = [lax.axis_index(COLUMN), lax.axis_index("lon") % 2]
    place += [(spot >> bit) % 2 for bit in range(bits)]
    place = jnp.broadcast_to(jnp.stack(place).astype(I32)[None], (slots, 2 + bits))
    ints = jnp.concatenate([send_rows[0], incoming_rows[0], border_mesh_rows[0], place], axis=1)
    unit = 2 * nodes * width * width

    loads = (grid_latent, embed_weight, target_row.reshape(1, chosen), mesh_senders.T,
             mesh_latent, merge_weight, cotangent)
    grid, embed, targets, senders_raw, mesh, merge, cot, sends, *pay1 = call(
        lambda *refs: first_payload(column, capacity, len(loads), *refs), "first_payload",
        [shape(taken, 1, dtype=I32)] + [shape(capacity, width)] * peers,
        (ints,), flops=unit // 2, loads=loads,
    )
    arr1 = exchange(pay1, dims)
    (local, slope_g, sends_row, incoming, bounds, bounds_row, senders_t, senders, place) = call(
        lambda *refs: embed_local(column, capacity, *refs), "embed_local",
        [shape(nodes, width, dtype=F32), shape(chosen, width), shape(1, taken, dtype=I32),
         shape(1, taken, dtype=I32), shape(halo, 1, dtype=I32), shape(1, halo, dtype=I32),
         shape(degree, nodes, dtype=I32), shape(nodes, 8, dtype=I32),
         shape(slots, 2 + bits, dtype=I32)],
        (ints, senders_raw, grid, embed, targets, sends), flops=3 * unit,
    )
    merged, state0, slope_a, lat_a, *pay2 = call(
        lambda *refs: merge_nodes(peers, *refs), "merge_nodes",
        [shape(nodes, width), shape(nodes, width), shape(taken, width), shape(taken, width)]
        + [shape(4 * BORDER, width)] * peers,
        (*arr1, incoming, embed, local, mesh, merge, bounds, senders_t, cot),
        flops=2 * unit,
    )
    arr2 = exchange(pay2, dims)
    total0, slope0, recv_n0, sent_b0 = call(
        forward_local, "forward_local",
        [shape(nodes, width, dtype=F32), shape(degree, nodes, width),
         shape(halo, width, dtype=F32), shape(halo, width)],
        (state0, send_weight, recv_weight, senders, senders_t, bounds), flops=6 * unit,
    )
    summed0, state1, pre0, rows0, back0, merged_r, cot_r, *pay3 = call(
        lambda *refs: forward_halo(peers, *refs), "forward_halo",
        [shape(nodes, width), shape(nodes, width), shape(halo, width, dtype=F32)]
        + [shape(halo, width)] * 4 + [shape(2 * BORDER, width)] * peers,
        (*arr2, recv_n0, total0, state0, send_weight, update_weight, senders, senders_t, bounds),
        flops=2 * unit,
    )
    arr3 = exchange(pay3, dims)
    (total1, grecv_l, gsent_l, recv_n1, sent_b1, gsum_n1, gsum_r1, slope_k0, slope_d0,
     slope_r0) = call(
        turn_local, "turn_local",
        [shape(nodes, width, dtype=F32)] * 3 + [shape(halo, width, dtype=F32)]
        + [shape(halo, width)] * 6,
        (state1, send_weight, recv_weight, update_weight, cot, cot_r, pre0, recv_n0, back0,
         sent_b0, senders, senders_t, bounds),
        flops=10 * unit, scratch=[pltpu.VMEM((degree * nodes, width), BF)],
    )
    summed1, grecv1, gsent1, gin1, *pay4 = call(
        lambda *refs: turn_halo(peers, *refs), "turn_halo",
        [shape(nodes, width)] * 4 + [shape(BORDER, width)] * peers,
        (*arr3, recv_n1, sent_b1, gsum_n1, gsum_r1, total1, grecv_l, gsent_l, cot,
         send_weight, recv_weight, senders, senders_t, bounds_row),
        flops=3 * unit,
    )
    arr4 = exchange(pay4, dims)
    keep1, give1, mesh_out = call(
        lambda *refs: last_weights(dims, *refs), "last_weights",
        blocks_shapes(3, width, width, dims) + [shape(nodes, width)],
        (place, state1, summed1, cot, grecv1, gsent1, update_weight), flops=4 * unit,
    )
    split = fine(width, dims)
    if split:
        give1, last = lax.optimization_barrier((give1, arr4[-1]))
        arr4 = (*arr4[:-1], last)
        keep1, give1 = halve_step(1, keep1, swap(give1, 0, dims), place)
    part0, keep0, give0, keep2, give2 = call(
        lambda *refs: back_local(dims, *refs), "back_local",
        [shape(nodes, width, dtype=F32)] + blocks_shapes(2, width, width, dims) * 2,
        (place, gin1, slope0, slope_k0, slope_d0, send_weight, recv_weight, update_weight, senders,
         senders_t, state0, rows0, summed0, merged, merged_r, keep1),
        flops=10 * unit, scratch=[pltpu.VMEM((degree * nodes, width), BF)],
    )
    if split:
        give0, give2, *arr4 = lax.optimization_barrier((give0, give2, *arr4))
        keep0, give0 = halve_step(1, keep0, swap(give0, 0, dims), place)
        keep0, *arr4 = lax.optimization_barrier((keep0, *arr4))
    shapes = blocks_shapes(1, width, width, dims)
    if carry:
        shapes[1] = shape(shapes[1].shape[0] + 2 * capacity, width)
    gpre_g, keep_e, give_e, *pay5 = call(
        lambda *refs: embed_back(peers, dims, carry, *refs), "embed_back",
        [shape(chosen, width)] + shapes + [shape(capacity, width)] * peers,
        (*arr4, place, slope_r0, part0, update_weight, send_weight, merge, bounds_row,
         targets, sends, incoming, slope_g, slope_a, grid, lat_a, embed),
        flops=6 * unit,
    )
    if carry:
        arrived = swap(give_e, 0, dims)
        arrived1 = swap(give1, 1, dims)
        arrived, arrived1 = lax.optimization_barrier((arrived, arrived1))
        keep1, give1 = halve_step(2, keep1, arrived1, place)
        keep_e, give_e, from_sub, _ = carry_step(1, keep_e, arrived, (pay5[1],), place, capacity)
    else:
        arr5 = exchange(pay5, dims)
    if split:
        keep2, keep_e = lax.optimization_barrier((keep2, keep_e))
        keep2, give2 = halve_step(1, keep2, swap(give2, 0, dims), place)
    if carry:
        arrived = swap(give_e, 1, dims)
        keep_e, give_e, from_lat, from_diag = carry_step(
            2, keep_e, arrived, pay5[3:], place, capacity
        )
        arrived = swap(give_e, 2, dims)
        keep_e, give_e, from_near, _ = carry_step(3, keep_e, arrived, (), place, capacity)
        arr_e = swap(give_e, 3, dims)
        arr5 = (arr_e, from_near, from_diag, from_lat, from_sub)
    (grid_grad,) = call(
        lambda *refs: grid_place(peers, *refs), "grid_place", [shape(chosen, width)],
        (*arr5, gpre_g, embed, sends_row), flops=3 * unit,
    )
    depth = width // total
    if not split:
        last, first, second, embed = (
            scatter_plain(blocks, dims) for blocks in (keep1, keep0, keep2, keep_e)
        )
        grads = [jnp.stack([a, last[i]]) for i, a in enumerate((first[0], first[1], second[0]))]
        return (mesh_out, grid_grad, embed[0], second[1], *grads)
    if not carry:
        keep_e, arr_e = rest_of_halving(0, keep_e, give_e, place, dims)
    grads = call(
        finish, "finish",
        [shape(depth, width, dtype=F32)] * 2 + [shape(2, depth, width, dtype=F32)] * 3,
        (*rest_of_halving(2, keep1, give1, place, dims),
         *rest_of_halving(1, keep0, give0, place, dims),
         *rest_of_halving(1, keep2, give2, place, dims), keep_e, arr_e),
        flops=8 * depth * width,
    )
    return (mesh_out, grid_grad, *grads)


def solution(mesh):
    split = ("groups", "lon", "lat", "sub")
    dims = tuple(mesh.shape[axis] for axis in GROUP)
    rows = P(split, None)
    whole = P("groups", GROUP, None)
    in_specs = (
        rows, rows, rows, P(), P(), P(), P(), P(), P(split), P(split, None, None),
        P(split, None, None), P(split, None, None), rows,
    )
    out_specs = (rows, rows, rows, rows, whole, whole, whole)
    return jax.shard_map(
        lambda *args: body(dims, *args),
        mesh=mesh, in_specs=in_specs, out_specs=out_specs, check_vma=False,
    )
```

```python
import jax
import jax.numpy as jnp
from jax import lax
from jax.experimental import pallas as pl
from jax.experimental.pallas import tpu as pltpu
from jax.sharding import PartitionSpec as P

BF = jnp.bfloat16
F32 = jnp.float32
I32 = jnp.int32
NN = (((1,), (0,)), ((), ()))
NT = (((1,), (1,)), ((), ()))
TN = (((0,), (0,)), ((), ()))
BORDER = 8
GROUP = ("lon", "lat", "sub")
COLUMN = ("lat", "sub")


def dot(a, b, dims=NN):
    return lax.dot_general(a, b, dims, preferred_element_type=F32)


def low(value):
    return value.astype(BF)


def sigmoid(value):
    return 0.5 * jnp.tanh(0.5 * value) + 0.5


def silu(value):
    return value * sigmoid(value)


def silu_both(value):
    sig = sigmoid(value)
    act = value * sig
    return act, sig + act * (1.0 - sig)


def silu_slope(value):
    return silu_both(value)[1]


def iota(rows, columns, dim):
    return lax.broadcasted_iota(I32, (rows, columns), dim)


def hot(mask):
    return jnp.where(mask, 1.0, 0.0)


def slot_of(at, column, me, odd):
    far = jnp.where(at == column - 1, column + 1 - odd, column + odd)
    return jnp.where(at < column - 1, jnp.bitwise_xor(at + 1, me), far)


def as_column(values, wide, column, me, odd):
    slots = values.shape[0]
    count = (slots - 1) * wide
    row = iota(count, slots, 0)
    pick = low(hot(slot_of(row // wide, column, me, odd) == iota(count, slots, 1)))
    found = 16.0 * dot(pick, low((values // 16).astype(F32)))
    found = found + dot(pick, low((values % 16).astype(F32)))
    keep = iota(count, wide, 0) % wide == iota(count, wide, 1)
    return jnp.sum(jnp.where(keep, found, 0.0), axis=1, keepdims=True).astype(I32)


def as_row(values, wide, column, me, odd):
    slots = values.shape[0]
    count = (slots - 1) * wide
    pick = low(hot(iota(wide, count, 1) % wide == iota(wide, count, 0)))
    found = 16.0 * dot(low((values // 16).astype(F32)), pick)
    found = found + dot(low((values % 16).astype(F32)), pick)
    at = iota(slots, count, 1) // wide
    keep = slot_of(at, column, me, odd) == iota(slots, count, 0)
    return jnp.sum(jnp.where(keep, found, 0.0), axis=0, keepdims=True).astype(I32)


def split_parts(refs, starts, sizes):
    values = [ref[...].astype(F32) for ref in refs]
    return [
        jnp.concatenate([value[start : start + size] for value in values], axis=0)
        for start, size in zip(starts, sizes)
    ]


def store_parts(refs, parts):
    peers = len(refs)
    for at, ref in enumerate(refs):
        rows = []
        for part in parts:
            size = part.shape[0] // peers
            rows.append(part[at * size : (at + 1) * size])
        ref[...] = low(rows[0] if len(rows) == 1 else jnp.concatenate(rows, axis=0))


def receivers(senders_t, halo):
    degree, nodes = senders_t.shape
    found = jnp.zeros((halo, nodes), F32)
    ids = iota(halo, nodes, 0) + nodes
    for j in range(degree):
        found = found + hot(senders_t[j : j + 1, :] == ids)
    return found


def receivers_t(senders, degree, halo):
    nodes = senders.shape[0]
    found = jnp.zeros((nodes, halo), F32)
    ids = iota(nodes, halo, 1) + nodes
    for j in range(degree):
        found = found + hot(senders[:, j : j + 1] == ids)
    return found


def fine(rows, dims):
    return (rows // (dims[0] * dims[1] * dims[2])) % 16 == 0


def reverse_bits(block, bits):
    spot = 0
    for bit in range(bits):
        spot = 2 * spot + (block >> bit) % 2
    return spot


def store_blocks(keep_ref, give_ref, at, count, value, dims, bits_ref):
    value = low(value)
    rows = value.shape[0]
    total = dims[0] * dims[1] * dims[2]
    depth = rows // total
    if not fine(rows, dims):
        keep_ref[at] = value
        return
    bits = (total - 1).bit_length()
    upper = bits_ref[0:1, 2:3] == 1
    for block in range(0, total, 2):
        start = reverse_bits(block, bits) * count * depth + at * depth
        first = value[block * depth : (block + 1) * depth].astype(F32)
        second = value[(block + 1) * depth : (block + 2) * depth].astype(F32)
        keep_ref[start : start + depth, :] = low(jnp.where(upper, second, first))
        give_ref[start : start + depth, :] = low(jnp.where(upper, first, second))


def blocks_shapes(count, rows, width, dims):
    if fine(rows, dims):
        return [jax.ShapeDtypeStruct((count * rows // 2, width), BF)] * 2
    return [jax.ShapeDtypeStruct((count, rows, width), BF), jax.ShapeDtypeStruct((16, width), BF)]


def halve(bit, bits_ref, keep_ref, arr_ref, keep_out, give_out):
    half = keep_ref.shape[0] // 2
    upper = bits_ref[0:1, 2 + bit : 3 + bit] == 1
    first = keep_ref[:half, :].astype(F32) + arr_ref[:half, :].astype(F32)
    second = keep_ref[half:, :].astype(F32) + arr_ref[half:, :].astype(F32)
    keep_out[...] = low(jnp.where(upper, second, first))
    give_out[...] = low(jnp.where(upper, first, second))


def swap(block, bit, dims):
    total = dims[0] * dims[1] * dims[2]
    return lax.ppermute(block, GROUP, [(i, i ^ (1 << bit)) for i in range(total)])


def halve_step(bit, keep, arrived, place):
    rows, width = keep.shape[0] // 2, keep.shape[1]
    return call(
        lambda *refs: halve(bit, *refs), "halve", [shape(rows, width)] * 2,
        (place, keep, arrived), flops=4 * rows * width, size=0,
    )


def rest_of_halving(first, keep, give, place, dims):
    bits = (dims[0] * dims[1] * dims[2] - 1).bit_length()
    arrived = swap(give, first, dims)
    for bit in range(first + 1, bits):
        keep, give = halve_step(bit, keep, arrived, place)
        arrived = swap(give, bit, dims)
    return keep, arrived


def halve_carry(bit, bits_ref, keep_ref, arr_ref, *refs):
    *own_refs, keep_out, give_out, here_ref, on_ref = refs
    rows = keep_ref.shape[0]
    half = rows // 2
    size = here_ref.shape[0]
    upper = bits_ref[0:1, 2 + bit : 3 + bit] == 1
    value = arr_ref[...].astype(F32)
    first = keep_ref[:half, :].astype(F32) + value[:half]
    second = keep_ref[half:, :].astype(F32) + value[half:rows]
    keep_out[...] = low(jnp.where(upper, second, first))
    here_ref[...] = low(value[rows : rows + size])
    passed = value[rows + size : rows + 2 * size]
    on_ref[...] = low(passed)
    extra = [ref[...].astype(F32) for ref in own_refs]
    if len(extra) < 2:
        extra.append(passed)
    give_out[...] = low(jnp.concatenate([jnp.where(upper, first, second), *extra], axis=0))


def carry_step(bit, keep, arrived, own, place, capacity):
    rows, width = keep.shape[0] // 2, keep.shape[1]
    return call(
        lambda *refs: halve_carry(bit, *refs), "halve_carry",
        [shape(rows, width), shape(rows + min(len(own) + 1, 2) * capacity, width),
         shape(capacity, width), shape(capacity, width)],
        (place, keep, arrived, *own), flops=4 * rows * width, size=0,
    )


def scatter_plain(blocks, dims):
    lon, lat, sub = dims
    count, rows, width = blocks.shape
    depth = rows // (lon * lat * sub)
    blocks = blocks.reshape(count, lon, lat, sub, depth, width)
    blocks = blocks.transpose(3, 2, 1, 0, 4, 5)
    for axis in ("sub", "lat", "lon"):
        blocks = lax.psum_scatter(blocks, axis, scatter_dimension=0, tiled=False)
    return blocks.astype(F32)


def call(kernel, name, outs, args, flops, loads=(), scratch=(), size=None):
    if size is None:
        size = sum(a.size * a.dtype.itemsize for a in (*args, *outs, *loads))
    args = (*(pltpu.with_memory_space_constraint(a, pltpu.HBM) for a in loads), *args)
    scratch = list(scratch)
    if loads:
        scratch.append(pltpu.SemaphoreType.DMA((len(loads),)))
    in_specs = [pl.BlockSpec(memory_space=pltpu.HBM)] * len(loads)
    in_specs += [pl.BlockSpec(memory_space=pltpu.VMEM)] * (len(args) - len(loads))
    return pl.pallas_call(
        kernel,
        out_shape=[shape(*a.shape, dtype=a.dtype) for a in loads] + list(outs),
        in_specs=in_specs,
        out_specs=[pl.BlockSpec(memory_space=pltpu.VMEM)] * (len(outs) + len(loads)),
        scratch_shapes=scratch,
        compiler_params=pltpu.CompilerParams(vmem_limit_bytes=16 * 1024 * 1024),
        cost_estimate=pl.CostEstimate(flops=flops, bytes_accessed=size, transcendentals=0),
        name=name,
    )(*args)


def exchange(parts, dims):
    column = dims[1] * dims[2]
    count = dims[0]
    other = [(i, (i - 1 + 2 * (i % 2)) % count) for i in range(count)]
    far = lax.ppermute(parts[column], "lon", other)
    near = lax.ppermute(parts[column - 1], "lon", [(i, i ^ 1) for i in range(count)])
    arrived = [
        lax.ppermute(parts[r - 1], COLUMN, [(i, i ^ r) for i in range(column)])
        for r in range(column - 1, 0, -1)
    ]
    return (far, near, *arrived)


def shape(*dims, dtype=BF):
    return jax.ShapeDtypeStruct(dims, dtype)


def start_loads(sources, targets, sems):
    copies = [
        pltpu.make_async_copy(source, target, sems.at[at])
        for at, (source, target) in enumerate(zip(sources, targets))
    ]
    for copy in copies:
        copy.start()
    return copies


def first_payload(column, capacity, count, *refs):
    sources, ints_ref, targets = refs[:count], refs[count], refs[count + 1 : 2 * count + 1]
    sends_ref, *pay_refs, sems = refs[2 * count + 1 :]
    grid_ref = targets[0]
    grid_load, *loads = start_loads(sources, targets, sems)
    chosen = grid_ref.shape[0]
    ints = ints_ref[...]
    base = 2 * capacity + BORDER
    me, odd = ints[0:1, base : base + 1], ints[0:1, base + 1 : base + 2]
    sends = as_column(ints[:, :capacity], capacity, column, me, odd)
    sends_ref[...] = sends
    pick = low(hot(sends == iota(sends.shape[0], chosen, 1)))
    grid_load.wait()
    store_parts(pay_refs, [dot(pick, grid_ref[...])])
    for load in loads:
        load.wait()


def embed_local(
    column, capacity, ints_ref, senders_ref, grid_ref, weight_ref, target_ref, sends_ref,
    sum_ref, slope_ref, sends_row_ref, incoming_ref, bounds_ref, bounds_row_ref, senders_t_ref,
    senders_out_ref, place_ref,
):
    chosen = grid_ref.shape[0]
    nodes = sum_ref.shape[0]
    taken = sends_ref.shape[0]
    act, slope = silu_both(dot(grid_ref[...], weight_ref[...]))
    slope_ref[...] = low(slope)
    sent = jnp.max(hot(sends_ref[...] == iota(taken, chosen, 1)), axis=0, keepdims=True)
    label = jnp.where(sent > 0.0, nodes, target_ref[...])
    sum_ref[...] = dot(low(hot(label == iota(nodes, chosen, 0))), low(act))
    ints = ints_ref[...]
    base = 2 * capacity + BORDER
    place_ref[...] = ints[:, base:]
    me, odd = ints[0:1, base : base + 1], ints[0:1, base + 1 : base + 2]
    sends, incoming = ints[:, :capacity], ints[:, capacity : 2 * capacity]
    bounds = ints[:, 2 * capacity : base]
    sends_row_ref[...] = as_row(sends, capacity, column, me, odd)
    incoming_ref[...] = as_row(incoming, capacity, column, me, odd)
    bounds_ref[...] = as_column(bounds, BORDER, column, me, odd)
    bounds_row_ref[...] = as_row(bounds, BORDER, column, me, odd)
    senders = senders_ref[...]
    degree = senders.shape[0]
    offset = senders - nodes
    slot = offset // BORDER
    far = jnp.where(slot == column, column - odd, column - 1 + odd)
    at = jnp.where(slot < column, jnp.bitwise_xor(slot, me) - 1, far)
    senders = jnp.where(offset < 0, senders, nodes + at * BORDER + offset % BORDER)
    senders_t_ref[...] = senders
    filler = jnp.zeros((8 - degree, nodes), I32)
    senders_out_ref[...] = jnp.concatenate([senders, filler], axis=0).T


def merge_nodes(peers, *refs):
    arr_refs, refs = refs[:peers][::-1], refs[peers:]
    (incoming_ref, embed_ref, local_ref, mesh_ref, weight_ref, bounds_ref, senders_t_ref, cot_ref,
     merged_ref, state_ref, slope_ref, lat_ref, *pay_refs) = refs
    nodes = mesh_ref.shape[0]
    taken = incoming_ref.shape[1]
    halo = peers * BORDER
    lat = jnp.concatenate([ref[...] for ref in arr_refs], axis=0)
    lat_ref[...] = lat
    act, slope = silu_both(dot(lat, embed_ref[...]))
    slope_ref[...] = low(slope)
    place = low(hot(incoming_ref[...] == iota(nodes, taken, 0)))
    merged = low(local_ref[...] + dot(place, low(act)))
    merged_ref[...] = merged
    state = low(mesh_ref[...].astype(F32) + dot(merged, weight_ref[...]))
    state_ref[...] = state
    border = low(hot(bounds_ref[...] == iota(halo, nodes, 1)))
    back = low(receivers(senders_t_ref[...], halo))
    store_parts(
        pay_refs,
        [dot(border, state), dot(back, state), dot(border, merged), dot(back, cot_ref[...])],
    )


def local_edges(senders, degree, sent, recv, each):
    nodes = senders.shape[0]
    total = None
    ids = iota(nodes, nodes, 1)
    for j in range(degree):
        act, slope = silu_both(dot(low(hot(senders[:, j : j + 1] == ids)), sent) + recv)
        total = act if total is None else total + act
        each(j, slope)
    return total


def edge_targets(senders_t):
    degree, nodes = senders_t.shape
    ids = iota(nodes, nodes, 0)
    return jnp.concatenate(
        [low(hot(senders_t[j : j + 1, :] == ids)) for j in range(degree)], axis=1
    )


def forward_local(
    state_ref, send_ref, recv_ref, senders_ref, senders_t_ref, bounds_ref,
    total_ref, slope_ref, recv_n_ref, sent_b_ref,
):
    state = state_ref[...]
    nodes = state.shape[0]
    halo = bounds_ref.shape[0]
    sent = low(dot(state, send_ref[0]))
    recv = dot(state, recv_ref[0])

    def keep(j, slope):
        slope_ref[j] = low(slope)

    total_ref[...] = local_edges(senders_ref[...], senders_t_ref.shape[0], sent, recv, keep)
    back = low(receivers(senders_t_ref[...], halo))
    recv_n_ref[...] = dot(low(dot(back, state)), recv_ref[0])
    sent_b_ref[...] = low(dot(low(hot(bounds_ref[...] == iota(halo, nodes, 1))), sent))


def forward_halo(peers, *refs):
    arr_refs, refs = refs[:peers][::-1], refs[peers:]
    (recv_n_ref, total_ref, state_ref, send_ref, update_ref, senders_ref, senders_t_ref,
     bounds_ref, summed_ref, out_ref, pre_ref, rows_ref, back_ref, merged_ref, cot_ref,
     *pay_refs) = refs
    nodes = state_ref.shape[0]
    degree = senders_t_ref.shape[0]
    halo = peers * BORDER
    rows, back, merged, cot = split_parts(
        arr_refs, (0, BORDER, 2 * BORDER, 3 * BORDER), (BORDER,) * 4
    )
    rows_ref[...], back_ref[...] = low(rows), low(back)
    merged_ref[...], cot_ref[...] = low(merged), low(cot)
    pre = low(dot(low(rows), send_ref[0])).astype(F32) + recv_n_ref[...]
    pre_ref[...] = pre
    place = low(receivers_t(senders_ref[...], degree, halo))
    extra = silu(pre) - silu(recv_n_ref[...])
    summed = low(total_ref[...] + dot(place, low(extra)))
    summed_ref[...] = summed
    state = low(state_ref[...].astype(F32) + dot(summed, update_ref[0]))
    out_ref[...] = state
    border = low(hot(bounds_ref[...] == iota(halo, nodes, 1)))
    back = low(receivers(senders_t_ref[...], halo))
    store_parts(pay_refs, [dot(border, state), dot(back, state)])


def turn_local(
    state_ref, send_ref, recv_ref, update_ref, cot_ref, cot_r_ref, pre_ref, recv_n0_ref, back0_ref,
    sent_b0_ref, senders_ref, senders_t_ref, bounds_ref,
    total_ref, grecv_ref, gsent_ref, recv_n_ref, sent_b_ref, gsum_n_ref, gsum_r_ref,
    slope_k_ref, slope_d_ref, slope_r_ref, gpre_ref,
):
    halo = bounds_ref.shape[0]
    slope = silu_slope(pre_ref[...])
    slope_k_ref[...] = low(slope)
    slope_d_ref[...] = low(slope - silu_slope(recv_n0_ref[...]))
    pre = sent_b0_ref[...].astype(F32) + dot(back0_ref[...], recv_ref[0])
    slope_r_ref[...] = low(silu_slope(pre))
    state = state_ref[...]
    nodes = state.shape[0]
    sent = low(dot(state, send_ref[1]))
    recv = dot(state, recv_ref[1])
    gsum = low(dot(cot_ref[...], update_ref[1], NT))
    grad = gsum.astype(F32)
    grecv = []

    def back_edge(j, slope):
        gpre = grad * slope
        grecv.append(gpre if j == 0 else grecv[-1] + gpre)
        gpre_ref[j * nodes : (j + 1) * nodes, :] = low(gpre)

    degree = senders_t_ref.shape[0]
    total_ref[...] = local_edges(senders_ref[...], degree, sent, recv, back_edge)
    grecv_ref[...] = grecv[-1]
    gsent_ref[...] = dot(edge_targets(senders_t_ref[...]), gpre_ref[...])
    back = low(receivers(senders_t_ref[...], halo))
    recv_n_ref[...] = dot(low(dot(back, state)), recv_ref[1])
    sent_b_ref[...] = low(dot(low(hot(bounds_ref[...] == iota(halo, nodes, 1))), sent))
    gsum_n_ref[...] = low(dot(back, gsum))
    gsum_r_ref[...] = low(dot(cot_r_ref[...], update_ref[1], NT))


def turn_halo(peers, *refs):
    arr_refs, refs = refs[:peers][::-1], refs[peers:]
    (recv_n_ref, sent_b_ref, gsum_n_ref, gsum_r_ref, total_ref, grecv_ref, gsent_ref, cot_ref,
     send_ref, recv_ref, senders_ref, senders_t_ref, bounds_ref, summed_ref, grecv_out_ref,
     gsent_out_ref, gin_ref, *pay_refs) = refs
    nodes = cot_ref.shape[0]
    degree = senders_t_ref.shape[0]
    halo = peers * BORDER
    rows, back = split_parts(arr_refs, (0, BORDER), (BORDER,) * 2)
    pre = low(dot(low(rows), send_ref[1])).astype(F32) + recv_n_ref[...]
    act, slope = silu_both(pre)
    place = low(receivers_t(senders_ref[...], degree, halo))
    base, base_slope = silu_both(recv_n_ref[...])
    gpre = low(gsum_n_ref[...].astype(F32) * (slope - base_slope))
    grecv = low(grecv_ref[...] + dot(place, gpre))
    pre = sent_b_ref[...].astype(F32) + dot(low(back), recv_ref[1])
    gpre = low(gsum_r_ref[...].astype(F32) * silu_slope(pre))
    border = low(hot(bounds_ref[...] == iota(nodes, halo, 0)))
    gsent = low(gsent_ref[...] + dot(border, gpre))
    gin = cot_ref[...].astype(F32) + dot(grecv, recv_ref[1], NT) + dot(gsent, send_ref[1], NT)
    gin = low(gin)
    gin_ref[...] = gin
    store_parts(pay_refs, [dot(low(receivers(senders_t_ref[...], halo)), gin)])
    summed_ref[...] = low(total_ref[...] + dot(place, low(act - base)))
    grecv_out_ref[...] = grecv
    gsent_out_ref[...] = gsent


def last_weights(
    dims, place_ref, state_ref, summed_ref, cot_ref, grecv_ref, gsent_ref, update_ref,
    keep_ref, give_ref, mesh_ref,
):
    state, summed = state_ref[...], summed_ref[...]

    def store(at, value):
        store_blocks(keep_ref, give_ref, at, 3, value, dims, place_ref)

    store(0, dot(state, gsent_ref[...], TN))
    store(1, dot(state, grecv_ref[...], TN))
    store(2, dot(summed, cot_ref[...], TN))
    mesh_ref[...] = low(state.astype(F32) + dot(summed, update_ref[1]))


def back_local(
    dims, place_ref, gin_ref, slope_ref, slope_k_ref, slope_d_ref, send_ref, recv_ref, update_ref,
    senders_ref, senders_t_ref, state_ref, rows_ref, summed_ref, merged_ref, merged_r_ref,
    after_ref, part_ref, keep_ref, give_ref, keep2_ref, give2_ref, gpre_ref,
):
    nodes = gin_ref.shape[0]
    halo = slope_k_ref.shape[0]
    degree = senders_t_ref.shape[0]
    gin = gin_ref[...]
    gsum = low(dot(gin, update_ref[0], NT))
    place = low(receivers_t(senders_ref[...], degree, halo))
    back = low(receivers(senders_t_ref[...], halo))
    gsum_n = low(dot(back, gsum))
    gpre_k = gsum_n * slope_k_ref[...]
    grecv = dot(place, gsum_n * slope_d_ref[...])
    for j in range(degree):
        gpre = gsum * slope_ref[j]
        grecv = grecv + gpre.astype(F32)
        gpre_ref[j * nodes : (j + 1) * nodes, :] = gpre
    gsent = dot(edge_targets(senders_t_ref[...]), gpre_ref[...])
    grecv, gsent = low(grecv), low(gsent)
    part = gin.astype(F32) + dot(grecv, recv_ref[0], NT) + dot(gsent, send_ref[0], NT)
    part_ref[...] = part
    state = state_ref[...]

    def store(at, value):
        store_blocks(keep_ref, give_ref, at, 2, value, dims, place_ref)

    def store2(at, value):
        store_blocks(keep2_ref, give2_ref, at, 2, value, dims, place_ref)

    store(0, dot(state, gsent, TN) + dot(rows_ref[...], gpre_k, TN))
    store(1, dot(state, grecv, TN))
    store2(0, dot(summed_ref[...], gin, TN))
    far = low(dot(gpre_k, send_ref[0], NT))
    store2(1, dot(merged_ref[...], low(part), TN) + dot(merged_r_ref[...], far, TN))


def embed_back(peers, dims, carry, *refs):
    arr_refs, refs = refs[:peers][::-1], refs[peers:]
    (place_ref, slope_r_ref, part_ref, update_ref, send_ref, merge_ref, bounds_ref, target_ref,
     sends_ref, incoming_ref, slope_g_ref, slope_a_ref, grid_ref, lat_ref, embed_ref,
     gpre_ref, keep_ref, give_ref, *pay_refs) = refs
    nodes = part_ref.shape[0]
    halo = peers * BORDER
    chosen = grid_ref.shape[0]
    taken = sends_ref.shape[0]
    (arrived,) = split_parts(arr_refs, (0,), (BORDER,))
    gsum = low(dot(low(arrived), update_ref[0], NT)).astype(F32)
    gpre = low(gsum * slope_r_ref[...].astype(F32))
    border = low(hot(bounds_ref[...] == iota(nodes, halo, 0)))
    gsent = low(dot(border, gpre))
    gin = low(part_ref[...] + dot(gsent, send_ref[0], NT))
    gmerged = low(dot(gin, merge_ref[...], NT))
    place = low(hot(incoming_ref[...] == iota(nodes, taken, 0)))
    gpre_a = low(dot(place, gmerged, TN) * slope_a_ref[...].astype(F32))
    sent = jnp.max(hot(sends_ref[...] == iota(taken, chosen, 1)), axis=0, keepdims=True)
    label = jnp.where(sent > 0.0, nodes, target_ref[...])
    pick = low(hot(label == iota(nodes, chosen, 0)))
    gpre_g = low(dot(pick, gmerged, TN) * slope_g_ref[...].astype(F32))
    gpre_ref[...] = gpre_g
    grad = dot(grid_ref[...], gpre_g, TN) + dot(lat_ref[...], gpre_a, TN)
    store_blocks(keep_ref, give_ref, 0, 1, grad, dims, place_ref)
    rows = dot(gpre_a, embed_ref[...], NT)
    store_parts(pay_refs, [rows])
    if carry:
        size = taken // peers
        start = keep_ref.shape[0]
        give_ref[start : start + 2 * size, :] = low(
            jnp.concatenate([rows[:size], rows[2 * size : 3 * size]], axis=0)
        )


def grid_place(peers, *refs):
    arr_refs, refs = refs[:peers][::-1], refs[peers:]
    gpre_ref, weight_ref, sends_ref, out_ref = refs
    chosen = gpre_ref.shape[0]
    taken = sends_ref.shape[1]
    local = dot(gpre_ref[...], weight_ref[...], NT)
    place = low(hot(sends_ref[...] == iota(chosen, taken, 0)))
    size = taken // peers
    rows = [ref[...].astype(F32) for ref in arr_refs]
    rows = low(jnp.concatenate([row[row.shape[0] - size :] for row in rows], axis=0))
    out_ref[...] = low(local + dot(place, rows))


def finish(
    keep1_ref, arr1_ref, keep0_ref, arr0_ref, keep2_ref, arr2_ref, keep_e_ref, arr_e_ref,
    embed_ref, merge_ref, send_ref, recv_ref, update_ref,
):
    last = keep1_ref[...].astype(F32) + arr1_ref[...].astype(F32)
    first = keep0_ref[...].astype(F32) + arr0_ref[...].astype(F32)
    second = keep2_ref[...].astype(F32) + arr2_ref[...].astype(F32)
    depth = embed_ref.shape[0]
    embed_ref[...] = keep_e_ref[...].astype(F32) + arr_e_ref[:depth, :].astype(F32)
    for at, ref in enumerate((send_ref, recv_ref, update_ref)):
        ref[1] = last[at * depth : (at + 1) * depth]
    send_ref[0], recv_ref[0], update_ref[0] = first[:depth], first[depth:], second[:depth]
    merge_ref[...] = second[depth:]


def body(
    dims,
    grid_latent, mesh_latent, cotangent, embed_weight, merge_weight, send_weight, recv_weight,
    update_weight, target_row, send_rows, incoming_rows, border_mesh_rows, mesh_senders,
):
    chosen, width = grid_latent.shape
    nodes, degree = mesh_senders.shape
    slots, capacity = send_rows.shape[1:]
    column = dims[1] * dims[2]
    peers = slots - 1
    halo = peers * BORDER
    taken = peers * capacity
    total = dims[0] * dims[1] * dims[2]
    bits = (total - 1).bit_length()
    carry = dims == (4, 2, 2) and fine(width, dims)
    spot = lax.axis_index(GROUP)
    place = [lax.axis_index(COLUMN), lax.axis_index("lon") % 2]
    place += [(spot >> bit) % 2 for bit in range(bits)]
    place = jnp.broadcast_to(jnp.stack(place).astype(I32)[None], (slots, 2 + bits))
    ints = jnp.concatenate([send_rows[0], incoming_rows[0], border_mesh_rows[0], place], axis=1)
    unit = 2 * nodes * width * width

    loads = (grid_latent, embed_weight, target_row.reshape(1, chosen), mesh_senders.T,
             mesh_latent, merge_weight, cotangent)
    grid, embed, targets, senders_raw, mesh, merge, cot, sends, *pay1 = call(
        lambda *refs: first_payload(column, capacity, len(loads), *refs), "first_payload",
        [shape(taken, 1, dtype=I32)] + [shape(capacity, width)] * peers,
        (ints,), flops=unit // 2, loads=loads,
    )
    arr1 = exchange(pay1, dims)
    (local, slope_g, sends_row, incoming, bounds, bounds_row, senders_t, senders, place) = call(
        lambda *refs: embed_local(column, capacity, *refs), "embed_local",
        [shape(nodes, width, dtype=F32), shape(chosen, width), shape(1, taken, dtype=I32),
         shape(1, taken, dtype=I32), shape(halo, 1, dtype=I32), shape(1, halo, dtype=I32),
         shape(degree, nodes, dtype=I32), shape(nodes, 8, dtype=I32),
         shape(slots, 2 + bits, dtype=I32)],
        (ints, senders_raw, grid, embed, targets, sends), flops=3 * unit,
    )
    merged, state0, slope_a, lat_a, *pay2 = call(
        lambda *refs: merge_nodes(peers, *refs), "merge_nodes",
        [shape(nodes, width), shape(nodes, width), shape(taken, width), shape(taken, width)]
        + [shape(4 * BORDER, width)] * peers,
        (*arr1, incoming, embed, local, mesh, merge, bounds, senders_t, cot),
        flops=2 * unit,
    )
    arr2 = exchange(pay2, dims)
    total0, slope0, recv_n0, sent_b0 = call(
        forward_local, "forward_local",
        [shape(nodes, width, dtype=F32), shape(degree, nodes, width),
         shape(halo, width, dtype=F32), shape(halo, width)],
        (state0, send_weight, recv_weight, senders, senders_t, bounds), flops=6 * unit,
    )
    summed0, state1, pre0, rows0, back0, merged_r, cot_r, *pay3 = call(
        lambda *refs: forward_halo(peers, *refs), "forward_halo",
        [shape(nodes, width), shape(nodes, width), shape(halo, width, dtype=F32)]
        + [shape(halo, width)] * 4 + [shape(2 * BORDER, width)] * peers,
        (*arr2, recv_n0, total0, state0, send_weight, update_weight, senders, senders_t, bounds),
        flops=2 * unit,
    )
    arr3 = exchange(pay3, dims)
    (total1, grecv_l, gsent_l, recv_n1, sent_b1, gsum_n1, gsum_r1, slope_k0, slope_d0,
     slope_r0) = call(
        turn_local, "turn_local",
        [shape(nodes, width, dtype=F32)] * 3 + [shape(halo, width, dtype=F32)]
        + [shape(halo, width)] * 6,
        (state1, send_weight, recv_weight, update_weight, cot, cot_r, pre0, recv_n0, back0,
         sent_b0, senders, senders_t, bounds),
        flops=10 * unit, scratch=[pltpu.VMEM((degree * nodes, width), BF)],
    )
    summed1, grecv1, gsent1, gin1, *pay4 = call(
        lambda *refs: turn_halo(peers, *refs), "turn_halo",
        [shape(nodes, width)] * 4 + [shape(BORDER, width)] * peers,
        (*arr3, recv_n1, sent_b1, gsum_n1, gsum_r1, total1, grecv_l, gsent_l, cot,
         send_weight, recv_weight, senders, senders_t, bounds_row),
        flops=3 * unit,
    )
    arr4 = exchange(pay4, dims)
    keep1, give1, mesh_out = call(
        lambda *refs: last_weights(dims, *refs), "last_weights",
        blocks_shapes(3, width, width, dims) + [shape(nodes, width)],
        (place, state1, summed1, cot, grecv1, gsent1, update_weight), flops=4 * unit,
    )
    split = fine(width, dims)
    if split:
        give1, last = lax.optimization_barrier((give1, arr4[-1]))
        arr4 = (*arr4[:-1], last)
        keep1, give1 = halve_step(1, keep1, swap(give1, 0, dims), place)
    part0, keep0, give0, keep2, give2 = call(
        lambda *refs: back_local(dims, *refs), "back_local",
        [shape(nodes, width, dtype=F32)] + blocks_shapes(2, width, width, dims) * 2,
        (place, gin1, slope0, slope_k0, slope_d0, send_weight, recv_weight, update_weight, senders,
         senders_t, state0, rows0, summed0, merged, merged_r, keep1),
        flops=10 * unit, scratch=[pltpu.VMEM((degree * nodes, width), BF)],
    )
    if split:
        give0, *arr4 = lax.optimization_barrier((give0, *arr4))
        keep0, give0 = halve_step(1, keep0, swap(give0, 0, dims), place)
        keep0, *arr4 = lax.optimization_barrier((keep0, *arr4))
    shapes = blocks_shapes(1, width, width, dims)
    if carry:
        shapes[1] = shape(shapes[1].shape[0] + 2 * capacity, width)
    gpre_g, keep_e, give_e, *pay5 = call(
        lambda *refs: embed_back(peers, dims, carry, *refs), "embed_back",
        [shape(chosen, width)] + shapes + [shape(capacity, width)] * peers,
        (*arr4, place, slope_r0, part0, update_weight, send_weight, merge, bounds_row,
         targets, sends, incoming, slope_g, slope_a, grid, lat_a, embed),
        flops=6 * unit,
    )
    depth = width // total
    if not split:
        arr5 = exchange(pay5, dims)
        last, first, second, embed_sum = (
            scatter_plain(blocks, dims) for blocks in (keep1, keep0, keep2, keep_e)
        )
        grads = [jnp.stack([a, last[i]]) for i, a in enumerate((first[0], first[1], second[0]))]
        grads = [embed_sum[0], second[1], *grads]
    elif not carry:
        arr5 = exchange(pay5, dims)
        sums = [
            rest_of_halving(1, keep1, give1, place, dims),
            rest_of_halving(1, keep0, give0, place, dims),
            rest_of_halving(0, keep2, give2, place, dims),
            rest_of_halving(0, keep_e, give_e, place, dims),
        ]
    else:
        arr1 = swap(give1, 1, dims)
        arr0 = swap(give0, 1, dims)
        arr_e, arr1 = lax.optimization_barrier((swap(give_e, 0, dims), arr1))
        keep_e, give_e, from_sub, _ = carry_step(1, keep_e, arr_e, pay5[1:2], place, capacity)
        arr_e = swap(give_e, 1, dims)
        give2, keep1, keep_e = lax.optimization_barrier((give2, keep1, keep_e))
        arr2 = swap(give2, 0, dims)
        keep1, give1 = halve_step(2, keep1, arr1, place)
        arr1 = swap(give1, 2, dims)
        keep0, keep1 = lax.optimization_barrier((keep0, keep1))
        keep0, give0 = halve_step(2, keep0, arr0, place)
        arr0 = swap(give0, 2, dims)
        keep2, keep0 = lax.optimization_barrier((keep2, keep0))
        keep2, give2 = halve_step(1, keep2, arr2, place)
        arr2 = swap(give2, 1, dims)
        keep1, keep2 = lax.optimization_barrier((keep1, keep2))
        keep1, give1 = halve_step(3, keep1, arr1, place)
        arr1 = swap(give1, 3, dims)
        keep_e, keep1 = lax.optimization_barrier((keep_e, keep1))
        keep_e, give_e, from_lat, from_diag = carry_step(
            2, keep_e, arr_e, pay5[3:], place, capacity
        )
        arr_e = swap(give_e, 2, dims)
        keep0, keep_e = lax.optimization_barrier((keep0, keep_e))
        keep0, give0 = halve_step(3, keep0, arr0, place)
        arr0 = swap(give0, 3, dims)
        keep_e, keep0 = lax.optimization_barrier((keep_e, keep0))
        keep_e, give_e, from_near, _ = carry_step(3, keep_e, arr_e, (), place, capacity)
        arr_e = swap(give_e, 3, dims)
        keep2, keep_e, arr1 = lax.optimization_barrier((keep2, keep_e, arr1))
        keep2, give2 = halve_step(2, keep2, arr2, place)
        arr2 = swap(give2, 2, dims)
        arr5 = (arr_e, from_near, from_diag, from_lat, from_sub)
        gpre_g, keep2 = lax.optimization_barrier((gpre_g, keep2))
    (grid_grad,) = call(
        lambda *refs: grid_place(peers, *refs), "grid_place", [shape(chosen, width)],
        (*arr5, gpre_g, embed, sends_row), flops=3 * unit,
    )
    if carry:
        keep2, grid_grad, arr0 = lax.optimization_barrier((keep2, grid_grad, arr0))
        keep2, give2 = halve_step(3, keep2, arr2, place)
        sums = ((keep1, arr1), (keep0, arr0), (keep2, swap(give2, 3, dims)), (keep_e, arr_e))
    if split:
        grads = call(
            finish, "finish",
            [shape(depth, width, dtype=F32)] * 2 + [shape(2, depth, width, dtype=F32)] * 3,
            [part for pair in sums for part in pair], flops=8 * depth * width,
        )
    return (mesh_out, grid_grad, *grads)


def solution(mesh):
    split = ("groups", "lon", "lat", "sub")
    dims = tuple(mesh.shape[axis] for axis in GROUP)
    rows = P(split, None)
    whole = P("groups", GROUP, None)
    in_specs = (
        rows, rows, rows, P(), P(), P(), P(), P(), P(split), P(split, None, None),
        P(split, None, None), P(split, None, None), rows,
    )
    out_specs = (rows, rows, rows, rows, whole, whole, whole)
    return jax.shard_map(
        lambda *args: body(dims, *args),
        mesh=mesh, in_specs=in_specs, out_specs=out_specs, check_vma=False,
    )
```

```python
import jax
import jax.numpy as jnp
from jax import lax
from jax.experimental import pallas as pl
from jax.experimental.pallas import tpu as pltpu
from jax.sharding import PartitionSpec as P

BF = jnp.bfloat16
F32 = jnp.float32
I32 = jnp.int32
NN = (((1,), (0,)), ((), ()))
NT = (((1,), (1,)), ((), ()))
TN = (((0,), (0,)), ((), ()))
BORDER = 8
GROUP = ("lon", "lat", "sub")
COLUMN = ("lat", "sub")


def dot(a, b, dims=NN):
    return lax.dot_general(a, b, dims, preferred_element_type=F32)


def low(value):
    return value.astype(BF)


def sigmoid(value):
    return 0.5 * jnp.tanh(0.5 * value) + 0.5


def silu(value):
    return value * sigmoid(value)


def silu_both(value):
    sig = sigmoid(value)
    act = value * sig
    return act, sig + act * (1.0 - sig)


def silu_slope(value):
    return silu_both(value)[1]


def iota(rows, columns, dim):
    return lax.broadcasted_iota(I32, (rows, columns), dim)


def hot(mask):
    return jnp.where(mask, 1.0, 0.0)


def slot_of(at, column, me, odd):
    far = jnp.where(at == column - 1, column + 1 - odd, column + odd)
    return jnp.where(at < column - 1, jnp.bitwise_xor(at + 1, me), far)


def as_column(values, wide, column, me, odd):
    slots = values.shape[0]
    count = (slots - 1) * wide
    row = iota(count, slots, 0)
    pick = low(hot(slot_of(row // wide, column, me, odd) == iota(count, slots, 1)))
    found = 16.0 * dot(pick, low((values // 16).astype(F32)))
    found = found + dot(pick, low((values % 16).astype(F32)))
    keep = iota(count, wide, 0) % wide == iota(count, wide, 1)
    return jnp.sum(jnp.where(keep, found, 0.0), axis=1, keepdims=True).astype(I32)


def as_row(values, wide, column, me, odd):
    slots = values.shape[0]
    count = (slots - 1) * wide
    pick = low(hot(iota(wide, count, 1) % wide == iota(wide, count, 0)))
    found = 16.0 * dot(low((values // 16).astype(F32)), pick)
    found = found + dot(low((values % 16).astype(F32)), pick)
    at = iota(slots, count, 1) // wide
    keep = slot_of(at, column, me, odd) == iota(slots, count, 0)
    return jnp.sum(jnp.where(keep, found, 0.0), axis=0, keepdims=True).astype(I32)


def split_parts(refs, starts, sizes):
    values = [ref[...].astype(F32) for ref in refs]
    return [
        jnp.concatenate([value[start : start + size] for value in values], axis=0)
        for start, size in zip(starts, sizes)
    ]


def store_parts(refs, parts):
    peers = len(refs)
    for at, ref in enumerate(refs):
        rows = []
        for part in parts:
            size = part.shape[0] // peers
            rows.append(part[at * size : (at + 1) * size])
        ref[...] = low(rows[0] if len(rows) == 1 else jnp.concatenate(rows, axis=0))


def receivers(senders_t, halo):
    degree, nodes = senders_t.shape
    found = jnp.zeros((halo, nodes), F32)
    ids = iota(halo, nodes, 0) + nodes
    for j in range(degree):
        found = found + hot(senders_t[j : j + 1, :] == ids)
    return found


def receivers_t(senders, degree, halo):
    nodes = senders.shape[0]
    found = jnp.zeros((nodes, halo), F32)
    ids = iota(nodes, halo, 1) + nodes
    for j in range(degree):
        found = found + hot(senders[:, j : j + 1] == ids)
    return found


def fine(rows, dims):
    return (rows // (dims[0] * dims[1] * dims[2])) % 16 == 0


def reverse_bits(block, bits):
    spot = 0
    for bit in range(bits):
        spot = 2 * spot + (block >> bit) % 2
    return spot


def store_blocks(keep_ref, give_ref, at, count, value, dims, bits_ref):
    value = low(value)
    rows = value.shape[0]
    total = dims[0] * dims[1] * dims[2]
    depth = rows // total
    if not fine(rows, dims):
        keep_ref[at] = value
        return
    bits = (total - 1).bit_length()
    upper = bits_ref[0:1, 2:3] == 1
    for block in range(0, total, 2):
        start = reverse_bits(block, bits) * count * depth + at * depth
        first = value[block * depth : (block + 1) * depth].astype(F32)
        second = value[(block + 1) * depth : (block + 2) * depth].astype(F32)
        keep_ref[start : start + depth, :] = low(jnp.where(upper, second, first))
        give_ref[start : start + depth, :] = low(jnp.where(upper, first, second))


def blocks_shapes(count, rows, width, dims):
    if fine(rows, dims):
        return [jax.ShapeDtypeStruct((count * rows // 2, width), BF)] * 2
    return [jax.ShapeDtypeStruct((count, rows, width), BF), jax.ShapeDtypeStruct((16, width), BF)]


def halve(bit, bits_ref, keep_ref, arr_ref, keep_out, give_out):
    half = keep_ref.shape[0] // 2
    upper = bits_ref[0:1, 2 + bit : 3 + bit] == 1
    first = keep_ref[:half, :].astype(F32) + arr_ref[:half, :].astype(F32)
    second = keep_ref[half:, :].astype(F32) + arr_ref[half:, :].astype(F32)
    keep_out[...] = low(jnp.where(upper, second, first))
    give_out[...] = low(jnp.where(upper, first, second))


def swap(block, bit, dims):
    total = dims[0] * dims[1] * dims[2]
    return lax.ppermute(block, GROUP, [(i, i ^ (1 << bit)) for i in range(total)])


def halve_step(bit, keep, arrived, place):
    rows, width = keep.shape[0] // 2, keep.shape[1]
    return call(
        lambda *refs: halve(bit, *refs), "halve", [shape(rows, width)] * 2,
        (place, keep, arrived), flops=4 * rows * width, size=0,
    )


def rest_of_halving(first, keep, give, place, dims):
    bits = (dims[0] * dims[1] * dims[2] - 1).bit_length()
    arrived = swap(give, first, dims)
    for bit in range(first + 1, bits):
        keep, give = halve_step(bit, keep, arrived, place)
        arrived = swap(give, bit, dims)
    return keep, arrived


def halve_carry(bit, bits_ref, keep_ref, arr_ref, *refs):
    *own_refs, keep_out, give_out, here_ref, on_ref = refs
    rows = keep_ref.shape[0]
    half = rows // 2
    size = here_ref.shape[0]
    upper = bits_ref[0:1, 2 + bit : 3 + bit] == 1
    value = arr_ref[...].astype(F32)
    first = keep_ref[:half, :].astype(F32) + value[:half]
    second = keep_ref[half:, :].astype(F32) + value[half:rows]
    keep_out[...] = low(jnp.where(upper, second, first))
    here_ref[...] = low(value[rows : rows + size])
    passed = value[rows + size : rows + 2 * size]
    on_ref[...] = low(passed)
    extra = [ref[...].astype(F32) for ref in own_refs]
    if len(extra) < 2:
        extra.append(passed)
    give_out[...] = low(jnp.concatenate([jnp.where(upper, first, second), *extra], axis=0))


def carry_step(bit, keep, arrived, own, place, capacity):
    rows, width = keep.shape[0] // 2, keep.shape[1]
    return call(
        lambda *refs: halve_carry(bit, *refs), "halve_carry",
        [shape(rows, width), shape(rows + min(len(own) + 1, 2) * capacity, width),
         shape(capacity, width), shape(capacity, width)],
        (place, keep, arrived, *own), flops=4 * rows * width, size=0,
    )


def scatter_plain(blocks, dims):
    lon, lat, sub = dims
    count, rows, width = blocks.shape
    depth = rows // (lon * lat * sub)
    blocks = blocks.reshape(count, lon, lat, sub, depth, width)
    blocks = blocks.transpose(3, 2, 1, 0, 4, 5)
    for axis in ("sub", "lat", "lon"):
        blocks = lax.psum_scatter(blocks, axis, scatter_dimension=0, tiled=False)
    return blocks.astype(F32)


def call(kernel, name, outs, args, flops, loads=(), scratch=(), size=None):
    if size is None:
        size = sum(a.size * a.dtype.itemsize for a in (*args, *outs, *loads))
    args = (*(pltpu.with_memory_space_constraint(a, pltpu.HBM) for a in loads), *args)
    scratch = list(scratch)
    if loads:
        scratch.append(pltpu.SemaphoreType.DMA((len(loads),)))
    in_specs = [pl.BlockSpec(memory_space=pltpu.HBM)] * len(loads)
    in_specs += [pl.BlockSpec(memory_space=pltpu.VMEM)] * (len(args) - len(loads))
    return pl.pallas_call(
        kernel,
        out_shape=[shape(*a.shape, dtype=a.dtype) for a in loads] + list(outs),
        in_specs=in_specs,
        out_specs=[pl.BlockSpec(memory_space=pltpu.VMEM)] * (len(outs) + len(loads)),
        scratch_shapes=scratch,
        compiler_params=pltpu.CompilerParams(vmem_limit_bytes=16 * 1024 * 1024),
        cost_estimate=pl.CostEstimate(flops=flops, bytes_accessed=size, transcendentals=0),
        name=name,
    )(*args)


def exchange(parts, dims):
    column = dims[1] * dims[2]
    count = dims[0]
    other = [(i, (i - 1 + 2 * (i % 2)) % count) for i in range(count)]
    far = lax.ppermute(parts[column], "lon", other)
    near = lax.ppermute(parts[column - 1], "lon", [(i, i ^ 1) for i in range(count)])
    arrived = [
        lax.ppermute(parts[r - 1], COLUMN, [(i, i ^ r) for i in range(column)])
        for r in range(column - 1, 0, -1)
    ]
    return (far, near, *arrived)


def shape(*dims, dtype=BF):
    return jax.ShapeDtypeStruct(dims, dtype)


def start_loads(sources, targets, sems):
    copies = [
        pltpu.make_async_copy(source, target, sems.at[at])
        for at, (source, target) in enumerate(zip(sources, targets))
    ]
    for copy in copies:
        copy.start()
    return copies


def first_payload(column, capacity, count, *refs):
    sources, ints_ref, targets = refs[:count], refs[count], refs[count + 1 : 2 * count + 1]
    sends_ref, *pay_refs, sems = refs[2 * count + 1 :]
    grid_ref = targets[0]
    grid_load, *loads = start_loads(sources, targets, sems)
    chosen = grid_ref.shape[0]
    ints = ints_ref[...]
    base = 2 * capacity + BORDER
    me, odd = ints[0:1, base : base + 1], ints[0:1, base + 1 : base + 2]
    sends = as_column(ints[:, :capacity], capacity, column, me, odd)
    sends_ref[...] = sends
    pick = low(hot(sends == iota(sends.shape[0], chosen, 1)))
    grid_load.wait()
    store_parts(pay_refs, [dot(pick, grid_ref[...])])
    for load in loads:
        load.wait()


def embed_local(
    column, capacity, ints_ref, senders_ref, grid_ref, weight_ref, target_ref, sends_ref,
    sum_ref, slope_ref, sends_row_ref, incoming_ref, bounds_ref, bounds_row_ref, senders_t_ref,
    senders_out_ref, place_ref,
):
    chosen = grid_ref.shape[0]
    nodes = sum_ref.shape[0]
    taken = sends_ref.shape[0]
    act, slope = silu_both(dot(grid_ref[...], weight_ref[...]))
    slope_ref[...] = low(slope)
    sent = jnp.max(hot(sends_ref[...] == iota(taken, chosen, 1)), axis=0, keepdims=True)
    label = jnp.where(sent > 0.0, nodes, target_ref[...])
    sum_ref[...] = dot(low(hot(label == iota(nodes, chosen, 0))), low(act))
    ints = ints_ref[...]
    base = 2 * capacity + BORDER
    place_ref[...] = ints[:, base:]
    me, odd = ints[0:1, base : base + 1], ints[0:1, base + 1 : base + 2]
    sends, incoming = ints[:, :capacity], ints[:, capacity : 2 * capacity]
    bounds = ints[:, 2 * capacity : base]
    sends_row_ref[...] = as_row(sends, capacity, column, me, odd)
    incoming_ref[...] = as_row(incoming, capacity, column, me, odd)
    bounds_ref[...] = as_column(bounds, BORDER, column, me, odd)
    bounds_row_ref[...] = as_row(bounds, BORDER, column, me, odd)
    senders = senders_ref[...]
    degree = senders.shape[0]
    offset = senders - nodes
    slot = offset // BORDER
    far = jnp.where(slot == column, column - odd, column - 1 + odd)
    at = jnp.where(slot < column, jnp.bitwise_xor(slot, me) - 1, far)
    senders = jnp.where(offset < 0, senders, nodes + at * BORDER + offset % BORDER)
    senders_t_ref[...] = senders
    filler = jnp.zeros((8 - degree, nodes), I32)
    senders_out_ref[...] = jnp.concatenate([senders, filler], axis=0).T


def merge_nodes(peers, *refs):
    arr_refs, refs = refs[:peers][::-1], refs[peers:]
    (incoming_ref, embed_ref, local_ref, mesh_ref, weight_ref, bounds_ref, senders_t_ref, cot_ref,
     merged_ref, state_ref, slope_ref, lat_ref, *pay_refs) = refs
    nodes = mesh_ref.shape[0]
    taken = incoming_ref.shape[1]
    halo = peers * BORDER
    lat = jnp.concatenate([ref[...] for ref in arr_refs], axis=0)
    lat_ref[...] = lat
    act, slope = silu_both(dot(lat, embed_ref[...]))
    slope_ref[...] = low(slope)
    place = low(hot(incoming_ref[...] == iota(nodes, taken, 0)))
    merged = low(local_ref[...] + dot(place, low(act)))
    merged_ref[...] = merged
    state = low(mesh_ref[...].astype(F32) + dot(merged, weight_ref[...]))
    state_ref[...] = state
    border = low(hot(bounds_ref[...] == iota(halo, nodes, 1)))
    back = low(receivers(senders_t_ref[...], halo))
    store_parts(
        pay_refs,
        [dot(border, state), dot(back, state), dot(border, merged), dot(back, cot_ref[...])],
    )


def local_edges(senders, degree, sent, recv, each):
    nodes = senders.shape[0]
    total = None
    ids = iota(nodes, nodes, 1)
    for j in range(degree):
        act, slope = silu_both(dot(low(hot(senders[:, j : j + 1] == ids)), sent) + recv)
        total = act if total is None else total + act
        each(j, slope)
    return total


def edge_targets(senders_t):
    degree, nodes = senders_t.shape
    ids = iota(nodes, nodes, 0)
    return jnp.concatenate(
        [low(hot(senders_t[j : j + 1, :] == ids)) for j in range(degree)], axis=1
    )


def forward_local(
    state_ref, send_ref, recv_ref, senders_ref, senders_t_ref, bounds_ref,
    total_ref, slope_ref, recv_n_ref, sent_b_ref,
):
    state = state_ref[...]
    nodes = state.shape[0]
    halo = bounds_ref.shape[0]
    sent = low(dot(state, send_ref[0]))
    recv = dot(state, recv_ref[0])

    def keep(j, slope):
        slope_ref[j] = low(slope)

    total_ref[...] = local_edges(senders_ref[...], senders_t_ref.shape[0], sent, recv, keep)
    back = low(receivers(senders_t_ref[...], halo))
    recv_n_ref[...] = dot(low(dot(back, state)), recv_ref[0])
    sent_b_ref[...] = low(dot(low(hot(bounds_ref[...] == iota(halo, nodes, 1))), sent))


def forward_halo(peers, *refs):
    arr_refs, refs = refs[:peers][::-1], refs[peers:]
    (recv_n_ref, total_ref, state_ref, send_ref, update_ref, senders_ref, senders_t_ref,
     bounds_ref, summed_ref, out_ref, pre_ref, rows_ref, back_ref, merged_ref, cot_ref,
     *pay_refs) = refs
    nodes = state_ref.shape[0]
    degree = senders_t_ref.shape[0]
    halo = peers * BORDER
    rows, back, merged, cot = split_parts(
        arr_refs, (0, BORDER, 2 * BORDER, 3 * BORDER), (BORDER,) * 4
    )
    rows_ref[...], back_ref[...] = low(rows), low(back)
    merged_ref[...], cot_ref[...] = low(merged), low(cot)
    pre = low(dot(low(rows), send_ref[0])).astype(F32) + recv_n_ref[...]
    pre_ref[...] = pre
    place = low(receivers_t(senders_ref[...], degree, halo))
    extra = silu(pre) - silu(recv_n_ref[...])
    summed = low(total_ref[...] + dot(place, low(extra)))
    summed_ref[...] = summed
    state = low(state_ref[...].astype(F32) + dot(summed, update_ref[0]))
    out_ref[...] = state
    border = low(hot(bounds_ref[...] == iota(halo, nodes, 1)))
    back = low(receivers(senders_t_ref[...], halo))
    store_parts(pay_refs, [dot(border, state), dot(back, state)])


def turn_local(
    state_ref, send_ref, recv_ref, update_ref, cot_ref, cot_r_ref, pre_ref, recv_n0_ref, back0_ref,
    sent_b0_ref, senders_ref, senders_t_ref, bounds_ref,
    total_ref, grecv_ref, gsent_ref, recv_n_ref, sent_b_ref, gsum_n_ref, gsum_r_ref,
    slope_k_ref, slope_d_ref, slope_r_ref, gpre_ref,
):
    halo = bounds_ref.shape[0]
    slope = silu_slope(pre_ref[...])
    slope_k_ref[...] = low(slope)
    slope_d_ref[...] = low(slope - silu_slope(recv_n0_ref[...]))
    pre = sent_b0_ref[...].astype(F32) + dot(back0_ref[...], recv_ref[0])
    slope_r_ref[...] = low(silu_slope(pre))
    state = state_ref[...]
    nodes = state.shape[0]
    sent = low(dot(state, send_ref[1]))
    recv = dot(state, recv_ref[1])
    gsum = low(dot(cot_ref[...], update_ref[1], NT))
    grad = gsum.astype(F32)
    grecv = []

    def back_edge(j, slope):
        gpre = grad * slope
        grecv.append(gpre if j == 0 else grecv[-1] + gpre)
        gpre_ref[j * nodes : (j + 1) * nodes, :] = low(gpre)

    degree = senders_t_ref.shape[0]
    total_ref[...] = local_edges(senders_ref[...], degree, sent, recv, back_edge)
    grecv_ref[...] = grecv[-1]
    gsent_ref[...] = dot(edge_targets(senders_t_ref[...]), gpre_ref[...])
    back = low(receivers(senders_t_ref[...], halo))
    recv_n_ref[...] = dot(low(dot(back, state)), recv_ref[1])
    sent_b_ref[...] = low(dot(low(hot(bounds_ref[...] == iota(halo, nodes, 1))), sent))
    gsum_n_ref[...] = low(dot(back, gsum))
    gsum_r_ref[...] = low(dot(cot_r_ref[...], update_ref[1], NT))


def turn_halo(peers, *refs):
    arr_refs, refs = refs[:peers][::-1], refs[peers:]
    (recv_n_ref, sent_b_ref, gsum_n_ref, gsum_r_ref, total_ref, grecv_ref, gsent_ref, cot_ref,
     send_ref, recv_ref, senders_ref, senders_t_ref, bounds_ref, summed_ref, grecv_out_ref,
     gsent_out_ref, gin_ref, *pay_refs) = refs
    nodes = cot_ref.shape[0]
    degree = senders_t_ref.shape[0]
    halo = peers * BORDER
    rows, back = split_parts(arr_refs, (0, BORDER), (BORDER,) * 2)
    pre = low(dot(low(rows), send_ref[1])).astype(F32) + recv_n_ref[...]
    act, slope = silu_both(pre)
    place = low(receivers_t(senders_ref[...], degree, halo))
    base, base_slope = silu_both(recv_n_ref[...])
    gpre = low(gsum_n_ref[...].astype(F32) * (slope - base_slope))
    grecv = low(grecv_ref[...] + dot(place, gpre))
    pre = sent_b_ref[...].astype(F32) + dot(low(back), recv_ref[1])
    gpre = low(gsum_r_ref[...].astype(F32) * silu_slope(pre))
    border = low(hot(bounds_ref[...] == iota(nodes, halo, 0)))
    gsent = low(gsent_ref[...] + dot(border, gpre))
    gin = cot_ref[...].astype(F32) + dot(grecv, recv_ref[1], NT) + dot(gsent, send_ref[1], NT)
    gin = low(gin)
    gin_ref[...] = gin
    store_parts(pay_refs, [dot(low(receivers(senders_t_ref[...], halo)), gin)])
    summed_ref[...] = low(total_ref[...] + dot(place, low(act - base)))
    grecv_out_ref[...] = grecv
    gsent_out_ref[...] = gsent


def last_weights(
    dims, place_ref, state_ref, summed_ref, cot_ref, grecv_ref, gsent_ref, update_ref,
    keep_ref, give_ref, mesh_ref,
):
    state, summed = state_ref[...], summed_ref[...]

    def store(at, value):
        store_blocks(keep_ref, give_ref, at, 3, value, dims, place_ref)

    store(0, dot(state, gsent_ref[...], TN))
    store(1, dot(state, grecv_ref[...], TN))
    store(2, dot(summed, cot_ref[...], TN))
    mesh_ref[...] = low(state.astype(F32) + dot(summed, update_ref[1]))


def back_local(
    dims, place_ref, gin_ref, slope_ref, slope_k_ref, slope_d_ref, send_ref, recv_ref, update_ref,
    senders_ref, senders_t_ref, state_ref, rows_ref, summed_ref, merged_ref, merged_r_ref,
    after_ref, part_ref, keep_ref, give_ref, keep2_ref, give2_ref, gpre_ref,
):
    nodes = gin_ref.shape[0]
    halo = slope_k_ref.shape[0]
    degree = senders_t_ref.shape[0]
    gin = gin_ref[...]
    gsum = low(dot(gin, update_ref[0], NT))
    place = low(receivers_t(senders_ref[...], degree, halo))
    back = low(receivers(senders_t_ref[...], halo))
    gsum_n = low(dot(back, gsum))
    gpre_k = gsum_n * slope_k_ref[...]
    grecv = dot(place, gsum_n * slope_d_ref[...])
    for j in range(degree):
        gpre = gsum * slope_ref[j]
        grecv = grecv + gpre.astype(F32)
        gpre_ref[j * nodes : (j + 1) * nodes, :] = gpre
    gsent = dot(edge_targets(senders_t_ref[...]), gpre_ref[...])
    grecv, gsent = low(grecv), low(gsent)
    part = gin.astype(F32) + dot(grecv, recv_ref[0], NT) + dot(gsent, send_ref[0], NT)
    part_ref[...] = part
    state = state_ref[...]

    def store(at, value):
        store_blocks(keep_ref, give_ref, at, 2, value, dims, place_ref)

    def store2(at, value):
        store_blocks(keep2_ref, give2_ref, at, 2, value, dims, place_ref)

    store(0, dot(state, gsent, TN) + dot(rows_ref[...], gpre_k, TN))
    store(1, dot(state, grecv, TN))
    store2(0, dot(summed_ref[...], gin, TN))
    far = low(dot(gpre_k, send_ref[0], NT))
    store2(1, dot(merged_ref[...], low(part), TN) + dot(merged_r_ref[...], far, TN))


def embed_back(peers, dims, carry, *refs):
    arr_refs, refs = refs[:peers][::-1], refs[peers:]
    (place_ref, slope_r_ref, part_ref, update_ref, send_ref, merge_ref, bounds_ref, target_ref,
     sends_ref, incoming_ref, slope_g_ref, slope_a_ref, grid_ref, lat_ref, embed_ref,
     gpre_ref, keep_ref, give_ref, *pay_refs) = refs
    nodes = part_ref.shape[0]
    halo = peers * BORDER
    chosen = grid_ref.shape[0]
    taken = sends_ref.shape[0]
    (arrived,) = split_parts(arr_refs, (0,), (BORDER,))
    gsum = low(dot(low(arrived), update_ref[0], NT)).astype(F32)
    gpre = low(gsum * slope_r_ref[...].astype(F32))
    border = low(hot(bounds_ref[...] == iota(nodes, halo, 0)))
    gsent = low(dot(border, gpre))
    gin = low(part_ref[...] + dot(gsent, send_ref[0], NT))
    gmerged = low(dot(gin, merge_ref[...], NT))
    place = low(hot(incoming_ref[...] == iota(nodes, taken, 0)))
    gpre_a = low(dot(place, gmerged, TN) * slope_a_ref[...].astype(F32))
    sent = jnp.max(hot(sends_ref[...] == iota(taken, chosen, 1)), axis=0, keepdims=True)
    label = jnp.where(sent > 0.0, nodes, target_ref[...])
    pick = low(hot(label == iota(nodes, chosen, 0)))
    gpre_g = low(dot(pick, gmerged, TN) * slope_g_ref[...].astype(F32))
    gpre_ref[...] = gpre_g
    grad = dot(grid_ref[...], gpre_g, TN) + dot(lat_ref[...], gpre_a, TN)
    store_blocks(keep_ref, give_ref, 0, 1, grad, dims, place_ref)
    rows = dot(gpre_a, embed_ref[...], NT)
    store_parts(pay_refs, [rows])
    if carry:
        size = taken // peers
        start = keep_ref.shape[0]
        give_ref[start : start + 2 * size, :] = low(
            jnp.concatenate([rows[:size], rows[2 * size : 3 * size]], axis=0)
        )


def grid_place(peers, *refs):
    arr_refs, refs = refs[:peers][::-1], refs[peers:]
    gpre_ref, weight_ref, sends_ref, out_ref = refs
    chosen = gpre_ref.shape[0]
    taken = sends_ref.shape[1]
    local = dot(gpre_ref[...], weight_ref[...], NT)
    place = low(hot(sends_ref[...] == iota(chosen, taken, 0)))
    size = taken // peers
    rows = [ref[...].astype(F32) for ref in arr_refs]
    rows = low(jnp.concatenate([row[row.shape[0] - size :] for row in rows], axis=0))
    out_ref[...] = low(local + dot(place, rows))


def finish(
    keep1_ref, arr1_ref, keep0_ref, arr0_ref, keep2_ref, arr2_ref, keep_e_ref, arr_e_ref,
    embed_ref, merge_ref, send_ref, recv_ref, update_ref,
):
    last = keep1_ref[...].astype(F32) + arr1_ref[...].astype(F32)
    first = keep0_ref[...].astype(F32) + arr0_ref[...].astype(F32)
    second = keep2_ref[...].astype(F32) + arr2_ref[...].astype(F32)
    depth = embed_ref.shape[0]
    embed_ref[...] = keep_e_ref[...].astype(F32) + arr_e_ref[:depth, :].astype(F32)
    for at, ref in enumerate((send_ref, recv_ref, update_ref)):
        ref[1] = last[at * depth : (at + 1) * depth]
    send_ref[0], recv_ref[0], update_ref[0] = first[:depth], first[depth:], second[:depth]
    merge_ref[...] = second[depth:]


def body(
    dims,
    grid_latent, mesh_latent, cotangent, embed_weight, merge_weight, send_weight, recv_weight,
    update_weight, target_row, send_rows, incoming_rows, border_mesh_rows, mesh_senders,
):
    chosen, width = grid_latent.shape
    nodes, degree = mesh_senders.shape
    slots, capacity = send_rows.shape[1:]
    column = dims[1] * dims[2]
    peers = slots - 1
    halo = peers * BORDER
    taken = peers * capacity
    total = dims[0] * dims[1] * dims[2]
    bits = (total - 1).bit_length()
    carry = dims == (4, 2, 2) and fine(width, dims)
    spot = lax.axis_index(GROUP)
    place = [lax.axis_index(COLUMN), lax.axis_index("lon") % 2]
    place += [(spot >> bit) % 2 for bit in range(bits)]
    place = jnp.broadcast_to(jnp.stack(place).astype(I32)[None], (slots, 2 + bits))
    ints = jnp.concatenate([send_rows[0], incoming_rows[0], border_mesh_rows[0], place], axis=1)
    unit = 2 * nodes * width * width

    loads = (grid_latent, embed_weight, target_row.reshape(1, chosen), mesh_senders.T,
             mesh_latent, merge_weight, cotangent)
    grid, embed, targets, senders_raw, mesh, merge, cot, sends, *pay1 = call(
        lambda *refs: first_payload(column, capacity, len(loads), *refs), "first_payload",
        [shape(taken, 1, dtype=I32)] + [shape(capacity, width)] * peers,
        (ints,), flops=unit // 2, loads=loads,
    )
    arr1 = exchange(pay1, dims)
    (local, slope_g, sends_row, incoming, bounds, bounds_row, senders_t, senders, place) = call(
        lambda *refs: embed_local(column, capacity, *refs), "embed_local",
        [shape(nodes, width, dtype=F32), shape(chosen, width), shape(1, taken, dtype=I32),
         shape(1, taken, dtype=I32), shape(halo, 1, dtype=I32), shape(1, halo, dtype=I32),
         shape(degree, nodes, dtype=I32), shape(nodes, 8, dtype=I32),
         shape(slots, 2 + bits, dtype=I32)],
        (ints, senders_raw, grid, embed, targets, sends), flops=3 * unit,
    )
    merged, state0, slope_a, lat_a, *pay2 = call(
        lambda *refs: merge_nodes(peers, *refs), "merge_nodes",
        [shape(nodes, width), shape(nodes, width), shape(taken, width), shape(taken, width)]
        + [shape(4 * BORDER, width)] * peers,
        (*arr1, incoming, embed, local, mesh, merge, bounds, senders_t, cot),
        flops=2 * unit,
    )
    arr2 = exchange(pay2, dims)
    total0, slope0, recv_n0, sent_b0 = call(
        forward_local, "forward_local",
        [shape(nodes, width, dtype=F32), shape(degree, nodes, width),
         shape(halo, width, dtype=F32), shape(halo, width)],
        (state0, send_weight, recv_weight, senders, senders_t, bounds), flops=6 * unit,
    )
    summed0, state1, pre0, rows0, back0, merged_r, cot_r, *pay3 = call(
        lambda *refs: forward_halo(peers, *refs), "forward_halo",
        [shape(nodes, width), shape(nodes, width), shape(halo, width, dtype=F32)]
        + [shape(halo, width)] * 4 + [shape(2 * BORDER, width)] * peers,
        (*arr2, recv_n0, total0, state0, send_weight, update_weight, senders, senders_t, bounds),
        flops=2 * unit,
    )
    arr3 = exchange(pay3, dims)
    (total1, grecv_l, gsent_l, recv_n1, sent_b1, gsum_n1, gsum_r1, slope_k0, slope_d0,
     slope_r0) = call(
        turn_local, "turn_local",
        [shape(nodes, width, dtype=F32)] * 3 + [shape(halo, width, dtype=F32)]
        + [shape(halo, width)] * 6,
        (state1, send_weight, recv_weight, update_weight, cot, cot_r, pre0, recv_n0, back0,
         sent_b0, senders, senders_t, bounds),
        flops=10 * unit, scratch=[pltpu.VMEM((degree * nodes, width), BF)],
    )
    summed1, grecv1, gsent1, gin1, *pay4 = call(
        lambda *refs: turn_halo(peers, *refs), "turn_halo",
        [shape(nodes, width)] * 4 + [shape(BORDER, width)] * peers,
        (*arr3, recv_n1, sent_b1, gsum_n1, gsum_r1, total1, grecv_l, gsent_l, cot,
         send_weight, recv_weight, senders, senders_t, bounds_row),
        flops=3 * unit,
    )
    arr4 = exchange(pay4, dims)
    keep1, give1, mesh_out = call(
        lambda *refs: last_weights(dims, *refs), "last_weights",
        blocks_shapes(3, width, width, dims) + [shape(nodes, width)],
        (place, state1, summed1, cot, grecv1, gsent1, update_weight), flops=4 * unit,
    )
    split = fine(width, dims)
    if split:
        give1, last = lax.optimization_barrier((give1, arr4[-1]))
        arr4 = (*arr4[:-1], last)
        keep1, give1 = halve_step(1, keep1, swap(give1, 0, dims), place)
    part0, keep0, give0, keep2, give2 = call(
        lambda *refs: back_local(dims, *refs), "back_local",
        [shape(nodes, width, dtype=F32)] + blocks_shapes(2, width, width, dims) * 2,
        (place, gin1, slope0, slope_k0, slope_d0, send_weight, recv_weight, update_weight, senders,
         senders_t, state0, rows0, summed0, merged, merged_r, keep1),
        flops=10 * unit, scratch=[pltpu.VMEM((degree * nodes, width), BF)],
    )
    if split:
        give0, give2, *arr4 = lax.optimization_barrier((give0, give2, *arr4))
        keep0, give0 = halve_step(1, keep0, swap(give0, 0, dims), place)
        keep0, *arr4 = lax.optimization_barrier((keep0, *arr4))
    shapes = blocks_shapes(1, width, width, dims)
    if carry:
        shapes[1] = shape(shapes[1].shape[0] + 2 * capacity, width)
    gpre_g, keep_e, give_e, *pay5 = call(
        lambda *refs: embed_back(peers, dims, carry, *refs), "embed_back",
        [shape(chosen, width)] + shapes + [shape(capacity, width)] * peers,
        (*arr4, place, slope_r0, part0, update_weight, send_weight, merge, bounds_row,
         targets, sends, incoming, slope_g, slope_a, grid, lat_a, embed),
        flops=6 * unit,
    )
    depth = width // total
    if not split:
        arr5 = exchange(pay5, dims)
        last, first, second, embed_sum = (
            scatter_plain(blocks, dims) for blocks in (keep1, keep0, keep2, keep_e)
        )
        grads = [jnp.stack([a, last[i]]) for i, a in enumerate((first[0], first[1], second[0]))]
        grads = [embed_sum[0], second[1], *grads]
    elif not carry:
        arr5 = exchange(pay5, dims)
        sums = [
            rest_of_halving(1, keep1, give1, place, dims),
            rest_of_halving(1, keep0, give0, place, dims),
            rest_of_halving(0, keep2, give2, place, dims),
            rest_of_halving(0, keep_e, give_e, place, dims),
        ]
    else:
        arr1 = swap(give1, 1, dims)
        arr0 = swap(give0, 1, dims)
        arr2 = swap(give2, 0, dims)
        arr_e, arr1 = lax.optimization_barrier((swap(give_e, 0, dims), arr1))
        keep1, give1 = halve_step(2, keep1, arr1, place)
        arr1 = swap(give1, 2, dims)
        keep_e, keep1 = lax.optimization_barrier((keep_e, keep1))
        keep_e, give_e, from_sub, _ = carry_step(1, keep_e, arr_e, pay5[1:2], place, capacity)
        arr_e = swap(give_e, 1, dims)
        keep2, keep_e = lax.optimization_barrier((keep2, keep_e))
        keep2, give2 = halve_step(1, keep2, arr2, place)
        arr2 = swap(give2, 1, dims)
        keep0, keep2 = lax.optimization_barrier((keep0, keep2))
        keep0, give0 = halve_step(2, keep0, arr0, place)
        arr0 = swap(give0, 2, dims)
        keep1, keep0 = lax.optimization_barrier((keep1, keep0))
        keep1, give1 = halve_step(3, keep1, arr1, place)
        arr1 = swap(give1, 3, dims)
        keep2, keep1 = lax.optimization_barrier((keep2, keep1))
        keep2, give2 = halve_step(2, keep2, arr2, place)
        arr2 = swap(give2, 2, dims)
        keep0, keep2 = lax.optimization_barrier((keep0, keep2))
        keep0, give0 = halve_step(3, keep0, arr0, place)
        arr0 = swap(give0, 3, dims)
        keep_e, keep0, arr1 = lax.optimization_barrier((keep_e, keep0, arr1))
        keep_e, give_e, from_lat, from_diag = carry_step(
            2, keep_e, arr_e, pay5[3:], place, capacity
        )
        arr_e = swap(give_e, 2, dims)
        keep2, keep_e = lax.optimization_barrier((keep2, keep_e))
        keep2, give2 = halve_step(3, keep2, arr2, place)
        arr2 = swap(give2, 3, dims)
        keep_e, keep2, arr0 = lax.optimization_barrier((keep_e, keep2, arr0))
        keep_e, give_e, from_near, _ = carry_step(3, keep_e, arr_e, (), place, capacity)
        arr_e = swap(give_e, 3, dims)
        arr5 = (arr_e, from_near, from_diag, from_lat, from_sub)
        sums = ((keep1, arr1), (keep0, arr0), (keep2, arr2), (keep_e, arr_e))
    (grid_grad,) = call(
        lambda *refs: grid_place(peers, *refs), "grid_place", [shape(chosen, width)],
        (*arr5, gpre_g, embed, sends_row), flops=3 * unit,
    )
    if split:
        grads = call(
            finish, "finish",
            [shape(depth, width, dtype=F32)] * 2 + [shape(2, depth, width, dtype=F32)] * 3,
            [part for pair in sums for part in pair], flops=8 * depth * width,
        )
    return (mesh_out, grid_grad, *grads)


def solution(mesh):
    split = ("groups", "lon", "lat", "sub")
    dims = tuple(mesh.shape[axis] for axis in GROUP)
    rows = P(split, None)
    whole = P("groups", GROUP, None)
    in_specs = (
        rows, rows, rows, P(), P(), P(), P(), P(), P(split), P(split, None, None),
        P(split, None, None), P(split, None, None), rows,
    )
    out_specs = (rows, rows, rows, rows, whole, whole, whole)
    return jax.shard_map(
        lambda *args: body(dims, *args),
        mesh=mesh, in_specs=in_specs, out_specs=out_specs, check_vma=False,
    )
```

```python
import jax
import jax.numpy as jnp
from jax import lax
from jax.experimental import pallas as pl
from jax.experimental.pallas import tpu as pltpu
from jax.sharding import PartitionSpec as P

BF = jnp.bfloat16
F32 = jnp.float32
I32 = jnp.int32
NN = (((1,), (0,)), ((), ()))
NT = (((1,), (1,)), ((), ()))
TN = (((0,), (0,)), ((), ()))
BORDER = 8
GROUP = ("lon", "lat", "sub")
COLUMN = ("lat", "sub")


def dot(a, b, dims=NN):
    return lax.dot_general(a, b, dims, preferred_element_type=F32)


def low(value):
    return value.astype(BF)


def sigmoid(value):
    return 0.5 * jnp.tanh(0.5 * value) + 0.5


def silu(value):
    return value * sigmoid(value)


def silu_both(value):
    sig = sigmoid(value)
    act = value * sig
    return act, sig + act * (1.0 - sig)


def silu_slope(value):
    return silu_both(value)[1]


def iota(rows, columns, dim):
    return lax.broadcasted_iota(I32, (rows, columns), dim)


def hot(mask):
    return jnp.where(mask, 1.0, 0.0)


def slot_of(at, column, me, odd):
    far = jnp.where(at == column - 1, column + 1 - odd, column + odd)
    return jnp.where(at < column - 1, jnp.bitwise_xor(at + 1, me), far)


def as_column(values, wide, column, me, odd):
    slots = values.shape[0]
    count = (slots - 1) * wide
    row = iota(count, slots, 0)
    pick = low(hot(slot_of(row // wide, column, me, odd) == iota(count, slots, 1)))
    found = 16.0 * dot(pick, low((values // 16).astype(F32)))
    found = found + dot(pick, low((values % 16).astype(F32)))
    keep = iota(count, wide, 0) % wide == iota(count, wide, 1)
    return jnp.sum(jnp.where(keep, found, 0.0), axis=1, keepdims=True).astype(I32)


def as_row(values, wide, column, me, odd):
    slots = values.shape[0]
    count = (slots - 1) * wide
    pick = low(hot(iota(wide, count, 1) % wide == iota(wide, count, 0)))
    found = 16.0 * dot(low((values // 16).astype(F32)), pick)
    found = found + dot(low((values % 16).astype(F32)), pick)
    at = iota(slots, count, 1) // wide
    keep = slot_of(at, column, me, odd) == iota(slots, count, 0)
    return jnp.sum(jnp.where(keep, found, 0.0), axis=0, keepdims=True).astype(I32)


def split_parts(refs, starts, sizes):
    values = [ref[...].astype(F32) for ref in refs]
    return [
        jnp.concatenate([value[start : start + size] for value in values], axis=0)
        for start, size in zip(starts, sizes)
    ]


def store_parts(refs, parts):
    peers = len(refs)
    for at, ref in enumerate(refs):
        rows = []
        for part in parts:
            size = part.shape[0] // peers
            rows.append(part[at * size : (at + 1) * size])
        ref[...] = low(rows[0] if len(rows) == 1 else jnp.concatenate(rows, axis=0))


def receivers(senders_t, halo):
    degree, nodes = senders_t.shape
    found = jnp.zeros((halo, nodes), F32)
    ids = iota(halo, nodes, 0) + nodes
    for j in range(degree):
        found = found + hot(senders_t[j : j + 1, :] == ids)
    return found


def receivers_t(senders, degree, halo):
    nodes = senders.shape[0]
    found = jnp.zeros((nodes, halo), F32)
    ids = iota(nodes, halo, 1) + nodes
    for j in range(degree):
        found = found + hot(senders[:, j : j + 1] == ids)
    return found


def fine(rows, dims):
    return (rows // (dims[0] * dims[1] * dims[2])) % 16 == 0


def reverse_bits(block, bits):
    spot = 0
    for bit in range(bits):
        spot = 2 * spot + (block >> bit) % 2
    return spot


def store_blocks(keep_ref, give_ref, at, count, value, dims, bits_ref):
    value = low(value)
    rows = value.shape[0]
    total = dims[0] * dims[1] * dims[2]
    depth = rows // total
    if not fine(rows, dims):
        keep_ref[at] = value
        return
    bits = (total - 1).bit_length()
    upper = bits_ref[0:1, 2:3] == 1
    for block in range(0, total, 2):
        start = reverse_bits(block, bits) * count * depth + at * depth
        first = value[block * depth : (block + 1) * depth].astype(F32)
        second = value[(block + 1) * depth : (block + 2) * depth].astype(F32)
        keep_ref[start : start + depth, :] = low(jnp.where(upper, second, first))
        give_ref[start : start + depth, :] = low(jnp.where(upper, first, second))


def blocks_shapes(count, rows, width, dims):
    if fine(rows, dims):
        return [jax.ShapeDtypeStruct((count * rows // 2, width), BF)] * 2
    return [jax.ShapeDtypeStruct((count, rows, width), BF), jax.ShapeDtypeStruct((16, width), BF)]


def halve(bit, bits_ref, keep_ref, arr_ref, keep_out, give_out):
    half = keep_ref.shape[0] // 2
    upper = bits_ref[0:1, 2 + bit : 3 + bit] == 1
    first = keep_ref[:half, :].astype(F32) + arr_ref[:half, :].astype(F32)
    second = keep_ref[half:, :].astype(F32) + arr_ref[half:, :].astype(F32)
    keep_out[...] = low(jnp.where(upper, second, first))
    give_out[...] = low(jnp.where(upper, first, second))


def swap(block, bit, dims):
    total = dims[0] * dims[1] * dims[2]
    return lax.ppermute(block, GROUP, [(i, i ^ (1 << bit)) for i in range(total)])


def halve_step(bit, keep, arrived, place):
    rows, width = keep.shape[0] // 2, keep.shape[1]
    return call(
        lambda *refs: halve(bit, *refs), "halve", [shape(rows, width)] * 2,
        (place, keep, arrived), flops=4 * rows * width, size=0,
    )


def rest_of_halving(first, keep, give, place, dims):
    bits = (dims[0] * dims[1] * dims[2] - 1).bit_length()
    arrived = swap(give, first, dims)
    for bit in range(first + 1, bits):
        keep, give = halve_step(bit, keep, arrived, place)
        arrived = swap(give, bit, dims)
    return keep, arrived


def halve_carry(bit, bits_ref, keep_ref, arr_ref, *refs):
    *own_refs, keep_out, give_out, here_ref, on_ref = refs
    rows = keep_ref.shape[0]
    half = rows // 2
    size = here_ref.shape[0]
    upper = bits_ref[0:1, 2 + bit : 3 + bit] == 1
    value = arr_ref[...].astype(F32)
    first = keep_ref[:half, :].astype(F32) + value[:half]
    second = keep_ref[half:, :].astype(F32) + value[half:rows]
    keep_out[...] = low(jnp.where(upper, second, first))
    here_ref[...] = low(value[rows : rows + size])
    passed = value[rows + size : rows + 2 * size]
    on_ref[...] = low(passed)
    extra = [ref[...].astype(F32) for ref in own_refs]
    if len(extra) < 2:
        extra.append(passed)
    give_out[...] = low(jnp.concatenate([jnp.where(upper, first, second), *extra], axis=0))


def carry_step(bit, keep, arrived, own, place, capacity):
    rows, width = keep.shape[0] // 2, keep.shape[1]
    return call(
        lambda *refs: halve_carry(bit, *refs), "halve_carry",
        [shape(rows, width), shape(rows + min(len(own) + 1, 2) * capacity, width),
         shape(capacity, width), shape(capacity, width)],
        (place, keep, arrived, *own), flops=4 * rows * width, size=0,
    )


def scatter_plain(blocks, dims):
    lon, lat, sub = dims
    count, rows, width = blocks.shape
    depth = rows // (lon * lat * sub)
    blocks = blocks.reshape(count, lon, lat, sub, depth, width)
    blocks = blocks.transpose(3, 2, 1, 0, 4, 5)
    for axis in ("sub", "lat", "lon"):
        blocks = lax.psum_scatter(blocks, axis, scatter_dimension=0, tiled=False)
    return blocks.astype(F32)


def call(kernel, name, outs, args, flops, loads=(), scratch=(), size=None):
    if size is None:
        size = sum(a.size * a.dtype.itemsize for a in (*args, *outs, *loads))
    args = (*(pltpu.with_memory_space_constraint(a, pltpu.HBM) for a in loads), *args)
    scratch = list(scratch)
    if loads:
        scratch.append(pltpu.SemaphoreType.DMA((len(loads),)))
    in_specs = [pl.BlockSpec(memory_space=pltpu.HBM)] * len(loads)
    in_specs += [pl.BlockSpec(memory_space=pltpu.VMEM)] * (len(args) - len(loads))
    return pl.pallas_call(
        kernel,
        out_shape=[shape(*a.shape, dtype=a.dtype) for a in loads] + list(outs),
        in_specs=in_specs,
        out_specs=[pl.BlockSpec(memory_space=pltpu.VMEM)] * (len(outs) + len(loads)),
        scratch_shapes=scratch,
        compiler_params=pltpu.CompilerParams(vmem_limit_bytes=16 * 1024 * 1024),
        cost_estimate=pl.CostEstimate(flops=flops, bytes_accessed=size, transcendentals=0),
        name=name,
    )(*args)


def exchange(parts, dims):
    column = dims[1] * dims[2]
    count = dims[0]
    other = [(i, (i - 1 + 2 * (i % 2)) % count) for i in range(count)]
    far = lax.ppermute(parts[column], "lon", other)
    near = lax.ppermute(parts[column - 1], "lon", [(i, i ^ 1) for i in range(count)])
    arrived = [
        lax.ppermute(parts[r - 1], COLUMN, [(i, i ^ r) for i in range(column)])
        for r in range(column - 1, 0, -1)
    ]
    return (far, near, *arrived)


def shape(*dims, dtype=BF):
    return jax.ShapeDtypeStruct(dims, dtype)


def start_loads(sources, targets, sems):
    copies = [
        pltpu.make_async_copy(source, target, sems.at[at])
        for at, (source, target) in enumerate(zip(sources, targets))
    ]
    for copy in copies:
        copy.start()
    return copies


def first_payload(column, capacity, count, *refs):
    sources, ints_ref, targets = refs[:count], refs[count], refs[count + 1 : 2 * count + 1]
    sends_ref, *pay_refs, sems = refs[2 * count + 1 :]
    grid_ref = targets[0]
    grid_load, *loads = start_loads(sources, targets, sems)
    chosen = grid_ref.shape[0]
    ints = ints_ref[...]
    base = 2 * capacity + BORDER
    me, odd = ints[0:1, base : base + 1], ints[0:1, base + 1 : base + 2]
    sends = as_column(ints[:, :capacity], capacity, column, me, odd)
    sends_ref[...] = sends
    pick = low(hot(sends == iota(sends.shape[0], chosen, 1)))
    grid_load.wait()
    store_parts(pay_refs, [dot(pick, grid_ref[...])])
    for load in loads:
        load.wait()


def embed_local(
    column, capacity, ints_ref, senders_ref, grid_ref, weight_ref, target_ref, sends_ref,
    sum_ref, slope_ref, sends_row_ref, incoming_ref, bounds_ref, bounds_row_ref, senders_t_ref,
    senders_out_ref, place_ref,
):
    chosen = grid_ref.shape[0]
    nodes = sum_ref.shape[0]
    taken = sends_ref.shape[0]
    act, slope = silu_both(dot(grid_ref[...], weight_ref[...]))
    slope_ref[...] = low(slope)
    sent = jnp.max(hot(sends_ref[...] == iota(taken, chosen, 1)), axis=0, keepdims=True)
    label = jnp.where(sent > 0.0, nodes, target_ref[...])
    sum_ref[...] = dot(low(hot(label == iota(nodes, chosen, 0))), low(act))
    ints = ints_ref[...]
    base = 2 * capacity + BORDER
    place_ref[...] = ints[:, base:]
    me, odd = ints[0:1, base : base + 1], ints[0:1, base + 1 : base + 2]
    sends, incoming = ints[:, :capacity], ints[:, capacity : 2 * capacity]
    bounds = ints[:, 2 * capacity : base]
    sends_row_ref[...] = as_row(sends, capacity, column, me, odd)
    incoming_ref[...] = as_row(incoming, capacity, column, me, odd)
    bounds_ref[...] = as_column(bounds, BORDER, column, me, odd)
    bounds_row_ref[...] = as_row(bounds, BORDER, column, me, odd)
    senders = senders_ref[...]
    degree = senders.shape[0]
    offset = senders - nodes
    slot = offset // BORDER
    far = jnp.where(slot == column, column - odd, column - 1 + odd)
    at = jnp.where(slot < column, jnp.bitwise_xor(slot, me) - 1, far)
    senders = jnp.where(offset < 0, senders, nodes + at * BORDER + offset % BORDER)
    senders_t_ref[...] = senders
    filler = jnp.zeros((8 - degree, nodes), I32)
    senders_out_ref[...] = jnp.concatenate([senders, filler], axis=0).T


def merge_nodes(peers, *refs):
    arr_refs, refs = refs[:peers][::-1], refs[peers:]
    (incoming_ref, embed_ref, local_ref, mesh_ref, weight_ref, bounds_ref, senders_t_ref, cot_ref,
     merged_ref, state_ref, slope_ref, lat_ref, *pay_refs) = refs
    nodes = mesh_ref.shape[0]
    taken = incoming_ref.shape[1]
    halo = peers * BORDER
    lat = jnp.concatenate([ref[...] for ref in arr_refs], axis=0)
    lat_ref[...] = lat
    act, slope = silu_both(dot(lat, embed_ref[...]))
    slope_ref[...] = low(slope)
    place = low(hot(incoming_ref[...] == iota(nodes, taken, 0)))
    merged = low(local_ref[...] + dot(place, low(act)))
    merged_ref[...] = merged
    state = low(mesh_ref[...].astype(F32) + dot(merged, weight_ref[...]))
    state_ref[...] = state
    border = low(hot(bounds_ref[...] == iota(halo, nodes, 1)))
    back = low(receivers(senders_t_ref[...], halo))
    store_parts(
        pay_refs,
        [dot(border, state), dot(back, state), dot(border, merged), dot(back, cot_ref[...])],
    )


def local_edges(senders, degree, sent, recv, each):
    nodes = senders.shape[0]
    total = None
    ids = iota(nodes, nodes, 1)
    for j in range(degree):
        act, slope = silu_both(dot(low(hot(senders[:, j : j + 1] == ids)), sent) + recv)
        total = act if total is None else total + act
        each(j, slope)
    return total


def edge_targets(senders_t):
    degree, nodes = senders_t.shape
    ids = iota(nodes, nodes, 0)
    return jnp.concatenate(
        [low(hot(senders_t[j : j + 1, :] == ids)) for j in range(degree)], axis=1
    )


def forward_local(
    state_ref, send_ref, recv_ref, senders_ref, senders_t_ref, bounds_ref,
    total_ref, slope_ref, recv_n_ref, sent_b_ref,
):
    state = state_ref[...]
    nodes = state.shape[0]
    halo = bounds_ref.shape[0]
    sent = low(dot(state, send_ref[0]))
    recv = dot(state, recv_ref[0])

    def keep(j, slope):
        slope_ref[j] = low(slope)

    total_ref[...] = local_edges(senders_ref[...], senders_t_ref.shape[0], sent, recv, keep)
    back = low(receivers(senders_t_ref[...], halo))
    recv_n_ref[...] = dot(low(dot(back, state)), recv_ref[0])
    sent_b_ref[...] = low(dot(low(hot(bounds_ref[...] == iota(halo, nodes, 1))), sent))


def forward_halo(peers, *refs):
    arr_refs, refs = refs[:peers][::-1], refs[peers:]
    (recv_n_ref, total_ref, state_ref, send_ref, update_ref, senders_ref, senders_t_ref,
     bounds_ref, summed_ref, out_ref, pre_ref, rows_ref, back_ref, merged_ref, cot_ref,
     *pay_refs) = refs
    nodes = state_ref.shape[0]
    degree = senders_t_ref.shape[0]
    halo = peers * BORDER
    rows, back, merged, cot = split_parts(
        arr_refs, (0, BORDER, 2 * BORDER, 3 * BORDER), (BORDER,) * 4
    )
    rows_ref[...], back_ref[...] = low(rows), low(back)
    merged_ref[...], cot_ref[...] = low(merged), low(cot)
    pre = low(dot(low(rows), send_ref[0])).astype(F32) + recv_n_ref[...]
    pre_ref[...] = pre
    place = low(receivers_t(senders_ref[...], degree, halo))
    extra = silu(pre) - silu(recv_n_ref[...])
    summed = low(total_ref[...] + dot(place, low(extra)))
    summed_ref[...] = summed
    state = low(state_ref[...].astype(F32) + dot(summed, update_ref[0]))
    out_ref[...] = state
    border = low(hot(bounds_ref[...] == iota(halo, nodes, 1)))
    back = low(receivers(senders_t_ref[...], halo))
    store_parts(pay_refs, [dot(border, state), dot(back, state)])


def turn_local(
    state_ref, send_ref, recv_ref, update_ref, cot_ref, cot_r_ref, pre_ref, recv_n0_ref, back0_ref,
    sent_b0_ref, senders_ref, senders_t_ref, bounds_ref,
    total_ref, grecv_ref, gsent_ref, recv_n_ref, sent_b_ref, gsum_n_ref, gsum_r_ref,
    slope_k_ref, slope_d_ref, slope_r_ref, gpre_ref,
):
    halo = bounds_ref.shape[0]
    slope = silu_slope(pre_ref[...])
    slope_k_ref[...] = low(slope)
    slope_d_ref[...] = low(slope - silu_slope(recv_n0_ref[...]))
    pre = sent_b0_ref[...].astype(F32) + dot(back0_ref[...], recv_ref[0])
    slope_r_ref[...] = low(silu_slope(pre))
    state = state_ref[...]
    nodes = state.shape[0]
    sent = low(dot(state, send_ref[1]))
    recv = dot(state, recv_ref[1])
    gsum = low(dot(cot_ref[...], update_ref[1], NT))
    grad = gsum.astype(F32)
    grecv = []

    def back_edge(j, slope):
        gpre = grad * slope
        grecv.append(gpre if j == 0 else grecv[-1] + gpre)
        gpre_ref[j * nodes : (j + 1) * nodes, :] = low(gpre)

    degree = senders_t_ref.shape[0]
    total_ref[...] = local_edges(senders_ref[...], degree, sent, recv, back_edge)
    grecv_ref[...] = grecv[-1]
    gsent_ref[...] = dot(edge_targets(senders_t_ref[...]), gpre_ref[...])
    back = low(receivers(senders_t_ref[...], halo))
    recv_n_ref[...] = dot(low(dot(back, state)), recv_ref[1])
    sent_b_ref[...] = low(dot(low(hot(bounds_ref[...] == iota(halo, nodes, 1))), sent))
    gsum_n_ref[...] = low(dot(back, gsum))
    gsum_r_ref[...] = low(dot(cot_r_ref[...], update_ref[1], NT))


def turn_halo(peers, *refs):
    arr_refs, refs = refs[:peers][::-1], refs[peers:]
    (recv_n_ref, sent_b_ref, gsum_n_ref, gsum_r_ref, total_ref, grecv_ref, gsent_ref, cot_ref,
     send_ref, recv_ref, senders_ref, senders_t_ref, bounds_ref, summed_ref, grecv_out_ref,
     gsent_out_ref, gin_ref, *pay_refs) = refs
    nodes = cot_ref.shape[0]
    degree = senders_t_ref.shape[0]
    halo = peers * BORDER
    rows, back = split_parts(arr_refs, (0, BORDER), (BORDER,) * 2)
    pre = low(dot(low(rows), send_ref[1])).astype(F32) + recv_n_ref[...]
    act, slope = silu_both(pre)
    place = low(receivers_t(senders_ref[...], degree, halo))
    base, base_slope = silu_both(recv_n_ref[...])
    gpre = low(gsum_n_ref[...].astype(F32) * (slope - base_slope))
    grecv = low(grecv_ref[...] + dot(place, gpre))
    pre = sent_b_ref[...].astype(F32) + dot(low(back), recv_ref[1])
    gpre = low(gsum_r_ref[...].astype(F32) * silu_slope(pre))
    border = low(hot(bounds_ref[...] == iota(nodes, halo, 0)))
    gsent = low(gsent_ref[...] + dot(border, gpre))
    gin = cot_ref[...].astype(F32) + dot(grecv, recv_ref[1], NT) + dot(gsent, send_ref[1], NT)
    gin = low(gin)
    gin_ref[...] = gin
    store_parts(pay_refs, [dot(low(receivers(senders_t_ref[...], halo)), gin)])
    summed_ref[...] = low(total_ref[...] + dot(place, low(act - base)))
    grecv_out_ref[...] = grecv
    gsent_out_ref[...] = gsent


def last_weights(
    dims, place_ref, state_ref, summed_ref, cot_ref, grecv_ref, gsent_ref, update_ref,
    keep_ref, give_ref, mesh_ref,
):
    state, summed = state_ref[...], summed_ref[...]

    def store(at, value):
        store_blocks(keep_ref, give_ref, at, 3, value, dims, place_ref)

    store(0, dot(state, gsent_ref[...], TN))
    store(1, dot(state, grecv_ref[...], TN))
    store(2, dot(summed, cot_ref[...], TN))
    mesh_ref[...] = low(state.astype(F32) + dot(summed, update_ref[1]))


def back_local(
    dims, place_ref, gin_ref, slope_ref, slope_k_ref, slope_d_ref, send_ref, recv_ref, update_ref,
    senders_ref, senders_t_ref, state_ref, rows_ref, summed_ref, merged_ref, merged_r_ref,
    after_ref, part_ref, keep_ref, give_ref, keep2_ref, give2_ref, gpre_ref,
):
    nodes = gin_ref.shape[0]
    halo = slope_k_ref.shape[0]
    degree = senders_t_ref.shape[0]
    gin = gin_ref[...]
    gsum = low(dot(gin, update_ref[0], NT))
    place = low(receivers_t(senders_ref[...], degree, halo))
    back = low(receivers(senders_t_ref[...], halo))
    gsum_n = low(dot(back, gsum))
    gpre_k = gsum_n * slope_k_ref[...]
    grecv = dot(place, gsum_n * slope_d_ref[...])
    for j in range(degree):
        gpre = gsum * slope_ref[j]
        grecv = grecv + gpre.astype(F32)
        gpre_ref[j * nodes : (j + 1) * nodes, :] = gpre
    gsent = dot(edge_targets(senders_t_ref[...]), gpre_ref[...])
    grecv, gsent = low(grecv), low(gsent)
    part = gin.astype(F32) + dot(grecv, recv_ref[0], NT) + dot(gsent, send_ref[0], NT)
    part_ref[...] = part
    state = state_ref[...]

    def store(at, value):
        store_blocks(keep_ref, give_ref, at, 2, value, dims, place_ref)

    def store2(at, value):
        store_blocks(keep2_ref, give2_ref, at, 2, value, dims, place_ref)

    store(0, dot(state, gsent, TN) + dot(rows_ref[...], gpre_k, TN))
    store(1, dot(state, grecv, TN))
    store2(0, dot(summed_ref[...], gin, TN))
    far = low(dot(gpre_k, send_ref[0], NT))
    store2(1, dot(merged_ref[...], low(part), TN) + dot(merged_r_ref[...], far, TN))


def embed_back(peers, dims, carry, *refs):
    arr_refs, refs = refs[:peers][::-1], refs[peers:]
    (place_ref, slope_r_ref, part_ref, update_ref, send_ref, merge_ref, bounds_ref, target_ref,
     sends_ref, incoming_ref, slope_g_ref, slope_a_ref, grid_ref, lat_ref, embed_ref,
     gpre_ref, keep_ref, give_ref, *pay_refs) = refs
    nodes = part_ref.shape[0]
    halo = peers * BORDER
    chosen = grid_ref.shape[0]
    taken = sends_ref.shape[0]
    (arrived,) = split_parts(arr_refs, (0,), (BORDER,))
    gsum = low(dot(low(arrived), update_ref[0], NT)).astype(F32)
    gpre = low(gsum * slope_r_ref[...].astype(F32))
    border = low(hot(bounds_ref[...] == iota(nodes, halo, 0)))
    gsent = low(dot(border, gpre))
    gin = low(part_ref[...] + dot(gsent, send_ref[0], NT))
    gmerged = low(dot(gin, merge_ref[...], NT))
    place = low(hot(incoming_ref[...] == iota(nodes, taken, 0)))
    gpre_a = low(dot(place, gmerged, TN) * slope_a_ref[...].astype(F32))
    sent = jnp.max(hot(sends_ref[...] == iota(taken, chosen, 1)), axis=0, keepdims=True)
    label = jnp.where(sent > 0.0, nodes, target_ref[...])
    pick = low(hot(label == iota(nodes, chosen, 0)))
    gpre_g = low(dot(pick, gmerged, TN) * slope_g_ref[...].astype(F32))
    gpre_ref[...] = gpre_g
    grad = dot(grid_ref[...], gpre_g, TN) + dot(lat_ref[...], gpre_a, TN)
    store_blocks(keep_ref, give_ref, 0, 1, grad, dims, place_ref)
    rows = dot(gpre_a, embed_ref[...], NT)
    store_parts(pay_refs, [rows])
    if carry:
        size = taken // peers
        start = keep_ref.shape[0]
        give_ref[start : start + 2 * size, :] = low(
            jnp.concatenate([rows[:size], rows[2 * size : 3 * size]], axis=0)
        )


def grid_place(peers, *refs):
    arr_refs, refs = refs[:peers][::-1], refs[peers:]
    gpre_ref, weight_ref, sends_ref, out_ref = refs
    chosen = gpre_ref.shape[0]
    taken = sends_ref.shape[1]
    local = dot(gpre_ref[...], weight_ref[...], NT)
    place = low(hot(sends_ref[...] == iota(chosen, taken, 0)))
    size = taken // peers
    rows = [ref[...].astype(F32) for ref in arr_refs]
    rows = low(jnp.concatenate([row[row.shape[0] - size :] for row in rows], axis=0))
    out_ref[...] = low(local + dot(place, rows))


def finish(
    keep1_ref, arr1_ref, keep0_ref, arr0_ref, keep2_ref, arr2_ref, keep_e_ref, arr_e_ref,
    embed_ref, merge_ref, send_ref, recv_ref, update_ref,
):
    last = keep1_ref[...].astype(F32) + arr1_ref[...].astype(F32)
    first = keep0_ref[...].astype(F32) + arr0_ref[...].astype(F32)
    second = keep2_ref[...].astype(F32) + arr2_ref[...].astype(F32)
    depth = embed_ref.shape[0]
    embed_ref[...] = keep_e_ref[...].astype(F32) + arr_e_ref[:depth, :].astype(F32)
    for at, ref in enumerate((send_ref, recv_ref, update_ref)):
        ref[1] = last[at * depth : (at + 1) * depth]
    send_ref[0], recv_ref[0], update_ref[0] = first[:depth], first[depth:], second[:depth]
    merge_ref[...] = second[depth:]


def body(
    dims,
    grid_latent, mesh_latent, cotangent, embed_weight, merge_weight, send_weight, recv_weight,
    update_weight, target_row, send_rows, incoming_rows, border_mesh_rows, mesh_senders,
):
    chosen, width = grid_latent.shape
    nodes, degree = mesh_senders.shape
    slots, capacity = send_rows.shape[1:]
    column = dims[1] * dims[2]
    peers = slots - 1
    halo = peers * BORDER
    taken = peers * capacity
    total = dims[0] * dims[1] * dims[2]
    bits = (total - 1).bit_length()
    carry = dims == (4, 2, 2) and fine(width, dims)
    spot = lax.axis_index(GROUP)
    place = [lax.axis_index(COLUMN), lax.axis_index("lon") % 2]
    place += [(spot >> bit) % 2 for bit in range(bits)]
    place = jnp.broadcast_to(jnp.stack(place).astype(I32)[None], (slots, 2 + bits))
    ints = jnp.concatenate([send_rows[0], incoming_rows[0], border_mesh_rows[0], place], axis=1)
    unit = 2 * nodes * width * width

    loads = (grid_latent, embed_weight, target_row.reshape(1, chosen), mesh_senders.T,
             mesh_latent, merge_weight, cotangent)
    grid, embed, targets, senders_raw, mesh, merge, cot, sends, *pay1 = call(
        lambda *refs: first_payload(column, capacity, len(loads), *refs), "first_payload",
        [shape(taken, 1, dtype=I32)] + [shape(capacity, width)] * peers,
        (ints,), flops=unit // 2, loads=loads,
    )
    arr1 = exchange(pay1, dims)
    (local, slope_g, sends_row, incoming, bounds, bounds_row, senders_t, senders, place) = call(
        lambda *refs: embed_local(column, capacity, *refs), "embed_local",
        [shape(nodes, width, dtype=F32), shape(chosen, width), shape(1, taken, dtype=I32),
         shape(1, taken, dtype=I32), shape(halo, 1, dtype=I32), shape(1, halo, dtype=I32),
         shape(degree, nodes, dtype=I32), shape(nodes, 8, dtype=I32),
         shape(slots, 2 + bits, dtype=I32)],
        (ints, senders_raw, grid, embed, targets, sends), flops=3 * unit,
    )
    merged, state0, slope_a, lat_a, *pay2 = call(
        lambda *refs: merge_nodes(peers, *refs), "merge_nodes",
        [shape(nodes, width), shape(nodes, width), shape(taken, width), shape(taken, width)]
        + [shape(4 * BORDER, width)] * peers,
        (*arr1, incoming, embed, local, mesh, merge, bounds, senders_t, cot),
        flops=2 * unit,
    )
    arr2 = exchange(pay2, dims)
    total0, slope0, recv_n0, sent_b0 = call(
        forward_local, "forward_local",
        [shape(nodes, width, dtype=F32), shape(degree, nodes, width),
         shape(halo, width, dtype=F32), shape(halo, width)],
        (state0, send_weight, recv_weight, senders, senders_t, bounds), flops=6 * unit,
    )
    summed0, state1, pre0, rows0, back0, merged_r, cot_r, *pay3 = call(
        lambda *refs: forward_halo(peers, *refs), "forward_halo",
        [shape(nodes, width), shape(nodes, width), shape(halo, width, dtype=F32)]
        + [shape(halo, width)] * 4 + [shape(2 * BORDER, width)] * peers,
        (*arr2, recv_n0, total0, state0, send_weight, update_weight, senders, senders_t, bounds),
        flops=2 * unit,
    )
    arr3 = exchange(pay3, dims)
    (total1, grecv_l, gsent_l, recv_n1, sent_b1, gsum_n1, gsum_r1, slope_k0, slope_d0,
     slope_r0) = call(
        turn_local, "turn_local",
        [shape(nodes, width, dtype=F32)] * 3 + [shape(halo, width, dtype=F32)]
        + [shape(halo, width)] * 6,
        (state1, send_weight, recv_weight, update_weight, cot, cot_r, pre0, recv_n0, back0,
         sent_b0, senders, senders_t, bounds),
        flops=10 * unit, scratch=[pltpu.VMEM((degree * nodes, width), BF)],
    )
    summed1, grecv1, gsent1, gin1, *pay4 = call(
        lambda *refs: turn_halo(peers, *refs), "turn_halo",
        [shape(nodes, width)] * 4 + [shape(BORDER, width)] * peers,
        (*arr3, recv_n1, sent_b1, gsum_n1, gsum_r1, total1, grecv_l, gsent_l, cot,
         send_weight, recv_weight, senders, senders_t, bounds_row),
        flops=3 * unit,
    )
    arr4 = exchange(pay4, dims)
    keep1, give1, mesh_out = call(
        lambda *refs: last_weights(dims, *refs), "last_weights",
        blocks_shapes(3, width, width, dims) + [shape(nodes, width)],
        (place, state1, summed1, cot, grecv1, gsent1, update_weight), flops=4 * unit,
    )
    split = fine(width, dims)
    if split:
        give1, last = lax.optimization_barrier((give1, arr4[-1]))
        arr4 = (*arr4[:-1], last)
        keep1, give1 = halve_step(1, keep1, swap(give1, 0, dims), place)
    part0, keep0, give0, keep2, give2 = call(
        lambda *refs: back_local(dims, *refs), "back_local",
        [shape(nodes, width, dtype=F32)] + blocks_shapes(2, width, width, dims) * 2,
        (place, gin1, slope0, slope_k0, slope_d0, send_weight, recv_weight, update_weight, senders,
         senders_t, state0, rows0, summed0, merged, merged_r, keep1),
        flops=10 * unit, scratch=[pltpu.VMEM((degree * nodes, width), BF)],
    )
    if split:
        give0, give2, *arr4 = lax.optimization_barrier((give0, give2, *arr4))
        keep0, give0 = halve_step(1, keep0, swap(give0, 0, dims), place)
        keep0, *arr4 = lax.optimization_barrier((keep0, *arr4))
    shapes = blocks_shapes(1, width, width, dims)
    if carry:
        shapes[1] = shape(shapes[1].shape[0] + 2 * capacity, width)
    gpre_g, keep_e, give_e, *pay5 = call(
        lambda *refs: embed_back(peers, dims, carry, *refs), "embed_back",
        [shape(chosen, width)] + shapes + [shape(capacity, width)] * peers,
        (*arr4, place, slope_r0, part0, update_weight, send_weight, merge, bounds_row,
         targets, sends, incoming, slope_g, slope_a, grid, lat_a, embed),
        flops=6 * unit,
    )
    depth = width // total
    if not split:
        arr5 = exchange(pay5, dims)
        last, first, second, embed_sum = (
            scatter_plain(blocks, dims) for blocks in (keep1, keep0, keep2, keep_e)
        )
        grads = [jnp.stack([a, last[i]]) for i, a in enumerate((first[0], first[1], second[0]))]
        grads = [embed_sum[0], second[1], *grads]
    elif not carry:
        arr5 = exchange(pay5, dims)
        sums = [
            rest_of_halving(1, keep1, give1, place, dims),
            rest_of_halving(1, keep0, give0, place, dims),
            rest_of_halving(0, keep2, give2, place, dims),
            rest_of_halving(0, keep_e, give_e, place, dims),
        ]
    else:
        arr1 = swap(give1, 1, dims)
        arr0 = swap(give0, 1, dims)
        arr2 = swap(give2, 0, dims)
        arr_e, arr1 = lax.optimization_barrier((swap(give_e, 0, dims), arr1))
        keep1, give1 = halve_step(2, keep1, arr1, place)
        arr1 = swap(give1, 2, dims)
        keep_e, keep1 = lax.optimization_barrier((keep_e, keep1))
        keep_e, give_e, from_sub, _ = carry_step(1, keep_e, arr_e, pay5[1:2], place, capacity)
        arr_e = swap(give_e, 1, dims)
        keep2, keep_e = lax.optimization_barrier((keep2, keep_e))
        keep2, give2 = halve_step(1, keep2, arr2, place)
        arr2 = swap(give2, 1, dims)
        keep0, keep2 = lax.optimization_barrier((keep0, keep2))
        keep0, give0 = halve_step(2, keep0, arr0, place)
        arr0 = swap(give0, 2, dims)
        keep1, keep0 = lax.optimization_barrier((keep1, keep0))
        keep1, give1 = halve_step(3, keep1, arr1, place)
        arr1 = swap(give1, 3, dims)
        keep_e, keep1 = lax.optimization_barrier((keep_e, keep1))
        keep_e, give_e, from_lat, from_diag = carry_step(
            2, keep_e, arr_e, pay5[3:], place, capacity
        )
        arr_e = swap(give_e, 2, dims)
        keep0, keep_e = lax.optimization_barrier((keep0, keep_e))
        keep0, give0 = halve_step(3, keep0, arr0, place)
        arr0 = swap(give0, 3, dims)
        keep_e, keep0 = lax.optimization_barrier((keep_e, keep0))
        keep_e, give_e, from_near, _ = carry_step(3, keep_e, arr_e, (), place, capacity)
        arr_e = swap(give_e, 3, dims)
        keep2, keep_e = lax.optimization_barrier((keep2, keep_e))
        keep2, give2 = halve_step(2, keep2, arr2, place)
        arr2 = swap(give2, 2, dims)
        arr_e, arr1 = lax.optimization_barrier((arr_e, arr1))
        arr5 = (arr_e, from_near, from_diag, from_lat, from_sub)
        gpre_g, keep2 = lax.optimization_barrier((gpre_g, keep2))
    (grid_grad,) = call(
        lambda *refs: grid_place(peers, *refs), "grid_place", [shape(chosen, width)],
        (*arr5, gpre_g, embed, sends_row), flops=3 * unit,
    )
    if carry:
        keep2, grid_grad, arr0 = lax.optimization_barrier((keep2, grid_grad, arr0))
        keep2, give2 = halve_step(3, keep2, arr2, place)
        sums = ((keep1, arr1), (keep0, arr0), (keep2, swap(give2, 3, dims)), (keep_e, arr_e))
    if split:
        grads = call(
            finish, "finish",
            [shape(depth, width, dtype=F32)] * 2 + [shape(2, depth, width, dtype=F32)] * 3,
            [part for pair in sums for part in pair], flops=8 * depth * width,
        )
    return (mesh_out, grid_grad, *grads)


def solution(mesh):
    split = ("groups", "lon", "lat", "sub")
    dims = tuple(mesh.shape[axis] for axis in GROUP)
    rows = P(split, None)
    whole = P("groups", GROUP, None)
    in_specs = (
        rows, rows, rows, P(), P(), P(), P(), P(), P(split), P(split, None, None),
        P(split, None, None), P(split, None, None), rows,
    )
    out_specs = (rows, rows, rows, rows, whole, whole, whole)
    return jax.shard_map(
        lambda *args: body(dims, *args),
        mesh=mesh, in_specs=in_specs, out_specs=out_specs, check_vma=False,
    )
```

```python
import jax
import jax.numpy as jnp
from jax import lax
from jax.experimental import pallas as pl
from jax.experimental.pallas import tpu as pltpu
from jax.sharding import PartitionSpec as P

BF = jnp.bfloat16
F32 = jnp.float32
I32 = jnp.int32
NN = (((1,), (0,)), ((), ()))
NT = (((1,), (1,)), ((), ()))
TN = (((0,), (0,)), ((), ()))
BORDER = 8
GROUP = ("lon", "lat", "sub")
COLUMN = ("lat", "sub")


def dot(a, b, dims=NN):
    return lax.dot_general(a, b, dims, preferred_element_type=F32)


def low(value):
    return value.astype(BF)


def sigmoid(value):
    return 0.5 * jnp.tanh(0.5 * value) + 0.5


def silu(value):
    return value * sigmoid(value)


def silu_both(value):
    sig = sigmoid(value)
    act = value * sig
    return act, sig + act * (1.0 - sig)


def silu_slope(value):
    return silu_both(value)[1]


def iota(rows, columns, dim):
    return lax.broadcasted_iota(I32, (rows, columns), dim)


def hot(mask):
    return jnp.where(mask, 1.0, 0.0)


def slot_of(at, column, me, odd):
    far = jnp.where(at == column - 1, column + 1 - odd, column + odd)
    return jnp.where(at < column - 1, jnp.bitwise_xor(at + 1, me), far)


def as_column(values, wide, column, me, odd):
    slots = values.shape[0]
    count = (slots - 1) * wide
    row = iota(count, slots, 0)
    pick = low(hot(slot_of(row // wide, column, me, odd) == iota(count, slots, 1)))
    found = 16.0 * dot(pick, low((values // 16).astype(F32)))
    found = found + dot(pick, low((values % 16).astype(F32)))
    keep = iota(count, wide, 0) % wide == iota(count, wide, 1)
    return jnp.sum(jnp.where(keep, found, 0.0), axis=1, keepdims=True).astype(I32)


def as_row(values, wide, column, me, odd):
    slots = values.shape[0]
    count = (slots - 1) * wide
    pick = low(hot(iota(wide, count, 1) % wide == iota(wide, count, 0)))
    found = 16.0 * dot(low((values // 16).astype(F32)), pick)
    found = found + dot(low((values % 16).astype(F32)), pick)
    at = iota(slots, count, 1) // wide
    keep = slot_of(at, column, me, odd) == iota(slots, count, 0)
    return jnp.sum(jnp.where(keep, found, 0.0), axis=0, keepdims=True).astype(I32)


def split_parts(refs, starts, sizes):
    values = [ref[...].astype(F32) for ref in refs]
    return [
        jnp.concatenate([value[start : start + size] for value in values], axis=0)
        for start, size in zip(starts, sizes)
    ]


def store_parts(refs, parts):
    peers = len(refs)
    for at, ref in enumerate(refs):
        rows = []
        for part in parts:
            size = part.shape[0] // peers
            rows.append(part[at * size : (at + 1) * size])
        ref[...] = low(rows[0] if len(rows) == 1 else jnp.concatenate(rows, axis=0))


def receivers(senders_t, halo):
    degree, nodes = senders_t.shape
    found = jnp.zeros((halo, nodes), F32)
    ids = iota(halo, nodes, 0) + nodes
    for j in range(degree):
        found = found + hot(senders_t[j : j + 1, :] == ids)
    return found


def receivers_t(senders, degree, halo):
    nodes = senders.shape[0]
    found = jnp.zeros((nodes, halo), F32)
    ids = iota(nodes, halo, 1) + nodes
    for j in range(degree):
        found = found + hot(senders[:, j : j + 1] == ids)
    return found


def fine(rows, dims):
    return (rows // (dims[0] * dims[1] * dims[2])) % 16 == 0


def block_spot(block, order):
    spot = 0
    for bit in order:
        spot = 2 * spot + (block >> bit) % 2
    return spot


def store_blocks(keep_ref, give_ref, at, count, value, dims, bits_ref, order=None):
    value = low(value)
    rows = value.shape[0]
    total = dims[0] * dims[1] * dims[2]
    depth = rows // total
    if not fine(rows, dims):
        keep_ref[at] = value
        return
    if order is None:
        order = range((total - 1).bit_length())
    upper = bits_ref[0:1, 2:3] == 1
    for block in range(0, total, 2):
        start = block_spot(block, order) * count * depth + at * depth
        first = value[block * depth : (block + 1) * depth].astype(F32)
        second = value[(block + 1) * depth : (block + 2) * depth].astype(F32)
        keep_ref[start : start + depth, :] = low(jnp.where(upper, second, first))
        give_ref[start : start + depth, :] = low(jnp.where(upper, first, second))


def blocks_shapes(count, rows, width, dims):
    if fine(rows, dims):
        return [jax.ShapeDtypeStruct((count * rows // 2, width), BF)] * 2
    return [jax.ShapeDtypeStruct((count, rows, width), BF), jax.ShapeDtypeStruct((16, width), BF)]


def halve(bit, bits_ref, keep_ref, arr_ref, keep_out, give_out):
    half = keep_ref.shape[0] // 2
    upper = bits_ref[0:1, 2 + bit : 3 + bit] == 1
    first = keep_ref[:half, :].astype(F32) + arr_ref[:half, :].astype(F32)
    second = keep_ref[half:, :].astype(F32) + arr_ref[half:, :].astype(F32)
    keep_out[...] = low(jnp.where(upper, second, first))
    give_out[...] = low(jnp.where(upper, first, second))


def swap(block, bit, dims):
    total = dims[0] * dims[1] * dims[2]
    return lax.ppermute(block, GROUP, [(i, i ^ (1 << bit)) for i in range(total)])


def halve_step(bit, keep, arrived, place):
    rows, width = keep.shape[0] // 2, keep.shape[1]
    return call(
        lambda *refs: halve(bit, *refs), "halve", [shape(rows, width)] * 2,
        (place, keep, arrived), flops=4 * rows * width, size=0,
    )


def rest_of_halving(first, keep, give, place, dims):
    bits = (dims[0] * dims[1] * dims[2] - 1).bit_length()
    arrived = swap(give, first, dims)
    for bit in range(first + 1, bits):
        keep, give = halve_step(bit, keep, arrived, place)
        arrived = swap(give, bit, dims)
    return keep, arrived


def halve_carry(bit, bits_ref, keep_ref, arr_ref, *refs):
    *own_refs, keep_out, give_out, here_ref, on_ref = refs
    rows = keep_ref.shape[0]
    half = rows // 2
    size = here_ref.shape[0]
    upper = bits_ref[0:1, 2 + bit : 3 + bit] == 1
    value = arr_ref[...].astype(F32)
    first = keep_ref[:half, :].astype(F32) + value[:half]
    second = keep_ref[half:, :].astype(F32) + value[half:rows]
    keep_out[...] = low(jnp.where(upper, second, first))
    here_ref[...] = low(value[rows : rows + size])
    passed = value[rows + size : rows + 2 * size]
    on_ref[...] = low(passed)
    extra = [ref[...].astype(F32) for ref in own_refs]
    if len(extra) < 2:
        extra.append(passed)
    give_out[...] = low(jnp.concatenate([jnp.where(upper, first, second), *extra], axis=0))


def carry_step(bit, keep, arrived, own, place, capacity):
    rows, width = keep.shape[0] // 2, keep.shape[1]
    return call(
        lambda *refs: halve_carry(bit, *refs), "halve_carry",
        [shape(rows, width), shape(rows + min(len(own) + 1, 2) * capacity, width),
         shape(capacity, width), shape(capacity, width)],
        (place, keep, arrived, *own), flops=4 * rows * width, size=0,
    )


def scatter_plain(blocks, dims):
    lon, lat, sub = dims
    count, rows, width = blocks.shape
    depth = rows // (lon * lat * sub)
    blocks = blocks.reshape(count, lon, lat, sub, depth, width)
    blocks = blocks.transpose(3, 2, 1, 0, 4, 5)
    for axis in ("sub", "lat", "lon"):
        blocks = lax.psum_scatter(blocks, axis, scatter_dimension=0, tiled=False)
    return blocks.astype(F32)


def call(kernel, name, outs, args, flops, loads=(), scratch=(), size=None):
    if size is None:
        size = sum(a.size * a.dtype.itemsize for a in (*args, *outs, *loads))
    args = (*(pltpu.with_memory_space_constraint(a, pltpu.HBM) for a in loads), *args)
    scratch = list(scratch)
    if loads:
        scratch.append(pltpu.SemaphoreType.DMA((len(loads),)))
    in_specs = [pl.BlockSpec(memory_space=pltpu.HBM)] * len(loads)
    in_specs += [pl.BlockSpec(memory_space=pltpu.VMEM)] * (len(args) - len(loads))
    return pl.pallas_call(
        kernel,
        out_shape=[shape(*a.shape, dtype=a.dtype) for a in loads] + list(outs),
        in_specs=in_specs,
        out_specs=[pl.BlockSpec(memory_space=pltpu.VMEM)] * (len(outs) + len(loads)),
        scratch_shapes=scratch,
        compiler_params=pltpu.CompilerParams(vmem_limit_bytes=16 * 1024 * 1024),
        cost_estimate=pl.CostEstimate(flops=flops, bytes_accessed=size, transcendentals=0),
        name=name,
    )(*args)


def exchange(parts, dims):
    column = dims[1] * dims[2]
    count = dims[0]
    other = [(i, (i - 1 + 2 * (i % 2)) % count) for i in range(count)]
    far = lax.ppermute(parts[column], "lon", other)
    near = lax.ppermute(parts[column - 1], "lon", [(i, i ^ 1) for i in range(count)])
    arrived = [
        lax.ppermute(parts[r - 1], COLUMN, [(i, i ^ r) for i in range(column)])
        for r in range(column - 1, 0, -1)
    ]
    return (far, near, *arrived)


def shape(*dims, dtype=BF):
    return jax.ShapeDtypeStruct(dims, dtype)


def start_loads(sources, targets, sems):
    copies = [
        pltpu.make_async_copy(source, target, sems.at[at])
        for at, (source, target) in enumerate(zip(sources, targets))
    ]
    for copy in copies:
        copy.start()
    return copies


def first_payload(column, capacity, count, *refs):
    sources, ints_ref, targets = refs[:count], refs[count], refs[count + 1 : 2 * count + 1]
    sends_ref, *pay_refs, sems = refs[2 * count + 1 :]
    grid_ref = targets[0]
    grid_load, *loads = start_loads(sources, targets, sems)
    chosen = grid_ref.shape[0]
    ints = ints_ref[...]
    base = 2 * capacity + BORDER
    me, odd = ints[0:1, base : base + 1], ints[0:1, base + 1 : base + 2]
    sends = as_column(ints[:, :capacity], capacity, column, me, odd)
    sends_ref[...] = sends
    pick = low(hot(sends == iota(sends.shape[0], chosen, 1)))
    grid_load.wait()
    store_parts(pay_refs, [dot(pick, grid_ref[...])])
    for load in loads:
        load.wait()


def embed_local(
    column, capacity, ints_ref, senders_ref, grid_ref, weight_ref, target_ref, sends_ref,
    sum_ref, slope_ref, sends_row_ref, incoming_ref, bounds_ref, bounds_row_ref, senders_t_ref,
    senders_out_ref, place_ref,
):
    chosen = grid_ref.shape[0]
    nodes = sum_ref.shape[0]
    taken = sends_ref.shape[0]
    act, slope = silu_both(dot(grid_ref[...], weight_ref[...]))
    slope_ref[...] = low(slope)
    sent = jnp.max(hot(sends_ref[...] == iota(taken, chosen, 1)), axis=0, keepdims=True)
    label = jnp.where(sent > 0.0, nodes, target_ref[...])
    sum_ref[...] = dot(low(hot(label == iota(nodes, chosen, 0))), low(act))
    ints = ints_ref[...]
    base = 2 * capacity + BORDER
    place_ref[...] = ints[:, base:]
    me, odd = ints[0:1, base : base + 1], ints[0:1, base + 1 : base + 2]
    sends, incoming = ints[:, :capacity], ints[:, capacity : 2 * capacity]
    bounds = ints[:, 2 * capacity : base]
    sends_row_ref[...] = as_row(sends, capacity, column, me, odd)
    incoming_ref[...] = as_row(incoming, capacity, column, me, odd)
    bounds_ref[...] = as_column(bounds, BORDER, column, me, odd)
    bounds_row_ref[...] = as_row(bounds, BORDER, column, me, odd)
    senders = senders_ref[...]
    degree = senders.shape[0]
    offset = senders - nodes
    slot = offset // BORDER
    far = jnp.where(slot == column, column - odd, column - 1 + odd)
    at = jnp.where(slot < column, jnp.bitwise_xor(slot, me) - 1, far)
    senders = jnp.where(offset < 0, senders, nodes + at * BORDER + offset % BORDER)
    senders_t_ref[...] = senders
    filler = jnp.zeros((8 - degree, nodes), I32)
    senders_out_ref[...] = jnp.concatenate([senders, filler], axis=0).T


def merge_nodes(peers, *refs):
    arr_refs, refs = refs[:peers][::-1], refs[peers:]
    (incoming_ref, embed_ref, local_ref, mesh_ref, weight_ref, bounds_ref, senders_t_ref, cot_ref,
     merged_ref, state_ref, slope_ref, lat_ref, *pay_refs) = refs
    nodes = mesh_ref.shape[0]
    taken = incoming_ref.shape[1]
    halo = peers * BORDER
    lat = jnp.concatenate([ref[...] for ref in arr_refs], axis=0)
    lat_ref[...] = lat
    act, slope = silu_both(dot(lat, embed_ref[...]))
    slope_ref[...] = low(slope)
    place = low(hot(incoming_ref[...] == iota(nodes, taken, 0)))
    merged = low(local_ref[...] + dot(place, low(act)))
    merged_ref[...] = merged
    state = low(mesh_ref[...].astype(F32) + dot(merged, weight_ref[...]))
    state_ref[...] = state
    border = low(hot(bounds_ref[...] == iota(halo, nodes, 1)))
    back = low(receivers(senders_t_ref[...], halo))
    store_parts(
        pay_refs,
        [dot(border, state), dot(back, state), dot(border, merged), dot(back, cot_ref[...])],
    )


def local_edges(senders, degree, sent, recv, each):
    nodes = senders.shape[0]
    total = None
    ids = iota(nodes, nodes, 1)
    for j in range(degree):
        act, slope = silu_both(dot(low(hot(senders[:, j : j + 1] == ids)), sent) + recv)
        total = act if total is None else total + act
        each(j, slope)
    return total


def edge_targets(senders_t):
    degree, nodes = senders_t.shape
    ids = iota(nodes, nodes, 0)
    return jnp.concatenate(
        [low(hot(senders_t[j : j + 1, :] == ids)) for j in range(degree)], axis=1
    )


def forward_local(
    state_ref, send_ref, recv_ref, senders_ref, senders_t_ref, bounds_ref,
    total_ref, slope_ref, recv_n_ref, sent_b_ref,
):
    state = state_ref[...]
    nodes = state.shape[0]
    halo = bounds_ref.shape[0]
    sent = low(dot(state, send_ref[0]))
    recv = dot(state, recv_ref[0])

    def keep(j, slope):
        slope_ref[j] = low(slope)

    total_ref[...] = local_edges(senders_ref[...], senders_t_ref.shape[0], sent, recv, keep)
    back = low(receivers(senders_t_ref[...], halo))
    recv_n_ref[...] = dot(low(dot(back, state)), recv_ref[0])
    sent_b_ref[...] = low(dot(low(hot(bounds_ref[...] == iota(halo, nodes, 1))), sent))


def forward_halo(peers, *refs):
    arr_refs, refs = refs[:peers][::-1], refs[peers:]
    (recv_n_ref, total_ref, state_ref, send_ref, update_ref, senders_ref, senders_t_ref,
     bounds_ref, summed_ref, out_ref, pre_ref, rows_ref, back_ref, merged_ref, cot_ref,
     *pay_refs) = refs
    nodes = state_ref.shape[0]
    degree = senders_t_ref.shape[0]
    halo = peers * BORDER
    rows, back, merged, cot = split_parts(
        arr_refs, (0, BORDER, 2 * BORDER, 3 * BORDER), (BORDER,) * 4
    )
    rows_ref[...], back_ref[...] = low(rows), low(back)
    merged_ref[...], cot_ref[...] = low(merged), low(cot)
    pre = low(dot(low(rows), send_ref[0])).astype(F32) + recv_n_ref[...]
    pre_ref[...] = pre
    place = low(receivers_t(senders_ref[...], degree, halo))
    extra = silu(pre) - silu(recv_n_ref[...])
    summed = low(total_ref[...] + dot(place, low(extra)))
    summed_ref[...] = summed
    state = low(state_ref[...].astype(F32) + dot(summed, update_ref[0]))
    out_ref[...] = state
    border = low(hot(bounds_ref[...] == iota(halo, nodes, 1)))
    back = low(receivers(senders_t_ref[...], halo))
    store_parts(pay_refs, [dot(border, state), dot(back, state)])


def turn_local(
    state_ref, send_ref, recv_ref, update_ref, cot_ref, cot_r_ref, pre_ref, recv_n0_ref, back0_ref,
    sent_b0_ref, senders_ref, senders_t_ref, bounds_ref,
    total_ref, grecv_ref, gsent_ref, recv_n_ref, sent_b_ref, gsum_n_ref, gsum_r_ref,
    slope_k_ref, slope_d_ref, slope_r_ref, gpre_ref,
):
    halo = bounds_ref.shape[0]
    slope = silu_slope(pre_ref[...])
    slope_k_ref[...] = low(slope)
    slope_d_ref[...] = low(slope - silu_slope(recv_n0_ref[...]))
    pre = sent_b0_ref[...].astype(F32) + dot(back0_ref[...], recv_ref[0])
    slope_r_ref[...] = low(silu_slope(pre))
    state = state_ref[...]
    nodes = state.shape[0]
    sent = low(dot(state, send_ref[1]))
    recv = dot(state, recv_ref[1])
    gsum = low(dot(cot_ref[...], update_ref[1], NT))
    grad = gsum.astype(F32)
    grecv = []

    def back_edge(j, slope):
        gpre = grad * slope
        grecv.append(gpre if j == 0 else grecv[-1] + gpre)
        gpre_ref[j * nodes : (j + 1) * nodes, :] = low(gpre)

    degree = senders_t_ref.shape[0]
    total_ref[...] = local_edges(senders_ref[...], degree, sent, recv, back_edge)
    grecv_ref[...] = grecv[-1]
    gsent_ref[...] = dot(edge_targets(senders_t_ref[...]), gpre_ref[...])
    back = low(receivers(senders_t_ref[...], halo))
    recv_n_ref[...] = dot(low(dot(back, state)), recv_ref[1])
    sent_b_ref[...] = low(dot(low(hot(bounds_ref[...] == iota(halo, nodes, 1))), sent))
    gsum_n_ref[...] = low(dot(back, gsum))
    gsum_r_ref[...] = low(dot(cot_r_ref[...], update_ref[1], NT))


def turn_halo(peers, *refs):
    arr_refs, refs = refs[:peers][::-1], refs[peers:]
    (recv_n_ref, sent_b_ref, gsum_n_ref, gsum_r_ref, total_ref, grecv_ref, gsent_ref, cot_ref,
     send_ref, recv_ref, senders_ref, senders_t_ref, bounds_ref, summed_ref, grecv_out_ref,
     gsent_out_ref, gin_ref, *pay_refs) = refs
    nodes = cot_ref.shape[0]
    degree = senders_t_ref.shape[0]
    halo = peers * BORDER
    rows, back = split_parts(arr_refs, (0, BORDER), (BORDER,) * 2)
    pre = low(dot(low(rows), send_ref[1])).astype(F32) + recv_n_ref[...]
    act, slope = silu_both(pre)
    place = low(receivers_t(senders_ref[...], degree, halo))
    base, base_slope = silu_both(recv_n_ref[...])
    gpre = low(gsum_n_ref[...].astype(F32) * (slope - base_slope))
    grecv = low(grecv_ref[...] + dot(place, gpre))
    pre = sent_b_ref[...].astype(F32) + dot(low(back), recv_ref[1])
    gpre = low(gsum_r_ref[...].astype(F32) * silu_slope(pre))
    border = low(hot(bounds_ref[...] == iota(nodes, halo, 0)))
    gsent = low(gsent_ref[...] + dot(border, gpre))
    gin = cot_ref[...].astype(F32) + dot(grecv, recv_ref[1], NT) + dot(gsent, send_ref[1], NT)
    gin = low(gin)
    gin_ref[...] = gin
    store_parts(pay_refs, [dot(low(receivers(senders_t_ref[...], halo)), gin)])
    summed_ref[...] = low(total_ref[...] + dot(place, low(act - base)))
    grecv_out_ref[...] = grecv
    gsent_out_ref[...] = gsent


def last_weights(
    dims, order, place_ref, state_ref, summed_ref, cot_ref, grecv_ref, gsent_ref, update_ref,
    keep_ref, give_ref, mesh_ref,
):
    state, summed = state_ref[...], summed_ref[...]

    def store(at, value):
        store_blocks(keep_ref, give_ref, at, 3, value, dims, place_ref, order)

    store(0, dot(state, gsent_ref[...], TN))
    store(1, dot(state, grecv_ref[...], TN))
    store(2, dot(summed, cot_ref[...], TN))
    mesh_ref[...] = low(state.astype(F32) + dot(summed, update_ref[1]))


def back_local(
    dims, place_ref, gin_ref, slope_ref, slope_k_ref, slope_d_ref, send_ref, recv_ref, update_ref,
    senders_ref, senders_t_ref, state_ref, rows_ref, summed_ref, merged_ref, merged_r_ref,
    after_ref, part_ref, keep_ref, give_ref, keep2_ref, give2_ref, gpre_ref,
):
    nodes = gin_ref.shape[0]
    halo = slope_k_ref.shape[0]
    degree = senders_t_ref.shape[0]
    gin = gin_ref[...]
    gsum = low(dot(gin, update_ref[0], NT))
    place = low(receivers_t(senders_ref[...], degree, halo))
    back = low(receivers(senders_t_ref[...], halo))
    gsum_n = low(dot(back, gsum))
    gpre_k = gsum_n * slope_k_ref[...]
    grecv = dot(place, gsum_n * slope_d_ref[...])
    for j in range(degree):
        gpre = gsum * slope_ref[j]
        grecv = grecv + gpre.astype(F32)
        gpre_ref[j * nodes : (j + 1) * nodes, :] = gpre
    gsent = dot(edge_targets(senders_t_ref[...]), gpre_ref[...])
    grecv, gsent = low(grecv), low(gsent)
    part = gin.astype(F32) + dot(grecv, recv_ref[0], NT) + dot(gsent, send_ref[0], NT)
    part_ref[...] = part
    state = state_ref[...]

    def store(at, value):
        store_blocks(keep_ref, give_ref, at, 2, value, dims, place_ref)

    def store2(at, value):
        store_blocks(keep2_ref, give2_ref, at, 2, value, dims, place_ref)

    store(0, dot(state, gsent, TN) + dot(rows_ref[...], gpre_k, TN))
    store(1, dot(state, grecv, TN))
    store2(0, dot(summed_ref[...], gin, TN))
    far = low(dot(gpre_k, send_ref[0], NT))
    store2(1, dot(merged_ref[...], low(part), TN) + dot(merged_r_ref[...], far, TN))


def embed_back(peers, dims, carry, *refs):
    arr_refs, refs = refs[:peers][::-1], refs[peers:]
    (place_ref, slope_r_ref, part_ref, update_ref, send_ref, merge_ref, bounds_ref, target_ref,
     sends_ref, incoming_ref, slope_g_ref, slope_a_ref, grid_ref, lat_ref, embed_ref,
     gpre_ref, keep_ref, give_ref, *pay_refs) = refs
    nodes = part_ref.shape[0]
    halo = peers * BORDER
    chosen = grid_ref.shape[0]
    taken = sends_ref.shape[0]
    (arrived,) = split_parts(arr_refs, (0,), (BORDER,))
    gsum = low(dot(low(arrived), update_ref[0], NT)).astype(F32)
    gpre = low(gsum * slope_r_ref[...].astype(F32))
    border = low(hot(bounds_ref[...] == iota(nodes, halo, 0)))
    gsent = low(dot(border, gpre))
    gin = low(part_ref[...] + dot(gsent, send_ref[0], NT))
    gmerged = low(dot(gin, merge_ref[...], NT))
    place = low(hot(incoming_ref[...] == iota(nodes, taken, 0)))
    gpre_a = low(dot(place, gmerged, TN) * slope_a_ref[...].astype(F32))
    sent = jnp.max(hot(sends_ref[...] == iota(taken, chosen, 1)), axis=0, keepdims=True)
    label = jnp.where(sent > 0.0, nodes, target_ref[...])
    pick = low(hot(label == iota(nodes, chosen, 0)))
    gpre_g = low(dot(pick, gmerged, TN) * slope_g_ref[...].astype(F32))
    gpre_ref[...] = gpre_g
    grad = dot(grid_ref[...], gpre_g, TN) + dot(lat_ref[...], gpre_a, TN)
    store_blocks(keep_ref, give_ref, 0, 1, grad, dims, place_ref)
    rows = dot(gpre_a, embed_ref[...], NT)
    store_parts(pay_refs, [rows])
    if carry:
        size = taken // peers
        start = keep_ref.shape[0]
        give_ref[start : start + 2 * size, :] = low(
            jnp.concatenate([rows[:size], rows[2 * size : 3 * size]], axis=0)
        )


def grid_place(peers, *refs):
    arr_refs, refs = refs[:peers][::-1], refs[peers:]
    gpre_ref, weight_ref, sends_ref, out_ref = refs
    chosen = gpre_ref.shape[0]
    taken = sends_ref.shape[1]
    local = dot(gpre_ref[...], weight_ref[...], NT)
    place = low(hot(sends_ref[...] == iota(chosen, taken, 0)))
    size = taken // peers
    rows = [ref[...].astype(F32) for ref in arr_refs]
    rows = low(jnp.concatenate([row[row.shape[0] - size :] for row in rows], axis=0))
    out_ref[...] = low(local + dot(place, rows))


def finish(
    keep1_ref, arr1_ref, keep0_ref, arr0_ref, keep2_ref, arr2_ref, keep_e_ref, arr_e_ref,
    embed_ref, merge_ref, send_ref, recv_ref, update_ref,
):
    last = keep1_ref[...].astype(F32) + arr1_ref[...].astype(F32)
    first = keep0_ref[...].astype(F32) + arr0_ref[...].astype(F32)
    second = keep2_ref[...].astype(F32) + arr2_ref[...].astype(F32)
    depth = embed_ref.shape[0]
    embed_ref[...] = keep_e_ref[...].astype(F32) + arr_e_ref[:depth, :].astype(F32)
    for at, ref in enumerate((send_ref, recv_ref, update_ref)):
        ref[1] = last[at * depth : (at + 1) * depth]
    send_ref[0], recv_ref[0], update_ref[0] = first[:depth], first[depth:], second[:depth]
    merge_ref[...] = second[depth:]


def body(
    dims,
    grid_latent, mesh_latent, cotangent, embed_weight, merge_weight, send_weight, recv_weight,
    update_weight, target_row, send_rows, incoming_rows, border_mesh_rows, mesh_senders,
):
    chosen, width = grid_latent.shape
    nodes, degree = mesh_senders.shape
    slots, capacity = send_rows.shape[1:]
    column = dims[1] * dims[2]
    peers = slots - 1
    halo = peers * BORDER
    taken = peers * capacity
    total = dims[0] * dims[1] * dims[2]
    bits = (total - 1).bit_length()
    carry = dims == (4, 2, 2) and fine(width, dims)
    order1 = (0, 2, 3, 1) if carry else None
    spot = lax.axis_index(GROUP)
    place = [lax.axis_index(COLUMN), lax.axis_index("lon") % 2]
    place += [(spot >> bit) % 2 for bit in range(bits)]
    place = jnp.broadcast_to(jnp.stack(place).astype(I32)[None], (slots, 2 + bits))
    ints = jnp.concatenate([send_rows[0], incoming_rows[0], border_mesh_rows[0], place], axis=1)
    unit = 2 * nodes * width * width

    loads = (grid_latent, embed_weight, target_row.reshape(1, chosen), mesh_senders.T,
             mesh_latent, merge_weight, cotangent)
    grid, embed, targets, senders_raw, mesh, merge, cot, sends, *pay1 = call(
        lambda *refs: first_payload(column, capacity, len(loads), *refs), "first_payload",
        [shape(taken, 1, dtype=I32)] + [shape(capacity, width)] * peers,
        (ints,), flops=unit // 2, loads=loads,
    )
    arr1 = exchange(pay1, dims)
    (local, slope_g, sends_row, incoming, bounds, bounds_row, senders_t, senders, place) = call(
        lambda *refs: embed_local(column, capacity, *refs), "embed_local",
        [shape(nodes, width, dtype=F32), shape(chosen, width), shape(1, taken, dtype=I32),
         shape(1, taken, dtype=I32), shape(halo, 1, dtype=I32), shape(1, halo, dtype=I32),
         shape(degree, nodes, dtype=I32), shape(nodes, 8, dtype=I32),
         shape(slots, 2 + bits, dtype=I32)],
        (ints, senders_raw, grid, embed, targets, sends), flops=3 * unit,
    )
    merged, state0, slope_a, lat_a, *pay2 = call(
        lambda *refs: merge_nodes(peers, *refs), "merge_nodes",
        [shape(nodes, width), shape(nodes, width), shape(taken, width), shape(taken, width)]
        + [shape(4 * BORDER, width)] * peers,
        (*arr1, incoming, embed, local, mesh, merge, bounds, senders_t, cot),
        flops=2 * unit,
    )
    arr2 = exchange(pay2, dims)
    total0, slope0, recv_n0, sent_b0 = call(
        forward_local, "forward_local",
        [shape(nodes, width, dtype=F32), shape(degree, nodes, width),
         shape(halo, width, dtype=F32), shape(halo, width)],
        (state0, send_weight, recv_weight, senders, senders_t, bounds), flops=6 * unit,
    )
    summed0, state1, pre0, rows0, back0, merged_r, cot_r, *pay3 = call(
        lambda *refs: forward_halo(peers, *refs), "forward_halo",
        [shape(nodes, width), shape(nodes, width), shape(halo, width, dtype=F32)]
        + [shape(halo, width)] * 4 + [shape(2 * BORDER, width)] * peers,
        (*arr2, recv_n0, total0, state0, send_weight, update_weight, senders, senders_t, bounds),
        flops=2 * unit,
    )
    arr3 = exchange(pay3, dims)
    (total1, grecv_l, gsent_l, recv_n1, sent_b1, gsum_n1, gsum_r1, slope_k0, slope_d0,
     slope_r0) = call(
        turn_local, "turn_local",
        [shape(nodes, width, dtype=F32)] * 3 + [shape(halo, width, dtype=F32)]
        + [shape(halo, width)] * 6,
        (state1, send_weight, recv_weight, update_weight, cot, cot_r, pre0, recv_n0, back0,
         sent_b0, senders, senders_t, bounds),
        flops=10 * unit, scratch=[pltpu.VMEM((degree * nodes, width), BF)],
    )
    summed1, grecv1, gsent1, gin1, *pay4 = call(
        lambda *refs: turn_halo(peers, *refs), "turn_halo",
        [shape(nodes, width)] * 4 + [shape(BORDER, width)] * peers,
        (*arr3, recv_n1, sent_b1, gsum_n1, gsum_r1, total1, grecv_l, gsent_l, cot,
         send_weight, recv_weight, senders, senders_t, bounds_row),
        flops=3 * unit,
    )
    arr4 = exchange(pay4, dims)
    keep1, give1, mesh_out = call(
        lambda *refs: last_weights(dims, order1, *refs), "last_weights",
        blocks_shapes(3, width, width, dims) + [shape(nodes, width)],
        (place, state1, summed1, cot, grecv1, gsent1, update_weight), flops=4 * unit,
    )
    split = fine(width, dims)
    if split:
        give1, last = lax.optimization_barrier((give1, arr4[-1]))
        arr4 = (*arr4[:-1], last)
        keep1, give1 = halve_step(order1[1] if carry else 1, keep1, swap(give1, 0, dims), place)
    part0, keep0, give0, keep2, give2 = call(
        lambda *refs: back_local(dims, *refs), "back_local",
        [shape(nodes, width, dtype=F32)] + blocks_shapes(2, width, width, dims) * 2,
        (place, gin1, slope0, slope_k0, slope_d0, send_weight, recv_weight, update_weight, senders,
         senders_t, state0, rows0, summed0, merged, merged_r, keep1),
        flops=10 * unit, scratch=[pltpu.VMEM((degree * nodes, width), BF)],
    )
    if split:
        give0, give2, *arr4 = lax.optimization_barrier((give0, give2, *arr4))
        keep0, give0 = halve_step(1, keep0, swap(give0, 0, dims), place)
        keep0, *arr4 = lax.optimization_barrier((keep0, *arr4))
    shapes = blocks_shapes(1, width, width, dims)
    if carry:
        shapes[1] = shape(shapes[1].shape[0] + 2 * capacity, width)
    gpre_g, keep_e, give_e, *pay5 = call(
        lambda *refs: embed_back(peers, dims, carry, *refs), "embed_back",
        [shape(chosen, width)] + shapes + [shape(capacity, width)] * peers,
        (*arr4, place, slope_r0, part0, update_weight, send_weight, merge, bounds_row,
         targets, sends, incoming, slope_g, slope_a, grid, lat_a, embed),
        flops=6 * unit,
    )
    depth = width // total
    if not split:
        arr5 = exchange(pay5, dims)
        last, first, second, embed_sum = (
            scatter_plain(blocks, dims) for blocks in (keep1, keep0, keep2, keep_e)
        )
        grads = [jnp.stack([a, last[i]]) for i, a in enumerate((first[0], first[1], second[0]))]
        grads = [embed_sum[0], second[1], *grads]
    elif not carry:
        arr5 = exchange(pay5, dims)
        sums = [
            rest_of_halving(1, keep1, give1, place, dims),
            rest_of_halving(1, keep0, give0, place, dims),
            rest_of_halving(0, keep2, give2, place, dims),
            rest_of_halving(0, keep_e, give_e, place, dims),
        ]
    else:
        arr1 = swap(give1, 2, dims)
        arr0 = swap(give0, 1, dims)
        arr2 = swap(give2, 0, dims)
        arr_e, arr1 = lax.optimization_barrier((swap(give_e, 0, dims), arr1))
        keep1, give1 = halve_step(3, keep1, arr1, place)
        arr1 = swap(give1, 3, dims)
        keep_e, keep1 = lax.optimization_barrier((keep_e, keep1))
        keep_e, give_e, from_sub, _ = carry_step(1, keep_e, arr_e, pay5[1:2], place, capacity)
        arr_e = swap(give_e, 1, dims)
        keep2, keep_e = lax.optimization_barrier((keep2, keep_e))
        keep2, give2 = halve_step(1, keep2, arr2, place)
        arr2 = swap(give2, 1, dims)
        keep0, keep2 = lax.optimization_barrier((keep0, keep2))
        keep0, give0 = halve_step(2, keep0, arr0, place)
        arr0 = swap(give0, 2, dims)
        keep_e, keep0 = lax.optimization_barrier((keep_e, keep0))
        keep_e, give_e, from_lat, from_diag = carry_step(
            2, keep_e, arr_e, pay5[3:], place, capacity
        )
        arr_e = swap(give_e, 2, dims)
        keep0, keep_e = lax.optimization_barrier((keep0, keep_e))
        keep0, give0 = halve_step(3, keep0, arr0, place)
        arr0 = swap(give0, 3, dims)
        keep_e, keep0 = lax.optimization_barrier((keep_e, keep0))
        keep_e, give_e, from_near, _ = carry_step(3, keep_e, arr_e, (), place, capacity)
        arr_e = swap(give_e, 3, dims)
        keep1, keep_e, arr0 = lax.optimization_barrier((keep1, keep_e, arr0))
        keep1, give1 = halve_step(1, keep1, arr1, place)
        arr1 = swap(give1, 1, dims)
        keep2, keep1 = lax.optimization_barrier((keep2, keep1))
        keep2, give2 = halve_step(2, keep2, arr2, place)
        arr2 = swap(give2, 2, dims)
        gpre_g, keep2 = lax.optimization_barrier((gpre_g, keep2))
        arr5 = (arr_e, from_near, from_diag, from_lat, from_sub)
    (grid_grad,) = call(
        lambda *refs: grid_place(peers, *refs), "grid_place", [shape(chosen, width)],
        (*arr5, gpre_g, embed, sends_row), flops=3 * unit,
    )
    if carry:
        keep2, grid_grad, arr1 = lax.optimization_barrier((keep2, grid_grad, arr1))
        keep2, give2 = halve_step(3, keep2, arr2, place)
        sums = ((keep1, arr1), (keep0, arr0), (keep2, swap(give2, 3, dims)), (keep_e, arr_e))
    if split:
        grads = call(
            finish, "finish",
            [shape(depth, width, dtype=F32)] * 2 + [shape(2, depth, width, dtype=F32)] * 3,
            [part for pair in sums for part in pair], flops=8 * depth * width,
        )
    return (mesh_out, grid_grad, *grads)


def solution(mesh):
    split = ("groups", "lon", "lat", "sub")
    dims = tuple(mesh.shape[axis] for axis in GROUP)
    rows = P(split, None)
    whole = P("groups", GROUP, None)
    in_specs = (
        rows, rows, rows, P(), P(), P(), P(), P(), P(split), P(split, None, None),
        P(split, None, None), P(split, None, None), rows,
    )
    out_specs = (rows, rows, rows, rows, whole, whole, whole)
    return jax.shard_map(
        lambda *args: body(dims, *args),
        mesh=mesh, in_specs=in_specs, out_specs=out_specs, check_vma=False,
    )
```

```python
import jax
import jax.numpy as jnp
from jax import lax
from jax.experimental import pallas as pl
from jax.experimental.pallas import tpu as pltpu
from jax.sharding import PartitionSpec as P

BF = jnp.bfloat16
F32 = jnp.float32
I32 = jnp.int32
NN = (((1,), (0,)), ((), ()))
NT = (((1,), (1,)), ((), ()))
TN = (((0,), (0,)), ((), ()))
BORDER = 8
GROUP = ("lon", "lat", "sub")
COLUMN = ("lat", "sub")


def dot(a, b, dims=NN):
    return lax.dot_general(a, b, dims, preferred_element_type=F32)


def low(value):
    return value.astype(BF)


def sigmoid(value):
    return 0.5 * jnp.tanh(0.5 * value) + 0.5


def silu(value):
    return value * sigmoid(value)


def silu_both(value):
    sig = sigmoid(value)
    act = value * sig
    return act, sig + act * (1.0 - sig)


def silu_slope(value):
    return silu_both(value)[1]


def iota(rows, columns, dim):
    return lax.broadcasted_iota(I32, (rows, columns), dim)


def hot(mask):
    return jnp.where(mask, 1.0, 0.0)


def slot_of(at, column, me, odd):
    far = jnp.where(at == column - 1, column + 1 - odd, column + odd)
    return jnp.where(at < column - 1, jnp.bitwise_xor(at + 1, me), far)


def as_column(values, wide, column, me, odd):
    slots = values.shape[0]
    count = (slots - 1) * wide
    row = iota(count, slots, 0)
    pick = low(hot(slot_of(row // wide, column, me, odd) == iota(count, slots, 1)))
    found = 16.0 * dot(pick, low((values // 16).astype(F32)))
    found = found + dot(pick, low((values % 16).astype(F32)))
    keep = iota(count, wide, 0) % wide == iota(count, wide, 1)
    return jnp.sum(jnp.where(keep, found, 0.0), axis=1, keepdims=True).astype(I32)


def as_row(values, wide, column, me, odd):
    slots = values.shape[0]
    count = (slots - 1) * wide
    pick = low(hot(iota(wide, count, 1) % wide == iota(wide, count, 0)))
    found = 16.0 * dot(low((values // 16).astype(F32)), pick)
    found = found + dot(low((values % 16).astype(F32)), pick)
    at = iota(slots, count, 1) // wide
    keep = slot_of(at, column, me, odd) == iota(slots, count, 0)
    return jnp.sum(jnp.where(keep, found, 0.0), axis=0, keepdims=True).astype(I32)


def split_parts(refs, starts, sizes):
    values = [ref[...].astype(F32) for ref in refs]
    return [
        jnp.concatenate([value[start : start + size] for value in values], axis=0)
        for start, size in zip(starts, sizes)
    ]


def store_parts(refs, parts):
    peers = len(refs)
    for at, ref in enumerate(refs):
        rows = []
        for part in parts:
            size = part.shape[0] // peers
            rows.append(part[at * size : (at + 1) * size])
        ref[...] = low(rows[0] if len(rows) == 1 else jnp.concatenate(rows, axis=0))


def receivers(senders_t, halo):
    degree, nodes = senders_t.shape
    found = jnp.zeros((halo, nodes), F32)
    ids = iota(halo, nodes, 0) + nodes
    for j in range(degree):
        found = found + hot(senders_t[j : j + 1, :] == ids)
    return found


def receivers_t(senders, degree, halo):
    nodes = senders.shape[0]
    found = jnp.zeros((nodes, halo), F32)
    ids = iota(nodes, halo, 1) + nodes
    for j in range(degree):
        found = found + hot(senders[:, j : j + 1] == ids)
    return found


def fine(rows, dims):
    return (rows // (dims[0] * dims[1] * dims[2])) % 16 == 0


def reverse_bits(block, bits):
    spot = 0
    for bit in range(bits):
        spot = 2 * spot + (block >> bit) % 2
    return spot


def store_blocks(keep_ref, give_ref, at, count, value, dims, bits_ref):
    value = low(value)
    rows = value.shape[0]
    total = dims[0] * dims[1] * dims[2]
    depth = rows // total
    if not fine(rows, dims):
        keep_ref[at] = value
        return
    bits = (total - 1).bit_length()
    upper = bits_ref[0:1, 2:3] == 1
    for block in range(0, total, 2):
        start = reverse_bits(block, bits) * count * depth + at * depth
        first = value[block * depth : (block + 1) * depth].astype(F32)
        second = value[(block + 1) * depth : (block + 2) * depth].astype(F32)
        keep_ref[start : start + depth, :] = low(jnp.where(upper, second, first))
        give_ref[start : start + depth, :] = low(jnp.where(upper, first, second))


def blocks_shapes(count, rows, width, dims):
    if fine(rows, dims):
        return [jax.ShapeDtypeStruct((count * rows // 2, width), BF)] * 2
    return [jax.ShapeDtypeStruct((count, rows, width), BF), jax.ShapeDtypeStruct((16, width), BF)]


def halve(bit, bits_ref, keep_ref, arr_ref, keep_out, give_out):
    half = keep_ref.shape[0] // 2
    upper = bits_ref[0:1, 2 + bit : 3 + bit] == 1
    first = keep_ref[:half, :].astype(F32) + arr_ref[:half, :].astype(F32)
    second = keep_ref[half:, :].astype(F32) + arr_ref[half:, :].astype(F32)
    keep_out[...] = low(jnp.where(upper, second, first))
    give_out[...] = low(jnp.where(upper, first, second))


def swap(block, bit, dims):
    total = dims[0] * dims[1] * dims[2]
    return lax.ppermute(block, GROUP, [(i, i ^ (1 << bit)) for i in range(total)])


def halve_step(bit, keep, arrived, place):
    rows, width = keep.shape[0] // 2, keep.shape[1]
    return call(
        lambda *refs: halve(bit, *refs), "halve", [shape(rows, width)] * 2,
        (place, keep, arrived), flops=4 * rows * width, size=0,
    )


def rest_of_halving(first, keep, give, place, dims):
    bits = (dims[0] * dims[1] * dims[2] - 1).bit_length()
    arrived = swap(give, first, dims)
    for bit in range(first + 1, bits):
        keep, give = halve_step(bit, keep, arrived, place)
        arrived = swap(give, bit, dims)
    return keep, arrived


def halve_carry(bit, bits_ref, keep_ref, arr_ref, *refs):
    *own_refs, keep_out, give_out, here_ref, on_ref = refs
    rows = keep_ref.shape[0]
    half = rows // 2
    size = here_ref.shape[0]
    upper = bits_ref[0:1, 2 + bit : 3 + bit] == 1
    value = arr_ref[...].astype(F32)
    first = keep_ref[:half, :].astype(F32) + value[:half]
    second = keep_ref[half:, :].astype(F32) + value[half:rows]
    keep_out[...] = low(jnp.where(upper, second, first))
    here_ref[...] = low(value[rows : rows + size])
    passed = value[rows + size : rows + 2 * size]
    on_ref[...] = low(passed)
    extra = [ref[...].astype(F32) for ref in own_refs]
    if len(extra) < 2:
        extra.append(passed)
    give_out[...] = low(jnp.concatenate([jnp.where(upper, first, second), *extra], axis=0))


def carry_step(bit, keep, arrived, own, place, capacity):
    rows, width = keep.shape[0] // 2, keep.shape[1]
    return call(
        lambda *refs: halve_carry(bit, *refs), "halve_carry",
        [shape(rows, width), shape(rows + min(len(own) + 1, 2) * capacity, width),
         shape(capacity, width), shape(capacity, width)],
        (place, keep, arrived, *own), flops=4 * rows * width, size=0,
    )


def scatter_plain(blocks, dims):
    lon, lat, sub = dims
    count, rows, width = blocks.shape
    depth = rows // (lon * lat * sub)
    blocks = blocks.reshape(count, lon, lat, sub, depth, width)
    blocks = blocks.transpose(3, 2, 1, 0, 4, 5)
    for axis in ("sub", "lat", "lon"):
        blocks = lax.psum_scatter(blocks, axis, scatter_dimension=0, tiled=False)
    return blocks.astype(F32)


def call(kernel, name, outs, args, flops, loads=(), scratch=(), size=None):
    if size is None:
        size = sum(a.size * a.dtype.itemsize for a in (*args, *outs, *loads))
    args = (*(pltpu.with_memory_space_constraint(a, pltpu.HBM) for a in loads), *args)
    scratch = list(scratch)
    if loads:
        scratch.append(pltpu.SemaphoreType.DMA((len(loads),)))
    in_specs = [pl.BlockSpec(memory_space=pltpu.HBM)] * len(loads)
    in_specs += [pl.BlockSpec(memory_space=pltpu.VMEM)] * (len(args) - len(loads))
    return pl.pallas_call(
        kernel,
        out_shape=[shape(*a.shape, dtype=a.dtype) for a in loads] + list(outs),
        in_specs=in_specs,
        out_specs=[pl.BlockSpec(memory_space=pltpu.VMEM)] * (len(outs) + len(loads)),
        scratch_shapes=scratch,
        compiler_params=pltpu.CompilerParams(vmem_limit_bytes=16 * 1024 * 1024),
        cost_estimate=pl.CostEstimate(flops=flops, bytes_accessed=size, transcendentals=0),
        name=name,
    )(*args)


def exchange(parts, dims):
    column = dims[1] * dims[2]
    count = dims[0]
    other = [(i, (i - 1 + 2 * (i % 2)) % count) for i in range(count)]
    far = lax.ppermute(parts[column], "lon", other)
    near = lax.ppermute(parts[column - 1], "lon", [(i, i ^ 1) for i in range(count)])
    arrived = [
        lax.ppermute(parts[r - 1], COLUMN, [(i, i ^ r) for i in range(column)])
        for r in range(column - 1, 0, -1)
    ]
    return (far, near, *arrived)


def shape(*dims, dtype=BF):
    return jax.ShapeDtypeStruct(dims, dtype)


def start_loads(sources, targets, sems):
    copies = [
        pltpu.make_async_copy(source, target, sems.at[at])
        for at, (source, target) in enumerate(zip(sources, targets))
    ]
    for copy in copies:
        copy.start()
    return copies


def first_payload(column, capacity, count, *refs):
    sources, ints_ref, targets = refs[:count], refs[count], refs[count + 1 : 2 * count + 1]
    sends_ref, *pay_refs, sems = refs[2 * count + 1 :]
    grid_ref = targets[0]
    grid_load, *loads = start_loads(sources, targets, sems)
    chosen = grid_ref.shape[0]
    ints = ints_ref[...]
    base = 2 * capacity + BORDER
    me, odd = ints[0:1, base : base + 1], ints[0:1, base + 1 : base + 2]
    sends = as_column(ints[:, :capacity], capacity, column, me, odd)
    sends_ref[...] = sends
    pick = low(hot(sends == iota(sends.shape[0], chosen, 1)))
    grid_load.wait()
    store_parts(pay_refs, [dot(pick, grid_ref[...])])
    for load in loads:
        load.wait()


def embed_local(
    column, capacity, ints_ref, senders_ref, grid_ref, weight_ref, target_ref, sends_ref,
    sum_ref, slope_ref, sends_row_ref, incoming_ref, bounds_ref, bounds_row_ref, senders_t_ref,
    senders_out_ref, place_ref,
):
    chosen = grid_ref.shape[0]
    nodes = sum_ref.shape[0]
    taken = sends_ref.shape[0]
    act, slope = silu_both(dot(grid_ref[...], weight_ref[...]))
    slope_ref[...] = low(slope)
    sent = jnp.max(hot(sends_ref[...] == iota(taken, chosen, 1)), axis=0, keepdims=True)
    label = jnp.where(sent > 0.0, nodes, target_ref[...])
    sum_ref[...] = dot(low(hot(label == iota(nodes, chosen, 0))), low(act))
    ints = ints_ref[...]
    base = 2 * capacity + BORDER
    place_ref[...] = ints[:, base:]
    me, odd = ints[0:1, base : base + 1], ints[0:1, base + 1 : base + 2]
    sends, incoming = ints[:, :capacity], ints[:, capacity : 2 * capacity]
    bounds = ints[:, 2 * capacity : base]
    sends_row_ref[...] = as_row(sends, capacity, column, me, odd)
    incoming_ref[...] = as_row(incoming, capacity, column, me, odd)
    bounds_ref[...] = as_column(bounds, BORDER, column, me, odd)
    bounds_row_ref[...] = as_row(bounds, BORDER, column, me, odd)
    senders = senders_ref[...]
    degree = senders.shape[0]
    offset = senders - nodes
    slot = offset // BORDER
    far = jnp.where(slot == column, column - odd, column - 1 + odd)
    at = jnp.where(slot < column, jnp.bitwise_xor(slot, me) - 1, far)
    senders = jnp.where(offset < 0, senders, nodes + at * BORDER + offset % BORDER)
    senders_t_ref[...] = senders
    filler = jnp.zeros((8 - degree, nodes), I32)
    senders_out_ref[...] = jnp.concatenate([senders, filler], axis=0).T


def merge_nodes(peers, *refs):
    arr_refs, refs = refs[:peers][::-1], refs[peers:]
    (incoming_ref, embed_ref, local_ref, mesh_ref, weight_ref, bounds_ref, senders_t_ref, cot_ref,
     merged_ref, state_ref, slope_ref, lat_ref, *pay_refs) = refs
    nodes = mesh_ref.shape[0]
    taken = incoming_ref.shape[1]
    halo = peers * BORDER
    lat = jnp.concatenate([ref[...] for ref in arr_refs], axis=0)
    lat_ref[...] = lat
    act, slope = silu_both(dot(lat, embed_ref[...]))
    slope_ref[...] = low(slope)
    place = low(hot(incoming_ref[...] == iota(nodes, taken, 0)))
    merged = low(local_ref[...] + dot(place, low(act)))
    merged_ref[...] = merged
    state = low(mesh_ref[...].astype(F32) + dot(merged, weight_ref[...]))
    state_ref[...] = state
    border = low(hot(bounds_ref[...] == iota(halo, nodes, 1)))
    back = low(receivers(senders_t_ref[...], halo))
    store_parts(
        pay_refs,
        [dot(border, state), dot(back, state), dot(border, merged), dot(back, cot_ref[...])],
    )


def local_edges(senders, degree, sent, recv, each):
    nodes = senders.shape[0]
    total = None
    ids = iota(nodes, nodes, 1)
    for j in range(degree):
        act, slope = silu_both(dot(low(hot(senders[:, j : j + 1] == ids)), sent) + recv)
        total = act if total is None else total + act
        each(j, slope)
    return total


def edge_targets(senders_t):
    degree, nodes = senders_t.shape
    ids = iota(nodes, nodes, 0)
    return jnp.concatenate(
        [low(hot(senders_t[j : j + 1, :] == ids)) for j in range(degree)], axis=1
    )


def forward_local(
    state_ref, send_ref, recv_ref, senders_ref, senders_t_ref, bounds_ref,
    total_ref, slope_ref, recv_n_ref, sent_b_ref,
):
    state = state_ref[...]
    nodes = state.shape[0]
    halo = bounds_ref.shape[0]
    sent = low(dot(state, send_ref[0]))
    recv = dot(state, recv_ref[0])

    def keep(j, slope):
        slope_ref[j] = low(slope)

    total_ref[...] = local_edges(senders_ref[...], senders_t_ref.shape[0], sent, recv, keep)
    back = low(receivers(senders_t_ref[...], halo))
    recv_n_ref[...] = dot(low(dot(back, state)), recv_ref[0])
    sent_b_ref[...] = low(dot(low(hot(bounds_ref[...] == iota(halo, nodes, 1))), sent))


def forward_halo(peers, *refs):
    arr_refs, refs = refs[:peers][::-1], refs[peers:]
    (recv_n_ref, total_ref, state_ref, send_ref, update_ref, senders_ref, senders_t_ref,
     bounds_ref, summed_ref, out_ref, pre_ref, rows_ref, back_ref, merged_ref, cot_ref,
     *pay_refs) = refs
    nodes = state_ref.shape[0]
    degree = senders_t_ref.shape[0]
    halo = peers * BORDER
    rows, back, merged, cot = split_parts(
        arr_refs, (0, BORDER, 2 * BORDER, 3 * BORDER), (BORDER,) * 4
    )
    rows_ref[...], back_ref[...] = low(rows), low(back)
    merged_ref[...], cot_ref[...] = low(merged), low(cot)
    pre = low(dot(low(rows), send_ref[0])).astype(F32) + recv_n_ref[...]
    pre_ref[...] = pre
    place = low(receivers_t(senders_ref[...], degree, halo))
    extra = silu(pre) - silu(recv_n_ref[...])
    summed = low(total_ref[...] + dot(place, low(extra)))
    summed_ref[...] = summed
    state = low(state_ref[...].astype(F32) + dot(summed, update_ref[0]))
    out_ref[...] = state
    border = low(hot(bounds_ref[...] == iota(halo, nodes, 1)))
    back = low(receivers(senders_t_ref[...], halo))
    store_parts(pay_refs, [dot(border, state), dot(back, state)])


def turn_local(
    state_ref, send_ref, recv_ref, update_ref, cot_ref, cot_r_ref, pre_ref, recv_n0_ref, back0_ref,
    sent_b0_ref, senders_ref, senders_t_ref, bounds_ref,
    total_ref, grecv_ref, gsent_ref, recv_n_ref, sent_b_ref, gsum_n_ref, gsum_r_ref,
    slope_k_ref, slope_d_ref, slope_r_ref, gpre_ref,
):
    halo = bounds_ref.shape[0]
    slope = silu_slope(pre_ref[...])
    slope_k_ref[...] = low(slope)
    slope_d_ref[...] = low(slope - silu_slope(recv_n0_ref[...]))
    pre = sent_b0_ref[...].astype(F32) + dot(back0_ref[...], recv_ref[0])
    slope_r_ref[...] = low(silu_slope(pre))
    state = state_ref[...]
    nodes = state.shape[0]
    sent = low(dot(state, send_ref[1]))
    recv = dot(state, recv_ref[1])
    gsum = low(dot(cot_ref[...], update_ref[1], NT))
    grad = gsum.astype(F32)
    grecv = []

    def back_edge(j, slope):
        gpre = grad * slope
        grecv.append(gpre if j == 0 else grecv[-1] + gpre)
        gpre_ref[j * nodes : (j + 1) * nodes, :] = low(gpre)

    degree = senders_t_ref.shape[0]
    total_ref[...] = local_edges(senders_ref[...], degree, sent, recv, back_edge)
    grecv_ref[...] = grecv[-1]
    gsent_ref[...] = dot(edge_targets(senders_t_ref[...]), gpre_ref[...])
    back = low(receivers(senders_t_ref[...], halo))
    recv_n_ref[...] = dot(low(dot(back, state)), recv_ref[1])
    sent_b_ref[...] = low(dot(low(hot(bounds_ref[...] == iota(halo, nodes, 1))), sent))
    gsum_n_ref[...] = low(dot(back, gsum))
    gsum_r_ref[...] = low(dot(cot_r_ref[...], update_ref[1], NT))


def turn_halo(peers, *refs):
    arr_refs, refs = refs[:peers][::-1], refs[peers:]
    (recv_n_ref, sent_b_ref, gsum_n_ref, gsum_r_ref, total_ref, grecv_ref, gsent_ref, cot_ref,
     send_ref, recv_ref, senders_ref, senders_t_ref, bounds_ref, summed_ref, grecv_out_ref,
     gsent_out_ref, gin_ref, *pay_refs) = refs
    nodes = cot_ref.shape[0]
    degree = senders_t_ref.shape[0]
    halo = peers * BORDER
    rows, back = split_parts(arr_refs, (0, BORDER), (BORDER,) * 2)
    pre = low(dot(low(rows), send_ref[1])).astype(F32) + recv_n_ref[...]
    act, slope = silu_both(pre)
    place = low(receivers_t(senders_ref[...], degree, halo))
    base, base_slope = silu_both(recv_n_ref[...])
    gpre = low(gsum_n_ref[...].astype(F32) * (slope - base_slope))
    grecv = low(grecv_ref[...] + dot(place, gpre))
    pre = sent_b_ref[...].astype(F32) + dot(low(back), recv_ref[1])
    gpre = low(gsum_r_ref[...].astype(F32) * silu_slope(pre))
    border = low(hot(bounds_ref[...] == iota(nodes, halo, 0)))
    gsent = low(gsent_ref[...] + dot(border, gpre))
    gin = cot_ref[...].astype(F32) + dot(grecv, recv_ref[1], NT) + dot(gsent, send_ref[1], NT)
    gin = low(gin)
    gin_ref[...] = gin
    store_parts(pay_refs, [dot(low(receivers(senders_t_ref[...], halo)), gin)])
    summed_ref[...] = low(total_ref[...] + dot(place, low(act - base)))
    grecv_out_ref[...] = grecv
    gsent_out_ref[...] = gsent


def last_weights(
    dims, place_ref, state_ref, summed_ref, cot_ref, grecv_ref, gsent_ref, update_ref,
    keep_ref, give_ref, mesh_ref,
):
    state, summed = state_ref[...], summed_ref[...]

    def store(at, value):
        store_blocks(keep_ref, give_ref, at, 3, value, dims, place_ref)

    store(0, dot(state, gsent_ref[...], TN))
    store(1, dot(state, grecv_ref[...], TN))
    store(2, dot(summed, cot_ref[...], TN))
    mesh_ref[...] = low(state.astype(F32) + dot(summed, update_ref[1]))


def back_local(
    dims, place_ref, gin_ref, slope_ref, slope_k_ref, slope_d_ref, send_ref, recv_ref, update_ref,
    senders_ref, senders_t_ref, state_ref, rows_ref, summed_ref, merged_ref, merged_r_ref,
    after_ref, part_ref, keep_ref, give_ref, keep2_ref, give2_ref, gpre_ref,
):
    nodes = gin_ref.shape[0]
    halo = slope_k_ref.shape[0]
    degree = senders_t_ref.shape[0]
    gin = gin_ref[...]
    gsum = low(dot(gin, update_ref[0], NT))
    place = low(receivers_t(senders_ref[...], degree, halo))
    back = low(receivers(senders_t_ref[...], halo))
    gsum_n = low(dot(back, gsum))
    gpre_k = gsum_n * slope_k_ref[...]
    grecv = dot(place, gsum_n * slope_d_ref[...])
    for j in range(degree):
        gpre = gsum * slope_ref[j]
        grecv = grecv + gpre.astype(F32)
        gpre_ref[j * nodes : (j + 1) * nodes, :] = gpre
    gsent = dot(edge_targets(senders_t_ref[...]), gpre_ref[...])
    grecv, gsent = low(grecv), low(gsent)
    part = gin.astype(F32) + dot(grecv, recv_ref[0], NT) + dot(gsent, send_ref[0], NT)
    part_ref[...] = part
    state = state_ref[...]

    def store(at, value):
        store_blocks(keep_ref, give_ref, at, 2, value, dims, place_ref)

    def store2(at, value):
        store_blocks(keep2_ref, give2_ref, at, 2, value, dims, place_ref)

    store(0, dot(state, gsent, TN) + dot(rows_ref[...], gpre_k, TN))
    store(1, dot(state, grecv, TN))
    store2(0, dot(summed_ref[...], gin, TN))
    far = low(dot(gpre_k, send_ref[0], NT))
    store2(1, dot(merged_ref[...], low(part), TN) + dot(merged_r_ref[...], far, TN))


def embed_back(peers, dims, carry, *refs):
    arr_refs, refs = refs[:peers][::-1], refs[peers:]
    (place_ref, slope_r_ref, part_ref, update_ref, send_ref, merge_ref, bounds_ref, target_ref,
     sends_ref, incoming_ref, slope_g_ref, slope_a_ref, grid_ref, lat_ref, embed_ref,
     gpre_ref, keep_ref, give_ref, *pay_refs) = refs
    nodes = part_ref.shape[0]
    halo = peers * BORDER
    chosen = grid_ref.shape[0]
    taken = sends_ref.shape[0]
    (arrived,) = split_parts(arr_refs, (0,), (BORDER,))
    gsum = low(dot(low(arrived), update_ref[0], NT)).astype(F32)
    gpre = low(gsum * slope_r_ref[...].astype(F32))
    border = low(hot(bounds_ref[...] == iota(nodes, halo, 0)))
    gsent = low(dot(border, gpre))
    gin = low(part_ref[...] + dot(gsent, send_ref[0], NT))
    gmerged = low(dot(gin, merge_ref[...], NT))
    place = low(hot(incoming_ref[...] == iota(nodes, taken, 0)))
    gpre_a = low(dot(place, gmerged, TN) * slope_a_ref[...].astype(F32))
    sent = jnp.max(hot(sends_ref[...] == iota(taken, chosen, 1)), axis=0, keepdims=True)
    label = jnp.where(sent > 0.0, nodes, target_ref[...])
    pick = low(hot(label == iota(nodes, chosen, 0)))
    gpre_g = low(dot(pick, gmerged, TN) * slope_g_ref[...].astype(F32))
    gpre_ref[...] = gpre_g
    grad = dot(grid_ref[...], gpre_g, TN) + dot(lat_ref[...], gpre_a, TN)
    store_blocks(keep_ref, give_ref, 0, 1, grad, dims, place_ref)
    rows = dot(gpre_a, embed_ref[...], NT)
    store_parts(pay_refs, [rows])
    if carry:
        size = taken // peers
        start = keep_ref.shape[0]
        give_ref[start : start + 2 * size, :] = low(
            jnp.concatenate([rows[:size], rows[2 * size : 3 * size]], axis=0)
        )


def grid_place(peers, *refs):
    arr_refs, refs = refs[:peers][::-1], refs[peers:]
    gpre_ref, weight_ref, sends_ref, out_ref = refs
    chosen = gpre_ref.shape[0]
    taken = sends_ref.shape[1]
    local = dot(gpre_ref[...], weight_ref[...], NT)
    place = low(hot(sends_ref[...] == iota(chosen, taken, 0)))
    size = taken // peers
    rows = [ref[...].astype(F32) for ref in arr_refs]
    rows = low(jnp.concatenate([row[row.shape[0] - size :] for row in rows], axis=0))
    out_ref[...] = low(local + dot(place, rows))


def finish(
    keep1_ref, arr1_ref, keep0_ref, arr0_ref, keep2_ref, arr2_ref, keep_e_ref, arr_e_ref,
    embed_ref, merge_ref, send_ref, recv_ref, update_ref,
):
    last = keep1_ref[...].astype(F32) + arr1_ref[...].astype(F32)
    first = keep0_ref[...].astype(F32) + arr0_ref[...].astype(F32)
    second = keep2_ref[...].astype(F32) + arr2_ref[...].astype(F32)
    depth = embed_ref.shape[0]
    embed_ref[...] = keep_e_ref[...].astype(F32) + arr_e_ref[:depth, :].astype(F32)
    for at, ref in enumerate((send_ref, recv_ref, update_ref)):
        ref[1] = last[at * depth : (at + 1) * depth]
    send_ref[0], recv_ref[0], update_ref[0] = first[:depth], first[depth:], second[:depth]
    merge_ref[...] = second[depth:]


def body(
    dims,
    grid_latent, mesh_latent, cotangent, embed_weight, merge_weight, send_weight, recv_weight,
    update_weight, target_row, send_rows, incoming_rows, border_mesh_rows, mesh_senders,
):
    chosen, width = grid_latent.shape
    nodes, degree = mesh_senders.shape
    slots, capacity = send_rows.shape[1:]
    column = dims[1] * dims[2]
    peers = slots - 1
    halo = peers * BORDER
    taken = peers * capacity
    total = dims[0] * dims[1] * dims[2]
    bits = (total - 1).bit_length()
    carry = dims == (4, 2, 2) and fine(width, dims)
    spot = lax.axis_index(GROUP)
    place = [lax.axis_index(COLUMN), lax.axis_index("lon") % 2]
    place += [(spot >> bit) % 2 for bit in range(bits)]
    place = jnp.broadcast_to(jnp.stack(place).astype(I32)[None], (slots, 2 + bits))
    ints = jnp.concatenate([send_rows[0], incoming_rows[0], border_mesh_rows[0], place], axis=1)
    unit = 2 * nodes * width * width

    loads = (grid_latent, embed_weight, target_row.reshape(1, chosen), mesh_senders.T,
             mesh_latent, merge_weight, cotangent)
    grid, embed, targets, senders_raw, mesh, merge, cot, sends, *pay1 = call(
        lambda *refs: first_payload(column, capacity, len(loads), *refs), "first_payload",
        [shape(taken, 1, dtype=I32)] + [shape(capacity, width)] * peers,
        (ints,), flops=unit // 2, loads=loads,
    )
    arr1 = exchange(pay1, dims)
    (local, slope_g, sends_row, incoming, bounds, bounds_row, senders_t, senders, place) = call(
        lambda *refs: embed_local(column, capacity, *refs), "embed_local",
        [shape(nodes, width, dtype=F32), shape(chosen, width), shape(1, taken, dtype=I32),
         shape(1, taken, dtype=I32), shape(halo, 1, dtype=I32), shape(1, halo, dtype=I32),
         shape(degree, nodes, dtype=I32), shape(nodes, 8, dtype=I32),
         shape(slots, 2 + bits, dtype=I32)],
        (ints, senders_raw, grid, embed, targets, sends), flops=3 * unit,
    )
    merged, state0, slope_a, lat_a, *pay2 = call(
        lambda *refs: merge_nodes(peers, *refs), "merge_nodes",
        [shape(nodes, width), shape(nodes, width), shape(taken, width), shape(taken, width)]
        + [shape(4 * BORDER, width)] * peers,
        (*arr1, incoming, embed, local, mesh, merge, bounds, senders_t, cot),
        flops=2 * unit,
    )
    arr2 = exchange(pay2, dims)
    total0, slope0, recv_n0, sent_b0 = call(
        forward_local, "forward_local",
        [shape(nodes, width, dtype=F32), shape(degree, nodes, width),
         shape(halo, width, dtype=F32), shape(halo, width)],
        (state0, send_weight, recv_weight, senders, senders_t, bounds), flops=6 * unit,
    )
    summed0, state1, pre0, rows0, back0, merged_r, cot_r, *pay3 = call(
        lambda *refs: forward_halo(peers, *refs), "forward_halo",
        [shape(nodes, width), shape(nodes, width), shape(halo, width, dtype=F32)]
        + [shape(halo, width)] * 4 + [shape(2 * BORDER, width)] * peers,
        (*arr2, recv_n0, total0, state0, send_weight, update_weight, senders, senders_t, bounds),
        flops=2 * unit,
    )
    arr3 = exchange(pay3, dims)
    (total1, grecv_l, gsent_l, recv_n1, sent_b1, gsum_n1, gsum_r1, slope_k0, slope_d0,
     slope_r0) = call(
        turn_local, "turn_local",
        [shape(nodes, width, dtype=F32)] * 3 + [shape(halo, width, dtype=F32)]
        + [shape(halo, width)] * 6,
        (state1, send_weight, recv_weight, update_weight, cot, cot_r, pre0, recv_n0, back0,
         sent_b0, senders, senders_t, bounds),
        flops=10 * unit, scratch=[pltpu.VMEM((degree * nodes, width), BF)],
    )
    summed1, grecv1, gsent1, gin1, *pay4 = call(
        lambda *refs: turn_halo(peers, *refs), "turn_halo",
        [shape(nodes, width)] * 4 + [shape(BORDER, width)] * peers,
        (*arr3, recv_n1, sent_b1, gsum_n1, gsum_r1, total1, grecv_l, gsent_l, cot,
         send_weight, recv_weight, senders, senders_t, bounds_row),
        flops=3 * unit,
    )
    arr4 = exchange(pay4, dims)
    keep1, give1, mesh_out = call(
        lambda *refs: last_weights(dims, *refs), "last_weights",
        blocks_shapes(3, width, width, dims) + [shape(nodes, width)],
        (place, state1, summed1, cot, grecv1, gsent1, update_weight), flops=4 * unit,
    )
    split = fine(width, dims)
    if split:
        give1, last = lax.optimization_barrier((give1, arr4[-1]))
        arr4 = (*arr4[:-1], last)
        keep1, give1 = halve_step(1, keep1, swap(give1, 0, dims), place)
    part0, keep0, give0, keep2, give2 = call(
        lambda *refs: back_local(dims, *refs), "back_local",
        [shape(nodes, width, dtype=F32)] + blocks_shapes(2, width, width, dims) * 2,
        (place, gin1, slope0, slope_k0, slope_d0, send_weight, recv_weight, update_weight, senders,
         senders_t, state0, rows0, summed0, merged, merged_r, keep1),
        flops=10 * unit, scratch=[pltpu.VMEM((degree * nodes, width), BF)],
    )
    if split:
        give0, give2, *arr4 = lax.optimization_barrier((give0, give2, *arr4))
        keep0, give0 = halve_step(1, keep0, swap(give0, 0, dims), place)
        keep0, *arr4 = lax.optimization_barrier((keep0, *arr4))
    shapes = blocks_shapes(1, width, width, dims)
    if carry:
        shapes[1] = shape(shapes[1].shape[0] + 2 * capacity, width)
    gpre_g, keep_e, give_e, *pay5 = call(
        lambda *refs: embed_back(peers, dims, carry, *refs), "embed_back",
        [shape(chosen, width)] + shapes + [shape(capacity, width)] * peers,
        (*arr4, place, slope_r0, part0, update_weight, send_weight, merge, bounds_row,
         targets, sends, incoming, slope_g, slope_a, grid, lat_a, embed),
        flops=6 * unit,
    )
    depth = width // total
    if not split:
        arr5 = exchange(pay5, dims)
        last, first, second, embed_sum = (
            scatter_plain(blocks, dims) for blocks in (keep1, keep0, keep2, keep_e)
        )
        grads = [jnp.stack([a, last[i]]) for i, a in enumerate((first[0], first[1], second[0]))]
        grads = [embed_sum[0], second[1], *grads]
    elif not carry:
        arr5 = exchange(pay5, dims)
        sums = [
            rest_of_halving(1, keep1, give1, place, dims),
            rest_of_halving(1, keep0, give0, place, dims),
            rest_of_halving(0, keep2, give2, place, dims),
            rest_of_halving(0, keep_e, give_e, place, dims),
        ]
    else:
        arr1 = swap(give1, 1, dims)
        arr0 = swap(give0, 1, dims)
        arr2 = swap(give2, 0, dims)
        arr_e, arr1 = lax.optimization_barrier((swap(give_e, 0, dims), arr1))
        keep1, give1 = halve_step(2, keep1, arr1, place)
        arr1 = swap(give1, 2, dims)
        keep_e, keep1 = lax.optimization_barrier((keep_e, keep1))
        keep_e, give_e, from_sub, _ = carry_step(1, keep_e, arr_e, pay5[1:2], place, capacity)
        arr_e = swap(give_e, 1, dims)
        keep2, keep_e = lax.optimization_barrier((keep2, keep_e))
        keep2, give2 = halve_step(1, keep2, arr2, place)
        arr2 = swap(give2, 1, dims)
        keep0, keep2 = lax.optimization_barrier((keep0, keep2))
        keep0, give0 = halve_step(2, keep0, arr0, place)
        arr0 = swap(give0, 2, dims)
        keep1, keep0 = lax.optimization_barrier((keep1, keep0))
        keep1, give1 = halve_step(3, keep1, arr1, place)
        arr1 = swap(give1, 3, dims)
        keep0, keep1 = lax.optimization_barrier((keep0, keep1))
        keep0, give0 = halve_step(3, keep0, arr0, place)
        arr0 = swap(give0, 3, dims)
        keep2, keep0 = lax.optimization_barrier((keep2, keep0))
        keep2, give2 = halve_step(2, keep2, arr2, place)
        arr2 = swap(give2, 2, dims)
        keep_e, keep2, arr1, arr0 = lax.optimization_barrier((keep_e, keep2, arr1, arr0))
        keep_e, give_e, from_lat, from_diag = carry_step(
            2, keep_e, arr_e, pay5[3:], place, capacity
        )
        arr_e = swap(give_e, 2, dims)
        keep2, keep_e = lax.optimization_barrier((keep2, keep_e))
        keep2, give2 = halve_step(3, keep2, arr2, place)
        arr2 = swap(give2, 3, dims)
        keep_e, keep2 = lax.optimization_barrier((keep_e, keep2))
        keep_e, give_e, from_near, _ = carry_step(3, keep_e, arr_e, (), place, capacity)
        arr_e = swap(give_e, 3, dims)
        arr5 = (arr_e, from_near, from_diag, from_lat, from_sub)
        sums = ((keep1, arr1), (keep0, arr0), (keep2, arr2), (keep_e, arr_e))
    (grid_grad,) = call(
        lambda *refs: grid_place(peers, *refs), "grid_place", [shape(chosen, width)],
        (*arr5, gpre_g, embed, sends_row), flops=3 * unit,
    )
    if split:
        grads = call(
            finish, "finish",
            [shape(depth, width, dtype=F32)] * 2 + [shape(2, depth, width, dtype=F32)] * 3,
            [part for pair in sums for part in pair], flops=8 * depth * width,
        )
    return (mesh_out, grid_grad, *grads)


def solution(mesh):
    split = ("groups", "lon", "lat", "sub")
    dims = tuple(mesh.shape[axis] for axis in GROUP)
    rows = P(split, None)
    whole = P("groups", GROUP, None)
    in_specs = (
        rows, rows, rows, P(), P(), P(), P(), P(), P(split), P(split, None, None),
        P(split, None, None), P(split, None, None), rows,
    )
    out_specs = (rows, rows, rows, rows, whole, whole, whole)
    return jax.shard_map(
        lambda *args: body(dims, *args),
        mesh=mesh, in_specs=in_specs, out_specs=out_specs, check_vma=False,
    )
```

```python
import jax
import jax.numpy as jnp
from jax import lax
from jax.experimental import pallas as pl
from jax.experimental.pallas import tpu as pltpu
from jax.sharding import PartitionSpec as P

BF = jnp.bfloat16
F32 = jnp.float32
I32 = jnp.int32
NN = (((1,), (0,)), ((), ()))
NT = (((1,), (1,)), ((), ()))
TN = (((0,), (0,)), ((), ()))
BORDER = 8
GROUP = ("lon", "lat", "sub")
COLUMN = ("lat", "sub")


def dot(a, b, dims=NN):
    return lax.dot_general(a, b, dims, preferred_element_type=F32)


def low(value):
    return value.astype(BF)


def sigmoid(value):
    return 0.5 * jnp.tanh(0.5 * value) + 0.5


def silu(value):
    return value * sigmoid(value)


def silu_both(value):
    sig = sigmoid(value)
    act = value * sig
    return act, sig + act * (1.0 - sig)


def silu_slope(value):
    return silu_both(value)[1]


def iota(rows, columns, dim):
    return lax.broadcasted_iota(I32, (rows, columns), dim)


def hot(mask):
    return jnp.where(mask, 1.0, 0.0)


def slot_of(at, column, me, odd):
    far = jnp.where(at == column - 1, column + 1 - odd, column + odd)
    return jnp.where(at < column - 1, jnp.bitwise_xor(at + 1, me), far)


def as_column(values, wide, column, me, odd):
    slots = values.shape[0]
    count = (slots - 1) * wide
    row = iota(count, slots, 0)
    pick = low(hot(slot_of(row // wide, column, me, odd) == iota(count, slots, 1)))
    found = 16.0 * dot(pick, low((values // 16).astype(F32)))
    found = found + dot(pick, low((values % 16).astype(F32)))
    keep = iota(count, wide, 0) % wide == iota(count, wide, 1)
    return jnp.sum(jnp.where(keep, found, 0.0), axis=1, keepdims=True).astype(I32)


def as_row(values, wide, column, me, odd):
    slots = values.shape[0]
    count = (slots - 1) * wide
    pick = low(hot(iota(wide, count, 1) % wide == iota(wide, count, 0)))
    found = 16.0 * dot(low((values // 16).astype(F32)), pick)
    found = found + dot(low((values % 16).astype(F32)), pick)
    at = iota(slots, count, 1) // wide
    keep = slot_of(at, column, me, odd) == iota(slots, count, 0)
    return jnp.sum(jnp.where(keep, found, 0.0), axis=0, keepdims=True).astype(I32)


def split_parts(refs, starts, sizes):
    values = [ref[...].astype(F32) for ref in refs]
    return [
        jnp.concatenate([value[start : start + size] for value in values], axis=0)
        for start, size in zip(starts, sizes)
    ]


def store_parts(refs, parts):
    peers = len(refs)
    for at, ref in enumerate(refs):
        rows = []
        for part in parts:
            size = part.shape[0] // peers
            rows.append(part[at * size : (at + 1) * size])
        ref[...] = low(rows[0] if len(rows) == 1 else jnp.concatenate(rows, axis=0))


def receivers(senders_t, halo):
    degree, nodes = senders_t.shape
    found = jnp.zeros((halo, nodes), F32)
    ids = iota(halo, nodes, 0) + nodes
    for j in range(degree):
        found = found + hot(senders_t[j : j + 1, :] == ids)
    return found


def receivers_t(senders, degree, halo):
    nodes = senders.shape[0]
    found = jnp.zeros((nodes, halo), F32)
    ids = iota(nodes, halo, 1) + nodes
    for j in range(degree):
        found = found + hot(senders[:, j : j + 1] == ids)
    return found


def fine(rows, dims):
    return (rows // (dims[0] * dims[1] * dims[2])) % 16 == 0


def reverse_bits(block, bits):
    spot = 0
    for bit in range(bits):
        spot = 2 * spot + (block >> bit) % 2
    return spot


def store_blocks(keep_ref, give_ref, at, count, value, dims, bits_ref):
    value = low(value)
    rows = value.shape[0]
    total = dims[0] * dims[1] * dims[2]
    depth = rows // total
    if not fine(rows, dims):
        keep_ref[at] = value
        return
    bits = (total - 1).bit_length()
    upper = bits_ref[0:1, 2:3] == 1
    for block in range(0, total, 2):
        start = reverse_bits(block, bits) * count * depth + at * depth
        first = value[block * depth : (block + 1) * depth].astype(F32)
        second = value[(block + 1) * depth : (block + 2) * depth].astype(F32)
        keep_ref[start : start + depth, :] = low(jnp.where(upper, second, first))
        give_ref[start : start + depth, :] = low(jnp.where(upper, first, second))


def blocks_shapes(count, rows, width, dims):
    if fine(rows, dims):
        return [jax.ShapeDtypeStruct((count * rows // 2, width), BF)] * 2
    return [jax.ShapeDtypeStruct((count, rows, width), BF), jax.ShapeDtypeStruct((16, width), BF)]


def halve(bit, bits_ref, keep_ref, arr_ref, keep_out, give_out):
    half = keep_ref.shape[0] // 2
    upper = bits_ref[0:1, 2 + bit : 3 + bit] == 1
    first = keep_ref[:half, :].astype(F32) + arr_ref[:half, :].astype(F32)
    second = keep_ref[half:, :].astype(F32) + arr_ref[half:, :].astype(F32)
    keep_out[...] = low(jnp.where(upper, second, first))
    give_out[...] = low(jnp.where(upper, first, second))


def swap(block, bit, dims):
    total = dims[0] * dims[1] * dims[2]
    return lax.ppermute(block, GROUP, [(i, i ^ (1 << bit)) for i in range(total)])


def halve_step(bit, keep, arrived, place):
    rows, width = keep.shape[0] // 2, keep.shape[1]
    return call(
        lambda *refs: halve(bit, *refs), "halve", [shape(rows, width)] * 2,
        (place, keep, arrived), flops=4 * rows * width, size=0,
    )


def rest_of_halving(first, keep, give, place, dims):
    bits = (dims[0] * dims[1] * dims[2] - 1).bit_length()
    arrived = swap(give, first, dims)
    for bit in range(first + 1, bits):
        keep, give = halve_step(bit, keep, arrived, place)
        arrived = swap(give, bit, dims)
    return keep, arrived


def halve_carry(bit, bits_ref, keep_ref, arr_ref, *refs):
    *own_refs, keep_out, give_out, here_ref, on_ref = refs
    rows = keep_ref.shape[0]
    half = rows // 2
    size = here_ref.shape[0]
    upper = bits_ref[0:1, 2 + bit : 3 + bit] == 1
    value = arr_ref[...].astype(F32)
    first = keep_ref[:half, :].astype(F32) + value[:half]
    second = keep_ref[half:, :].astype(F32) + value[half:rows]
    keep_out[...] = low(jnp.where(upper, second, first))
    here_ref[...] = low(value[rows : rows + size])
    passed = value[rows + size : rows + 2 * size]
    on_ref[...] = low(passed)
    extra = [ref[...].astype(F32) for ref in own_refs]
    if len(extra) < 2:
        extra.append(passed)
    give_out[...] = low(jnp.concatenate([jnp.where(upper, first, second), *extra], axis=0))


def carry_step(bit, keep, arrived, own, place, capacity):
    rows, width = keep.shape[0] // 2, keep.shape[1]
    return call(
        lambda *refs: halve_carry(bit, *refs), "halve_carry",
        [shape(rows, width), shape(rows + min(len(own) + 1, 2) * capacity, width),
         shape(capacity, width), shape(capacity, width)],
        (place, keep, arrived, *own), flops=4 * rows * width, size=0,
    )


def scatter_plain(blocks, dims):
    lon, lat, sub = dims
    count, rows, width = blocks.shape
    depth = rows // (lon * lat * sub)
    blocks = blocks.reshape(count, lon, lat, sub, depth, width)
    blocks = blocks.transpose(3, 2, 1, 0, 4, 5)
    for axis in ("sub", "lat", "lon"):
        blocks = lax.psum_scatter(blocks, axis, scatter_dimension=0, tiled=False)
    return blocks.astype(F32)


def call(kernel, name, outs, args, flops, loads=(), scratch=(), size=None):
    if size is None:
        size = sum(a.size * a.dtype.itemsize for a in (*args, *outs, *loads))
    args = (*(pltpu.with_memory_space_constraint(a, pltpu.HBM) for a in loads), *args)
    scratch = list(scratch)
    if loads:
        scratch.append(pltpu.SemaphoreType.DMA((len(loads),)))
    in_specs = [pl.BlockSpec(memory_space=pltpu.HBM)] * len(loads)
    in_specs += [pl.BlockSpec(memory_space=pltpu.VMEM)] * (len(args) - len(loads))
    return pl.pallas_call(
        kernel,
        out_shape=[shape(*a.shape, dtype=a.dtype) for a in loads] + list(outs),
        in_specs=in_specs,
        out_specs=[pl.BlockSpec(memory_space=pltpu.VMEM)] * (len(outs) + len(loads)),
        scratch_shapes=scratch,
        compiler_params=pltpu.CompilerParams(vmem_limit_bytes=16 * 1024 * 1024),
        cost_estimate=pl.CostEstimate(flops=flops, bytes_accessed=size, transcendentals=0),
        name=name,
    )(*args)


def exchange(parts, dims):
    column = dims[1] * dims[2]
    count = dims[0]
    other = [(i, (i - 1 + 2 * (i % 2)) % count) for i in range(count)]
    far = lax.ppermute(parts[column], "lon", other)
    near = lax.ppermute(parts[column - 1], "lon", [(i, i ^ 1) for i in range(count)])
    arrived = [
        lax.ppermute(parts[r - 1], COLUMN, [(i, i ^ r) for i in range(column)])
        for r in range(column - 1, 0, -1)
    ]
    return (far, near, *arrived)


def shape(*dims, dtype=BF):
    return jax.ShapeDtypeStruct(dims, dtype)


def start_loads(sources, targets, sems):
    copies = [
        pltpu.make_async_copy(source, target, sems.at[at])
        for at, (source, target) in enumerate(zip(sources, targets))
    ]
    for copy in copies:
        copy.start()
    return copies


def first_payload(column, capacity, count, *refs):
    sources, ints_ref, targets = refs[:count], refs[count], refs[count + 1 : 2 * count + 1]
    sends_ref, *pay_refs, sems = refs[2 * count + 1 :]
    grid_ref = targets[0]
    grid_load, *loads = start_loads(sources, targets, sems)
    chosen = grid_ref.shape[0]
    ints = ints_ref[...]
    base = 2 * capacity + BORDER
    me, odd = ints[0:1, base : base + 1], ints[0:1, base + 1 : base + 2]
    sends = as_column(ints[:, :capacity], capacity, column, me, odd)
    sends_ref[...] = sends
    pick = low(hot(sends == iota(sends.shape[0], chosen, 1)))
    grid_load.wait()
    store_parts(pay_refs, [dot(pick, grid_ref[...])])
    for load in loads:
        load.wait()


def embed_local(
    column, capacity, ints_ref, senders_ref, grid_ref, weight_ref, target_ref, sends_ref,
    sum_ref, slope_ref, sends_row_ref, incoming_ref, bounds_ref, bounds_row_ref, senders_t_ref,
    senders_out_ref, place_ref,
):
    chosen = grid_ref.shape[0]
    nodes = sum_ref.shape[0]
    taken = sends_ref.shape[0]
    act, slope = silu_both(dot(grid_ref[...], weight_ref[...]))
    slope_ref[...] = low(slope)
    sent = jnp.max(hot(sends_ref[...] == iota(taken, chosen, 1)), axis=0, keepdims=True)
    label = jnp.where(sent > 0.0, nodes, target_ref[...])
    sum_ref[...] = dot(low(hot(label == iota(nodes, chosen, 0))), low(act))
    ints = ints_ref[...]
    base = 2 * capacity + BORDER
    place_ref[...] = ints[:, base:]
    me, odd = ints[0:1, base : base + 1], ints[0:1, base + 1 : base + 2]
    sends, incoming = ints[:, :capacity], ints[:, capacity : 2 * capacity]
    bounds = ints[:, 2 * capacity : base]
    sends_row_ref[...] = as_row(sends, capacity, column, me, odd)
    incoming_ref[...] = as_row(incoming, capacity, column, me, odd)
    bounds_ref[...] = as_column(bounds, BORDER, column, me, odd)
    bounds_row_ref[...] = as_row(bounds, BORDER, column, me, odd)
    senders = senders_ref[...]
    degree = senders.shape[0]
    offset = senders - nodes
    slot = offset // BORDER
    far = jnp.where(slot == column, column - odd, column - 1 + odd)
    at = jnp.where(slot < column, jnp.bitwise_xor(slot, me) - 1, far)
    senders = jnp.where(offset < 0, senders, nodes + at * BORDER + offset % BORDER)
    senders_t_ref[...] = senders
    filler = jnp.zeros((8 - degree, nodes), I32)
    senders_out_ref[...] = jnp.concatenate([senders, filler], axis=0).T


def merge_nodes(peers, *refs):
    arr_refs, refs = refs[:peers][::-1], refs[peers:]
    (incoming_ref, embed_ref, local_ref, mesh_ref, weight_ref, bounds_ref, senders_t_ref, cot_ref,
     merged_ref, state_ref, slope_ref, lat_ref, *pay_refs) = refs
    nodes = mesh_ref.shape[0]
    taken = incoming_ref.shape[1]
    halo = peers * BORDER
    lat = jnp.concatenate([ref[...] for ref in arr_refs], axis=0)
    lat_ref[...] = lat
    act, slope = silu_both(dot(lat, embed_ref[...]))
    slope_ref[...] = low(slope)
    place = low(hot(incoming_ref[...] == iota(nodes, taken, 0)))
    merged = low(local_ref[...] + dot(place, low(act)))
    merged_ref[...] = merged
    state = low(mesh_ref[...].astype(F32) + dot(merged, weight_ref[...]))
    state_ref[...] = state
    border = low(hot(bounds_ref[...] == iota(halo, nodes, 1)))
    back = low(receivers(senders_t_ref[...], halo))
    store_parts(
        pay_refs,
        [dot(border, state), dot(back, state), dot(back, cot_ref[...])],
    )


def local_edges(senders, degree, sent, recv, each):
    nodes = senders.shape[0]
    total = None
    ids = iota(nodes, nodes, 1)
    for j in range(degree):
        act, slope = silu_both(dot(low(hot(senders[:, j : j + 1] == ids)), sent) + recv)
        total = act if total is None else total + act
        each(j, slope)
    return total


def edge_targets(senders_t):
    degree, nodes = senders_t.shape
    ids = iota(nodes, nodes, 0)
    return jnp.concatenate(
        [low(hot(senders_t[j : j + 1, :] == ids)) for j in range(degree)], axis=1
    )


def forward_local(
    state_ref, send_ref, recv_ref, senders_ref, senders_t_ref, bounds_ref,
    total_ref, slope_ref, recv_n_ref, sent_b_ref,
):
    state = state_ref[...]
    nodes = state.shape[0]
    halo = bounds_ref.shape[0]
    sent = low(dot(state, send_ref[0]))
    recv = dot(state, recv_ref[0])

    def keep(j, slope):
        slope_ref[j] = low(slope)

    total_ref[...] = local_edges(senders_ref[...], senders_t_ref.shape[0], sent, recv, keep)
    back = low(receivers(senders_t_ref[...], halo))
    recv_n_ref[...] = dot(low(dot(back, state)), recv_ref[0])
    sent_b_ref[...] = low(dot(low(hot(bounds_ref[...] == iota(halo, nodes, 1))), sent))


def forward_halo(peers, *refs):
    arr_refs, refs = refs[:peers][::-1], refs[peers:]
    (recv_n_ref, total_ref, state_ref, send_ref, update_ref, senders_ref, senders_t_ref,
     bounds_ref, summed_ref, out_ref, pre_ref, back_ref, cot_ref, *pay_refs) = refs
    nodes = state_ref.shape[0]
    degree = senders_t_ref.shape[0]
    halo = peers * BORDER
    rows, back, cot = split_parts(arr_refs, (0, BORDER, 2 * BORDER), (BORDER,) * 3)
    back_ref[...], cot_ref[...] = low(back), low(cot)
    pre = low(dot(low(rows), send_ref[0])).astype(F32) + recv_n_ref[...]
    pre_ref[...] = pre
    place = low(receivers_t(senders_ref[...], degree, halo))
    extra = silu(pre) - silu(recv_n_ref[...])
    summed = low(total_ref[...] + dot(place, low(extra)))
    summed_ref[...] = summed
    state = low(state_ref[...].astype(F32) + dot(summed, update_ref[0]))
    out_ref[...] = state
    border = low(hot(bounds_ref[...] == iota(halo, nodes, 1)))
    back = low(receivers(senders_t_ref[...], halo))
    store_parts(pay_refs, [dot(border, state), dot(back, state)])


def turn_local(
    state_ref, send_ref, recv_ref, update_ref, cot_ref, cot_r_ref, pre_ref, recv_n0_ref, back0_ref,
    sent_b0_ref, senders_ref, senders_t_ref, bounds_ref,
    total_ref, grecv_ref, gsent_ref, recv_n_ref, sent_b_ref, gsum_n_ref, gsum_r_ref,
    slope_d_ref, slope_r_ref, gpre_ref,
):
    halo = bounds_ref.shape[0]
    slope_d_ref[...] = low(silu_slope(pre_ref[...]) - silu_slope(recv_n0_ref[...]))
    pre = sent_b0_ref[...].astype(F32) + dot(back0_ref[...], recv_ref[0])
    slope_r_ref[...] = low(silu_slope(pre))
    state = state_ref[...]
    nodes = state.shape[0]
    sent = low(dot(state, send_ref[1]))
    recv = dot(state, recv_ref[1])
    gsum = low(dot(cot_ref[...], update_ref[1], NT))
    grad = gsum.astype(F32)
    grecv = []

    def back_edge(j, slope):
        gpre = grad * slope
        grecv.append(gpre if j == 0 else grecv[-1] + gpre)
        gpre_ref[j * nodes : (j + 1) * nodes, :] = low(gpre)

    degree = senders_t_ref.shape[0]
    total_ref[...] = local_edges(senders_ref[...], degree, sent, recv, back_edge)
    grecv_ref[...] = grecv[-1]
    gsent_ref[...] = dot(edge_targets(senders_t_ref[...]), gpre_ref[...])
    back = low(receivers(senders_t_ref[...], halo))
    recv_n_ref[...] = dot(low(dot(back, state)), recv_ref[1])
    sent_b_ref[...] = low(dot(low(hot(bounds_ref[...] == iota(halo, nodes, 1))), sent))
    gsum_n_ref[...] = low(dot(back, gsum))
    gsum_r_ref[...] = low(dot(cot_r_ref[...], update_ref[1], NT))


def turn_halo(peers, *refs):
    arr_refs, refs = refs[:peers][::-1], refs[peers:]
    (recv_n_ref, sent_b_ref, gsum_n_ref, gsum_r_ref, total_ref, grecv_ref, gsent_ref, cot_ref,
     send_ref, recv_ref, senders_ref, senders_t_ref, bounds_ref, summed_ref, grecv_out_ref,
     gsent_out_ref, gin_ref, *pay_refs) = refs
    nodes = cot_ref.shape[0]
    degree = senders_t_ref.shape[0]
    halo = peers * BORDER
    rows, back = split_parts(arr_refs, (0, BORDER), (BORDER,) * 2)
    pre = low(dot(low(rows), send_ref[1])).astype(F32) + recv_n_ref[...]
    act, slope = silu_both(pre)
    place = low(receivers_t(senders_ref[...], degree, halo))
    base, base_slope = silu_both(recv_n_ref[...])
    gpre = low(gsum_n_ref[...].astype(F32) * (slope - base_slope))
    grecv = low(grecv_ref[...] + dot(place, gpre))
    pre = sent_b_ref[...].astype(F32) + dot(low(back), recv_ref[1])
    gpre = low(gsum_r_ref[...].astype(F32) * silu_slope(pre))
    border = low(hot(bounds_ref[...] == iota(nodes, halo, 0)))
    gsent = low(gsent_ref[...] + dot(border, gpre))
    gin = cot_ref[...].astype(F32) + dot(grecv, recv_ref[1], NT) + dot(gsent, send_ref[1], NT)
    gin = low(gin)
    gin_ref[...] = gin
    store_parts(pay_refs, [dot(low(receivers(senders_t_ref[...], halo)), gin)])
    summed_ref[...] = low(total_ref[...] + dot(place, low(act - base)))
    grecv_out_ref[...] = grecv
    gsent_out_ref[...] = gsent


def last_weights(
    dims, place_ref, state_ref, summed_ref, cot_ref, grecv_ref, gsent_ref, update_ref,
    keep_ref, give_ref, mesh_ref,
):
    state, summed = state_ref[...], summed_ref[...]

    def store(at, value):
        store_blocks(keep_ref, give_ref, at, 3, value, dims, place_ref)

    both = dot(state, jnp.concatenate([gsent_ref[...], grecv_ref[...]], axis=1), TN)
    store(0, both[:, : state.shape[1]])
    store(1, both[:, state.shape[1] :])
    store(2, dot(summed, cot_ref[...], TN))
    mesh_ref[...] = low(state.astype(F32) + dot(summed, update_ref[1]))


def first_layer_back(peers, dims, carry, *refs):
    arr_refs, refs = refs[:peers][::-1], refs[peers:]
    (place_ref, gin_ref, slope_ref, slope_d_ref, slope_r_ref, send_ref, recv_ref, update_ref,
     merge_ref, embed_ref, senders_ref, senders_t_ref, bounds_ref, target_ref, sends_ref,
     incoming_ref, state_ref, summed_ref, merged_ref, slope_g_ref, slope_a_ref, grid_ref, lat_ref,
     _, gpre_g_ref, keep_ref, give_ref, keep2_ref, give2_ref, *pay_refs, gpre_ref) = refs
    nodes = gin_ref.shape[0]
    halo = peers * BORDER
    degree = senders_t_ref.shape[0]
    chosen = grid_ref.shape[0]
    taken = sends_ref.shape[0]
    gin = gin_ref[...]
    gsum = low(dot(gin, update_ref[0], NT))
    back = low(receivers(senders_t_ref[...], halo))
    place = low(receivers_t(senders_ref[...], degree, halo))
    grecv = dot(place, low(dot(back, gsum)) * slope_d_ref[...])
    for j in range(degree):
        gpre = gsum * slope_ref[j]
        grecv = grecv + gpre.astype(F32)
        gpre_ref[j * nodes : (j + 1) * nodes, :] = gpre
    grecv = low(grecv)
    (arrived,) = split_parts(arr_refs, (0,), (BORDER,))
    gsum_r = low(dot(low(arrived), update_ref[0], NT))
    border = low(hot(bounds_ref[...] == iota(nodes, halo, 0)))
    gsent = dot(edge_targets(senders_t_ref[...]), gpre_ref[...])
    gsent = low(gsent + dot(border, gsum_r * slope_r_ref[...]))
    gin0 = gin.astype(F32) + dot(grecv, recv_ref[0], NT) + dot(gsent, send_ref[0], NT)
    gin0 = low(gin0)
    gmerged = low(dot(gin0, merge_ref[...], NT))
    place = low(hot(incoming_ref[...] == iota(nodes, taken, 0)))
    gpre_a = low(dot(place, gmerged, TN) * slope_a_ref[...].astype(F32))
    sent = jnp.max(hot(sends_ref[...] == iota(taken, chosen, 1)), axis=0, keepdims=True)
    label = jnp.where(sent > 0.0, nodes, target_ref[...])
    pick = low(hot(label == iota(nodes, chosen, 0)))
    gpre_g = low(dot(pick, gmerged, TN) * slope_g_ref[...].astype(F32))
    gpre_g_ref[...] = gpre_g
    state = state_ref[...]

    def store(at, value):
        store_blocks(keep_ref, give_ref, at, 3, value, dims, place_ref)

    store(0, dot(grid_ref[...], gpre_g, TN) + dot(lat_ref[...], gpre_a, TN))
    both = dot(state, jnp.concatenate([gsent, grecv], axis=1), TN)
    store(1, both[:, : state.shape[1]])
    store(2, both[:, state.shape[1] :])
    store_blocks(keep2_ref, give2_ref, 0, 2, dot(summed_ref[...], gin, TN), dims, place_ref)
    store_blocks(keep2_ref, give2_ref, 1, 2, dot(merged_ref[...], gin0, TN), dims, place_ref)
    rows = dot(gpre_a, embed_ref[...], NT)
    store_parts(pay_refs, [rows])
    if carry:
        size = taken // peers
        start = keep_ref.shape[0]
        give_ref[start : start + 2 * size, :] = low(
            jnp.concatenate([rows[:size], rows[2 * size : 3 * size]], axis=0)
        )


def grid_place(peers, *refs):
    arr_refs, refs = refs[:peers][::-1], refs[peers:]
    gpre_ref, weight_ref, sends_ref, out_ref = refs
    chosen = gpre_ref.shape[0]
    taken = sends_ref.shape[1]
    local = dot(gpre_ref[...], weight_ref[...], NT)
    place = low(hot(sends_ref[...] == iota(chosen, taken, 0)))
    size = taken // peers
    rows = [ref[...].astype(F32) for ref in arr_refs]
    rows = low(jnp.concatenate([row[row.shape[0] - size :] for row in rows], axis=0))
    out_ref[...] = low(local + dot(place, rows))


def finish(
    keep1_ref, arr1_ref, keep0_ref, arr0_ref, keep2_ref, arr2_ref,
    embed_ref, merge_ref, send_ref, recv_ref, update_ref,
):
    depth = embed_ref.shape[0]
    last = keep1_ref[...].astype(F32) + arr1_ref[...].astype(F32)
    first = keep0_ref[...].astype(F32) + arr0_ref[: 3 * depth, :].astype(F32)
    second = keep2_ref[...].astype(F32) + arr2_ref[...].astype(F32)
    for at, ref in enumerate((send_ref, recv_ref, update_ref)):
        ref[1] = last[at * depth : (at + 1) * depth]
    embed_ref[...] = first[:depth]
    send_ref[0], recv_ref[0] = first[depth : 2 * depth], first[2 * depth :]
    update_ref[0], merge_ref[...] = second[:depth], second[depth:]


def body(
    dims,
    grid_latent, mesh_latent, cotangent, embed_weight, merge_weight, send_weight, recv_weight,
    update_weight, target_row, send_rows, incoming_rows, border_mesh_rows, mesh_senders,
):
    chosen, width = grid_latent.shape
    nodes, degree = mesh_senders.shape
    slots, capacity = send_rows.shape[1:]
    column = dims[1] * dims[2]
    peers = slots - 1
    halo = peers * BORDER
    taken = peers * capacity
    total = dims[0] * dims[1] * dims[2]
    bits = (total - 1).bit_length()
    carry = dims == (4, 2, 2) and fine(width, dims)
    spot = lax.axis_index(GROUP)
    place = [lax.axis_index(COLUMN), lax.axis_index("lon") % 2]
    place += [(spot >> bit) % 2 for bit in range(bits)]
    place = jnp.broadcast_to(jnp.stack(place).astype(I32)[None], (slots, 2 + bits))
    ints = jnp.concatenate([send_rows[0], incoming_rows[0], border_mesh_rows[0], place], axis=1)
    unit = 2 * nodes * width * width

    loads = (grid_latent, embed_weight, target_row.reshape(1, chosen), mesh_senders.T,
             mesh_latent, merge_weight, cotangent)
    grid, embed, targets, senders_raw, mesh, merge, cot, sends, *pay1 = call(
        lambda *refs: first_payload(column, capacity, len(loads), *refs), "first_payload",
        [shape(taken, 1, dtype=I32)] + [shape(capacity, width)] * peers,
        (ints,), flops=unit // 2, loads=loads,
    )
    arr1 = exchange(pay1, dims)
    (local, slope_g, sends_row, incoming, bounds, bounds_row, senders_t, senders, place) = call(
        lambda *refs: embed_local(column, capacity, *refs), "embed_local",
        [shape(nodes, width, dtype=F32), shape(chosen, width), shape(1, taken, dtype=I32),
         shape(1, taken, dtype=I32), shape(halo, 1, dtype=I32), shape(1, halo, dtype=I32),
         shape(degree, nodes, dtype=I32), shape(nodes, 8, dtype=I32),
         shape(slots, 2 + bits, dtype=I32)],
        (ints, senders_raw, grid, embed, targets, sends), flops=3 * unit,
    )
    merged, state0, slope_a, lat_a, *pay2 = call(
        lambda *refs: merge_nodes(peers, *refs), "merge_nodes",
        [shape(nodes, width), shape(nodes, width), shape(taken, width), shape(taken, width)]
        + [shape(3 * BORDER, width)] * peers,
        (*arr1, incoming, embed, local, mesh, merge, bounds, senders_t, cot),
        flops=2 * unit,
    )
    arr2 = exchange(pay2, dims)
    total0, slope0, recv_n0, sent_b0 = call(
        forward_local, "forward_local",
        [shape(nodes, width, dtype=F32), shape(degree, nodes, width),
         shape(halo, width, dtype=F32), shape(halo, width)],
        (state0, send_weight, recv_weight, senders, senders_t, bounds), flops=6 * unit,
    )
    summed0, state1, pre0, back0, cot_r, *pay3 = call(
        lambda *refs: forward_halo(peers, *refs), "forward_halo",
        [shape(nodes, width), shape(nodes, width), shape(halo, width, dtype=F32)]
        + [shape(halo, width)] * 2 + [shape(2 * BORDER, width)] * peers,
        (*arr2, recv_n0, total0, state0, send_weight, update_weight, senders, senders_t, bounds),
        flops=2 * unit,
    )
    arr3 = exchange(pay3, dims)
    (total1, grecv_l, gsent_l, recv_n1, sent_b1, gsum_n1, gsum_r1, slope_d0, slope_r0) = call(
        turn_local, "turn_local",
        [shape(nodes, width, dtype=F32)] * 3 + [shape(halo, width, dtype=F32)]
        + [shape(halo, width)] * 5,
        (state1, send_weight, recv_weight, update_weight, cot, cot_r, pre0, recv_n0, back0,
         sent_b0, senders, senders_t, bounds),
        flops=10 * unit, scratch=[pltpu.VMEM((degree * nodes, width), BF)],
    )
    summed1, grecv1, gsent1, gin1, *pay4 = call(
        lambda *refs: turn_halo(peers, *refs), "turn_halo",
        [shape(nodes, width)] * 4 + [shape(BORDER, width)] * peers,
        (*arr3, recv_n1, sent_b1, gsum_n1, gsum_r1, total1, grecv_l, gsent_l, cot,
         send_weight, recv_weight, senders, senders_t, bounds_row),
        flops=3 * unit,
    )
    arr4 = exchange(pay4, dims)
    keep1, give1, mesh_out = call(
        lambda *refs: last_weights(dims, *refs), "last_weights",
        blocks_shapes(3, width, width, dims) + [shape(nodes, width)],
        (place, state1, summed1, cot, grecv1, gsent1, update_weight), flops=4 * unit,
    )
    split = fine(width, dims)
    if split:
        give1, *arr4 = lax.optimization_barrier((give1, *arr4))
    shapes = blocks_shapes(3, width, width, dims)
    if carry:
        shapes[1] = shape(shapes[1].shape[0] + 2 * capacity, width)
    gpre_g, keep0, give0, keep2, give2, *pay5 = call(
        lambda *refs: first_layer_back(peers, dims, carry, *refs), "first_layer_back",
        [shape(chosen, width)] + shapes + blocks_shapes(2, width, width, dims)
        + [shape(capacity, width)] * peers,
        (*arr4, place, gin1, slope0, slope_d0, slope_r0, send_weight, recv_weight, update_weight,
         merge, embed, senders, senders_t, bounds_row, targets, sends, incoming, state0, summed0,
         merged, slope_g, slope_a, grid, lat_a, give1),
        flops=16 * unit, scratch=[pltpu.VMEM((degree * nodes, width), BF)],
    )
    depth = width // total
    if not split:
        arr5 = exchange(pay5, dims)
        last, first, second = (scatter_plain(blocks, dims) for blocks in (keep1, keep0, keep2))
        grads = [jnp.stack([a, last[i]]) for i, a in enumerate((first[1], first[2], second[0]))]
        grads = [first[0], second[1], *grads]
    elif not carry:
        arr5 = exchange(pay5, dims)
        sums = [
            rest_of_halving(0, keep1, give1, place, dims),
            rest_of_halving(0, keep0, give0, place, dims),
            rest_of_halving(0, keep2, give2, place, dims),
        ]
    else:
        arr1, keep0 = lax.optimization_barrier((swap(give1, 0, dims), keep0))
        keep1, give1 = halve_step(1, keep1, arr1, place)
        arr1 = swap(give1, 1, dims)
        give0, give2, keep1 = lax.optimization_barrier((give0, give2, keep1))
        arr0 = swap(give0, 0, dims)
        arr2 = swap(give2, 0, dims)
        keep0, give0, from_sub, _ = carry_step(1, keep0, arr0, pay5[1:2], place, capacity)
        arr0 = swap(give0, 1, dims)
        keep2, keep0 = lax.optimization_barrier((keep2, keep0))
        keep2, give2 = halve_step(1, keep2, arr2, place)
        arr2 = swap(give2, 1, dims)
        keep1, keep2 = lax.optimization_barrier((keep1, keep2))
        keep1, give1 = halve_step(2, keep1, arr1, place)
        arr1 = swap(give1, 2, dims)
        keep1, give1 = halve_step(3, keep1, arr1, place)
        arr1 = swap(give1, 3, dims)
        keep0, keep1 = lax.optimization_barrier((keep0, keep1))
        keep0, give0, from_lat, from_diag = carry_step(
            2, keep0, arr0, pay5[3:], place, capacity
        )
        arr0 = swap(give0, 2, dims)
        keep2, keep0 = lax.optimization_barrier((keep2, keep0))
        keep2, give2 = halve_step(2, keep2, arr2, place)
        arr2 = swap(give2, 2, dims)
        keep0, keep2, arr1 = lax.optimization_barrier((keep0, keep2, arr1))
        keep0, give0, from_near, _ = carry_step(3, keep0, arr0, (), place, capacity)
        arr0 = swap(give0, 3, dims)
        keep2, keep0 = lax.optimization_barrier((keep2, keep0))
        keep2, give2 = halve_step(3, keep2, arr2, place)
        arr2 = swap(give2, 3, dims)
        arr5 = (arr0, from_near, from_diag, from_lat, from_sub)
    (grid_grad,) = call(
        lambda *refs: grid_place(peers, *refs), "grid_place", [shape(chosen, width)],
        (*arr5, gpre_g, embed, sends_row), flops=3 * unit,
    )
    if carry:
        keep2, grid_grad = lax.optimization_barrier((keep2, grid_grad))
        sums = ((keep1, arr1), (keep0, arr0), (keep2, arr2))
    if split:
        grads = call(
            finish, "finish",
            [shape(depth, width, dtype=F32)] * 2 + [shape(2, depth, width, dtype=F32)] * 3,
            [part for pair in sums for part in pair], flops=8 * depth * width,
        )
    return (mesh_out, grid_grad, *grads)


def solution(mesh):
    split = ("groups", "lon", "lat", "sub")
    dims = tuple(mesh.shape[axis] for axis in GROUP)
    rows = P(split, None)
    whole = P("groups", GROUP, None)
    in_specs = (
        rows, rows, rows, P(), P(), P(), P(), P(), P(split), P(split, None, None),
        P(split, None, None), P(split, None, None), rows,
    )
    out_specs = (rows, rows, rows, rows, whole, whole, whole)
    return jax.shard_map(
        lambda *args: body(dims, *args),
        mesh=mesh, in_specs=in_specs, out_specs=out_specs, check_vma=False,
    )
```

```python
import jax
import jax.numpy as jnp
from jax import lax
from jax.experimental import pallas as pl
from jax.experimental.pallas import tpu as pltpu
from jax.sharding import PartitionSpec as P

BF = jnp.bfloat16
F32 = jnp.float32
I32 = jnp.int32
NN = (((1,), (0,)), ((), ()))
NT = (((1,), (1,)), ((), ()))
TN = (((0,), (0,)), ((), ()))
BORDER = 8
GROUP = ("lon", "lat", "sub")
COLUMN = ("lat", "sub")


def dot(a, b, dims=NN):
    return lax.dot_general(a, b, dims, preferred_element_type=F32)


def low(value):
    return value.astype(BF)


def sigmoid(value):
    return 0.5 * jnp.tanh(0.5 * value) + 0.5


def silu(value):
    return value * sigmoid(value)


def silu_both(value):
    sig = sigmoid(value)
    act = value * sig
    return act, sig + act * (1.0 - sig)


def silu_slope(value):
    return silu_both(value)[1]


def iota(rows, columns, dim):
    return lax.broadcasted_iota(I32, (rows, columns), dim)


def hot(mask):
    return jnp.where(mask, 1.0, 0.0)


def slot_of(at, column, me, odd):
    far = jnp.where(at == column - 1, column + 1 - odd, column + odd)
    return jnp.where(at < column - 1, jnp.bitwise_xor(at + 1, me), far)


def as_column(values, wide, column, me, odd):
    slots = values.shape[0]
    count = (slots - 1) * wide
    row = iota(count, slots, 0)
    pick = low(hot(slot_of(row // wide, column, me, odd) == iota(count, slots, 1)))
    found = 16.0 * dot(pick, low((values // 16).astype(F32)))
    found = found + dot(pick, low((values % 16).astype(F32)))
    keep = iota(count, wide, 0) % wide == iota(count, wide, 1)
    return jnp.sum(jnp.where(keep, found, 0.0), axis=1, keepdims=True).astype(I32)


def as_row(values, wide, column, me, odd):
    slots = values.shape[0]
    count = (slots - 1) * wide
    pick = low(hot(iota(wide, count, 1) % wide == iota(wide, count, 0)))
    found = 16.0 * dot(low((values // 16).astype(F32)), pick)
    found = found + dot(low((values % 16).astype(F32)), pick)
    at = iota(slots, count, 1) // wide
    keep = slot_of(at, column, me, odd) == iota(slots, count, 0)
    return jnp.sum(jnp.where(keep, found, 0.0), axis=0, keepdims=True).astype(I32)


def split_parts(refs, starts, sizes):
    values = [ref[...].astype(F32) for ref in refs]
    return [
        jnp.concatenate([value[start : start + size] for value in values], axis=0)
        for start, size in zip(starts, sizes)
    ]


def store_parts(refs, parts):
    peers = len(refs)
    for at, ref in enumerate(refs):
        rows = []
        for part in parts:
            size = part.shape[0] // peers
            rows.append(part[at * size : (at + 1) * size])
        ref[...] = low(rows[0] if len(rows) == 1 else jnp.concatenate(rows, axis=0))


def receivers(senders_t, halo):
    degree, nodes = senders_t.shape
    found = jnp.zeros((halo, nodes), F32)
    ids = iota(halo, nodes, 0) + nodes
    for j in range(degree):
        found = found + hot(senders_t[j : j + 1, :] == ids)
    return found


def receivers_t(senders, degree, halo):
    nodes = senders.shape[0]
    found = jnp.zeros((nodes, halo), F32)
    ids = iota(nodes, halo, 1) + nodes
    for j in range(degree):
        found = found + hot(senders[:, j : j + 1] == ids)
    return found


def fine(rows, dims):
    return (rows // (dims[0] * dims[1] * dims[2])) % 16 == 0


def reverse_bits(block, bits):
    spot = 0
    for bit in range(bits):
        spot = 2 * spot + (block >> bit) % 2
    return spot


def store_blocks(keep_ref, give_ref, at, count, value, dims, bits_ref):
    value = low(value)
    rows = value.shape[0]
    total = dims[0] * dims[1] * dims[2]
    depth = rows // total
    if not fine(rows, dims):
        keep_ref[at] = value
        return
    bits = (total - 1).bit_length()
    upper = bits_ref[0:1, 2:3] == 1
    for block in range(0, total, 2):
        start = reverse_bits(block, bits) * count * depth + at * depth
        first = value[block * depth : (block + 1) * depth].astype(F32)
        second = value[(block + 1) * depth : (block + 2) * depth].astype(F32)
        keep_ref[start : start + depth, :] = low(jnp.where(upper, second, first))
        give_ref[start : start + depth, :] = low(jnp.where(upper, first, second))


def blocks_shapes(count, rows, width, dims):
    if fine(rows, dims):
        return [jax.ShapeDtypeStruct((count * rows // 2, width), BF)] * 2
    return [jax.ShapeDtypeStruct((count, rows, width), BF), jax.ShapeDtypeStruct((16, width), BF)]


def halve(bit, bits_ref, keep_ref, arr_ref, keep_out, give_out):
    half = keep_ref.shape[0] // 2
    upper = bits_ref[0:1, 2 + bit : 3 + bit] == 1
    first = keep_ref[:half, :].astype(F32) + arr_ref[:half, :].astype(F32)
    second = keep_ref[half:, :].astype(F32) + arr_ref[half:, :].astype(F32)
    keep_out[...] = low(jnp.where(upper, second, first))
    give_out[...] = low(jnp.where(upper, first, second))


def swap(block, bit, dims):
    total = dims[0] * dims[1] * dims[2]
    return lax.ppermute(block, GROUP, [(i, i ^ (1 << bit)) for i in range(total)])


def halve_step(bit, keep, arrived, place):
    rows, width = keep.shape[0] // 2, keep.shape[1]
    return call(
        lambda *refs: halve(bit, *refs), "halve", [shape(rows, width)] * 2,
        (place, keep, arrived), flops=4 * rows * width, size=0,
    )


def rest_of_halving(first, keep, give, place, dims):
    bits = (dims[0] * dims[1] * dims[2] - 1).bit_length()
    arrived = swap(give, first, dims)
    for bit in range(first + 1, bits):
        keep, give = halve_step(bit, keep, arrived, place)
        arrived = swap(give, bit, dims)
    return keep, arrived


def halve_carry(bit, bits_ref, keep_ref, arr_ref, *refs):
    *own_refs, keep_out, give_out, here_ref, on_ref = refs
    rows = keep_ref.shape[0]
    half = rows // 2
    size = here_ref.shape[0]
    upper = bits_ref[0:1, 2 + bit : 3 + bit] == 1
    value = arr_ref[...].astype(F32)
    first = keep_ref[:half, :].astype(F32) + value[:half]
    second = keep_ref[half:, :].astype(F32) + value[half:rows]
    keep_out[...] = low(jnp.where(upper, second, first))
    here_ref[...] = low(value[rows : rows + size])
    passed = value[rows + size : rows + 2 * size]
    on_ref[...] = low(passed)
    extra = [ref[...].astype(F32) for ref in own_refs]
    if len(extra) < 2:
        extra.append(passed)
    give_out[...] = low(jnp.concatenate([jnp.where(upper, first, second), *extra], axis=0))


def carry_step(bit, keep, arrived, own, place, capacity):
    rows, width = keep.shape[0] // 2, keep.shape[1]
    return call(
        lambda *refs: halve_carry(bit, *refs), "halve_carry",
        [shape(rows, width), shape(rows + min(len(own) + 1, 2) * capacity, width),
         shape(capacity, width), shape(capacity, width)],
        (place, keep, arrived, *own), flops=4 * rows * width, size=0,
    )


def scatter_plain(blocks, dims):
    lon, lat, sub = dims
    count, rows, width = blocks.shape
    depth = rows // (lon * lat * sub)
    blocks = blocks.reshape(count, lon, lat, sub, depth, width)
    blocks = blocks.transpose(3, 2, 1, 0, 4, 5)
    for axis in ("sub", "lat", "lon"):
        blocks = lax.psum_scatter(blocks, axis, scatter_dimension=0, tiled=False)
    return blocks.astype(F32)


def call(kernel, name, outs, args, flops, loads=(), scratch=(), size=None):
    if size is None:
        size = sum(a.size * a.dtype.itemsize for a in (*args, *outs, *loads))
    args = (*(pltpu.with_memory_space_constraint(a, pltpu.HBM) for a in loads), *args)
    scratch = list(scratch)
    if loads:
        scratch.append(pltpu.SemaphoreType.DMA((len(loads),)))
    in_specs = [pl.BlockSpec(memory_space=pltpu.HBM)] * len(loads)
    in_specs += [pl.BlockSpec(memory_space=pltpu.VMEM)] * (len(args) - len(loads))
    return pl.pallas_call(
        kernel,
        out_shape=[shape(*a.shape, dtype=a.dtype) for a in loads] + list(outs),
        in_specs=in_specs,
        out_specs=[pl.BlockSpec(memory_space=pltpu.VMEM)] * (len(outs) + len(loads)),
        scratch_shapes=scratch,
        compiler_params=pltpu.CompilerParams(vmem_limit_bytes=16 * 1024 * 1024),
        cost_estimate=pl.CostEstimate(flops=flops, bytes_accessed=size, transcendentals=0),
        name=name,
    )(*args)


def exchange(parts, dims):
    column = dims[1] * dims[2]
    count = dims[0]
    other = [(i, (i - 1 + 2 * (i % 2)) % count) for i in range(count)]
    far = lax.ppermute(parts[column], "lon", other)
    near = lax.ppermute(parts[column - 1], "lon", [(i, i ^ 1) for i in range(count)])
    arrived = [
        lax.ppermute(parts[r - 1], COLUMN, [(i, i ^ r) for i in range(column)])
        for r in range(column - 1, 0, -1)
    ]
    return (far, near, *arrived)


def shape(*dims, dtype=BF):
    return jax.ShapeDtypeStruct(dims, dtype)


def start_loads(sources, targets, sems):
    copies = [
        pltpu.make_async_copy(source, target, sems.at[at])
        for at, (source, target) in enumerate(zip(sources, targets))
    ]
    for copy in copies:
        copy.start()
    return copies


def first_payload(column, capacity, count, *refs):
    sources, ints_ref, targets = refs[:count], refs[count], refs[count + 1 : 2 * count + 1]
    sends_ref, *pay_refs, sems = refs[2 * count + 1 :]
    grid_ref = targets[0]
    grid_load, *loads = start_loads(sources, targets, sems)
    chosen = grid_ref.shape[0]
    ints = ints_ref[...]
    base = 2 * capacity + BORDER
    me, odd = ints[0:1, base : base + 1], ints[0:1, base + 1 : base + 2]
    sends = as_column(ints[:, :capacity], capacity, column, me, odd)
    sends_ref[...] = sends
    pick = low(hot(sends == iota(sends.shape[0], chosen, 1)))
    grid_load.wait()
    store_parts(pay_refs, [dot(pick, grid_ref[...])])
    for load in loads:
        load.wait()


def embed_local(
    column, capacity, mesh_far, merge_far, cot_far, ints_ref, senders_ref, grid_ref, weight_ref,
    target_ref, sends_ref, mesh_ref, merge_ref, cot_ref,
    sum_ref, slope_ref, sends_row_ref, incoming_ref, bounds_ref, bounds_row_ref, senders_t_ref,
    senders_out_ref, place_ref, sems,
):
    loads = start_loads((mesh_far, merge_far, cot_far), (mesh_ref, merge_ref, cot_ref), sems)
    chosen = grid_ref.shape[0]
    nodes = sum_ref.shape[0]
    taken = sends_ref.shape[0]
    act, slope = silu_both(dot(grid_ref[...], weight_ref[...]))
    slope_ref[...] = low(slope)
    sent = jnp.max(hot(sends_ref[...] == iota(taken, chosen, 1)), axis=0, keepdims=True)
    label = jnp.where(sent > 0.0, nodes, target_ref[...])
    sum_ref[...] = dot(low(hot(label == iota(nodes, chosen, 0))), low(act))
    ints = ints_ref[...]
    base = 2 * capacity + BORDER
    place_ref[...] = ints[:, base:]
    me, odd = ints[0:1, base : base + 1], ints[0:1, base + 1 : base + 2]
    sends, incoming = ints[:, :capacity], ints[:, capacity : 2 * capacity]
    bounds = ints[:, 2 * capacity : base]
    sends_row_ref[...] = as_row(sends, capacity, column, me, odd)
    incoming_ref[...] = as_row(incoming, capacity, column, me, odd)
    bounds_ref[...] = as_column(bounds, BORDER, column, me, odd)
    bounds_row_ref[...] = as_row(bounds, BORDER, column, me, odd)
    senders = senders_ref[...]
    degree = senders.shape[0]
    offset = senders - nodes
    slot = offset // BORDER
    far = jnp.where(slot == column, column - odd, column - 1 + odd)
    at = jnp.where(slot < column, jnp.bitwise_xor(slot, me) - 1, far)
    senders = jnp.where(offset < 0, senders, nodes + at * BORDER + offset % BORDER)
    senders_t_ref[...] = senders
    filler = jnp.zeros((8 - degree, nodes), I32)
    senders_out_ref[...] = jnp.concatenate([senders, filler], axis=0).T
    for load in loads:
        load.wait()


def merge_nodes(peers, *refs):
    arr_refs, refs = refs[:peers][::-1], refs[peers:]
    (incoming_ref, embed_ref, local_ref, mesh_ref, weight_ref, bounds_ref, senders_t_ref, cot_ref,
     merged_ref, state_ref, slope_ref, lat_ref, *pay_refs) = refs
    nodes = mesh_ref.shape[0]
    taken = incoming_ref.shape[1]
    halo = peers * BORDER
    lat = jnp.concatenate([ref[...] for ref in arr_refs], axis=0)
    lat_ref[...] = lat
    act, slope = silu_both(dot(lat, embed_ref[...]))
    slope_ref[...] = low(slope)
    place = low(hot(incoming_ref[...] == iota(nodes, taken, 0)))
    merged = low(local_ref[...] + dot(place, low(act)))
    merged_ref[...] = merged
    state = low(mesh_ref[...].astype(F32) + dot(merged, weight_ref[...]))
    state_ref[...] = state
    border = low(hot(bounds_ref[...] == iota(halo, nodes, 1)))
    back = low(receivers(senders_t_ref[...], halo))
    store_parts(
        pay_refs,
        [dot(border, state), dot(back, state), dot(border, merged), dot(back, cot_ref[...])],
    )


def local_edges(senders, degree, sent, recv, each):
    nodes = senders.shape[0]
    total = None
    ids = iota(nodes, nodes, 1)
    for j in range(degree):
        act, slope = silu_both(dot(low(hot(senders[:, j : j + 1] == ids)), sent) + recv)
        total = act if total is None else total + act
        each(j, slope)
    return total


def edge_targets(senders_t):
    degree, nodes = senders_t.shape
    ids = iota(nodes, nodes, 0)
    return jnp.concatenate(
        [low(hot(senders_t[j : j + 1, :] == ids)) for j in range(degree)], axis=1
    )


def forward_local(
    state_ref, send_ref, recv_ref, senders_ref, senders_t_ref, bounds_ref,
    total_ref, slope_ref, recv_n_ref, sent_b_ref,
):
    state = state_ref[...]
    nodes = state.shape[0]
    halo = bounds_ref.shape[0]
    sent = low(dot(state, send_ref[0]))
    recv = dot(state, recv_ref[0])

    def keep(j, slope):
        slope_ref[j] = low(slope)

    total_ref[...] = local_edges(senders_ref[...], senders_t_ref.shape[0], sent, recv, keep)
    back = low(receivers(senders_t_ref[...], halo))
    recv_n_ref[...] = dot(low(dot(back, state)), recv_ref[0])
    sent_b_ref[...] = low(dot(low(hot(bounds_ref[...] == iota(halo, nodes, 1))), sent))


def forward_halo(peers, *refs):
    arr_refs, refs = refs[:peers][::-1], refs[peers:]
    (recv_n_ref, total_ref, state_ref, send_ref, update_ref, senders_ref, senders_t_ref,
     bounds_ref, summed_ref, out_ref, pre_ref, rows_ref, back_ref, merged_ref, cot_ref,
     *pay_refs) = refs
    nodes = state_ref.shape[0]
    degree = senders_t_ref.shape[0]
    halo = peers * BORDER
    rows, back, merged, cot = split_parts(
        arr_refs, (0, BORDER, 2 * BORDER, 3 * BORDER), (BORDER,) * 4
    )
    rows_ref[...], back_ref[...] = low(rows), low(back)
    merged_ref[...], cot_ref[...] = low(merged), low(cot)
    pre = low(dot(low(rows), send_ref[0])).astype(F32) + recv_n_ref[...]
    pre_ref[...] = pre
    place = low(receivers_t(senders_ref[...], degree, halo))
    extra = silu(pre) - silu(recv_n_ref[...])
    summed = low(total_ref[...] + dot(place, low(extra)))
    summed_ref[...] = summed
    state = low(state_ref[...].astype(F32) + dot(summed, update_ref[0]))
    out_ref[...] = state
    border = low(hot(bounds_ref[...] == iota(halo, nodes, 1)))
    back = low(receivers(senders_t_ref[...], halo))
    store_parts(pay_refs, [dot(border, state), dot(back, state)])


def turn_local(
    state_ref, send_ref, recv_ref, update_ref, cot_ref, cot_r_ref, pre_ref, recv_n0_ref, back0_ref,
    sent_b0_ref, senders_ref, senders_t_ref, bounds_ref,
    total_ref, grecv_ref, gsent_ref, recv_n_ref, sent_b_ref, gsum_n_ref, gsum_r_ref,
    slope_k_ref, slope_d_ref, slope_r_ref, gpre_ref,
):
    halo = bounds_ref.shape[0]
    slope = silu_slope(pre_ref[...])
    slope_k_ref[...] = low(slope)
    slope_d_ref[...] = low(slope - silu_slope(recv_n0_ref[...]))
    pre = sent_b0_ref[...].astype(F32) + dot(back0_ref[...], recv_ref[0])
    slope_r_ref[...] = low(silu_slope(pre))
    state = state_ref[...]
    nodes = state.shape[0]
    sent = low(dot(state, send_ref[1]))
    recv = dot(state, recv_ref[1])
    gsum = low(dot(cot_ref[...], update_ref[1], NT))
    grad = gsum.astype(F32)
    grecv = []

    def back_edge(j, slope):
        gpre = grad * slope
        grecv.append(gpre if j == 0 else grecv[-1] + gpre)
        gpre_ref[j * nodes : (j + 1) * nodes, :] = low(gpre)

    degree = senders_t_ref.shape[0]
    total_ref[...] = local_edges(senders_ref[...], degree, sent, recv, back_edge)
    grecv_ref[...] = grecv[-1]
    gsent_ref[...] = dot(edge_targets(senders_t_ref[...]), gpre_ref[...])
    back = low(receivers(senders_t_ref[...], halo))
    recv_n_ref[...] = dot(low(dot(back, state)), recv_ref[1])
    sent_b_ref[...] = low(dot(low(hot(bounds_ref[...] == iota(halo, nodes, 1))), sent))
    gsum_n_ref[...] = low(dot(back, gsum))
    gsum_r_ref[...] = low(dot(cot_r_ref[...], update_ref[1], NT))


def turn_halo(peers, *refs):
    arr_refs, refs = refs[:peers][::-1], refs[peers:]
    (recv_n_ref, sent_b_ref, gsum_n_ref, gsum_r_ref, total_ref, grecv_ref, gsent_ref, cot_ref,
     send_ref, recv_ref, senders_ref, senders_t_ref, bounds_ref, summed_ref, grecv_out_ref,
     gsent_out_ref, gin_ref, *pay_refs) = refs
    nodes = cot_ref.shape[0]
    degree = senders_t_ref.shape[0]
    halo = peers * BORDER
    rows, back = split_parts(arr_refs, (0, BORDER), (BORDER,) * 2)
    pre = low(dot(low(rows), send_ref[1])).astype(F32) + recv_n_ref[...]
    act, slope = silu_both(pre)
    place = low(receivers_t(senders_ref[...], degree, halo))
    base, base_slope = silu_both(recv_n_ref[...])
    gpre = low(gsum_n_ref[...].astype(F32) * (slope - base_slope))
    grecv = low(grecv_ref[...] + dot(place, gpre))
    pre = sent_b_ref[...].astype(F32) + dot(low(back), recv_ref[1])
    gpre = low(gsum_r_ref[...].astype(F32) * silu_slope(pre))
    border = low(hot(bounds_ref[...] == iota(nodes, halo, 0)))
    gsent = low(gsent_ref[...] + dot(border, gpre))
    gin = cot_ref[...].astype(F32) + dot(grecv, recv_ref[1], NT) + dot(gsent, send_ref[1], NT)
    gin = low(gin)
    gin_ref[...] = gin
    store_parts(pay_refs, [dot(low(receivers(senders_t_ref[...], halo)), gin)])
    summed_ref[...] = low(total_ref[...] + dot(place, low(act - base)))
    grecv_out_ref[...] = grecv
    gsent_out_ref[...] = gsent


def last_weights(
    dims, place_ref, state_ref, summed_ref, cot_ref, grecv_ref, gsent_ref, update_ref,
    keep_ref, give_ref, mesh_ref,
):
    state, summed = state_ref[...], summed_ref[...]

    def store(at, value):
        store_blocks(keep_ref, give_ref, at, 3, value, dims, place_ref)

    both = dot(state, jnp.concatenate([gsent_ref[...], grecv_ref[...]], axis=1), TN)
    store(0, both[:, : state.shape[1]])
    store(1, both[:, state.shape[1] :])
    store(2, dot(summed, cot_ref[...], TN))
    mesh_ref[...] = low(state.astype(F32) + dot(summed, update_ref[1]))


def back_local(
    dims, place_ref, gin_ref, slope_ref, slope_k_ref, slope_d_ref, send_ref, recv_ref, update_ref,
    senders_ref, senders_t_ref, state_ref, rows_ref, summed_ref, merged_ref, merged_r_ref,
    after_ref, part_ref, keep_ref, give_ref, keep2_ref, give2_ref, gpre_ref,
):
    nodes = gin_ref.shape[0]
    halo = slope_k_ref.shape[0]
    degree = senders_t_ref.shape[0]
    gin = gin_ref[...]
    gsum = low(dot(gin, update_ref[0], NT))
    place = low(receivers_t(senders_ref[...], degree, halo))
    back = low(receivers(senders_t_ref[...], halo))
    gsum_n = low(dot(back, gsum))
    gpre_k = gsum_n * slope_k_ref[...]
    grecv = dot(place, gsum_n * slope_d_ref[...])
    for j in range(degree):
        gpre = gsum * slope_ref[j]
        grecv = grecv + gpre.astype(F32)
        gpre_ref[j * nodes : (j + 1) * nodes, :] = gpre
    gsent = dot(edge_targets(senders_t_ref[...]), gpre_ref[...])
    grecv, gsent = low(grecv), low(gsent)
    part = gin.astype(F32) + dot(grecv, recv_ref[0], NT) + dot(gsent, send_ref[0], NT)
    part_ref[...] = part
    state = state_ref[...]

    def store(at, value):
        store_blocks(keep_ref, give_ref, at, 2, value, dims, place_ref)

    def store2(at, value):
        store_blocks(keep2_ref, give2_ref, at, 2, value, dims, place_ref)

    both = dot(state, jnp.concatenate([gsent, grecv], axis=1), TN)
    store(0, both[:, : state.shape[1]] + dot(rows_ref[...], gpre_k, TN))
    store(1, both[:, state.shape[1] :])
    store2(0, dot(summed_ref[...], gin, TN))
    far = low(dot(gpre_k, send_ref[0], NT))
    store2(1, dot(merged_ref[...], low(part), TN) + dot(merged_r_ref[...], far, TN))


def embed_back(peers, dims, carry, *refs):
    arr_refs, refs = refs[:peers][::-1], refs[peers:]
    (place_ref, slope_r_ref, part_ref, update_ref, send_ref, merge_ref, bounds_ref, target_ref,
     sends_ref, incoming_ref, slope_g_ref, slope_a_ref, grid_ref, lat_ref, embed_ref,
     gpre_ref, keep_ref, give_ref, *pay_refs) = refs
    nodes = part_ref.shape[0]
    halo = peers * BORDER
    chosen = grid_ref.shape[0]
    taken = sends_ref.shape[0]
    (arrived,) = split_parts(arr_refs, (0,), (BORDER,))
    gsum = low(dot(low(arrived), update_ref[0], NT)).astype(F32)
    gpre = low(gsum * slope_r_ref[...].astype(F32))
    border = low(hot(bounds_ref[...] == iota(nodes, halo, 0)))
    gsent = low(dot(border, gpre))
    gin = low(part_ref[...] + dot(gsent, send_ref[0], NT))
    gmerged = low(dot(gin, merge_ref[...], NT))
    place = low(hot(incoming_ref[...] == iota(nodes, taken, 0)))
    gpre_a = low(dot(place, gmerged, TN) * slope_a_ref[...].astype(F32))
    sent = jnp.max(hot(sends_ref[...] == iota(taken, chosen, 1)), axis=0, keepdims=True)
    label = jnp.where(sent > 0.0, nodes, target_ref[...])
    pick = low(hot(label == iota(nodes, chosen, 0)))
    gpre_g = low(dot(pick, gmerged, TN) * slope_g_ref[...].astype(F32))
    gpre_ref[...] = gpre_g
    grad = dot(grid_ref[...], gpre_g, TN) + dot(lat_ref[...], gpre_a, TN)
    store_blocks(keep_ref, give_ref, 0, 1, grad, dims, place_ref)
    rows = dot(gpre_a, embed_ref[...], NT)
    store_parts(pay_refs, [rows])
    if carry:
        size = taken // peers
        start = keep_ref.shape[0]
        give_ref[start : start + 2 * size, :] = low(
            jnp.concatenate([rows[:size], rows[2 * size : 3 * size]], axis=0)
        )


def grid_local(gpre_ref, weight_ref, out_ref):
    out_ref[...] = low(dot(gpre_ref[...], weight_ref[...], NT))


def grid_patch(local_ref, sends_ref, arr_refs, out_ref):
    chosen = local_ref.shape[0]
    taken = sends_ref.shape[1]
    size = taken // len(arr_refs)
    place = low(hot(sends_ref[...] == iota(chosen, taken, 0)))
    rows = [ref[...].astype(F32) for ref in arr_refs]
    rows = low(jnp.concatenate([row[row.shape[0] - size :] for row in rows], axis=0))
    out_ref[...] = low(local_ref[...].astype(F32) + dot(place, rows))


def grid_place(peers, *refs):
    arr_refs, (local_ref, sends_ref, out_ref) = refs[:peers][::-1], refs[peers:]
    grid_patch(local_ref, sends_ref, arr_refs, out_ref)


def sum_last(sums, outs):
    (keep1_ref, arr1_ref, keep0_ref, arr0_ref, keep2_ref, arr2_ref, keep_e_ref, arr_e_ref) = sums
    embed_ref, merge_ref, send_ref, recv_ref, update_ref = outs
    last = keep1_ref[...].astype(F32) + arr1_ref[...].astype(F32)
    first = keep0_ref[...].astype(F32) + arr0_ref[...].astype(F32)
    second = keep2_ref[...].astype(F32) + arr2_ref[...].astype(F32)
    depth = embed_ref.shape[0]
    embed_ref[...] = keep_e_ref[...].astype(F32) + arr_e_ref[:depth, :].astype(F32)
    for at, ref in enumerate((send_ref, recv_ref, update_ref)):
        ref[1] = last[at * depth : (at + 1) * depth]
    send_ref[0], recv_ref[0], update_ref[0] = first[:depth], first[depth:], second[:depth]
    merge_ref[...] = second[depth:]


def finish(*refs):
    sum_last(refs[:8], refs[8:])


def finish_all(*refs):
    sums, rows, (local_ref, sends_ref), outs = refs[:8], refs[8:12], refs[12:14], refs[14:]
    grid_patch(local_ref, sends_ref, (*rows, sums[7]), outs[0])
    sum_last(sums, outs[1:])


def body(
    dims,
    grid_latent, mesh_latent, cotangent, embed_weight, merge_weight, send_weight, recv_weight,
    update_weight, target_row, send_rows, incoming_rows, border_mesh_rows, mesh_senders,
):
    chosen, width = grid_latent.shape
    nodes, degree = mesh_senders.shape
    slots, capacity = send_rows.shape[1:]
    column = dims[1] * dims[2]
    peers = slots - 1
    halo = peers * BORDER
    taken = peers * capacity
    total = dims[0] * dims[1] * dims[2]
    bits = (total - 1).bit_length()
    carry = dims == (4, 2, 2) and fine(width, dims)
    spot = lax.axis_index(GROUP)
    place = [lax.axis_index(COLUMN), lax.axis_index("lon") % 2]
    place += [(spot >> bit) % 2 for bit in range(bits)]
    place = jnp.broadcast_to(jnp.stack(place).astype(I32)[None], (slots, 2 + bits))
    ints = jnp.concatenate([send_rows[0], incoming_rows[0], border_mesh_rows[0], place], axis=1)
    unit = 2 * nodes * width * width

    loads = (grid_latent, embed_weight, target_row.reshape(1, chosen), mesh_senders.T)
    grid, embed, targets, senders_raw, sends, *pay1 = call(
        lambda *refs: first_payload(column, capacity, len(loads), *refs), "first_payload",
        [shape(taken, 1, dtype=I32)] + [shape(capacity, width)] * peers,
        (ints,), flops=unit // 2, loads=loads,
    )
    arr1 = exchange(pay1, dims)
    (mesh, merge, cot, local, slope_g, sends_row, incoming, bounds, bounds_row, senders_t, senders,
     place) = call(
        lambda *refs: embed_local(column, capacity, *refs), "embed_local",
        [shape(nodes, width, dtype=F32), shape(chosen, width), shape(1, taken, dtype=I32),
         shape(1, taken, dtype=I32), shape(halo, 1, dtype=I32), shape(1, halo, dtype=I32),
         shape(degree, nodes, dtype=I32), shape(nodes, 8, dtype=I32),
         shape(slots, 2 + bits, dtype=I32)],
        (ints, senders_raw, grid, embed, targets, sends), flops=3 * unit,
        loads=(mesh_latent, merge_weight, cotangent),
    )
    merged, state0, slope_a, lat_a, *pay2 = call(
        lambda *refs: merge_nodes(peers, *refs), "merge_nodes",
        [shape(nodes, width), shape(nodes, width), shape(taken, width), shape(taken, width)]
        + [shape(4 * BORDER, width)] * peers,
        (*arr1, incoming, embed, local, mesh, merge, bounds, senders_t, cot),
        flops=2 * unit,
    )
    arr2 = exchange(pay2, dims)
    total0, slope0, recv_n0, sent_b0 = call(
        forward_local, "forward_local",
        [shape(nodes, width, dtype=F32), shape(degree, nodes, width),
         shape(halo, width, dtype=F32), shape(halo, width)],
        (state0, send_weight, recv_weight, senders, senders_t, bounds), flops=6 * unit,
    )
    summed0, state1, pre0, rows0, back0, merged_r, cot_r, *pay3 = call(
        lambda *refs: forward_halo(peers, *refs), "forward_halo",
        [shape(nodes, width), shape(nodes, width), shape(halo, width, dtype=F32)]
        + [shape(halo, width)] * 4 + [shape(2 * BORDER, width)] * peers,
        (*arr2, recv_n0, total0, state0, send_weight, update_weight, senders, senders_t, bounds),
        flops=2 * unit,
    )
    arr3 = exchange(pay3, dims)
    (total1, grecv_l, gsent_l, recv_n1, sent_b1, gsum_n1, gsum_r1, slope_k0, slope_d0,
     slope_r0) = call(
        turn_local, "turn_local",
        [shape(nodes, width, dtype=F32)] * 3 + [shape(halo, width, dtype=F32)]
        + [shape(halo, width)] * 6,
        (state1, send_weight, recv_weight, update_weight, cot, cot_r, pre0, recv_n0, back0,
         sent_b0, senders, senders_t, bounds),
        flops=10 * unit, scratch=[pltpu.VMEM((degree * nodes, width), BF)],
    )
    summed1, grecv1, gsent1, gin1, *pay4 = call(
        lambda *refs: turn_halo(peers, *refs), "turn_halo",
        [shape(nodes, width)] * 4 + [shape(BORDER, width)] * peers,
        (*arr3, recv_n1, sent_b1, gsum_n1, gsum_r1, total1, grecv_l, gsent_l, cot,
         send_weight, recv_weight, senders, senders_t, bounds_row),
        flops=3 * unit,
    )
    arr4 = exchange(pay4, dims)
    keep1, give1, mesh_out = call(
        lambda *refs: last_weights(dims, *refs), "last_weights",
        blocks_shapes(3, width, width, dims) + [shape(nodes, width)],
        (place, state1, summed1, cot, grecv1, gsent1, update_weight), flops=4 * unit,
    )
    split = fine(width, dims)
    if split:
        give1, last = lax.optimization_barrier((give1, arr4[-1]))
        arr4 = (*arr4[:-1], last)
        keep1, give1 = halve_step(1, keep1, swap(give1, 0, dims), place)
    part0, keep0, give0, keep2, give2 = call(
        lambda *refs: back_local(dims, *refs), "back_local",
        [shape(nodes, width, dtype=F32)] + blocks_shapes(2, width, width, dims) * 2,
        (place, gin1, slope0, slope_k0, slope_d0, send_weight, recv_weight, update_weight, senders,
         senders_t, state0, rows0, summed0, merged, merged_r, keep1),
        flops=10 * unit, scratch=[pltpu.VMEM((degree * nodes, width), BF)],
    )
    if split:
        give0, give2, *arr4 = lax.optimization_barrier((give0, give2, *arr4))
        keep0, give0 = halve_step(1, keep0, swap(give0, 0, dims), place)
        keep0, *arr4 = lax.optimization_barrier((keep0, *arr4))
    shapes = blocks_shapes(1, width, width, dims)
    if carry:
        shapes[1] = shape(shapes[1].shape[0] + 2 * capacity, width)
    gpre_g, keep_e, give_e, *pay5 = call(
        lambda *refs: embed_back(peers, dims, carry, *refs), "embed_back",
        [shape(chosen, width)] + shapes + [shape(capacity, width)] * peers,
        (*arr4, place, slope_r0, part0, update_weight, send_weight, merge, bounds_row,
         targets, sends, incoming, slope_g, slope_a, grid, lat_a, embed),
        flops=6 * unit,
    )
    depth = width // total
    if not split:
        arr5 = exchange(pay5, dims)
        last, first, second, embed_sum = (
            scatter_plain(blocks, dims) for blocks in (keep1, keep0, keep2, keep_e)
        )
        plain = [jnp.stack([a, last[i]]) for i, a in enumerate((first[0], first[1], second[0]))]
        plain = [embed_sum[0], second[1], *plain]
    elif not carry:
        arr5 = exchange(pay5, dims)
        sums = [
            rest_of_halving(1, keep1, give1, place, dims),
            rest_of_halving(1, keep0, give0, place, dims),
            rest_of_halving(0, keep2, give2, place, dims),
            rest_of_halving(0, keep_e, give_e, place, dims),
        ]
    else:
        arr1 = swap(give1, 1, dims)
        arr0 = swap(give0, 1, dims)
        arr2 = swap(give2, 0, dims)
        (local_rows,) = call(
            grid_local, "grid_local", [shape(chosen, width)], (gpre_g, embed), flops=0, size=0
        )
        arr_e, arr1 = lax.optimization_barrier((swap(give_e, 0, dims), arr1))
        keep1, local_rows = lax.optimization_barrier((keep1, local_rows))
        keep1, give1 = halve_step(2, keep1, arr1, place)
        arr1 = swap(give1, 2, dims)
        keep_e, keep1 = lax.optimization_barrier((keep_e, keep1))
        keep_e, give_e, from_sub, _ = carry_step(1, keep_e, arr_e, pay5[1:2], place, capacity)
        arr_e = swap(give_e, 1, dims)
        keep2, keep_e = lax.optimization_barrier((keep2, keep_e))
        keep2, give2 = halve_step(1, keep2, arr2, place)
        arr2 = swap(give2, 1, dims)
        keep0, keep2 = lax.optimization_barrier((keep0, keep2))
        keep0, give0 = halve_step(2, keep0, arr0, place)
        arr0 = swap(give0, 2, dims)
        keep1, keep0 = lax.optimization_barrier((keep1, keep0))
        keep1, give1 = halve_step(3, keep1, arr1, place)
        arr1 = swap(give1, 3, dims)
        keep2, keep1 = lax.optimization_barrier((keep2, keep1))
        keep2, give2 = halve_step(2, keep2, arr2, place)
        arr2 = swap(give2, 2, dims)
        keep0, keep2 = lax.optimization_barrier((keep0, keep2))
        keep0, give0 = halve_step(3, keep0, arr0, place)
        arr0 = swap(give0, 3, dims)
        keep_e, keep0, arr1 = lax.optimization_barrier((keep_e, keep0, arr1))
        keep_e, give_e, from_lat, from_diag = carry_step(
            2, keep_e, arr_e, pay5[3:], place, capacity
        )
        arr_e = swap(give_e, 2, dims)
        keep2, keep_e = lax.optimization_barrier((keep2, keep_e))
        keep2, give2 = halve_step(3, keep2, arr2, place)
        arr2 = swap(give2, 3, dims)
        keep_e, keep2, arr0 = lax.optimization_barrier((keep_e, keep2, arr0))
        keep_e, give_e, from_near, _ = carry_step(3, keep_e, arr_e, (), place, capacity)
        arr_e = swap(give_e, 3, dims)
        sums = ((keep1, arr1), (keep0, arr0), (keep2, arr2), (keep_e, arr_e))
    grads = [shape(depth, width, dtype=F32)] * 2 + [shape(2, depth, width, dtype=F32)] * 3
    if carry:
        return (mesh_out, *call(
            finish_all, "finish_all", [shape(chosen, width)] + grads,
            (*(part for pair in sums for part in pair), from_sub, from_lat, from_diag, from_near,
             local_rows, sends_row),
            flops=unit,
        ))
    (local_rows,) = call(
        grid_local, "grid_local", [shape(chosen, width)], (gpre_g, embed), flops=2 * unit
    )
    (grid_grad,) = call(
        lambda *refs: grid_place(peers, *refs), "grid_place", [shape(chosen, width)],
        (*arr5, local_rows, sends_row), flops=unit,
    )
    if split:
        grads = call(
            finish, "finish", grads, [part for pair in sums for part in pair],
            flops=8 * depth * width,
        )
    else:
        grads = plain
    return (mesh_out, grid_grad, *grads)


def solution(mesh):
    split = ("groups", "lon", "lat", "sub")
    dims = tuple(mesh.shape[axis] for axis in GROUP)
    rows = P(split, None)
    whole = P("groups", GROUP, None)
    in_specs = (
        rows, rows, rows, P(), P(), P(), P(), P(), P(split), P(split, None, None),
        P(split, None, None), P(split, None, None), rows,
    )
    out_specs = (rows, rows, rows, rows, whole, whole, whole)
    return jax.shard_map(
        lambda *args: body(dims, *args),
        mesh=mesh, in_specs=in_specs, out_specs=out_specs, check_vma=False,
    )
```

```python
import jax
import jax.numpy as jnp
from jax import lax
from jax.experimental import pallas as pl
from jax.experimental.pallas import tpu as pltpu
from jax.sharding import PartitionSpec as P

BF = jnp.bfloat16
F32 = jnp.float32
I32 = jnp.int32
NN = (((1,), (0,)), ((), ()))
NT = (((1,), (1,)), ((), ()))
TN = (((0,), (0,)), ((), ()))
BORDER = 8
GROUP = ("lon", "lat", "sub")
COLUMN = ("lat", "sub")


def dot(a, b, dims=NN):
    return lax.dot_general(a, b, dims, preferred_element_type=F32)


def low(value):
    return value.astype(BF)


def sigmoid(value):
    return 0.5 * jnp.tanh(0.5 * value) + 0.5


def silu(value):
    return value * sigmoid(value)


def silu_both(value):
    sig = sigmoid(value)
    act = value * sig
    return act, sig + act * (1.0 - sig)


def silu_slope(value):
    return silu_both(value)[1]


def iota(rows, columns, dim):
    return lax.broadcasted_iota(I32, (rows, columns), dim)


def hot(mask):
    return jnp.where(mask, 1.0, 0.0)


def slot_rows(ref):
    return jnp.concatenate([ref[s] for s in range(ref.shape[0])], axis=0)


def slot_of(at, column, me, odd):
    far = jnp.where(at == column - 1, column + 1 - odd, column + odd)
    return jnp.where(at < column - 1, jnp.bitwise_xor(at + 1, me), far)


def as_column(values, wide, column, me, odd):
    slots = values.shape[0]
    count = (slots - 1) * wide
    row = iota(count, slots, 0)
    pick = low(hot(slot_of(row // wide, column, me, odd) == iota(count, slots, 1)))
    found = 16.0 * dot(pick, low((values // 16).astype(F32)))
    found = found + dot(pick, low((values % 16).astype(F32)))
    keep = iota(count, wide, 0) % wide == iota(count, wide, 1)
    return jnp.sum(jnp.where(keep, found, 0.0), axis=1, keepdims=True).astype(I32)


def as_row(values, wide, column, me, odd):
    slots = values.shape[0]
    count = (slots - 1) * wide
    pick = low(hot(iota(wide, count, 1) % wide == iota(wide, count, 0)))
    found = 16.0 * dot(low((values // 16).astype(F32)), pick)
    found = found + dot(low((values % 16).astype(F32)), pick)
    at = iota(slots, count, 1) // wide
    keep = slot_of(at, column, me, odd) == iota(slots, count, 0)
    return jnp.sum(jnp.where(keep, found, 0.0), axis=0, keepdims=True).astype(I32)


def split_parts(refs, starts, sizes):
    values = [ref[...].astype(F32) for ref in refs]
    return [
        jnp.concatenate([value[start : start + size] for value in values], axis=0)
        for start, size in zip(starts, sizes)
    ]


def store_parts(refs, parts):
    peers = len(refs)
    for at, ref in enumerate(refs):
        rows = []
        for part in parts:
            size = part.shape[0] // peers
            rows.append(part[at * size : (at + 1) * size])
        ref[...] = low(rows[0] if len(rows) == 1 else jnp.concatenate(rows, axis=0))


def receivers(senders_t, halo):
    degree, nodes = senders_t.shape
    found = jnp.zeros((halo, nodes), F32)
    ids = iota(halo, nodes, 0) + nodes
    for j in range(degree):
        found = found + hot(senders_t[j : j + 1, :] == ids)
    return found


def receivers_t(senders, degree, halo):
    nodes = senders.shape[0]
    found = jnp.zeros((nodes, halo), F32)
    ids = iota(nodes, halo, 1) + nodes
    for j in range(degree):
        found = found + hot(senders[:, j : j + 1] == ids)
    return found


def fine(rows, dims):
    return (rows // (dims[0] * dims[1] * dims[2])) % 16 == 0


def reverse_bits(block, bits):
    spot = 0
    for bit in range(bits):
        spot = 2 * spot + (block >> bit) % 2
    return spot


def store_blocks(keep_ref, give_ref, at, count, value, dims, bits_ref):
    value = low(value)
    rows = value.shape[0]
    total = dims[0] * dims[1] * dims[2]
    depth = rows // total
    if not fine(rows, dims):
        keep_ref[at] = value
        return
    bits = (total - 1).bit_length()
    upper = bits_ref[0:1, 2:3] == 1
    for block in range(0, total, 2):
        start = reverse_bits(block, bits) * count * depth + at * depth
        first = value[block * depth : (block + 1) * depth].astype(F32)
        second = value[(block + 1) * depth : (block + 2) * depth].astype(F32)
        keep_ref[start : start + depth, :] = low(jnp.where(upper, second, first))
        give_ref[start : start + depth, :] = low(jnp.where(upper, first, second))


def blocks_shapes(count, rows, width, dims):
    if fine(rows, dims):
        return [jax.ShapeDtypeStruct((count * rows // 2, width), BF)] * 2
    return [jax.ShapeDtypeStruct((count, rows, width), BF), jax.ShapeDtypeStruct((16, width), BF)]


def halve(bit, bits_ref, keep_ref, arr_ref, keep_out, give_out):
    half = keep_ref.shape[0] // 2
    upper = bits_ref[0:1, 2 + bit : 3 + bit] == 1
    first = keep_ref[:half, :].astype(F32) + arr_ref[:half, :].astype(F32)
    second = keep_ref[half:, :].astype(F32) + arr_ref[half:, :].astype(F32)
    keep_out[...] = low(jnp.where(upper, second, first))
    give_out[...] = low(jnp.where(upper, first, second))


def swap(block, bit, dims):
    total = dims[0] * dims[1] * dims[2]
    return lax.ppermute(block, GROUP, [(i, i ^ (1 << bit)) for i in range(total)])


def halve_step(bit, keep, arrived, place):
    rows, width = keep.shape[0] // 2, keep.shape[1]
    return call(
        lambda *refs: halve(bit, *refs), "halve", [shape(rows, width)] * 2,
        (place, keep, arrived), flops=4 * rows * width, size=0,
    )


def rest_of_halving(first, keep, give, place, dims):
    bits = (dims[0] * dims[1] * dims[2] - 1).bit_length()
    arrived = swap(give, first, dims)
    for bit in range(first + 1, bits):
        keep, give = halve_step(bit, keep, arrived, place)
        arrived = swap(give, bit, dims)
    return keep, arrived


def halve_carry(bit, count, bits_ref, keep_ref, arr_ref, *refs):
    own_refs, (keep_out, give_out, *here_refs) = refs[:count], refs[count:]
    rows = keep_ref.shape[0]
    half = rows // 2
    size = here_refs[0].shape[0]
    upper = bits_ref[0:1, 2 + bit : 3 + bit] == 1
    value = arr_ref[...].astype(F32)
    first = keep_ref[:half, :].astype(F32) + value[:half]
    second = keep_ref[half:, :].astype(F32) + value[half:rows]
    keep_out[...] = low(jnp.where(upper, second, first))
    here_refs[0][...] = low(value[rows : rows + size])
    passed = value[rows + size : rows + 2 * size]
    extra = [ref[...].astype(F32) for ref in own_refs]
    if count < 2:
        extra.append(passed)
    else:
        here_refs[1][...] = low(passed)
    give_out[...] = low(jnp.concatenate([jnp.where(upper, first, second), *extra], axis=0))


def carry_step(bit, keep, arrived, own, place, capacity):
    rows, width = keep.shape[0] // 2, keep.shape[1]
    count = len(own)
    return call(
        lambda *refs: halve_carry(bit, count, *refs), "halve_carry",
        [shape(rows, width), shape(rows + min(count + 1, 2) * capacity, width)]
        + [shape(capacity, width)] * (2 if count == 2 else 1),
        (place, keep, arrived, *own), flops=4 * rows * width, size=0,
    )


def scatter_plain(blocks, dims):
    lon, lat, sub = dims
    count, rows, width = blocks.shape
    depth = rows // (lon * lat * sub)
    blocks = blocks.reshape(count, lon, lat, sub, depth, width)
    blocks = blocks.transpose(3, 2, 1, 0, 4, 5)
    for axis in ("sub", "lat", "lon"):
        blocks = lax.psum_scatter(blocks, axis, scatter_dimension=0, tiled=False)
    return blocks.astype(F32)


def call(kernel, name, outs, args, flops, loads=(), scratch=(), size=None):
    if size is None:
        size = sum(a.size * a.dtype.itemsize for a in (*args, *outs, *loads))
    args = (*(pltpu.with_memory_space_constraint(a, pltpu.HBM) for a in loads), *args)
    scratch = list(scratch)
    if loads:
        scratch.append(pltpu.SemaphoreType.DMA((len(loads),)))
    in_specs = [pl.BlockSpec(memory_space=pltpu.HBM)] * len(loads)
    in_specs += [pl.BlockSpec(memory_space=pltpu.VMEM)] * (len(args) - len(loads))
    return pl.pallas_call(
        kernel,
        out_shape=[shape(*a.shape, dtype=a.dtype) for a in loads] + list(outs),
        in_specs=in_specs,
        out_specs=[pl.BlockSpec(memory_space=pltpu.VMEM)] * (len(outs) + len(loads)),
        scratch_shapes=scratch,
        compiler_params=pltpu.CompilerParams(vmem_limit_bytes=16 * 1024 * 1024),
        cost_estimate=pl.CostEstimate(flops=flops, bytes_accessed=size, transcendentals=0),
        name=name,
    )(*args)


def exchange(parts, dims):
    column = dims[1] * dims[2]
    count = dims[0]
    other = [(i, (i - 1 + 2 * (i % 2)) % count) for i in range(count)]
    far = lax.ppermute(parts[column], "lon", other)
    near = lax.ppermute(parts[column - 1], "lon", [(i, i ^ 1) for i in range(count)])
    arrived = [
        lax.ppermute(parts[r - 1], COLUMN, [(i, i ^ r) for i in range(column)])
        for r in range(column - 1, 0, -1)
    ]
    return (far, near, *arrived)


def shape(*dims, dtype=BF):
    return jax.ShapeDtypeStruct(dims, dtype)


def start_loads(sources, targets, sems):
    copies = [
        pltpu.make_async_copy(source, target, sems.at[at])
        for at, (source, target) in enumerate(zip(sources, targets))
    ]
    for copy in copies:
        copy.start()
    return copies


def first_payload(column, count, *refs):
    sources, place_ref, targets = refs[:count], refs[count], refs[count + 1 : 2 * count + 1]
    sends_out, *pay_refs, sems = refs[2 * count + 1 :]
    sends_ref, grid_ref = targets[:2]
    sends_load, grid_load, *loads = start_loads(sources, targets, sems)
    chosen = grid_ref.shape[0]
    me, odd = place_ref[:, 0:1], place_ref[:, 1:2]
    sends_load.wait()
    sends = slot_rows(sends_ref)
    sends = as_column(sends, sends.shape[1], column, me, odd)
    sends_out[...] = sends
    pick = low(hot(sends == iota(sends.shape[0], chosen, 1)))
    grid_load.wait()
    store_parts(pay_refs, [dot(pick, grid_ref[...])])
    for load in loads:
        load.wait()


def embed_local(
    column, mesh_far, merge_far, cot_far, place_in_ref, raw_sends_ref, raw_incoming_ref,
    raw_bounds_ref, senders_ref, grid_ref, weight_ref, target_ref, sends_ref, mesh_ref, merge_ref,
    cot_ref, sum_ref, slope_ref, sends_row_ref, incoming_ref, bounds_ref, bounds_row_ref, senders_t_ref,
    senders_out_ref, place_ref, sems,
):
    loads = start_loads((mesh_far, merge_far, cot_far), (mesh_ref, merge_ref, cot_ref), sems)
    chosen = grid_ref.shape[0]
    nodes = sum_ref.shape[0]
    taken = sends_ref.shape[0]
    act, slope = silu_both(dot(grid_ref[...], weight_ref[...]))
    slope_ref[...] = low(slope)
    sent = jnp.max(hot(sends_ref[...] == iota(taken, chosen, 1)), axis=0, keepdims=True)
    label = jnp.where(sent > 0.0, nodes, target_ref[...])
    sum_ref[...] = dot(low(hot(label == iota(nodes, chosen, 0))), low(act))
    place_ref[...] = place_in_ref[...]
    me, odd = place_in_ref[:, 0:1], place_in_ref[:, 1:2]
    raw_sends, incoming = slot_rows(raw_sends_ref), slot_rows(raw_incoming_ref)
    bounds = slot_rows(raw_bounds_ref)
    capacity = incoming.shape[1]
    sends_row_ref[...] = as_row(raw_sends, capacity, column, me, odd)
    incoming_ref[...] = as_row(incoming, capacity, column, me, odd)
    bounds_ref[...] = as_column(bounds, BORDER, column, me, odd)
    bounds_row_ref[...] = as_row(bounds, BORDER, column, me, odd)
    senders = senders_ref[...]
    degree = senders.shape[0]
    offset = senders - nodes
    slot = offset // BORDER
    far = jnp.where(slot == column, column - odd, column - 1 + odd)
    at = jnp.where(slot < column, jnp.bitwise_xor(slot, me) - 1, far)
    senders = jnp.where(offset < 0, senders, nodes + at * BORDER + offset % BORDER)
    senders_t_ref[...] = senders
    filler = jnp.zeros((8 - degree, nodes), I32)
    senders_out_ref[...] = jnp.concatenate([senders, filler], axis=0).T
    for load in loads:
        load.wait()


def merge_nodes(peers, *refs):
    arr_refs, refs = refs[:peers][::-1], refs[peers:]
    (incoming_ref, embed_ref, local_ref, mesh_ref, weight_ref, bounds_ref, senders_t_ref, cot_ref,
     merged_ref, state_ref, slope_ref, lat_ref, *pay_refs) = refs
    nodes = mesh_ref.shape[0]
    taken = incoming_ref.shape[1]
    halo = peers * BORDER
    lat = jnp.concatenate([ref[...] for ref in arr_refs], axis=0)
    lat_ref[...] = lat
    act, slope = silu_both(dot(lat, embed_ref[...]))
    slope_ref[...] = low(slope)
    place = low(hot(incoming_ref[...] == iota(nodes, taken, 0)))
    merged = low(local_ref[...] + dot(place, low(act)))
    merged_ref[...] = merged
    state = low(mesh_ref[...].astype(F32) + dot(merged, weight_ref[...]))
    state_ref[...] = state
    border = low(hot(bounds_ref[...] == iota(halo, nodes, 1)))
    back = low(receivers(senders_t_ref[...], halo))
    store_parts(
        pay_refs,
        [dot(border, state), dot(back, state), dot(border, merged), dot(back, cot_ref[...])],
    )


def local_edges(senders, degree, sent, recv, each):
    nodes = senders.shape[0]
    total = None
    ids = iota(nodes, nodes, 1)
    for j in range(degree):
        act, slope = silu_both(dot(low(hot(senders[:, j : j + 1] == ids)), sent) + recv)
        total = act if total is None else total + act
        each(j, slope)
    return total


def edge_targets(senders_t):
    degree, nodes = senders_t.shape
    ids = iota(nodes, nodes, 0)
    return jnp.concatenate(
        [low(hot(senders_t[j : j + 1, :] == ids)) for j in range(degree)], axis=1
    )


def forward_local(
    state_ref, send_ref, recv_ref, senders_ref, senders_t_ref, bounds_ref,
    total_ref, slope_ref, recv_n_ref, sent_b_ref,
):
    state = state_ref[...]
    nodes = state.shape[0]
    halo = bounds_ref.shape[0]
    sent = low(dot(state, send_ref[0]))
    recv = dot(state, recv_ref[0])

    def keep(j, slope):
        slope_ref[j] = low(slope)

    total_ref[...] = local_edges(senders_ref[...], senders_t_ref.shape[0], sent, recv, keep)
    back = low(receivers(senders_t_ref[...], halo))
    recv_n_ref[...] = dot(low(dot(back, state)), recv_ref[0])
    sent_b_ref[...] = low(dot(low(hot(bounds_ref[...] == iota(halo, nodes, 1))), sent))


def forward_halo(peers, *refs):
    arr_refs, refs = refs[:peers][::-1], refs[peers:]
    (recv_n_ref, total_ref, state_ref, send_ref, update_ref, senders_ref, senders_t_ref,
     bounds_ref, summed_ref, out_ref, pre_ref, rows_ref, back_ref, merged_ref, cot_ref,
     *pay_refs) = refs
    nodes = state_ref.shape[0]
    degree = senders_t_ref.shape[0]
    halo = peers * BORDER
    rows, back, merged, cot = split_parts(
        arr_refs, (0, BORDER, 2 * BORDER, 3 * BORDER), (BORDER,) * 4
    )
    rows_ref[...], back_ref[...] = low(rows), low(back)
    merged_ref[...], cot_ref[...] = low(merged), low(cot)
    pre = low(dot(low(rows), send_ref[0])).astype(F32) + recv_n_ref[...]
    pre_ref[...] = pre
    place = low(receivers_t(senders_ref[...], degree, halo))
    extra = silu(pre) - silu(recv_n_ref[...])
    summed = low(total_ref[...] + dot(place, low(extra)))
    summed_ref[...] = summed
    state = low(state_ref[...].astype(F32) + dot(summed, update_ref[0]))
    out_ref[...] = state
    border = low(hot(bounds_ref[...] == iota(halo, nodes, 1)))
    back = low(receivers(senders_t_ref[...], halo))
    store_parts(pay_refs, [dot(border, state), dot(back, state)])


def turn_local(
    state_ref, send_ref, recv_ref, update_ref, cot_ref, cot_r_ref, pre_ref, recv_n0_ref, back0_ref,
    sent_b0_ref, senders_ref, senders_t_ref, bounds_ref,
    total_ref, grecv_ref, gsent_ref, recv_n_ref, sent_b_ref, gsum_n_ref, gsum_r_ref,
    slope_k_ref, slope_d_ref, slope_r_ref, gpre_ref,
):
    halo = bounds_ref.shape[0]
    slope = silu_slope(pre_ref[...])
    slope_k_ref[...] = low(slope)
    slope_d_ref[...] = low(slope - silu_slope(recv_n0_ref[...]))
    pre = sent_b0_ref[...].astype(F32) + dot(back0_ref[...], recv_ref[0])
    slope_r_ref[...] = low(silu_slope(pre))
    state = state_ref[...]
    nodes = state.shape[0]
    sent = low(dot(state, send_ref[1]))
    recv = dot(state, recv_ref[1])
    gsum = low(dot(cot_ref[...], update_ref[1], NT))
    grad = gsum.astype(F32)
    grecv = []

    def back_edge(j, slope):
        gpre = grad * slope
        grecv.append(gpre if j == 0 else grecv[-1] + gpre)
        gpre_ref[j * nodes : (j + 1) * nodes, :] = low(gpre)

    degree = senders_t_ref.shape[0]
    total_ref[...] = local_edges(senders_ref[...], degree, sent, recv, back_edge)
    grecv_ref[...] = grecv[-1]
    gsent_ref[...] = dot(edge_targets(senders_t_ref[...]), gpre_ref[...])
    back = low(receivers(senders_t_ref[...], halo))
    recv_n_ref[...] = dot(low(dot(back, state)), recv_ref[1])
    sent_b_ref[...] = low(dot(low(hot(bounds_ref[...] == iota(halo, nodes, 1))), sent))
    gsum_n_ref[...] = low(dot(back, gsum))
    gsum_r_ref[...] = low(dot(cot_r_ref[...], update_ref[1], NT))


def turn_halo(peers, *refs):
    arr_refs, refs = refs[:peers][::-1], refs[peers:]
    (recv_n_ref, sent_b_ref, gsum_n_ref, gsum_r_ref, total_ref, grecv_ref, gsent_ref, cot_ref,
     send_ref, recv_ref, senders_ref, senders_t_ref, bounds_ref, summed_ref, grecv_out_ref,
     gsent_out_ref, gin_ref, *pay_refs) = refs
    nodes = cot_ref.shape[0]
    degree = senders_t_ref.shape[0]
    halo = peers * BORDER
    rows, back = split_parts(arr_refs, (0, BORDER), (BORDER,) * 2)
    pre = low(dot(low(rows), send_ref[1])).astype(F32) + recv_n_ref[...]
    act, slope = silu_both(pre)
    place = low(receivers_t(senders_ref[...], degree, halo))
    base, base_slope = silu_both(recv_n_ref[...])
    gpre = low(gsum_n_ref[...].astype(F32) * (slope - base_slope))
    grecv = low(grecv_ref[...] + dot(place, gpre))
    pre = sent_b_ref[...].astype(F32) + dot(low(back), recv_ref[1])
    gpre = low(gsum_r_ref[...].astype(F32) * silu_slope(pre))
    border = low(hot(bounds_ref[...] == iota(nodes, halo, 0)))
    gsent = low(gsent_ref[...] + dot(border, gpre))
    gin = cot_ref[...].astype(F32) + dot(grecv, recv_ref[1], NT) + dot(gsent, send_ref[1], NT)
    gin = low(gin)
    gin_ref[...] = gin
    store_parts(pay_refs, [dot(low(receivers(senders_t_ref[...], halo)), gin)])
    summed_ref[...] = low(total_ref[...] + dot(place, low(act - base)))
    grecv_out_ref[...] = grecv
    gsent_out_ref[...] = gsent


def last_weights(
    dims, place_ref, state_ref, summed_ref, cot_ref, grecv_ref, gsent_ref, update_ref,
    keep_ref, give_ref, mesh_ref,
):
    state, summed = state_ref[...], summed_ref[...]

    def store(at, value):
        store_blocks(keep_ref, give_ref, at, 3, value, dims, place_ref)

    both = dot(state, jnp.concatenate([gsent_ref[...], grecv_ref[...]], axis=1), TN)
    store(0, both[:, : state.shape[1]])
    store(1, both[:, state.shape[1] :])
    store(2, dot(summed, cot_ref[...], TN))
    mesh_ref[...] = low(state.astype(F32) + dot(summed, update_ref[1]))


def back_local(
    dims, place_ref, gin_ref, slope_ref, slope_k_ref, slope_d_ref, send_ref, recv_ref, update_ref,
    senders_ref, senders_t_ref, state_ref, rows_ref, summed_ref, merged_ref, merged_r_ref,
    after_ref, part_ref, keep_ref, give_ref, keep2_ref, give2_ref, gpre_ref,
):
    nodes = gin_ref.shape[0]
    halo = slope_k_ref.shape[0]
    degree = senders_t_ref.shape[0]
    gin = gin_ref[...]
    gsum = low(dot(gin, update_ref[0], NT))
    place = low(receivers_t(senders_ref[...], degree, halo))
    back = low(receivers(senders_t_ref[...], halo))
    gsum_n = low(dot(back, gsum))
    gpre_k = gsum_n * slope_k_ref[...]
    grecv = dot(place, gsum_n * slope_d_ref[...])
    for j in range(degree):
        gpre = gsum * slope_ref[j]
        grecv = grecv + gpre.astype(F32)
        gpre_ref[j * nodes : (j + 1) * nodes, :] = gpre
    gsent = dot(edge_targets(senders_t_ref[...]), gpre_ref[...])
    grecv, gsent = low(grecv), low(gsent)
    part = gin.astype(F32) + dot(grecv, recv_ref[0], NT) + dot(gsent, send_ref[0], NT)
    part_ref[...] = part
    state = state_ref[...]

    def store(at, value):
        store_blocks(keep_ref, give_ref, at, 2, value, dims, place_ref)

    def store2(at, value):
        store_blocks(keep2_ref, give2_ref, at, 2, value, dims, place_ref)

    both = dot(state, jnp.concatenate([gsent, grecv], axis=1), TN)
    store(0, both[:, : state.shape[1]] + dot(rows_ref[...], gpre_k, TN))
    store(1, both[:, state.shape[1] :])
    store2(0, dot(summed_ref[...], gin, TN))
    far = low(dot(gpre_k, send_ref[0], NT))
    store2(1, dot(merged_ref[...], low(part), TN) + dot(merged_r_ref[...], far, TN))


def embed_back(peers, dims, carry, *refs):
    arr_refs, refs = refs[:peers][::-1], refs[peers:]
    (place_ref, slope_r_ref, part_ref, update_ref, send_ref, merge_ref, bounds_ref, target_ref,
     sends_ref, incoming_ref, slope_g_ref, slope_a_ref, grid_ref, lat_ref, embed_ref,
     gpre_ref, keep_ref, give_ref, *pay_refs) = refs
    nodes = part_ref.shape[0]
    halo = peers * BORDER
    chosen = grid_ref.shape[0]
    taken = sends_ref.shape[0]
    (arrived,) = split_parts(arr_refs, (0,), (BORDER,))
    gsum = low(dot(low(arrived), update_ref[0], NT)).astype(F32)
    gpre = low(gsum * slope_r_ref[...].astype(F32))
    border = low(hot(bounds_ref[...] == iota(nodes, halo, 0)))
    gsent = low(dot(border, gpre))
    gin = low(part_ref[...] + dot(gsent, send_ref[0], NT))
    gmerged = low(dot(gin, merge_ref[...], NT))
    place = low(hot(incoming_ref[...] == iota(nodes, taken, 0)))
    gpre_a = low(dot(place, gmerged, TN) * slope_a_ref[...].astype(F32))
    sent = jnp.max(hot(sends_ref[...] == iota(taken, chosen, 1)), axis=0, keepdims=True)
    label = jnp.where(sent > 0.0, nodes, target_ref[...])
    pick = low(hot(label == iota(nodes, chosen, 0)))
    gpre_g = low(dot(pick, gmerged, TN) * slope_g_ref[...].astype(F32))
    gpre_ref[...] = gpre_g
    grad = dot(grid_ref[...], gpre_g, TN) + dot(lat_ref[...], gpre_a, TN)
    store_blocks(keep_ref, give_ref, 0, 1, grad, dims, place_ref)
    rows = dot(gpre_a, embed_ref[...], NT)
    store_parts(pay_refs, [rows])
    if carry:
        size = taken // peers
        start = keep_ref.shape[0]
        give_ref[start : start + 2 * size, :] = low(
            jnp.concatenate([rows[:size], rows[2 * size : 3 * size]], axis=0)
        )


def grid_local(gpre_ref, weight_ref, out_ref):
    out_ref[...] = low(dot(gpre_ref[...], weight_ref[...], NT))


def grid_patch(local_ref, sends_ref, arr_refs, out_ref):
    chosen = local_ref.shape[0]
    taken = sends_ref.shape[1]
    size = taken // len(arr_refs)
    place = low(hot(sends_ref[...] == iota(chosen, taken, 0)))
    rows = [ref[...].astype(F32) for ref in arr_refs]
    rows = low(jnp.concatenate([row[row.shape[0] - size :] for row in rows], axis=0))
    out_ref[...] = low(local_ref[...].astype(F32) + dot(place, rows))


def grid_place(peers, *refs):
    arr_refs, (local_ref, sends_ref, out_ref) = refs[:peers][::-1], refs[peers:]
    grid_patch(local_ref, sends_ref, arr_refs, out_ref)


def sum_last(sums, outs):
    (keep1_ref, arr1_ref, keep0_ref, arr0_ref, keep2_ref, arr2_ref, keep_e_ref, arr_e_ref) = sums
    embed_ref, merge_ref, send_ref, recv_ref, update_ref = outs
    last = keep1_ref[...].astype(F32) + arr1_ref[...].astype(F32)
    first = keep0_ref[...].astype(F32) + arr0_ref[...].astype(F32)
    second = keep2_ref[...].astype(F32) + arr2_ref[...].astype(F32)
    depth = embed_ref.shape[0]
    embed_ref[...] = keep_e_ref[...].astype(F32) + arr_e_ref[:depth, :].astype(F32)
    for at, ref in enumerate((send_ref, recv_ref, update_ref)):
        ref[1] = last[at * depth : (at + 1) * depth]
    send_ref[0], recv_ref[0], update_ref[0] = first[:depth], first[depth:], second[:depth]
    merge_ref[...] = second[depth:]


def finish(*refs):
    sum_last(refs[:8], refs[8:])


def finish_all(*refs):
    sums, rows, (local_ref, sends_ref), outs = refs[:8], refs[8:12], refs[12:14], refs[14:]
    grid_patch(local_ref, sends_ref, (*rows, sums[7]), outs[0])
    sum_last(sums, outs[1:])


def body(
    dims,
    grid_latent, mesh_latent, cotangent, embed_weight, merge_weight, send_weight, recv_weight,
    update_weight, target_row, send_rows, incoming_rows, border_mesh_rows, mesh_senders,
):
    chosen, width = grid_latent.shape
    nodes, degree = mesh_senders.shape
    slots, capacity = send_rows.shape[1:]
    column = dims[1] * dims[2]
    peers = slots - 1
    halo = peers * BORDER
    taken = peers * capacity
    total = dims[0] * dims[1] * dims[2]
    bits = (total - 1).bit_length()
    carry = dims == (4, 2, 2) and fine(width, dims)
    spot = lax.axis_index(GROUP)
    place = [lax.axis_index(COLUMN), lax.axis_index("lon") % 2]
    place += [(spot >> bit) % 2 for bit in range(bits)]
    place = jnp.stack(place).astype(I32).reshape(1, 2 + bits)
    raw = [a.transpose(1, 0, 2) for a in (send_rows, incoming_rows, border_mesh_rows)]
    unit = 2 * nodes * width * width

    loads = (raw[0], grid_latent, embed_weight, target_row.reshape(1, chosen), mesh_senders.T,
             *raw[1:])
    raw_sends, grid, embed, targets, senders_raw, raw_incoming, raw_bounds, sends, *pay1 = call(
        lambda *refs: first_payload(column, len(loads), *refs), "first_payload",
        [shape(taken, 1, dtype=I32)] + [shape(capacity, width)] * peers,
        (place,), flops=unit // 2, loads=loads,
    )
    arr1 = exchange(pay1, dims)
    (mesh, merge, cot, local, slope_g, sends_row, incoming, bounds, bounds_row, senders_t, senders,
     place) = call(
        lambda *refs: embed_local(column, *refs), "embed_local",
        [shape(nodes, width, dtype=F32), shape(chosen, width), shape(1, taken, dtype=I32),
         shape(1, taken, dtype=I32), shape(halo, 1, dtype=I32), shape(1, halo, dtype=I32),
         shape(degree, nodes, dtype=I32), shape(nodes, 8, dtype=I32),
         shape(1, 2 + bits, dtype=I32)],
        (place, raw_sends, raw_incoming, raw_bounds, senders_raw, grid, embed, targets, sends),
        flops=3 * unit,
        loads=(mesh_latent, merge_weight, cotangent),
    )
    merged, state0, slope_a, lat_a, *pay2 = call(
        lambda *refs: merge_nodes(peers, *refs), "merge_nodes",
        [shape(nodes, width), shape(nodes, width), shape(taken, width), shape(taken, width)]
        + [shape(4 * BORDER, width)] * peers,
        (*arr1, incoming, embed, local, mesh, merge, bounds, senders_t, cot),
        flops=2 * unit,
    )
    arr2 = exchange(pay2, dims)
    total0, slope0, recv_n0, sent_b0 = call(
        forward_local, "forward_local",
        [shape(nodes, width, dtype=F32), shape(degree, nodes, width),
         shape(halo, width, dtype=F32), shape(halo, width)],
        (state0, send_weight, recv_weight, senders, senders_t, bounds), flops=6 * unit,
    )
    summed0, state1, pre0, rows0, back0, merged_r, cot_r, *pay3 = call(
        lambda *refs: forward_halo(peers, *refs), "forward_halo",
        [shape(nodes, width), shape(nodes, width), shape(halo, width, dtype=F32)]
        + [shape(halo, width)] * 4 + [shape(2 * BORDER, width)] * peers,
        (*arr2, recv_n0, total0, state0, send_weight, update_weight, senders, senders_t, bounds),
        flops=2 * unit,
    )
    arr3 = exchange(pay3, dims)
    (total1, grecv_l, gsent_l, recv_n1, sent_b1, gsum_n1, gsum_r1, slope_k0, slope_d0,
     slope_r0) = call(
        turn_local, "turn_local",
        [shape(nodes, width, dtype=F32)] * 3 + [shape(halo, width, dtype=F32)]
        + [shape(halo, width)] * 6,
        (state1, send_weight, recv_weight, update_weight, cot, cot_r, pre0, recv_n0, back0,
         sent_b0, senders, senders_t, bounds),
        flops=10 * unit, scratch=[pltpu.VMEM((degree * nodes, width), BF)],
    )
    summed1, grecv1, gsent1, gin1, *pay4 = call(
        lambda *refs: turn_halo(peers, *refs), "turn_halo",
        [shape(nodes, width)] * 4 + [shape(BORDER, width)] * peers,
        (*arr3, recv_n1, sent_b1, gsum_n1, gsum_r1, total1, grecv_l, gsent_l, cot,
         send_weight, recv_weight, senders, senders_t, bounds_row),
        flops=3 * unit,
    )
    arr4 = exchange(pay4, dims)
    keep1, give1, mesh_out = call(
        lambda *refs: last_weights(dims, *refs), "last_weights",
        blocks_shapes(3, width, width, dims) + [shape(nodes, width)],
        (place, state1, summed1, cot, grecv1, gsent1, update_weight), flops=4 * unit,
    )
    split = fine(width, dims)
    if split:
        give1, last = lax.optimization_barrier((give1, arr4[-1]))
        arr4 = (*arr4[:-1], last)
        keep1, give1 = halve_step(1, keep1, swap(give1, 0, dims), place)
    part0, keep0, give0, keep2, give2 = call(
        lambda *refs: back_local(dims, *refs), "back_local",
        [shape(nodes, width, dtype=F32)] + blocks_shapes(2, width, width, dims) * 2,
        (place, gin1, slope0, slope_k0, slope_d0, send_weight, recv_weight, update_weight, senders,
         senders_t, state0, rows0, summed0, merged, merged_r, keep1),
        flops=10 * unit, scratch=[pltpu.VMEM((degree * nodes, width), BF)],
    )
    if split:
        give0, give2, *arr4 = lax.optimization_barrier((give0, give2, *arr4))
        keep0, give0 = halve_step(1, keep0, swap(give0, 0, dims), place)
        keep0, *arr4 = lax.optimization_barrier((keep0, *arr4))
    shapes = blocks_shapes(1, width, width, dims)
    if carry:
        shapes[1] = shape(shapes[1].shape[0] + 2 * capacity, width)
    gpre_g, keep_e, give_e, *pay5 = call(
        lambda *refs: embed_back(peers, dims, carry, *refs), "embed_back",
        [shape(chosen, width)] + shapes + [shape(capacity, width)] * peers,
        (*arr4, place, slope_r0, part0, update_weight, send_weight, merge, bounds_row,
         targets, sends, incoming, slope_g, slope_a, grid, lat_a, embed),
        flops=6 * unit,
    )
    depth = width // total
    if not split:
        arr5 = exchange(pay5, dims)
        last, first, second, embed_sum = (
            scatter_plain(blocks, dims) for blocks in (keep1, keep0, keep2, keep_e)
        )
        plain = [jnp.stack([a, last[i]]) for i, a in enumerate((first[0], first[1], second[0]))]
        plain = [embed_sum[0], second[1], *plain]
    elif not carry:
        arr5 = exchange(pay5, dims)
        sums = [
            rest_of_halving(1, keep1, give1, place, dims),
            rest_of_halving(1, keep0, give0, place, dims),
            rest_of_halving(0, keep2, give2, place, dims),
            rest_of_halving(0, keep_e, give_e, place, dims),
        ]
    else:
        arr1 = swap(give1, 1, dims)
        arr0 = swap(give0, 1, dims)
        arr2 = swap(give2, 0, dims)
        (local_rows,) = call(
            grid_local, "grid_local", [shape(chosen, width)], (gpre_g, embed), flops=0, size=0
        )
        arr_e, arr1 = lax.optimization_barrier((swap(give_e, 0, dims), arr1))
        keep1, local_rows = lax.optimization_barrier((keep1, local_rows))
        keep1, give1 = halve_step(2, keep1, arr1, place)
        arr1 = swap(give1, 2, dims)
        keep_e, keep1 = lax.optimization_barrier((keep_e, keep1))
        keep_e, give_e, from_sub = carry_step(1, keep_e, arr_e, pay5[1:2], place, capacity)
        arr_e = swap(give_e, 1, dims)
        keep2, keep_e = lax.optimization_barrier((keep2, keep_e))
        keep2, give2 = halve_step(1, keep2, arr2, place)
        arr2 = swap(give2, 1, dims)
        keep0, keep2 = lax.optimization_barrier((keep0, keep2))
        keep0, give0 = halve_step(2, keep0, arr0, place)
        arr0 = swap(give0, 2, dims)
        keep1, keep0 = lax.optimization_barrier((keep1, keep0))
        keep1, give1 = halve_step(3, keep1, arr1, place)
        arr1 = swap(give1, 3, dims)
        keep2, keep1 = lax.optimization_barrier((keep2, keep1))
        keep2, give2 = halve_step(2, keep2, arr2, place)
        arr2 = swap(give2, 2, dims)
        keep0, keep2 = lax.optimization_barrier((keep0, keep2))
        keep0, give0 = halve_step(3, keep0, arr0, place)
        arr0 = swap(give0, 3, dims)
        keep_e, keep0, arr1 = lax.optimization_barrier((keep_e, keep0, arr1))
        keep_e, give_e, from_lat, from_diag = carry_step(
            2, keep_e, arr_e, pay5[3:], place, capacity
        )
        arr_e = swap(give_e, 2, dims)
        keep2, keep_e = lax.optimization_barrier((keep2, keep_e))
        keep2, give2 = halve_step(3, keep2, arr2, place)
        arr2 = swap(give2, 3, dims)
        keep_e, keep2 = lax.optimization_barrier((keep_e, keep2))
        keep_e, give_e, from_near = carry_step(3, keep_e, arr_e, (), place, capacity)
        give_e, arr0 = lax.optimization_barrier((give_e, arr0))
        arr_e = swap(give_e, 3, dims)
        sums = ((keep1, arr1), (keep0, arr0), (keep2, arr2), (keep_e, arr_e))
    grads = [shape(depth, width, dtype=F32)] * 2 + [shape(2, depth, width, dtype=F32)] * 3
    if carry:
        return (mesh_out, *call(
            finish_all, "finish_all", [shape(chosen, width)] + grads,
            (*(part for pair in sums for part in pair), from_sub, from_lat, from_diag, from_near,
             local_rows, sends_row),
            flops=unit,
        ))
    (local_rows,) = call(
        grid_local, "grid_local", [shape(chosen, width)], (gpre_g, embed), flops=2 * unit
    )
    (grid_grad,) = call(
        lambda *refs: grid_place(peers, *refs), "grid_place", [shape(chosen, width)],
        (*arr5, local_rows, sends_row), flops=unit,
    )
    if split:
        grads = call(
            finish, "finish", grads, [part for pair in sums for part in pair],
            flops=8 * depth * width,
        )
    else:
        grads = plain
    return (mesh_out, grid_grad, *grads)


def solution(mesh):
    split = ("groups", "lon", "lat", "sub")
    dims = tuple(mesh.shape[axis] for axis in GROUP)
    rows = P(split, None)
    whole = P("groups", GROUP, None)
    in_specs = (
        rows, rows, rows, P(), P(), P(), P(), P(), P(split), P(split, None, None),
        P(split, None, None), P(split, None, None), rows,
    )
    out_specs = (rows, rows, rows, rows, whole, whole, whole)
    return jax.shard_map(
        lambda *args: body(dims, *args),
        mesh=mesh, in_specs=in_specs, out_specs=out_specs, check_vma=False,
    )
```

```python
import jax
import jax.numpy as jnp
from jax import lax
from jax.experimental import pallas as pl
from jax.experimental.pallas import tpu as pltpu
from jax.sharding import PartitionSpec as P

BF = jnp.bfloat16
F32 = jnp.float32
I32 = jnp.int32
NN = (((1,), (0,)), ((), ()))
NT = (((1,), (1,)), ((), ()))
TN = (((0,), (0,)), ((), ()))
BORDER = 8
GROUP = ("lon", "lat", "sub")
COLUMN = ("lat", "sub")


def dot(a, b, dims=NN):
    return lax.dot_general(a, b, dims, preferred_element_type=F32)


def low(value):
    return value.astype(BF)


def sigmoid(value):
    return 0.5 * jnp.tanh(0.5 * value) + 0.5


def silu(value):
    return value * sigmoid(value)


def silu_both(value):
    sig = sigmoid(value)
    act = value * sig
    return act, sig + act * (1.0 - sig)


def silu_slope(value):
    return silu_both(value)[1]


def iota(rows, columns, dim):
    return lax.broadcasted_iota(I32, (rows, columns), dim)


def hot(mask):
    return jnp.where(mask, 1.0, 0.0)


def slot_rows(ref):
    return jnp.concatenate([ref[s] for s in range(ref.shape[0])], axis=0)


def slot_of(at, column, me, odd):
    far = jnp.where(at == column - 1, column + 1 - odd, column + odd)
    return jnp.where(at < column - 1, jnp.bitwise_xor(at + 1, me), far)


def as_column(values, wide, column, me, odd):
    slots = values.shape[0]
    count = (slots - 1) * wide
    row = iota(count, slots, 0)
    pick = low(hot(slot_of(row // wide, column, me, odd) == iota(count, slots, 1)))
    found = 16.0 * dot(pick, low((values // 16).astype(F32)))
    found = found + dot(pick, low((values % 16).astype(F32)))
    keep = iota(count, wide, 0) % wide == iota(count, wide, 1)
    return jnp.sum(jnp.where(keep, found, 0.0), axis=1, keepdims=True).astype(I32)


def as_row(values, wide, column, me, odd):
    slots = values.shape[0]
    count = (slots - 1) * wide
    pick = low(hot(iota(wide, count, 1) % wide == iota(wide, count, 0)))
    found = 16.0 * dot(low((values // 16).astype(F32)), pick)
    found = found + dot(low((values % 16).astype(F32)), pick)
    at = iota(slots, count, 1) // wide
    keep = slot_of(at, column, me, odd) == iota(slots, count, 0)
    return jnp.sum(jnp.where(keep, found, 0.0), axis=0, keepdims=True).astype(I32)


def split_parts(refs, starts, sizes):
    values = [ref[...].astype(F32) for ref in refs]
    return [
        jnp.concatenate([value[start : start + size] for value in values], axis=0)
        for start, size in zip(starts, sizes)
    ]


def store_parts(refs, parts):
    peers = len(refs)
    for at, ref in enumerate(refs):
        rows = []
        for part in parts:
            size = part.shape[0] // peers
            rows.append(part[at * size : (at + 1) * size])
        ref[...] = low(rows[0] if len(rows) == 1 else jnp.concatenate(rows, axis=0))


def receivers(senders_t, halo):
    degree, nodes = senders_t.shape
    found = jnp.zeros((halo, nodes), F32)
    ids = iota(halo, nodes, 0) + nodes
    for j in range(degree):
        found = found + hot(senders_t[j : j + 1, :] == ids)
    return found


def receivers_t(senders, degree, halo):
    nodes = senders.shape[0]
    found = jnp.zeros((nodes, halo), F32)
    ids = iota(nodes, halo, 1) + nodes
    for j in range(degree):
        found = found + hot(senders[:, j : j + 1] == ids)
    return found


def fine(rows, dims):
    return (rows // (dims[0] * dims[1] * dims[2])) % 16 == 0


def reverse_bits(block, bits):
    spot = 0
    for bit in range(bits):
        spot = 2 * spot + (block >> bit) % 2
    return spot


def store_blocks(keep_ref, give_ref, at, count, value, dims, bits_ref):
    value = low(value)
    rows = value.shape[0]
    total = dims[0] * dims[1] * dims[2]
    depth = rows // total
    if not fine(rows, dims):
        keep_ref[at] = value
        return
    bits = (total - 1).bit_length()
    upper = bits_ref[0:1, 2:3] == 1
    for block in range(0, total, 2):
        start = reverse_bits(block, bits) * count * depth + at * depth
        first = value[block * depth : (block + 1) * depth].astype(F32)
        second = value[(block + 1) * depth : (block + 2) * depth].astype(F32)
        keep_ref[start : start + depth, :] = low(jnp.where(upper, second, first))
        give_ref[start : start + depth, :] = low(jnp.where(upper, first, second))


def blocks_shapes(count, rows, width, dims):
    if fine(rows, dims):
        return [jax.ShapeDtypeStruct((count * rows // 2, width), BF)] * 2
    return [jax.ShapeDtypeStruct((count, rows, width), BF), jax.ShapeDtypeStruct((16, width), BF)]


def halve(bit, bits_ref, keep_ref, arr_ref, keep_out, give_out):
    half = keep_ref.shape[0] // 2
    upper = bits_ref[0:1, 2 + bit : 3 + bit] == 1
    first = keep_ref[:half, :].astype(F32) + arr_ref[:half, :].astype(F32)
    second = keep_ref[half:, :].astype(F32) + arr_ref[half:, :].astype(F32)
    keep_out[...] = low(jnp.where(upper, second, first))
    give_out[...] = low(jnp.where(upper, first, second))


def swap(block, bit, dims):
    total = dims[0] * dims[1] * dims[2]
    return lax.ppermute(block, GROUP, [(i, i ^ (1 << bit)) for i in range(total)])


def halve_step(bit, keep, arrived, place):
    rows, width = keep.shape[0] // 2, keep.shape[1]
    return call(
        lambda *refs: halve(bit, *refs), "halve", [shape(rows, width)] * 2,
        (place, keep, arrived), flops=4 * rows * width, size=0,
    )


def rest_of_halving(first, keep, give, place, dims):
    bits = (dims[0] * dims[1] * dims[2] - 1).bit_length()
    arrived = swap(give, first, dims)
    for bit in range(first + 1, bits):
        keep, give = halve_step(bit, keep, arrived, place)
        arrived = swap(give, bit, dims)
    return keep, arrived


def halve_carry(bit, count, bits_ref, keep_ref, arr_ref, *refs):
    own_refs, (keep_out, give_out, *here_refs) = refs[:count], refs[count:]
    rows = keep_ref.shape[0]
    half = rows // 2
    size = here_refs[0].shape[0]
    upper = bits_ref[0:1, 2 + bit : 3 + bit] == 1
    value = arr_ref[...].astype(F32)
    first = keep_ref[:half, :].astype(F32) + value[:half]
    second = keep_ref[half:, :].astype(F32) + value[half:rows]
    keep_out[...] = low(jnp.where(upper, second, first))
    here_refs[0][...] = low(value[rows : rows + size])
    passed = value[rows + size : rows + 2 * size]
    extra = [ref[...].astype(F32) for ref in own_refs]
    if count < 2:
        extra.append(passed)
    else:
        here_refs[1][...] = low(passed)
    give_out[...] = low(jnp.concatenate([jnp.where(upper, first, second), *extra], axis=0))


def carry_step(bit, keep, arrived, own, place, capacity):
    rows, width = keep.shape[0] // 2, keep.shape[1]
    count = len(own)
    return call(
        lambda *refs: halve_carry(bit, count, *refs), "halve_carry",
        [shape(rows, width), shape(rows + min(count + 1, 2) * capacity, width)]
        + [shape(capacity, width)] * (2 if count == 2 else 1),
        (place, keep, arrived, *own), flops=4 * rows * width, size=0,
    )


def scatter_plain(blocks, dims):
    lon, lat, sub = dims
    count, rows, width = blocks.shape
    depth = rows // (lon * lat * sub)
    blocks = blocks.reshape(count, lon, lat, sub, depth, width)
    blocks = blocks.transpose(3, 2, 1, 0, 4, 5)
    for axis in ("sub", "lat", "lon"):
        blocks = lax.psum_scatter(blocks, axis, scatter_dimension=0, tiled=False)
    return blocks.astype(F32)


def call(kernel, name, outs, args, flops, loads=(), scratch=(), size=None):
    if size is None:
        size = sum(a.size * a.dtype.itemsize for a in (*args, *outs, *loads))
    args = (*(pltpu.with_memory_space_constraint(a, pltpu.HBM) for a in loads), *args)
    scratch = list(scratch)
    if loads:
        scratch.append(pltpu.SemaphoreType.DMA((len(loads),)))
    in_specs = [pl.BlockSpec(memory_space=pltpu.HBM)] * len(loads)
    in_specs += [pl.BlockSpec(memory_space=pltpu.VMEM)] * (len(args) - len(loads))
    return pl.pallas_call(
        kernel,
        out_shape=[shape(*a.shape, dtype=a.dtype) for a in loads] + list(outs),
        in_specs=in_specs,
        out_specs=[pl.BlockSpec(memory_space=pltpu.VMEM)] * (len(outs) + len(loads)),
        scratch_shapes=scratch,
        compiler_params=pltpu.CompilerParams(vmem_limit_bytes=16 * 1024 * 1024),
        cost_estimate=pl.CostEstimate(flops=flops, bytes_accessed=size, transcendentals=0),
        name=name,
    )(*args)


def exchange(parts, dims):
    column = dims[1] * dims[2]
    count = dims[0]
    other = [(i, (i - 1 + 2 * (i % 2)) % count) for i in range(count)]
    far = lax.ppermute(parts[column], "lon", other)
    near = lax.ppermute(parts[column - 1], "lon", [(i, i ^ 1) for i in range(count)])
    arrived = [
        lax.ppermute(parts[r - 1], COLUMN, [(i, i ^ r) for i in range(column)])
        for r in range(column - 1, 0, -1)
    ]
    return (far, near, *arrived)


def shape(*dims, dtype=BF):
    return jax.ShapeDtypeStruct(dims, dtype)


def start_loads(sources, targets, sems):
    copies = [
        pltpu.make_async_copy(source, target, sems.at[at])
        for at, (source, target) in enumerate(zip(sources, targets))
    ]
    for copy in copies:
        copy.start()
    return copies


def first_payload(column, count, *refs):
    sources, place_ref, targets = refs[:count], refs[count], refs[count + 1 : 2 * count + 1]
    sends_out, *pay_refs, sems = refs[2 * count + 1 :]
    sends_ref, grid_ref = targets[:2]
    sends_load, grid_load, *loads = start_loads(sources, targets, sems)
    chosen = grid_ref.shape[0]
    me, odd = place_ref[:, 0:1], place_ref[:, 1:2]
    sends_load.wait()
    sends = slot_rows(sends_ref)
    sends = as_column(sends, sends.shape[1], column, me, odd)
    sends_out[...] = sends
    pick = low(hot(sends == iota(sends.shape[0], chosen, 1)))
    grid_load.wait()
    store_parts(pay_refs, [dot(pick, grid_ref[...])])
    for load in loads:
        load.wait()


def embed_local(
    column, mesh_far, merge_far, cot_far, place_in_ref, raw_sends_ref, raw_incoming_ref,
    raw_bounds_ref, senders_ref, grid_ref, weight_ref, target_ref, sends_ref, mesh_ref, merge_ref,
    cot_ref, sum_ref, slope_ref, sends_row_ref, incoming_ref, bounds_ref, bounds_row_ref, senders_t_ref,
    senders_out_ref, place_ref, sems,
):
    loads = start_loads((mesh_far, merge_far, cot_far), (mesh_ref, merge_ref, cot_ref), sems)
    chosen = grid_ref.shape[0]
    nodes = sum_ref.shape[0]
    taken = sends_ref.shape[0]
    act, slope = silu_both(dot(grid_ref[...], weight_ref[...]))
    slope_ref[...] = low(slope)
    sent = jnp.max(hot(sends_ref[...] == iota(taken, chosen, 1)), axis=0, keepdims=True)
    label = jnp.where(sent > 0.0, nodes, target_ref[...])
    sum_ref[...] = dot(low(hot(label == iota(nodes, chosen, 0))), low(act))
    place_ref[...] = place_in_ref[...]
    me, odd = place_in_ref[:, 0:1], place_in_ref[:, 1:2]
    raw_sends, incoming = slot_rows(raw_sends_ref), slot_rows(raw_incoming_ref)
    bounds = slot_rows(raw_bounds_ref)
    capacity = incoming.shape[1]
    sends_row_ref[...] = as_row(raw_sends, capacity, column, me, odd)
    incoming_ref[...] = as_row(incoming, capacity, column, me, odd)
    bounds_ref[...] = as_column(bounds, BORDER, column, me, odd)
    bounds_row_ref[...] = as_row(bounds, BORDER, column, me, odd)
    senders = senders_ref[...]
    degree = senders.shape[0]
    offset = senders - nodes
    slot = offset // BORDER
    far = jnp.where(slot == column, column - odd, column - 1 + odd)
    at = jnp.where(slot < column, jnp.bitwise_xor(slot, me) - 1, far)
    senders = jnp.where(offset < 0, senders, nodes + at * BORDER + offset % BORDER)
    senders_t_ref[...] = senders
    filler = jnp.zeros((8 - degree, nodes), I32)
    senders_out_ref[...] = jnp.concatenate([senders, filler], axis=0).T
    for load in loads:
        load.wait()


def merge_nodes(peers, *refs):
    arr_refs, refs = refs[:peers][::-1], refs[peers:]
    (incoming_ref, embed_ref, local_ref, mesh_ref, weight_ref, bounds_ref, senders_t_ref, cot_ref,
     merged_ref, state_ref, slope_ref, lat_ref, *pay_refs) = refs
    nodes = mesh_ref.shape[0]
    taken = incoming_ref.shape[1]
    halo = peers * BORDER
    lat = jnp.concatenate([ref[...] for ref in arr_refs], axis=0)
    lat_ref[...] = lat
    act, slope = silu_both(dot(lat, embed_ref[...]))
    slope_ref[...] = low(slope)
    place = low(hot(incoming_ref[...] == iota(nodes, taken, 0)))
    merged = low(local_ref[...] + dot(place, low(act)))
    merged_ref[...] = merged
    state = low(mesh_ref[...].astype(F32) + dot(merged, weight_ref[...]))
    state_ref[...] = state
    border = low(hot(bounds_ref[...] == iota(halo, nodes, 1)))
    back = low(receivers(senders_t_ref[...], halo))
    store_parts(
        pay_refs,
        [dot(border, state), dot(back, state), dot(border, merged), dot(back, cot_ref[...])],
    )


def local_edges(senders, degree, sent, recv, each):
    nodes = senders.shape[0]
    total = None
    ids = iota(nodes, nodes, 1)
    for j in range(degree):
        act, slope = silu_both(dot(low(hot(senders[:, j : j + 1] == ids)), sent) + recv)
        total = act if total is None else total + act
        each(j, slope)
    return total


def edge_targets(senders_t):
    degree, nodes = senders_t.shape
    ids = iota(nodes, nodes, 0)
    return jnp.concatenate(
        [low(hot(senders_t[j : j + 1, :] == ids)) for j in range(degree)], axis=1
    )


def forward_local(
    state_ref, send_ref, recv_ref, senders_ref, senders_t_ref, bounds_ref,
    total_ref, slope_ref, recv_n_ref, sent_b_ref,
):
    state = state_ref[...]
    nodes = state.shape[0]
    halo = bounds_ref.shape[0]
    sent = low(dot(state, send_ref[0]))
    recv = dot(state, recv_ref[0])

    def keep(j, slope):
        slope_ref[j] = low(slope)

    total_ref[...] = local_edges(senders_ref[...], senders_t_ref.shape[0], sent, recv, keep)
    back = low(receivers(senders_t_ref[...], halo))
    recv_n_ref[...] = dot(low(dot(back, state)), recv_ref[0])
    sent_b_ref[...] = low(dot(low(hot(bounds_ref[...] == iota(halo, nodes, 1))), sent))


def forward_halo(peers, *refs):
    arr_refs, refs = refs[:peers][::-1], refs[peers:]
    (recv_n_ref, total_ref, state_ref, send_ref, update_ref, senders_ref, senders_t_ref,
     bounds_ref, summed_ref, out_ref, pre_ref, rows_ref, back_ref, merged_ref, cot_ref,
     *pay_refs) = refs
    nodes = state_ref.shape[0]
    degree = senders_t_ref.shape[0]
    halo = peers * BORDER
    rows, back, merged, cot = split_parts(
        arr_refs, (0, BORDER, 2 * BORDER, 3 * BORDER), (BORDER,) * 4
    )
    rows_ref[...], back_ref[...] = low(rows), low(back)
    merged_ref[...], cot_ref[...] = low(merged), low(cot)
    pre = low(dot(low(rows), send_ref[0])).astype(F32) + recv_n_ref[...]
    pre_ref[...] = pre
    place = low(receivers_t(senders_ref[...], degree, halo))
    extra = silu(pre) - silu(recv_n_ref[...])
    summed = low(total_ref[...] + dot(place, low(extra)))
    summed_ref[...] = summed
    state = low(state_ref[...].astype(F32) + dot(summed, update_ref[0]))
    out_ref[...] = state
    border = low(hot(bounds_ref[...] == iota(halo, nodes, 1)))
    back = low(receivers(senders_t_ref[...], halo))
    store_parts(pay_refs, [dot(border, state), dot(back, state)])


def turn_local(
    state_ref, send_ref, recv_ref, update_ref, cot_ref, cot_r_ref, pre_ref, recv_n0_ref, back0_ref,
    sent_b0_ref, senders_ref, senders_t_ref, bounds_ref,
    total_ref, grecv_ref, gsent_ref, recv_n_ref, sent_b_ref, gsum_n_ref, gsum_r_ref,
    slope_k_ref, slope_d_ref, slope_r_ref, gpre_ref,
):
    halo = bounds_ref.shape[0]
    slope = silu_slope(pre_ref[...])
    slope_k_ref[...] = low(slope)
    slope_d_ref[...] = low(slope - silu_slope(recv_n0_ref[...]))
    pre = sent_b0_ref[...].astype(F32) + dot(back0_ref[...], recv_ref[0])
    slope_r_ref[...] = low(silu_slope(pre))
    state = state_ref[...]
    nodes = state.shape[0]
    sent = low(dot(state, send_ref[1]))
    recv = dot(state, recv_ref[1])
    gsum = low(dot(cot_ref[...], update_ref[1], NT))
    grad = gsum.astype(F32)
    grecv = []

    def back_edge(j, slope):
        gpre = grad * slope
        grecv.append(gpre if j == 0 else grecv[-1] + gpre)
        gpre_ref[j * nodes : (j + 1) * nodes, :] = low(gpre)

    degree = senders_t_ref.shape[0]
    total_ref[...] = local_edges(senders_ref[...], degree, sent, recv, back_edge)
    grecv_ref[...] = grecv[-1]
    gsent_ref[...] = dot(edge_targets(senders_t_ref[...]), gpre_ref[...])
    back = low(receivers(senders_t_ref[...], halo))
    recv_n_ref[...] = dot(low(dot(back, state)), recv_ref[1])
    sent_b_ref[...] = low(dot(low(hot(bounds_ref[...] == iota(halo, nodes, 1))), sent))
    gsum_n_ref[...] = low(dot(back, gsum))
    gsum_r_ref[...] = low(dot(cot_r_ref[...], update_ref[1], NT))


def turn_halo(peers, *refs):
    arr_refs, refs = refs[:peers][::-1], refs[peers:]
    (recv_n_ref, sent_b_ref, gsum_n_ref, gsum_r_ref, total_ref, grecv_ref, gsent_ref, cot_ref,
     send_ref, recv_ref, senders_ref, senders_t_ref, bounds_ref, summed_ref, grecv_out_ref,
     gsent_out_ref, gin_ref, *pay_refs) = refs
    nodes = cot_ref.shape[0]
    degree = senders_t_ref.shape[0]
    halo = peers * BORDER
    rows, back = split_parts(arr_refs, (0, BORDER), (BORDER,) * 2)
    pre = low(dot(low(rows), send_ref[1])).astype(F32) + recv_n_ref[...]
    act, slope = silu_both(pre)
    place = low(receivers_t(senders_ref[...], degree, halo))
    base, base_slope = silu_both(recv_n_ref[...])
    gpre = low(gsum_n_ref[...].astype(F32) * (slope - base_slope))
    grecv = low(grecv_ref[...] + dot(place, gpre))
    pre = sent_b_ref[...].astype(F32) + dot(low(back), recv_ref[1])
    gpre = low(gsum_r_ref[...].astype(F32) * silu_slope(pre))
    border = low(hot(bounds_ref[...] == iota(nodes, halo, 0)))
    gsent = low(gsent_ref[...] + dot(border, gpre))
    gin = cot_ref[...].astype(F32) + dot(grecv, recv_ref[1], NT) + dot(gsent, send_ref[1], NT)
    gin = low(gin)
    gin_ref[...] = gin
    store_parts(pay_refs, [dot(low(receivers(senders_t_ref[...], halo)), gin)])
    summed_ref[...] = low(total_ref[...] + dot(place, low(act - base)))
    grecv_out_ref[...] = grecv
    gsent_out_ref[...] = gsent


def last_weights(
    dims, place_ref, state_ref, summed_ref, cot_ref, grecv_ref, gsent_ref, update_ref,
    keep_ref, give_ref, mesh_ref,
):
    state, summed = state_ref[...], summed_ref[...]

    def store(at, value):
        store_blocks(keep_ref, give_ref, at, 3, value, dims, place_ref)

    both = dot(state, jnp.concatenate([gsent_ref[...], grecv_ref[...]], axis=1), TN)
    store(0, both[:, : state.shape[1]])
    store(1, both[:, state.shape[1] :])
    store(2, dot(summed, cot_ref[...], TN))
    mesh_ref[...] = low(state.astype(F32) + dot(summed, update_ref[1]))


def back_local(
    dims, place_ref, gin_ref, slope_ref, slope_k_ref, slope_d_ref, send_ref, recv_ref, update_ref,
    senders_ref, senders_t_ref, state_ref, rows_ref, summed_ref, merged_ref, merged_r_ref,
    after_ref, part_ref, keep_ref, give_ref, keep2_ref, give2_ref, gpre_ref,
):
    nodes = gin_ref.shape[0]
    halo = slope_k_ref.shape[0]
    degree = senders_t_ref.shape[0]
    gin = gin_ref[...]
    gsum = low(dot(gin, update_ref[0], NT))
    place = low(receivers_t(senders_ref[...], degree, halo))
    back = low(receivers(senders_t_ref[...], halo))
    gsum_n = low(dot(back, gsum))
    gpre_k = gsum_n * slope_k_ref[...]
    grecv = dot(place, gsum_n * slope_d_ref[...])
    for j in range(degree):
        gpre = gsum * slope_ref[j]
        grecv = grecv + gpre.astype(F32)
        gpre_ref[j * nodes : (j + 1) * nodes, :] = gpre
    gsent = dot(edge_targets(senders_t_ref[...]), gpre_ref[...])
    grecv, gsent = low(grecv), low(gsent)
    part = gin.astype(F32) + dot(grecv, recv_ref[0], NT) + dot(gsent, send_ref[0], NT)
    part_ref[...] = part
    state = state_ref[...]

    def store(at, value):
        store_blocks(keep_ref, give_ref, at, 2, value, dims, place_ref)

    def store2(at, value):
        store_blocks(keep2_ref, give2_ref, at, 2, value, dims, place_ref)

    both = dot(state, jnp.concatenate([gsent, grecv], axis=1), TN)
    store(0, both[:, : state.shape[1]] + dot(rows_ref[...], gpre_k, TN))
    store(1, both[:, state.shape[1] :])
    store2(0, dot(summed_ref[...], gin, TN))
    far = low(dot(gpre_k, send_ref[0], NT))
    store2(1, dot(merged_ref[...], low(part), TN) + dot(merged_r_ref[...], far, TN))


def embed_back(peers, dims, carry, *refs):
    arr_refs, refs = refs[:peers][::-1], refs[peers:]
    (place_ref, slope_r_ref, part_ref, update_ref, send_ref, merge_ref, bounds_ref, target_ref,
     sends_ref, incoming_ref, slope_g_ref, slope_a_ref, grid_ref, lat_ref, embed_ref,
     gpre_ref, keep_ref, give_ref, *pay_refs) = refs
    nodes = part_ref.shape[0]
    halo = peers * BORDER
    chosen = grid_ref.shape[0]
    taken = sends_ref.shape[0]
    (arrived,) = split_parts(arr_refs, (0,), (BORDER,))
    gsum = low(dot(low(arrived), update_ref[0], NT)).astype(F32)
    gpre = low(gsum * slope_r_ref[...].astype(F32))
    border = low(hot(bounds_ref[...] == iota(nodes, halo, 0)))
    gsent = low(dot(border, gpre))
    gin = low(part_ref[...] + dot(gsent, send_ref[0], NT))
    gmerged = low(dot(gin, merge_ref[...], NT))
    place = low(hot(incoming_ref[...] == iota(nodes, taken, 0)))
    gpre_a = low(dot(place, gmerged, TN) * slope_a_ref[...].astype(F32))
    sent = jnp.max(hot(sends_ref[...] == iota(taken, chosen, 1)), axis=0, keepdims=True)
    label = jnp.where(sent > 0.0, nodes, target_ref[...])
    pick = low(hot(label == iota(nodes, chosen, 0)))
    gpre_g = low(dot(pick, gmerged, TN) * slope_g_ref[...].astype(F32))
    gpre_ref[...] = gpre_g
    grad = dot(grid_ref[...], gpre_g, TN) + dot(lat_ref[...], gpre_a, TN)
    store_blocks(keep_ref, give_ref, 0, 1, grad, dims, place_ref)
    rows = dot(gpre_a, embed_ref[...], NT)
    store_parts(pay_refs, [rows])
    if carry:
        size = taken // peers
        start = keep_ref.shape[0]
        give_ref[start : start + 2 * size, :] = low(
            jnp.concatenate([rows[:size], rows[2 * size : 3 * size]], axis=0)
        )


def grid_local(gpre_ref, weight_ref, out_ref):
    out_ref[...] = low(dot(gpre_ref[...], weight_ref[...], NT))


def grid_patch(local_ref, sends_ref, arr_refs, out_ref):
    chosen = local_ref.shape[0]
    taken = sends_ref.shape[1]
    size = taken // len(arr_refs)
    place = low(hot(sends_ref[...] == iota(chosen, taken, 0)))
    rows = [ref[...].astype(F32) for ref in arr_refs]
    rows = low(jnp.concatenate([row[row.shape[0] - size :] for row in rows], axis=0))
    out_ref[...] = low(local_ref[...].astype(F32) + dot(place, rows))


def grid_place(peers, *refs):
    arr_refs, (local_ref, sends_ref, out_ref) = refs[:peers][::-1], refs[peers:]
    grid_patch(local_ref, sends_ref, arr_refs, out_ref)


def sum_last(sums, outs):
    (keep1_ref, arr1_ref, keep0_ref, arr0_ref, keep2_ref, arr2_ref, keep_e_ref, arr_e_ref) = sums
    embed_ref, merge_ref, send_ref, recv_ref, update_ref = outs
    last = keep1_ref[...].astype(F32) + arr1_ref[...].astype(F32)
    first = keep0_ref[...].astype(F32) + arr0_ref[...].astype(F32)
    second = keep2_ref[...].astype(F32) + arr2_ref[...].astype(F32)
    depth = embed_ref.shape[0]
    embed_ref[...] = keep_e_ref[...].astype(F32) + arr_e_ref[:depth, :].astype(F32)
    for at, ref in enumerate((send_ref, recv_ref, update_ref)):
        ref[1] = last[at * depth : (at + 1) * depth]
    send_ref[0], recv_ref[0], update_ref[0] = first[:depth], first[depth:], second[:depth]
    merge_ref[...] = second[depth:]


def finish(*refs):
    sum_last(refs[:8], refs[8:])


def finish_all(*refs):
    sums, rows, (local_ref, sends_ref), outs = refs[:8], refs[8:12], refs[12:14], refs[14:]
    grid_patch(local_ref, sends_ref, (*rows, sums[7]), outs[0])
    sum_last(sums, outs[1:])


def body(
    dims,
    grid_latent, mesh_latent, cotangent, embed_weight, merge_weight, send_weight, recv_weight,
    update_weight, target_row, send_rows, incoming_rows, border_mesh_rows, mesh_senders,
):
    chosen, width = grid_latent.shape
    nodes, degree = mesh_senders.shape
    slots, capacity = send_rows.shape[1:]
    column = dims[1] * dims[2]
    peers = slots - 1
    halo = peers * BORDER
    taken = peers * capacity
    total = dims[0] * dims[1] * dims[2]
    bits = (total - 1).bit_length()
    carry = dims == (4, 2, 2) and fine(width, dims)
    spot = lax.axis_index(GROUP)
    place = [lax.axis_index(COLUMN), lax.axis_index("lon") % 2]
    place += [(spot >> bit) % 2 for bit in range(bits)]
    place = jnp.stack(place).astype(I32).reshape(1, 2 + bits)
    raw = [a.transpose(1, 0, 2) for a in (send_rows, incoming_rows, border_mesh_rows)]
    unit = 2 * nodes * width * width

    loads = (raw[0], grid_latent, embed_weight, target_row.reshape(1, chosen), mesh_senders.T,
             *raw[1:])
    raw_sends, grid, embed, targets, senders_raw, raw_incoming, raw_bounds, sends, *pay1 = call(
        lambda *refs: first_payload(column, len(loads), *refs), "first_payload",
        [shape(taken, 1, dtype=I32)] + [shape(capacity, width)] * peers,
        (place,), flops=unit // 2, loads=loads,
    )
    arr1 = exchange(pay1, dims)
    (mesh, merge, cot, local, slope_g, sends_row, incoming, bounds, bounds_row, senders_t, senders,
     place) = call(
        lambda *refs: embed_local(column, *refs), "embed_local",
        [shape(nodes, width, dtype=F32), shape(chosen, width), shape(1, taken, dtype=I32),
         shape(1, taken, dtype=I32), shape(halo, 1, dtype=I32), shape(1, halo, dtype=I32),
         shape(degree, nodes, dtype=I32), shape(nodes, 8, dtype=I32),
         shape(1, 2 + bits, dtype=I32)],
        (place, raw_sends, raw_incoming, raw_bounds, senders_raw, grid, embed, targets, sends),
        flops=3 * unit,
        loads=(mesh_latent, merge_weight, cotangent),
    )
    merged, state0, slope_a, lat_a, *pay2 = call(
        lambda *refs: merge_nodes(peers, *refs), "merge_nodes",
        [shape(nodes, width), shape(nodes, width), shape(taken, width), shape(taken, width)]
        + [shape(4 * BORDER, width)] * peers,
        (*arr1, incoming, embed, local, mesh, merge, bounds, senders_t, cot),
        flops=2 * unit,
    )
    arr2 = exchange(pay2, dims)
    total0, slope0, recv_n0, sent_b0 = call(
        forward_local, "forward_local",
        [shape(nodes, width, dtype=F32), shape(degree, nodes, width),
         shape(halo, width, dtype=F32), shape(halo, width)],
        (state0, send_weight, recv_weight, senders, senders_t, bounds), flops=6 * unit,
    )
    summed0, state1, pre0, rows0, back0, merged_r, cot_r, *pay3 = call(
        lambda *refs: forward_halo(peers, *refs), "forward_halo",
        [shape(nodes, width), shape(nodes, width), shape(halo, width, dtype=F32)]
        + [shape(halo, width)] * 4 + [shape(2 * BORDER, width)] * peers,
        (*arr2, recv_n0, total0, state0, send_weight, update_weight, senders, senders_t, bounds),
        flops=2 * unit,
    )
    arr3 = exchange(pay3, dims)
    (total1, grecv_l, gsent_l, recv_n1, sent_b1, gsum_n1, gsum_r1, slope_k0, slope_d0,
     slope_r0) = call(
        turn_local, "turn_local",
        [shape(nodes, width, dtype=F32)] * 3 + [shape(halo, width, dtype=F32)]
        + [shape(halo, width)] * 6,
        (state1, send_weight, recv_weight, update_weight, cot, cot_r, pre0, recv_n0, back0,
         sent_b0, senders, senders_t, bounds),
        flops=10 * unit, scratch=[pltpu.VMEM((degree * nodes, width), BF)],
    )
    summed1, grecv1, gsent1, gin1, *pay4 = call(
        lambda *refs: turn_halo(peers, *refs), "turn_halo",
        [shape(nodes, width)] * 4 + [shape(BORDER, width)] * peers,
        (*arr3, recv_n1, sent_b1, gsum_n1, gsum_r1, total1, grecv_l, gsent_l, cot,
         send_weight, recv_weight, senders, senders_t, bounds_row),
        flops=3 * unit,
    )
    arr4 = exchange(pay4, dims)
    keep1, give1, mesh_out = call(
        lambda *refs: last_weights(dims, *refs), "last_weights",
        blocks_shapes(3, width, width, dims) + [shape(nodes, width)],
        (place, state1, summed1, cot, grecv1, gsent1, update_weight), flops=4 * unit,
    )
    split = fine(width, dims)
    if split:
        give1, last = lax.optimization_barrier((give1, arr4[-1]))
        arr4 = (*arr4[:-1], last)
        keep1, give1 = halve_step(1, keep1, swap(give1, 0, dims), place)
    part0, keep0, give0, keep2, give2 = call(
        lambda *refs: back_local(dims, *refs), "back_local",
        [shape(nodes, width, dtype=F32)] + blocks_shapes(2, width, width, dims) * 2,
        (place, gin1, slope0, slope_k0, slope_d0, send_weight, recv_weight, update_weight, senders,
         senders_t, state0, rows0, summed0, merged, merged_r, keep1),
        flops=10 * unit, scratch=[pltpu.VMEM((degree * nodes, width), BF)],
    )
    if split:
        give0, give2, *arr4 = lax.optimization_barrier((give0, give2, *arr4))
        keep0, give0 = halve_step(1, keep0, swap(give0, 0, dims), place)
        keep0, *arr4 = lax.optimization_barrier((keep0, *arr4))
    shapes = blocks_shapes(1, width, width, dims)
    if carry:
        shapes[1] = shape(shapes[1].shape[0] + 2 * capacity, width)
    gpre_g, keep_e, give_e, *pay5 = call(
        lambda *refs: embed_back(peers, dims, carry, *refs), "embed_back",
        [shape(chosen, width)] + shapes + [shape(capacity, width)] * peers,
        (*arr4, place, slope_r0, part0, update_weight, send_weight, merge, bounds_row,
         targets, sends, incoming, slope_g, slope_a, grid, lat_a, embed),
        flops=6 * unit,
    )
    depth = width // total
    if not split:
        arr5 = exchange(pay5, dims)
        last, first, second, embed_sum = (
            scatter_plain(blocks, dims) for blocks in (keep1, keep0, keep2, keep_e)
        )
        plain = [jnp.stack([a, last[i]]) for i, a in enumerate((first[0], first[1], second[0]))]
        plain = [embed_sum[0], second[1], *plain]
    elif not carry:
        arr5 = exchange(pay5, dims)
        sums = [
            rest_of_halving(1, keep1, give1, place, dims),
            rest_of_halving(1, keep0, give0, place, dims),
            rest_of_halving(0, keep2, give2, place, dims),
            rest_of_halving(0, keep_e, give_e, place, dims),
        ]
    else:
        arr1 = swap(give1, 1, dims)
        arr0 = swap(give0, 1, dims)
        arr2 = swap(give2, 0, dims)
        (local_rows,) = call(
            grid_local, "grid_local", [shape(chosen, width)], (gpre_g, embed), flops=0, size=0
        )
        arr_e, arr1 = lax.optimization_barrier((swap(give_e, 0, dims), arr1))
        keep1, local_rows = lax.optimization_barrier((keep1, local_rows))
        keep1, give1 = halve_step(2, keep1, arr1, place)
        arr1 = swap(give1, 2, dims)
        keep_e, keep1 = lax.optimization_barrier((keep_e, keep1))
        keep_e, give_e, from_sub = carry_step(1, keep_e, arr_e, pay5[1:2], place, capacity)
        arr_e = swap(give_e, 1, dims)
        keep2, keep_e = lax.optimization_barrier((keep2, keep_e))
        keep2, give2 = halve_step(1, keep2, arr2, place)
        arr2 = swap(give2, 1, dims)
        keep0, keep2 = lax.optimization_barrier((keep0, keep2))
        keep0, give0 = halve_step(2, keep0, arr0, place)
        arr0 = swap(give0, 2, dims)
        keep1, keep0 = lax.optimization_barrier((keep1, keep0))
        keep1, give1 = halve_step(3, keep1, arr1, place)
        arr1 = swap(give1, 3, dims)
        keep2, keep1 = lax.optimization_barrier((keep2, keep1))
        keep2, give2 = halve_step(2, keep2, arr2, place)
        arr2 = swap(give2, 2, dims)
        keep0, keep2 = lax.optimization_barrier((keep0, keep2))
        keep0, give0 = halve_step(3, keep0, arr0, place)
        arr0 = swap(give0, 3, dims)
        keep_e, keep0, arr1 = lax.optimization_barrier((keep_e, keep0, arr1))
        keep_e, give_e, from_lat, from_diag = carry_step(
            2, keep_e, arr_e, pay5[3:], place, capacity
        )
        arr_e = swap(give_e, 2, dims)
        keep2, keep_e = lax.optimization_barrier((keep2, keep_e))
        keep2, give2 = halve_step(3, keep2, arr2, place)
        arr2 = swap(give2, 3, dims)
        keep_e, keep2 = lax.optimization_barrier((keep_e, keep2))
        keep_e, give_e, from_near = carry_step(3, keep_e, arr_e, (), place, capacity)
        arr_e = swap(give_e, 3, dims)
        sums = ((keep1, arr1), (keep0, arr0), (keep2, arr2), (keep_e, arr_e))
    grads = [shape(depth, width, dtype=F32)] * 2 + [shape(2, depth, width, dtype=F32)] * 3
    if carry:
        return (mesh_out, *call(
            finish_all, "finish_all", [shape(chosen, width)] + grads,
            (*(part for pair in sums for part in pair), from_sub, from_lat, from_diag, from_near,
             local_rows, sends_row),
            flops=unit,
        ))
    (local_rows,) = call(
        grid_local, "grid_local", [shape(chosen, width)], (gpre_g, embed), flops=2 * unit
    )
    (grid_grad,) = call(
        lambda *refs: grid_place(peers, *refs), "grid_place", [shape(chosen, width)],
        (*arr5, local_rows, sends_row), flops=unit,
    )
    if split:
        grads = call(
            finish, "finish", grads, [part for pair in sums for part in pair],
            flops=8 * depth * width,
        )
    else:
        grads = plain
    return (mesh_out, grid_grad, *grads)


def solution(mesh):
    split = ("groups", "lon", "lat", "sub")
    dims = tuple(mesh.shape[axis] for axis in GROUP)
    rows = P(split, None)
    whole = P("groups", GROUP, None)
    in_specs = (
        rows, rows, rows, P(), P(), P(), P(), P(), P(split), P(split, None, None),
        P(split, None, None), P(split, None, None), rows,
    )
    out_specs = (rows, rows, rows, rows, whole, whole, whole)
    return jax.shard_map(
        lambda *args: body(dims, *args),
        mesh=mesh, in_specs=in_specs, out_specs=out_specs, check_vma=False,
    )
```

```python
import jax
import jax.numpy as jnp
from jax import lax
from jax.experimental import pallas as pl
from jax.experimental.pallas import tpu as pltpu
from jax.sharding import PartitionSpec as P

BF = jnp.bfloat16
F32 = jnp.float32
I32 = jnp.int32
NN = (((1,), (0,)), ((), ()))
NT = (((1,), (1,)), ((), ()))
TN = (((0,), (0,)), ((), ()))
BORDER = 8
GROUP = ("lon", "lat", "sub")
COLUMN = ("lat", "sub")


def dot(a, b, dims=NN):
    return lax.dot_general(a, b, dims, preferred_element_type=F32)


def low(value):
    return value.astype(BF)


def sigmoid(value):
    return 0.5 * jnp.tanh(0.5 * value) + 0.5


def silu(value):
    return value * sigmoid(value)


def silu_both(value):
    sig = sigmoid(value)
    act = value * sig
    return act, sig + act * (1.0 - sig)


def silu_slope(value):
    return silu_both(value)[1]


def iota(rows, columns, dim):
    return lax.broadcasted_iota(I32, (rows, columns), dim)


def hot(mask):
    return jnp.where(mask, 1.0, 0.0)


def slot_rows(ref):
    return jnp.concatenate([ref[s] for s in range(ref.shape[0])], axis=0)


def slot_of(at, column, me, odd):
    far = jnp.where(at == column - 1, column + 1 - odd, column + odd)
    return jnp.where(at < column - 1, jnp.bitwise_xor(at + 1, me), far)


def as_column(values, wide, column, me, odd):
    slots = values.shape[0]
    count = (slots - 1) * wide
    row = iota(count, slots, 0)
    pick = low(hot(slot_of(row // wide, column, me, odd) == iota(count, slots, 1)))
    found = 16.0 * dot(pick, low((values // 16).astype(F32)))
    found = found + dot(pick, low((values % 16).astype(F32)))
    keep = iota(count, wide, 0) % wide == iota(count, wide, 1)
    return jnp.sum(jnp.where(keep, found, 0.0), axis=1, keepdims=True).astype(I32)


def as_row(values, wide, column, me, odd):
    slots = values.shape[0]
    count = (slots - 1) * wide
    pick = low(hot(iota(wide, count, 1) % wide == iota(wide, count, 0)))
    found = 16.0 * dot(low((values // 16).astype(F32)), pick)
    found = found + dot(low((values % 16).astype(F32)), pick)
    at = iota(slots, count, 1) // wide
    keep = slot_of(at, column, me, odd) == iota(slots, count, 0)
    return jnp.sum(jnp.where(keep, found, 0.0), axis=0, keepdims=True).astype(I32)


def split_parts(refs, starts, sizes):
    values = [ref[...].astype(F32) for ref in refs]
    return [
        jnp.concatenate([value[start : start + size] for value in values], axis=0)
        for start, size in zip(starts, sizes)
    ]


def store_parts(refs, parts):
    peers = len(refs)
    for at, ref in enumerate(refs):
        rows = []
        for part in parts:
            size = part.shape[0] // peers
            rows.append(part[at * size : (at + 1) * size])
        ref[...] = low(rows[0] if len(rows) == 1 else jnp.concatenate(rows, axis=0))


def receivers(senders_t, halo):
    degree, nodes = senders_t.shape
    found = jnp.zeros((halo, nodes), F32)
    ids = iota(halo, nodes, 0) + nodes
    for j in range(degree):
        found = found + hot(senders_t[j : j + 1, :] == ids)
    return found


def receivers_t(senders, degree, halo):
    nodes = senders.shape[0]
    found = jnp.zeros((nodes, halo), F32)
    ids = iota(nodes, halo, 1) + nodes
    for j in range(degree):
        found = found + hot(senders[:, j : j + 1] == ids)
    return found


def fine(rows, dims):
    return (rows // (dims[0] * dims[1] * dims[2])) % 16 == 0


def reverse_bits(block, bits):
    spot = 0
    for bit in range(bits):
        spot = 2 * spot + (block >> bit) % 2
    return spot


def store_blocks(keep_ref, give_ref, at, count, value, dims, bits_ref):
    value = low(value)
    rows = value.shape[0]
    total = dims[0] * dims[1] * dims[2]
    depth = rows // total
    if not fine(rows, dims):
        keep_ref[at] = value
        return
    bits = (total - 1).bit_length()
    upper = bits_ref[0:1, 2:3] == 1
    for block in range(0, total, 2):
        start = reverse_bits(block, bits) * count * depth + at * depth
        first = value[block * depth : (block + 1) * depth].astype(F32)
        second = value[(block + 1) * depth : (block + 2) * depth].astype(F32)
        keep_ref[start : start + depth, :] = low(jnp.where(upper, second, first))
        give_ref[start : start + depth, :] = low(jnp.where(upper, first, second))


def blocks_shapes(count, rows, width, dims):
    if fine(rows, dims):
        return [jax.ShapeDtypeStruct((count * rows // 2, width), BF)] * 2
    return [jax.ShapeDtypeStruct((count, rows, width), BF), jax.ShapeDtypeStruct((16, width), BF)]


def halve(bit, bits_ref, keep_ref, arr_ref, keep_out, give_out):
    half = keep_ref.shape[0] // 2
    upper = bits_ref[0:1, 2 + bit : 3 + bit] == 1
    first = keep_ref[:half, :].astype(F32) + arr_ref[:half, :].astype(F32)
    second = keep_ref[half:, :].astype(F32) + arr_ref[half:, :].astype(F32)
    keep_out[...] = low(jnp.where(upper, second, first))
    give_out[...] = low(jnp.where(upper, first, second))


def swap(block, bit, dims):
    total = dims[0] * dims[1] * dims[2]
    return lax.ppermute(block, GROUP, [(i, i ^ (1 << bit)) for i in range(total)])


def halve_step(bit, keep, arrived, place):
    rows, width = keep.shape[0] // 2, keep.shape[1]
    return call(
        lambda *refs: halve(bit, *refs), "halve", [shape(rows, width)] * 2,
        (place, keep, arrived), flops=4 * rows * width, size=0,
    )


def rest_of_halving(first, keep, give, place, dims):
    bits = (dims[0] * dims[1] * dims[2] - 1).bit_length()
    arrived = swap(give, first, dims)
    for bit in range(first + 1, bits):
        keep, give = halve_step(bit, keep, arrived, place)
        arrived = swap(give, bit, dims)
    return keep, arrived


def halve_carry(bit, count, bits_ref, keep_ref, arr_ref, *refs):
    own_refs, (keep_out, give_out, *here_refs) = refs[:count], refs[count:]
    rows = keep_ref.shape[0]
    half = rows // 2
    size = here_refs[0].shape[0]
    upper = bits_ref[0:1, 2 + bit : 3 + bit] == 1
    value = arr_ref[...].astype(F32)
    first = keep_ref[:half, :].astype(F32) + value[:half]
    second = keep_ref[half:, :].astype(F32) + value[half:rows]
    keep_out[...] = low(jnp.where(upper, second, first))
    here_refs[0][...] = low(value[rows : rows + size])
    passed = value[rows + size : rows + 2 * size]
    extra = [ref[...].astype(F32) for ref in own_refs]
    if count < 2:
        extra.append(passed)
    else:
        here_refs[1][...] = low(passed)
    give_out[...] = low(jnp.concatenate([jnp.where(upper, first, second), *extra], axis=0))


def carry_step(bit, keep, arrived, own, place, capacity):
    rows, width = keep.shape[0] // 2, keep.shape[1]
    count = len(own)
    return call(
        lambda *refs: halve_carry(bit, count, *refs), "halve_carry",
        [shape(rows, width), shape(rows + min(count + 1, 2) * capacity, width)]
        + [shape(capacity, width)] * (2 if count == 2 else 1),
        (place, keep, arrived, *own), flops=4 * rows * width, size=0,
    )


def scatter_plain(blocks, dims):
    lon, lat, sub = dims
    count, rows, width = blocks.shape
    depth = rows // (lon * lat * sub)
    blocks = blocks.reshape(count, lon, lat, sub, depth, width)
    blocks = blocks.transpose(3, 2, 1, 0, 4, 5)
    for axis in ("sub", "lat", "lon"):
        blocks = lax.psum_scatter(blocks, axis, scatter_dimension=0, tiled=False)
    return blocks.astype(F32)


def call(kernel, name, outs, args, flops, loads=(), scratch=(), size=None):
    if size is None:
        size = sum(a.size * a.dtype.itemsize for a in (*args, *outs, *loads))
    args = (*(pltpu.with_memory_space_constraint(a, pltpu.HBM) for a in loads), *args)
    scratch = list(scratch)
    if loads:
        scratch.append(pltpu.SemaphoreType.DMA((len(loads),)))
    in_specs = [pl.BlockSpec(memory_space=pltpu.HBM)] * len(loads)
    in_specs += [pl.BlockSpec(memory_space=pltpu.VMEM)] * (len(args) - len(loads))
    return pl.pallas_call(
        kernel,
        out_shape=[shape(*a.shape, dtype=a.dtype) for a in loads] + list(outs),
        in_specs=in_specs,
        out_specs=[pl.BlockSpec(memory_space=pltpu.VMEM)] * (len(outs) + len(loads)),
        scratch_shapes=scratch,
        compiler_params=pltpu.CompilerParams(vmem_limit_bytes=16 * 1024 * 1024),
        cost_estimate=pl.CostEstimate(flops=flops, bytes_accessed=size, transcendentals=0),
        name=name,
    )(*args)


def exchange(parts, dims):
    column = dims[1] * dims[2]
    count = dims[0]
    other = [(i, (i - 1 + 2 * (i % 2)) % count) for i in range(count)]
    far = lax.ppermute(parts[column], "lon", other)
    near = lax.ppermute(parts[column - 1], "lon", [(i, i ^ 1) for i in range(count)])
    arrived = [
        lax.ppermute(parts[r - 1], COLUMN, [(i, i ^ r) for i in range(column)])
        for r in range(column - 1, 0, -1)
    ]
    return (far, near, *arrived)


def shape(*dims, dtype=BF):
    return jax.ShapeDtypeStruct(dims, dtype)


def start_loads(sources, targets, sems):
    copies = [
        pltpu.make_async_copy(source, target, sems.at[at])
        for at, (source, target) in enumerate(zip(sources, targets))
    ]
    for copy in copies:
        copy.start()
    return copies


def first_payload(column, count, *refs):
    sources, place_ref, targets = refs[:count], refs[count], refs[count + 1 : 2 * count + 1]
    sends_out, *pay_refs, sems = refs[2 * count + 1 :]
    sends_ref, grid_ref = targets[:2]
    sends_load, grid_load, *loads = start_loads(sources, targets, sems)
    chosen = grid_ref.shape[0]
    me, odd = place_ref[:, 0:1], place_ref[:, 1:2]
    sends_load.wait()
    sends = slot_rows(sends_ref)
    sends = as_column(sends, sends.shape[1], column, me, odd)
    sends_out[...] = sends
    pick = low(hot(sends == iota(sends.shape[0], chosen, 1)))
    grid_load.wait()
    store_parts(pay_refs, [dot(pick, grid_ref[...])])
    for load in loads:
        load.wait()


def embed_local(
    column, mesh_far, merge_far, cot_far, place_in_ref, raw_sends_ref, raw_incoming_ref,
    raw_bounds_ref, senders_ref, grid_ref, weight_ref, target_ref, sends_ref, mesh_ref, merge_ref,
    cot_ref, sum_ref, slope_ref, sends_row_ref, incoming_ref, border_ref, border_t_ref, back_ref,
    back_t_ref, senders_t_ref, senders_out_ref, place_ref, sems,
):
    loads = start_loads((mesh_far, merge_far, cot_far), (mesh_ref, merge_ref, cot_ref), sems)
    chosen = grid_ref.shape[0]
    nodes = sum_ref.shape[0]
    taken = sends_ref.shape[0]
    act, slope = silu_both(dot(grid_ref[...], weight_ref[...]))
    slope_ref[...] = low(slope)
    sent = jnp.max(hot(sends_ref[...] == iota(taken, chosen, 1)), axis=0, keepdims=True)
    label = jnp.where(sent > 0.0, nodes, target_ref[...])
    sum_ref[...] = dot(low(hot(label == iota(nodes, chosen, 0))), low(act))
    place_ref[...] = place_in_ref[...]
    me, odd = place_in_ref[:, 0:1], place_in_ref[:, 1:2]
    raw_sends, incoming = slot_rows(raw_sends_ref), slot_rows(raw_incoming_ref)
    bounds = slot_rows(raw_bounds_ref)
    capacity = incoming.shape[1]
    sends_row_ref[...] = as_row(raw_sends, capacity, column, me, odd)
    halo = border_ref.shape[0]
    incoming = as_row(incoming, capacity, column, me, odd)
    incoming_ref[...] = low(hot(incoming == iota(nodes, taken, 0)))
    border = as_column(bounds, BORDER, column, me, odd)
    border_ref[...] = low(hot(border == iota(halo, nodes, 1)))
    border = as_row(bounds, BORDER, column, me, odd)
    border_t_ref[...] = low(hot(border == iota(nodes, halo, 0)))
    senders = senders_ref[...]
    degree = senders.shape[0]
    offset = senders - nodes
    slot = offset // BORDER
    far = jnp.where(slot == column, column - odd, column - 1 + odd)
    at = jnp.where(slot < column, jnp.bitwise_xor(slot, me) - 1, far)
    senders = jnp.where(offset < 0, senders, nodes + at * BORDER + offset % BORDER)
    senders_t_ref[...] = senders
    filler = jnp.zeros((8 - degree, nodes), I32)
    back_ref[...] = low(receivers(senders, halo))
    senders_t = jnp.concatenate([senders, filler], axis=0).T
    senders_out_ref[...] = senders_t
    back_t_ref[...] = low(receivers_t(senders_t, degree, halo))
    for load in loads:
        load.wait()


def merge_nodes(peers, *refs):
    arr_refs, refs = refs[:peers][::-1], refs[peers:]
    (incoming_ref, embed_ref, local_ref, mesh_ref, weight_ref, border_ref, back_ref, cot_ref,
     merged_ref, state_ref, slope_ref, lat_ref, *pay_refs) = refs
    lat = jnp.concatenate([ref[...] for ref in arr_refs], axis=0)
    lat_ref[...] = lat
    act, slope = silu_both(dot(lat, embed_ref[...]))
    slope_ref[...] = low(slope)
    merged = low(local_ref[...] + dot(incoming_ref[...], low(act)))
    merged_ref[...] = merged
    state = low(mesh_ref[...].astype(F32) + dot(merged, weight_ref[...]))
    state_ref[...] = state
    border, back = border_ref[...], back_ref[...]
    store_parts(
        pay_refs,
        [dot(border, state), dot(back, state), dot(border, merged), dot(back, cot_ref[...])],
    )


def local_edges(senders, degree, sent, recv, each):
    nodes = senders.shape[0]
    total = None
    ids = iota(nodes, nodes, 1)
    for j in range(degree):
        act, slope = silu_both(dot(low(hot(senders[:, j : j + 1] == ids)), sent) + recv)
        total = act if total is None else total + act
        each(j, slope)
    return total


def edge_targets(senders_t):
    degree, nodes = senders_t.shape
    ids = iota(nodes, nodes, 0)
    return jnp.concatenate(
        [low(hot(senders_t[j : j + 1, :] == ids)) for j in range(degree)], axis=1
    )


def forward_local(
    state_ref, send_ref, recv_ref, update_ref, cot_ref, senders_ref, senders_t_ref, border_ref,
    back_ref, total_ref, slope_ref, recv_n_ref, sent_b_ref, gsum_ref, targets_ref,
):
    state = state_ref[...]
    sent = low(dot(state, send_ref[0]))
    recv = dot(state, recv_ref[0])

    def keep(j, slope):
        slope_ref[j] = low(slope)

    total_ref[...] = local_edges(senders_ref[...], senders_t_ref.shape[0], sent, recv, keep)
    recv_n_ref[...] = dot(low(dot(back_ref[...], state)), recv_ref[0])
    sent_b_ref[...] = low(dot(border_ref[...], sent))
    gsum_ref[...] = low(dot(cot_ref[...], update_ref[1], NT))
    targets_ref[...] = edge_targets(senders_t_ref[...])


def forward_halo(peers, *refs):
    arr_refs, refs = refs[:peers][::-1], refs[peers:]
    (recv_n_ref, total_ref, state_ref, send_ref, update_ref, back_t_ref, back_in_ref,
     border_ref, summed_ref, out_ref, pre_ref, rows_ref, back_ref, merged_ref, cot_ref,
     *pay_refs) = refs
    rows, back, merged, cot = split_parts(
        arr_refs, (0, BORDER, 2 * BORDER, 3 * BORDER), (BORDER,) * 4
    )
    rows_ref[...], back_ref[...] = low(rows), low(back)
    merged_ref[...], cot_ref[...] = low(merged), low(cot)
    pre = low(dot(low(rows), send_ref[0])).astype(F32) + recv_n_ref[...]
    pre_ref[...] = pre
    place = back_t_ref[...]
    extra = silu(pre) - silu(recv_n_ref[...])
    summed = low(total_ref[...] + dot(place, low(extra)))
    summed_ref[...] = summed
    state = low(state_ref[...].astype(F32) + dot(summed, update_ref[0]))
    out_ref[...] = state
    store_parts(pay_refs, [dot(border_ref[...], state), dot(back_in_ref[...], state)])


def turn_local(
    state_ref, send_ref, recv_ref, update_ref, gsum_ref, cot_r_ref, pre_ref, recv_n0_ref, back0_ref,
    sent_b0_ref, senders_ref, targets_ref, border_ref, back_ref,
    total_ref, grecv_ref, gsent_ref, recv_n_ref, sent_b_ref, gsum_n_ref, gsum_r_ref,
    slope_k_ref, slope_d_ref, slope_r_ref, gpre_ref,
):
    slope = silu_slope(pre_ref[...])
    slope_k_ref[...] = low(slope)
    slope_d_ref[...] = low(slope - silu_slope(recv_n0_ref[...]))
    pre = sent_b0_ref[...].astype(F32) + dot(back0_ref[...], recv_ref[0])
    slope_r_ref[...] = low(silu_slope(pre))
    state = state_ref[...]
    nodes = state.shape[0]
    sent = low(dot(state, send_ref[1]))
    recv = dot(state, recv_ref[1])
    gsum = gsum_ref[...]
    grad = gsum.astype(F32)
    grecv = []

    def back_edge(j, slope):
        gpre = grad * slope
        grecv.append(gpre if j == 0 else grecv[-1] + gpre)
        gpre_ref[j * nodes : (j + 1) * nodes, :] = low(gpre)

    degree = targets_ref.shape[1] // nodes
    total_ref[...] = local_edges(senders_ref[...], degree, sent, recv, back_edge)
    grecv_ref[...] = grecv[-1]
    gsent_ref[...] = dot(targets_ref[...], gpre_ref[...])
    back = back_ref[...]
    recv_n_ref[...] = dot(low(dot(back, state)), recv_ref[1])
    sent_b_ref[...] = low(dot(border_ref[...], sent))
    gsum_n_ref[...] = low(dot(back, gsum))
    gsum_r_ref[...] = low(dot(cot_r_ref[...], update_ref[1], NT))


def turn_halo(peers, *refs):
    arr_refs, refs = refs[:peers][::-1], refs[peers:]
    (recv_n_ref, sent_b_ref, gsum_n_ref, gsum_r_ref, total_ref, grecv_ref, gsent_ref, cot_ref,
     send_ref, recv_ref, back_t_ref, back_in_ref, border_t_ref, summed_ref, grecv_out_ref,
     gsent_out_ref, gin_ref, *pay_refs) = refs
    rows, back = split_parts(arr_refs, (0, BORDER), (BORDER,) * 2)
    pre = low(dot(low(rows), send_ref[1])).astype(F32) + recv_n_ref[...]
    act, slope = silu_both(pre)
    place = back_t_ref[...]
    base, base_slope = silu_both(recv_n_ref[...])
    gpre = low(gsum_n_ref[...].astype(F32) * (slope - base_slope))
    grecv = low(grecv_ref[...] + dot(place, gpre))
    pre = sent_b_ref[...].astype(F32) + dot(low(back), recv_ref[1])
    gpre = low(gsum_r_ref[...].astype(F32) * silu_slope(pre))
    gsent = low(gsent_ref[...] + dot(border_t_ref[...], gpre))
    gin = cot_ref[...].astype(F32) + dot(grecv, recv_ref[1], NT) + dot(gsent, send_ref[1], NT)
    gin = low(gin)
    gin_ref[...] = gin
    store_parts(pay_refs, [dot(back_in_ref[...], gin)])
    summed_ref[...] = low(total_ref[...] + dot(place, low(act - base)))
    grecv_out_ref[...] = grecv
    gsent_out_ref[...] = gsent


def last_weights(
    dims, place_ref, state_ref, summed_ref, cot_ref, grecv_ref, gsent_ref, update_ref,
    keep_ref, give_ref, mesh_ref,
):
    state, summed = state_ref[...], summed_ref[...]

    def store(at, value):
        store_blocks(keep_ref, give_ref, at, 3, value, dims, place_ref)

    both = dot(state, jnp.concatenate([gsent_ref[...], grecv_ref[...]], axis=1), TN)
    store(0, both[:, : state.shape[1]])
    store(1, both[:, state.shape[1] :])
    store(2, dot(summed, cot_ref[...], TN))
    mesh_ref[...] = low(state.astype(F32) + dot(summed, update_ref[1]))


def back_local(
    dims, place_ref, gin_ref, slope_ref, slope_k_ref, slope_d_ref, send_ref, recv_ref, update_ref,
    back_t_ref, back_ref, targets_ref, state_ref, rows_ref, summed_ref, merged_ref, merged_r_ref,
    after_ref, part_ref, keep_ref, give_ref, keep2_ref, give2_ref, gpre_ref,
):
    nodes = gin_ref.shape[0]
    degree = slope_ref.shape[0]
    gin = gin_ref[...]
    gsum = low(dot(gin, update_ref[0], NT))
    place, back = back_t_ref[...], back_ref[...]
    gsum_n = low(dot(back, gsum))
    gpre_k = gsum_n * slope_k_ref[...]
    grecv = dot(place, gsum_n * slope_d_ref[...])
    for j in range(degree):
        gpre = gsum * slope_ref[j]
        grecv = grecv + gpre.astype(F32)
        gpre_ref[j * nodes : (j + 1) * nodes, :] = gpre
    gsent = dot(targets_ref[...], gpre_ref[...])
    grecv, gsent = low(grecv), low(gsent)
    part = gin.astype(F32) + dot(grecv, recv_ref[0], NT) + dot(gsent, send_ref[0], NT)
    part_ref[...] = part
    state = state_ref[...]

    def store(at, value):
        store_blocks(keep_ref, give_ref, at, 2, value, dims, place_ref)

    def store2(at, value):
        store_blocks(keep2_ref, give2_ref, at, 2, value, dims, place_ref)

    both = dot(state, jnp.concatenate([gsent, grecv], axis=1), TN)
    store(0, both[:, : state.shape[1]] + dot(rows_ref[...], gpre_k, TN))
    store(1, both[:, state.shape[1] :])
    store2(0, dot(summed_ref[...], gin, TN))
    far = low(dot(gpre_k, send_ref[0], NT))
    store2(1, dot(merged_ref[...], low(part), TN) + dot(merged_r_ref[...], far, TN))


def embed_back(peers, dims, carry, *refs):
    arr_refs, refs = refs[:peers][::-1], refs[peers:]
    (place_ref, slope_r_ref, part_ref, update_ref, send_ref, merge_ref, border_t_ref, target_ref,
     sends_ref, incoming_ref, slope_g_ref, slope_a_ref, grid_ref, lat_ref, embed_ref,
     gpre_ref, keep_ref, give_ref, *pay_refs) = refs
    nodes = part_ref.shape[0]
    chosen = grid_ref.shape[0]
    taken = sends_ref.shape[0]
    (arrived,) = split_parts(arr_refs, (0,), (BORDER,))
    gsum = low(dot(low(arrived), update_ref[0], NT)).astype(F32)
    gpre = low(gsum * slope_r_ref[...].astype(F32))
    gsent = low(dot(border_t_ref[...], gpre))
    gin = low(part_ref[...] + dot(gsent, send_ref[0], NT))
    gmerged = low(dot(gin, merge_ref[...], NT))
    gpre_a = low(dot(incoming_ref[...], gmerged, TN) * slope_a_ref[...].astype(F32))
    sent = jnp.max(hot(sends_ref[...] == iota(taken, chosen, 1)), axis=0, keepdims=True)
    label = jnp.where(sent > 0.0, nodes, target_ref[...])
    pick = low(hot(label == iota(nodes, chosen, 0)))
    gpre_g = low(dot(pick, gmerged, TN) * slope_g_ref[...].astype(F32))
    gpre_ref[...] = gpre_g
    grad = dot(grid_ref[...], gpre_g, TN) + dot(lat_ref[...], gpre_a, TN)
    store_blocks(keep_ref, give_ref, 0, 1, grad, dims, place_ref)
    rows = dot(gpre_a, embed_ref[...], NT)
    store_parts(pay_refs, [rows])
    if carry:
        size = taken // peers
        start = keep_ref.shape[0]
        give_ref[start : start + 2 * size, :] = low(
            jnp.concatenate([rows[:size], rows[2 * size : 3 * size]], axis=0)
        )


def grid_local(gpre_ref, weight_ref, out_ref):
    out_ref[...] = low(dot(gpre_ref[...], weight_ref[...], NT))


def grid_patch(local_ref, sends_ref, arr_refs, out_ref):
    chosen = local_ref.shape[0]
    taken = sends_ref.shape[1]
    size = taken // len(arr_refs)
    place = low(hot(sends_ref[...] == iota(chosen, taken, 0)))
    rows = [ref[...].astype(F32) for ref in arr_refs]
    rows = low(jnp.concatenate([row[row.shape[0] - size :] for row in rows], axis=0))
    out_ref[...] = low(local_ref[...].astype(F32) + dot(place, rows))


def grid_place(peers, *refs):
    arr_refs, (local_ref, sends_ref, out_ref) = refs[:peers][::-1], refs[peers:]
    grid_patch(local_ref, sends_ref, arr_refs, out_ref)


def sum_last(sums, outs):
    (keep1_ref, arr1_ref, keep0_ref, arr0_ref, keep2_ref, arr2_ref, keep_e_ref, arr_e_ref) = sums
    embed_ref, merge_ref, send_ref, recv_ref, update_ref = outs
    last = keep1_ref[...].astype(F32) + arr1_ref[...].astype(F32)
    first = keep0_ref[...].astype(F32) + arr0_ref[...].astype(F32)
    second = keep2_ref[...].astype(F32) + arr2_ref[...].astype(F32)
    depth = embed_ref.shape[0]
    embed_ref[...] = keep_e_ref[...].astype(F32) + arr_e_ref[:depth, :].astype(F32)
    for at, ref in enumerate((send_ref, recv_ref, update_ref)):
        ref[1] = last[at * depth : (at + 1) * depth]
    send_ref[0], recv_ref[0], update_ref[0] = first[:depth], first[depth:], second[:depth]
    merge_ref[...] = second[depth:]


def finish(*refs):
    sum_last(refs[:8], refs[8:])


def finish_all(*refs):
    sums, rows, (local_ref, sends_ref), outs = refs[:8], refs[8:12], refs[12:14], refs[14:]
    grid_patch(local_ref, sends_ref, (*rows, sums[7]), outs[0])
    sum_last(sums, outs[1:])


def body(
    dims,
    grid_latent, mesh_latent, cotangent, embed_weight, merge_weight, send_weight, recv_weight,
    update_weight, target_row, send_rows, incoming_rows, border_mesh_rows, mesh_senders,
):
    chosen, width = grid_latent.shape
    nodes, degree = mesh_senders.shape
    slots, capacity = send_rows.shape[1:]
    column = dims[1] * dims[2]
    peers = slots - 1
    halo = peers * BORDER
    taken = peers * capacity
    total = dims[0] * dims[1] * dims[2]
    bits = (total - 1).bit_length()
    carry = dims == (4, 2, 2) and fine(width, dims)
    spot = lax.axis_index(GROUP)
    place = [lax.axis_index(COLUMN), lax.axis_index("lon") % 2]
    place += [(spot >> bit) % 2 for bit in range(bits)]
    place = jnp.stack(place).astype(I32).reshape(1, 2 + bits)
    raw = [a.transpose(1, 0, 2) for a in (send_rows, incoming_rows, border_mesh_rows)]
    unit = 2 * nodes * width * width

    loads = (raw[0], grid_latent, embed_weight, target_row.reshape(1, chosen), mesh_senders.T,
             *raw[1:])
    raw_sends, grid, embed, targets, senders_raw, raw_incoming, raw_bounds, sends, *pay1 = call(
        lambda *refs: first_payload(column, len(loads), *refs), "first_payload",
        [shape(taken, 1, dtype=I32)] + [shape(capacity, width)] * peers,
        (place,), flops=unit // 2, loads=loads,
    )
    arr1 = exchange(pay1, dims)
    (mesh, merge, cot, local, slope_g, sends_row, incoming, border, border_t, back, back_t, senders_t,
     senders, place) = call(
        lambda *refs: embed_local(column, *refs), "embed_local",
        [shape(nodes, width, dtype=F32), shape(chosen, width), shape(1, taken, dtype=I32),
         shape(nodes, taken), shape(halo, nodes), shape(nodes, halo), shape(halo, nodes),
         shape(nodes, halo), shape(degree, nodes, dtype=I32), shape(nodes, 8, dtype=I32),
         shape(1, 2 + bits, dtype=I32)],
        (place, raw_sends, raw_incoming, raw_bounds, senders_raw, grid, embed, targets, sends),
        flops=3 * unit,
        loads=(mesh_latent, merge_weight, cotangent),
    )
    merged, state0, slope_a, lat_a, *pay2 = call(
        lambda *refs: merge_nodes(peers, *refs), "merge_nodes",
        [shape(nodes, width), shape(nodes, width), shape(taken, width), shape(taken, width)]
        + [shape(4 * BORDER, width)] * peers,
        (*arr1, incoming, embed, local, mesh, merge, border, back, cot),
        flops=2 * unit,
    )
    arr2 = exchange(pay2, dims)
    total0, slope0, recv_n0, sent_b0, gsum1, edges = call(
        forward_local, "forward_local",
        [shape(nodes, width, dtype=F32), shape(degree, nodes, width),
         shape(halo, width, dtype=F32), shape(halo, width), shape(nodes, width),
         shape(nodes, degree * nodes)],
        (state0, send_weight, recv_weight, update_weight, cot, senders, senders_t, border, back),
        flops=6 * unit,
    )
    summed0, state1, pre0, rows0, back0, merged_r, cot_r, *pay3 = call(
        lambda *refs: forward_halo(peers, *refs), "forward_halo",
        [shape(nodes, width), shape(nodes, width), shape(halo, width, dtype=F32)]
        + [shape(halo, width)] * 4 + [shape(2 * BORDER, width)] * peers,
        (*arr2, recv_n0, total0, state0, send_weight, update_weight, back_t, back, border),
        flops=2 * unit,
    )
    arr3 = exchange(pay3, dims)
    (total1, grecv_l, gsent_l, recv_n1, sent_b1, gsum_n1, gsum_r1, slope_k0, slope_d0,
     slope_r0) = call(
        turn_local, "turn_local",
        [shape(nodes, width, dtype=F32)] * 3 + [shape(halo, width, dtype=F32)]
        + [shape(halo, width)] * 6,
        (state1, send_weight, recv_weight, update_weight, gsum1, cot_r, pre0, recv_n0, back0,
         sent_b0, senders, edges, border, back),
        flops=10 * unit, scratch=[pltpu.VMEM((degree * nodes, width), BF)],
    )
    summed1, grecv1, gsent1, gin1, *pay4 = call(
        lambda *refs: turn_halo(peers, *refs), "turn_halo",
        [shape(nodes, width)] * 4 + [shape(BORDER, width)] * peers,
        (*arr3, recv_n1, sent_b1, gsum_n1, gsum_r1, total1, grecv_l, gsent_l, cot,
         send_weight, recv_weight, back_t, back, border_t),
        flops=3 * unit,
    )
    arr4 = exchange(pay4, dims)
    keep1, give1, mesh_out = call(
        lambda *refs: last_weights(dims, *refs), "last_weights",
        blocks_shapes(3, width, width, dims) + [shape(nodes, width)],
        (place, state1, summed1, cot, grecv1, gsent1, update_weight), flops=4 * unit,
    )
    split = fine(width, dims)
    if split:
        give1, last = lax.optimization_barrier((give1, arr4[-1]))
        arr4 = (*arr4[:-1], last)
        keep1, give1 = halve_step(1, keep1, swap(give1, 0, dims), place)
    part0, keep0, give0, keep2, give2 = call(
        lambda *refs: back_local(dims, *refs), "back_local",
        [shape(nodes, width, dtype=F32)] + blocks_shapes(2, width, width, dims) * 2,
        (place, gin1, slope0, slope_k0, slope_d0, send_weight, recv_weight, update_weight, back_t,
         back, edges, state0, rows0, summed0, merged, merged_r, keep1),
        flops=10 * unit, scratch=[pltpu.VMEM((degree * nodes, width), BF)],
    )
    if split:
        give0, give2, *arr4 = lax.optimization_barrier((give0, give2, *arr4))
        keep0, give0 = halve_step(1, keep0, swap(give0, 0, dims), place)
        keep0, *arr4 = lax.optimization_barrier((keep0, *arr4))
    shapes = blocks_shapes(1, width, width, dims)
    if carry:
        shapes[1] = shape(shapes[1].shape[0] + 2 * capacity, width)
    gpre_g, keep_e, give_e, *pay5 = call(
        lambda *refs: embed_back(peers, dims, carry, *refs), "embed_back",
        [shape(chosen, width)] + shapes + [shape(capacity, width)] * peers,
        (*arr4, place, slope_r0, part0, update_weight, send_weight, merge, border_t,
         targets, sends, incoming, slope_g, slope_a, grid, lat_a, embed),
        flops=6 * unit,
    )
    depth = width // total
    if not split:
        arr5 = exchange(pay5, dims)
        last, first, second, embed_sum = (
            scatter_plain(blocks, dims) for blocks in (keep1, keep0, keep2, keep_e)
        )
        plain = [jnp.stack([a, last[i]]) for i, a in enumerate((first[0], first[1], second[0]))]
        plain = [embed_sum[0], second[1], *plain]
    elif not carry:
        arr5 = exchange(pay5, dims)
        sums = [
            rest_of_halving(1, keep1, give1, place, dims),
            rest_of_halving(1, keep0, give0, place, dims),
            rest_of_halving(0, keep2, give2, place, dims),
            rest_of_halving(0, keep_e, give_e, place, dims),
        ]
    else:
        arr1 = swap(give1, 1, dims)
        arr0 = swap(give0, 1, dims)
        arr2 = swap(give2, 0, dims)
        (local_rows,) = call(
            grid_local, "grid_local", [shape(chosen, width)], (gpre_g, embed), flops=0, size=0
        )
        arr_e, arr1 = lax.optimization_barrier((swap(give_e, 0, dims), arr1))
        keep1, local_rows = lax.optimization_barrier((keep1, local_rows))
        keep1, give1 = halve_step(2, keep1, arr1, place)
        arr1 = swap(give1, 2, dims)
        keep_e, keep1 = lax.optimization_barrier((keep_e, keep1))
        keep_e, give_e, from_sub = carry_step(1, keep_e, arr_e, pay5[1:2], place, capacity)
        arr_e = swap(give_e, 1, dims)
        keep2, keep_e = lax.optimization_barrier((keep2, keep_e))
        keep2, give2 = halve_step(1, keep2, arr2, place)
        arr2 = swap(give2, 1, dims)
        keep0, keep2 = lax.optimization_barrier((keep0, keep2))
        keep0, give0 = halve_step(2, keep0, arr0, place)
        arr0 = swap(give0, 2, dims)
        keep1, keep0 = lax.optimization_barrier((keep1, keep0))
        keep1, give1 = halve_step(3, keep1, arr1, place)
        arr1 = swap(give1, 3, dims)
        keep2, keep1 = lax.optimization_barrier((keep2, keep1))
        keep2, give2 = halve_step(2, keep2, arr2, place)
        arr2 = swap(give2, 2, dims)
        keep0, keep2 = lax.optimization_barrier((keep0, keep2))
        keep0, give0 = halve_step(3, keep0, arr0, place)
        arr0 = swap(give0, 3, dims)
        keep_e, keep0, arr1 = lax.optimization_barrier((keep_e, keep0, arr1))
        keep_e, give_e, from_lat, from_diag = carry_step(
            2, keep_e, arr_e, pay5[3:], place, capacity
        )
        arr_e = swap(give_e, 2, dims)
        keep2, keep_e = lax.optimization_barrier((keep2, keep_e))
        keep2, give2 = halve_step(3, keep2, arr2, place)
        arr2 = swap(give2, 3, dims)
        keep_e, keep2 = lax.optimization_barrier((keep_e, keep2))
        keep_e, give_e, from_near = carry_step(3, keep_e, arr_e, (), place, capacity)
        arr_e = swap(give_e, 3, dims)
        sums = ((keep1, arr1), (keep0, arr0), (keep2, arr2), (keep_e, arr_e))
    grads = [shape(depth, width, dtype=F32)] * 2 + [shape(2, depth, width, dtype=F32)] * 3
    if carry:
        return (mesh_out, *call(
            finish_all, "finish_all", [shape(chosen, width)] + grads,
            (*(part for pair in sums for part in pair), from_sub, from_lat, from_diag, from_near,
             local_rows, sends_row),
            flops=unit,
        ))
    (local_rows,) = call(
        grid_local, "grid_local", [shape(chosen, width)], (gpre_g, embed), flops=2 * unit
    )
    (grid_grad,) = call(
        lambda *refs: grid_place(peers, *refs), "grid_place", [shape(chosen, width)],
        (*arr5, local_rows, sends_row), flops=unit,
    )
    if split:
        grads = call(
            finish, "finish", grads, [part for pair in sums for part in pair],
            flops=8 * depth * width,
        )
    else:
        grads = plain
    return (mesh_out, grid_grad, *grads)


def solution(mesh):
    split = ("groups", "lon", "lat", "sub")
    dims = tuple(mesh.shape[axis] for axis in GROUP)
    rows = P(split, None)
    whole = P("groups", GROUP, None)
    in_specs = (
        rows, rows, rows, P(), P(), P(), P(), P(), P(split), P(split, None, None),
        P(split, None, None), P(split, None, None), rows,
    )
    out_specs = (rows, rows, rows, rows, whole, whole, whole)
    return jax.shard_map(
        lambda *args: body(dims, *args),
        mesh=mesh, in_specs=in_specs, out_specs=out_specs, check_vma=False,
    )
```

```python
import jax
import jax.numpy as jnp
from jax import lax
from jax.experimental import pallas as pl
from jax.experimental.pallas import tpu as pltpu
from jax.sharding import PartitionSpec as P

BF = jnp.bfloat16
F32 = jnp.float32
I32 = jnp.int32
NN = (((1,), (0,)), ((), ()))
NT = (((1,), (1,)), ((), ()))
TN = (((0,), (0,)), ((), ()))
BORDER = 8
GROUP = ("lon", "lat", "sub")
COLUMN = ("lat", "sub")


def dot(a, b, dims=NN):
    return lax.dot_general(a, b, dims, preferred_element_type=F32)


def low(value):
    return value.astype(BF)


def sigmoid(value):
    return 0.5 * jnp.tanh(0.5 * value) + 0.5


def silu(value):
    return value * sigmoid(value)


def silu_both(value):
    sig = sigmoid(value)
    act = value * sig
    return act, sig + act * (1.0 - sig)


def silu_slope(value):
    return silu_both(value)[1]


def iota(rows, columns, dim):
    return lax.broadcasted_iota(I32, (rows, columns), dim)


def hot(mask):
    return jnp.where(mask, 1.0, 0.0)


def slot_rows(ref):
    return jnp.concatenate([ref[s] for s in range(ref.shape[0])], axis=0)


def slot_of(at, column, me, odd):
    far = jnp.where(at == column - 1, column + 1 - odd, column + odd)
    return jnp.where(at < column - 1, jnp.bitwise_xor(at + 1, me), far)


def as_column(values, wide, column, me, odd):
    slots = values.shape[0]
    count = (slots - 1) * wide
    row = iota(count, slots, 0)
    pick = low(hot(slot_of(row // wide, column, me, odd) == iota(count, slots, 1)))
    found = 16.0 * dot(pick, low((values // 16).astype(F32)))
    found = found + dot(pick, low((values % 16).astype(F32)))
    keep = iota(count, wide, 0) % wide == iota(count, wide, 1)
    return jnp.sum(jnp.where(keep, found, 0.0), axis=1, keepdims=True).astype(I32)


def as_row(values, wide, column, me, odd):
    slots = values.shape[0]
    count = (slots - 1) * wide
    pick = low(hot(iota(wide, count, 1) % wide == iota(wide, count, 0)))
    found = 16.0 * dot(low((values // 16).astype(F32)), pick)
    found = found + dot(low((values % 16).astype(F32)), pick)
    at = iota(slots, count, 1) // wide
    keep = slot_of(at, column, me, odd) == iota(slots, count, 0)
    return jnp.sum(jnp.where(keep, found, 0.0), axis=0, keepdims=True).astype(I32)


def split_parts(refs, starts, sizes):
    values = [ref[...].astype(F32) for ref in refs]
    return [
        jnp.concatenate([value[start : start + size] for value in values], axis=0)
        for start, size in zip(starts, sizes)
    ]


def store_parts(refs, parts):
    peers = len(refs)
    for at, ref in enumerate(refs):
        rows = []
        for part in parts:
            size = part.shape[0] // peers
            rows.append(part[at * size : (at + 1) * size])
        ref[...] = low(rows[0] if len(rows) == 1 else jnp.concatenate(rows, axis=0))


def receivers(senders_t, halo):
    degree, nodes = senders_t.shape
    found = jnp.zeros((halo, nodes), F32)
    ids = iota(halo, nodes, 0) + nodes
    for j in range(degree):
        found = found + hot(senders_t[j : j + 1, :] == ids)
    return found


def receivers_t(senders, degree, halo):
    nodes = senders.shape[0]
    found = jnp.zeros((nodes, halo), F32)
    ids = iota(nodes, halo, 1) + nodes
    for j in range(degree):
        found = found + hot(senders[:, j : j + 1] == ids)
    return found


def fine(rows, dims):
    return (rows // (dims[0] * dims[1] * dims[2])) % 16 == 0


LON_FIRST = (0, 2, 3, 1)


def block_spot(block, order):
    spot = 0
    for bit in order:
        spot = 2 * spot + (block >> bit) % 2
    return spot


def store_blocks(keep_ref, give_ref, at, count, value, dims, bits_ref, order=None):
    value = low(value)
    rows = value.shape[0]
    total = dims[0] * dims[1] * dims[2]
    depth = rows // total
    if not fine(rows, dims):
        keep_ref[at] = value
        return
    bits = (total - 1).bit_length()
    upper = bits_ref[0:1, 2:3] == 1
    for block in range(0, total, 2):
        start = block_spot(block, order or range(bits)) * count * depth + at * depth
        first = value[block * depth : (block + 1) * depth].astype(F32)
        second = value[(block + 1) * depth : (block + 2) * depth].astype(F32)
        keep_ref[start : start + depth, :] = low(jnp.where(upper, second, first))
        give_ref[start : start + depth, :] = low(jnp.where(upper, first, second))


def blocks_shapes(count, rows, width, dims):
    if fine(rows, dims):
        return [jax.ShapeDtypeStruct((count * rows // 2, width), BF)] * 2
    return [jax.ShapeDtypeStruct((count, rows, width), BF), jax.ShapeDtypeStruct((16, width), BF)]


def halve(bit, bits_ref, keep_ref, arr_ref, keep_out, give_out):
    half = keep_ref.shape[0] // 2
    upper = bits_ref[0:1, 2 + bit : 3 + bit] == 1
    first = keep_ref[:half, :].astype(F32) + arr_ref[:half, :].astype(F32)
    second = keep_ref[half:, :].astype(F32) + arr_ref[half:, :].astype(F32)
    keep_out[...] = low(jnp.where(upper, second, first))
    give_out[...] = low(jnp.where(upper, first, second))


def swap(block, bit, dims):
    total = dims[0] * dims[1] * dims[2]
    return lax.ppermute(block, GROUP, [(i, i ^ (1 << bit)) for i in range(total)])


def halve_step(bit, keep, arrived, place):
    rows, width = keep.shape[0] // 2, keep.shape[1]
    return call(
        lambda *refs: halve(bit, *refs), "halve", [shape(rows, width)] * 2,
        (place, keep, arrived), flops=4 * rows * width, size=0,
    )


def rest_of_halving(first, keep, give, place, dims):
    bits = (dims[0] * dims[1] * dims[2] - 1).bit_length()
    arrived = swap(give, first, dims)
    for bit in range(first + 1, bits):
        keep, give = halve_step(bit, keep, arrived, place)
        arrived = swap(give, bit, dims)
    return keep, arrived


def halve_carry(bit, count, bits_ref, keep_ref, arr_ref, *refs):
    own_refs, (keep_out, give_out, *here_refs) = refs[:count], refs[count:]
    rows = keep_ref.shape[0]
    half = rows // 2
    size = here_refs[0].shape[0]
    upper = bits_ref[0:1, 2 + bit : 3 + bit] == 1
    value = arr_ref[...].astype(F32)
    first = keep_ref[:half, :].astype(F32) + value[:half]
    second = keep_ref[half:, :].astype(F32) + value[half:rows]
    keep_out[...] = low(jnp.where(upper, second, first))
    here_refs[0][...] = low(value[rows : rows + size])
    passed = value[rows + size :]
    extra = [ref[...].astype(F32) for ref in own_refs]
    if count < 2:
        extra.append(passed)
    elif len(here_refs) == 2:
        here_refs[1][...] = low(passed)
    give_out[...] = low(jnp.concatenate([jnp.where(upper, first, second), *extra], axis=0))


def carry_step(bit, keep, arrived, own, place, capacity):
    rows, width = keep.shape[0] // 2, keep.shape[1]
    count = len(own)
    both = count == 2 and arrived.shape[0] == 2 * (rows + capacity)
    return call(
        lambda *refs: halve_carry(bit, count, *refs), "halve_carry",
        [shape(rows, width), shape(rows + min(count + 1, 2) * capacity, width)]
        + [shape(capacity, width)] * (2 if both else 1),
        (place, keep, arrived, *own), flops=4 * rows * width, size=0,
    )


def scatter_plain(blocks, dims):
    lon, lat, sub = dims
    count, rows, width = blocks.shape
    depth = rows // (lon * lat * sub)
    blocks = blocks.reshape(count, lon, lat, sub, depth, width)
    blocks = blocks.transpose(3, 2, 1, 0, 4, 5)
    for axis in ("sub", "lat", "lon"):
        blocks = lax.psum_scatter(blocks, axis, scatter_dimension=0, tiled=False)
    return blocks.astype(F32)


def call(kernel, name, outs, args, flops, loads=(), scratch=(), size=None):
    if size is None:
        size = sum(a.size * a.dtype.itemsize for a in (*args, *outs, *loads))
    args = (*(pltpu.with_memory_space_constraint(a, pltpu.HBM) for a in loads), *args)
    scratch = list(scratch)
    if loads:
        scratch.append(pltpu.SemaphoreType.DMA((len(loads),)))
    in_specs = [pl.BlockSpec(memory_space=pltpu.HBM)] * len(loads)
    in_specs += [pl.BlockSpec(memory_space=pltpu.VMEM)] * (len(args) - len(loads))
    return pl.pallas_call(
        kernel,
        out_shape=[shape(*a.shape, dtype=a.dtype) for a in loads] + list(outs),
        in_specs=in_specs,
        out_specs=[pl.BlockSpec(memory_space=pltpu.VMEM)] * (len(outs) + len(loads)),
        scratch_shapes=scratch,
        compiler_params=pltpu.CompilerParams(vmem_limit_bytes=16 * 1024 * 1024),
        cost_estimate=pl.CostEstimate(flops=flops, bytes_accessed=size, transcendentals=0),
        name=name,
    )(*args)


def exchange(parts, dims):
    column = dims[1] * dims[2]
    count = dims[0]
    other = [(i, (i - 1 + 2 * (i % 2)) % count) for i in range(count)]
    far = lax.ppermute(parts[column], "lon", other)
    near = lax.ppermute(parts[column - 1], "lon", [(i, i ^ 1) for i in range(count)])
    arrived = [
        lax.ppermute(parts[r - 1], COLUMN, [(i, i ^ r) for i in range(column)])
        for r in range(column - 1, 0, -1)
    ]
    return (far, near, *arrived)


def shape(*dims, dtype=BF):
    return jax.ShapeDtypeStruct(dims, dtype)


def start_loads(sources, targets, sems):
    copies = [
        pltpu.make_async_copy(source, target, sems.at[at])
        for at, (source, target) in enumerate(zip(sources, targets))
    ]
    for copy in copies:
        copy.start()
    return copies


def first_payload(column, count, *refs):
    sources, place_ref, targets = refs[:count], refs[count], refs[count + 1 : 2 * count + 1]
    sends_out, *pay_refs, sems = refs[2 * count + 1 :]
    sends_ref, grid_ref = targets[:2]
    sends_load, grid_load, *loads = start_loads(sources, targets, sems)
    chosen = grid_ref.shape[0]
    me, odd = place_ref[:, 0:1], place_ref[:, 1:2]
    sends_load.wait()
    sends = slot_rows(sends_ref)
    sends = as_column(sends, sends.shape[1], column, me, odd)
    sends_out[...] = sends
    pick = low(hot(sends == iota(sends.shape[0], chosen, 1)))
    grid_load.wait()
    store_parts(pay_refs, [dot(pick, grid_ref[...])])
    for load in loads:
        load.wait()


def embed_local(
    column, mesh_far, merge_far, cot_far, place_in_ref, raw_sends_ref, raw_incoming_ref,
    raw_bounds_ref, senders_ref, grid_ref, weight_ref, target_ref, sends_ref, mesh_ref, merge_ref,
    cot_ref, sum_ref, slope_ref, sends_row_ref, incoming_ref, border_ref, border_t_ref, back_ref,
    back_t_ref, senders_t_ref, senders_out_ref, place_ref, sems,
):
    loads = start_loads((mesh_far, merge_far, cot_far), (mesh_ref, merge_ref, cot_ref), sems)
    chosen = grid_ref.shape[0]
    nodes = sum_ref.shape[0]
    taken = sends_ref.shape[0]
    act, slope = silu_both(dot(grid_ref[...], weight_ref[...]))
    slope_ref[...] = low(slope)
    sent = jnp.max(hot(sends_ref[...] == iota(taken, chosen, 1)), axis=0, keepdims=True)
    label = jnp.where(sent > 0.0, nodes, target_ref[...])
    sum_ref[...] = dot(low(hot(label == iota(nodes, chosen, 0))), low(act))
    place_ref[...] = place_in_ref[...]
    me, odd = place_in_ref[:, 0:1], place_in_ref[:, 1:2]
    raw_sends, incoming = slot_rows(raw_sends_ref), slot_rows(raw_incoming_ref)
    bounds = slot_rows(raw_bounds_ref)
    capacity = incoming.shape[1]
    sends_row_ref[...] = as_row(raw_sends, capacity, column, me, odd)
    halo = border_ref.shape[0]
    incoming = as_row(incoming, capacity, column, me, odd)
    incoming_ref[...] = low(hot(incoming == iota(nodes, taken, 0)))
    border = as_column(bounds, BORDER, column, me, odd)
    border_ref[...] = low(hot(border == iota(halo, nodes, 1)))
    border = as_row(bounds, BORDER, column, me, odd)
    border_t_ref[...] = low(hot(border == iota(nodes, halo, 0)))
    senders = senders_ref[...]
    degree = senders.shape[0]
    offset = senders - nodes
    slot = offset // BORDER
    far = jnp.where(slot == column, column - odd, column - 1 + odd)
    at = jnp.where(slot < column, jnp.bitwise_xor(slot, me) - 1, far)
    senders = jnp.where(offset < 0, senders, nodes + at * BORDER + offset % BORDER)
    senders_t_ref[...] = senders
    filler = jnp.zeros((8 - degree, nodes), I32)
    back_ref[...] = low(receivers(senders, halo))
    senders_t = jnp.concatenate([senders, filler], axis=0).T
    senders_out_ref[...] = senders_t
    back_t_ref[...] = low(receivers_t(senders_t, degree, halo))
    for load in loads:
        load.wait()


def merge_nodes(peers, *refs):
    arr_refs, refs = refs[:peers][::-1], refs[peers:]
    (incoming_ref, embed_ref, local_ref, mesh_ref, weight_ref, border_ref, back_ref, cot_ref,
     merged_ref, state_ref, slope_ref, lat_ref, *pay_refs) = refs
    lat = jnp.concatenate([ref[...] for ref in arr_refs], axis=0)
    lat_ref[...] = lat
    act, slope = silu_both(dot(lat, embed_ref[...]))
    slope_ref[...] = low(slope)
    merged = low(local_ref[...] + dot(incoming_ref[...], low(act)))
    merged_ref[...] = merged
    state = low(mesh_ref[...].astype(F32) + dot(merged, weight_ref[...]))
    state_ref[...] = state
    border, back = border_ref[...], back_ref[...]
    store_parts(
        pay_refs,
        [dot(border, state), dot(back, state), dot(border, merged), dot(back, cot_ref[...])],
    )


def local_edges(senders, degree, sent, recv, each):
    nodes = senders.shape[0]
    total = None
    ids = iota(nodes, nodes, 1)
    for j in range(degree):
        act, slope = silu_both(dot(low(hot(senders[:, j : j + 1] == ids)), sent) + recv)
        total = act if total is None else total + act
        each(j, slope)
    return total


def edge_targets(senders_t):
    degree, nodes = senders_t.shape
    ids = iota(nodes, nodes, 0)
    return jnp.concatenate(
        [low(hot(senders_t[j : j + 1, :] == ids)) for j in range(degree)], axis=1
    )


def forward_local(
    state_ref, send_ref, recv_ref, update_ref, cot_ref, senders_ref, senders_t_ref, border_ref,
    back_ref, total_ref, slope_ref, recv_n_ref, sent_b_ref, gsum_ref, targets_ref,
):
    state = state_ref[...]
    sent = low(dot(state, send_ref[0]))
    recv = dot(state, recv_ref[0])

    def keep(j, slope):
        slope_ref[j] = low(slope)

    total_ref[...] = local_edges(senders_ref[...], senders_t_ref.shape[0], sent, recv, keep)
    recv_n_ref[...] = dot(low(dot(back_ref[...], state)), recv_ref[0])
    sent_b_ref[...] = low(dot(border_ref[...], sent))
    gsum_ref[...] = low(dot(cot_ref[...], update_ref[1], NT))
    targets_ref[...] = edge_targets(senders_t_ref[...])


def forward_halo(peers, *refs):
    arr_refs, refs = refs[:peers][::-1], refs[peers:]
    (recv_n_ref, total_ref, state_ref, send_ref, update_ref, back_t_ref, back_in_ref,
     border_ref, summed_ref, out_ref, pre_ref, rows_ref, back_ref, merged_ref, cot_ref,
     *pay_refs) = refs
    rows, back, merged, cot = split_parts(
        arr_refs, (0, BORDER, 2 * BORDER, 3 * BORDER), (BORDER,) * 4
    )
    rows_ref[...], back_ref[...] = low(rows), low(back)
    merged_ref[...], cot_ref[...] = low(merged), low(cot)
    pre = low(dot(low(rows), send_ref[0])).astype(F32) + recv_n_ref[...]
    pre_ref[...] = pre
    place = back_t_ref[...]
    extra = silu(pre) - silu(recv_n_ref[...])
    summed = low(total_ref[...] + dot(place, low(extra)))
    summed_ref[...] = summed
    state = low(state_ref[...].astype(F32) + dot(summed, update_ref[0]))
    out_ref[...] = state
    store_parts(pay_refs, [dot(border_ref[...], state), dot(back_in_ref[...], state)])


def turn_local(
    state_ref, send_ref, recv_ref, update_ref, gsum_ref, cot_r_ref, pre_ref, recv_n0_ref, back0_ref,
    sent_b0_ref, senders_ref, targets_ref, border_ref, back_ref,
    total_ref, grecv_ref, gsent_ref, recv_n_ref, sent_b_ref, gsum_n_ref, gsum_r_ref,
    slope_k_ref, slope_d_ref, slope_r_ref, gpre_ref,
):
    slope = silu_slope(pre_ref[...])
    slope_k_ref[...] = low(slope)
    slope_d_ref[...] = low(slope - silu_slope(recv_n0_ref[...]))
    pre = sent_b0_ref[...].astype(F32) + dot(back0_ref[...], recv_ref[0])
    slope_r_ref[...] = low(silu_slope(pre))
    state = state_ref[...]
    nodes = state.shape[0]
    sent = low(dot(state, send_ref[1]))
    recv = dot(state, recv_ref[1])
    gsum = gsum_ref[...]
    grad = gsum.astype(F32)
    grecv = []

    def back_edge(j, slope):
        gpre = grad * slope
        grecv.append(gpre if j == 0 else grecv[-1] + gpre)
        gpre_ref[j * nodes : (j + 1) * nodes, :] = low(gpre)

    degree = targets_ref.shape[1] // nodes
    total_ref[...] = local_edges(senders_ref[...], degree, sent, recv, back_edge)
    grecv_ref[...] = grecv[-1]
    gsent_ref[...] = dot(targets_ref[...], gpre_ref[...])
    back = back_ref[...]
    recv_n_ref[...] = dot(low(dot(back, state)), recv_ref[1])
    sent_b_ref[...] = low(dot(border_ref[...], sent))
    gsum_n_ref[...] = low(dot(back, gsum))
    gsum_r_ref[...] = low(dot(cot_r_ref[...], update_ref[1], NT))


def turn_halo(peers, *refs):
    arr_refs, refs = refs[:peers][::-1], refs[peers:]
    (recv_n_ref, sent_b_ref, gsum_n_ref, gsum_r_ref, total_ref, grecv_ref, gsent_ref, cot_ref,
     send_ref, recv_ref, back_t_ref, back_in_ref, border_t_ref, summed_ref, grecv_out_ref,
     gsent_out_ref, gin_ref, *pay_refs) = refs
    rows, back = split_parts(arr_refs, (0, BORDER), (BORDER,) * 2)
    pre = low(dot(low(rows), send_ref[1])).astype(F32) + recv_n_ref[...]
    act, slope = silu_both(pre)
    place = back_t_ref[...]
    base, base_slope = silu_both(recv_n_ref[...])
    gpre = low(gsum_n_ref[...].astype(F32) * (slope - base_slope))
    grecv = low(grecv_ref[...] + dot(place, gpre))
    pre = sent_b_ref[...].astype(F32) + dot(low(back), recv_ref[1])
    gpre = low(gsum_r_ref[...].astype(F32) * silu_slope(pre))
    gsent = low(gsent_ref[...] + dot(border_t_ref[...], gpre))
    gin = cot_ref[...].astype(F32) + dot(grecv, recv_ref[1], NT) + dot(gsent, send_ref[1], NT)
    gin = low(gin)
    gin_ref[...] = gin
    store_parts(pay_refs, [dot(back_in_ref[...], gin)])
    summed_ref[...] = low(total_ref[...] + dot(place, low(act - base)))
    grecv_out_ref[...] = grecv
    gsent_out_ref[...] = gsent


def last_weights(
    dims, place_ref, state_ref, summed_ref, cot_ref, grecv_ref, gsent_ref, update_ref,
    keep_ref, give_ref, mesh_ref,
):
    state, summed = state_ref[...], summed_ref[...]

    def store(at, value):
        store_blocks(keep_ref, give_ref, at, 3, value, dims, place_ref)

    both = dot(state, jnp.concatenate([gsent_ref[...], grecv_ref[...]], axis=1), TN)
    store(0, both[:, : state.shape[1]])
    store(1, both[:, state.shape[1] :])
    store(2, dot(summed, cot_ref[...], TN))
    mesh_ref[...] = low(state.astype(F32) + dot(summed, update_ref[1]))


def back_local(
    dims, place_ref, gin_ref, slope_ref, slope_k_ref, slope_d_ref, send_ref, recv_ref, update_ref,
    back_t_ref, back_ref, targets_ref, state_ref, rows_ref, summed_ref, merged_ref, merged_r_ref,
    after_ref, part_ref, keep_ref, give_ref, keep2_ref, give2_ref, gpre_ref,
):
    nodes = gin_ref.shape[0]
    degree = slope_ref.shape[0]
    gin = gin_ref[...]
    gsum = low(dot(gin, update_ref[0], NT))
    place, back = back_t_ref[...], back_ref[...]
    gsum_n = low(dot(back, gsum))
    gpre_k = gsum_n * slope_k_ref[...]
    grecv = dot(place, gsum_n * slope_d_ref[...])
    for j in range(degree):
        gpre = gsum * slope_ref[j]
        grecv = grecv + gpre.astype(F32)
        gpre_ref[j * nodes : (j + 1) * nodes, :] = gpre
    gsent = dot(targets_ref[...], gpre_ref[...])
    grecv, gsent = low(grecv), low(gsent)
    part = gin.astype(F32) + dot(grecv, recv_ref[0], NT) + dot(gsent, send_ref[0], NT)
    part_ref[...] = part
    state = state_ref[...]

    def store(at, value):
        store_blocks(keep_ref, give_ref, at, 2, value, dims, place_ref)

    def store2(at, value):
        store_blocks(keep2_ref, give2_ref, at, 2, value, dims, place_ref)

    both = dot(state, jnp.concatenate([gsent, grecv], axis=1), TN)
    store(0, both[:, : state.shape[1]] + dot(rows_ref[...], gpre_k, TN))
    store(1, both[:, state.shape[1] :])
    store2(0, dot(summed_ref[...], gin, TN))
    far = low(dot(gpre_k, send_ref[0], NT))
    store2(1, dot(merged_ref[...], low(part), TN) + dot(merged_r_ref[...], far, TN))


def embed_back(peers, dims, carry, *refs):
    arr_refs, refs = refs[:peers][::-1], refs[peers:]
    (place_ref, slope_r_ref, part_ref, update_ref, send_ref, merge_ref, border_t_ref, target_ref,
     sends_ref, incoming_ref, slope_g_ref, slope_a_ref, grid_ref, lat_ref, embed_ref,
     gpre_ref, keep_ref, give_ref, *pay_refs) = refs
    nodes = part_ref.shape[0]
    chosen = grid_ref.shape[0]
    taken = sends_ref.shape[0]
    (arrived,) = split_parts(arr_refs, (0,), (BORDER,))
    gsum = low(dot(low(arrived), update_ref[0], NT)).astype(F32)
    gpre = low(gsum * slope_r_ref[...].astype(F32))
    gsent = low(dot(border_t_ref[...], gpre))
    gin = low(part_ref[...] + dot(gsent, send_ref[0], NT))
    gmerged = low(dot(gin, merge_ref[...], NT))
    gpre_a = low(dot(incoming_ref[...], gmerged, TN) * slope_a_ref[...].astype(F32))
    sent = jnp.max(hot(sends_ref[...] == iota(taken, chosen, 1)), axis=0, keepdims=True)
    label = jnp.where(sent > 0.0, nodes, target_ref[...])
    pick = low(hot(label == iota(nodes, chosen, 0)))
    gpre_g = low(dot(pick, gmerged, TN) * slope_g_ref[...].astype(F32))
    gpre_ref[...] = gpre_g
    grad = dot(grid_ref[...], gpre_g, TN) + dot(lat_ref[...], gpre_a, TN)
    store_blocks(
        keep_ref, give_ref, 0, 1, grad, dims, place_ref, LON_FIRST if carry else None
    )
    rows = dot(gpre_a, embed_ref[...], NT)
    store_parts(pay_refs, [rows])
    if carry:
        size = taken // peers
        start = keep_ref.shape[0]
        give_ref[start : start + 2 * size, :] = low(
            jnp.concatenate([rows[:size], rows[2 * size : 3 * size]], axis=0)
        )


def grid_local(gpre_ref, weight_ref, out_ref):
    out_ref[...] = low(dot(gpre_ref[...], weight_ref[...], NT))


def grid_patch(local_ref, sends_ref, arr_refs, out_ref):
    chosen = local_ref.shape[0]
    taken = sends_ref.shape[1]
    size = taken // len(arr_refs)
    place = low(hot(sends_ref[...] == iota(chosen, taken, 0)))
    rows = [ref[...].astype(F32) for ref in arr_refs]
    rows = low(jnp.concatenate([row[row.shape[0] - size :] for row in rows], axis=0))
    out_ref[...] = low(local_ref[...].astype(F32) + dot(place, rows))


def grid_place(peers, *refs):
    arr_refs, (local_ref, sends_ref, out_ref) = refs[:peers][::-1], refs[peers:]
    grid_patch(local_ref, sends_ref, arr_refs, out_ref)


def sum_last(sums, outs):
    (keep1_ref, arr1_ref, keep0_ref, arr0_ref, keep2_ref, arr2_ref, keep_e_ref, arr_e_ref) = sums
    embed_ref, merge_ref, send_ref, recv_ref, update_ref = outs
    last = keep1_ref[...].astype(F32) + arr1_ref[...].astype(F32)
    first = keep0_ref[...].astype(F32) + arr0_ref[...].astype(F32)
    second = keep2_ref[...].astype(F32) + arr2_ref[...].astype(F32)
    depth = embed_ref.shape[0]
    embed_ref[...] = keep_e_ref[...].astype(F32) + arr_e_ref[:depth, :].astype(F32)
    for at, ref in enumerate((send_ref, recv_ref, update_ref)):
        ref[1] = last[at * depth : (at + 1) * depth]
    send_ref[0], recv_ref[0], update_ref[0] = first[:depth], first[depth:], second[:depth]
    merge_ref[...] = second[depth:]


def finish(*refs):
    sum_last(refs[:8], refs[8:])


def finish_all(*refs):
    sums, (sub, near, far, local_ref, sends_ref), outs = refs[:8], refs[8:13], refs[13:]
    depth = outs[1].shape[0]
    size = sub.shape[0]
    lat, diag = sums[7].at[depth : depth + size], sums[7].at[depth + size :]
    grid_patch(local_ref, sends_ref, (sub, lat, diag, near, far), outs[0])
    sum_last(sums, outs[1:])


def body(
    dims,
    grid_latent, mesh_latent, cotangent, embed_weight, merge_weight, send_weight, recv_weight,
    update_weight, target_row, send_rows, incoming_rows, border_mesh_rows, mesh_senders,
):
    chosen, width = grid_latent.shape
    nodes, degree = mesh_senders.shape
    slots, capacity = send_rows.shape[1:]
    column = dims[1] * dims[2]
    peers = slots - 1
    halo = peers * BORDER
    taken = peers * capacity
    total = dims[0] * dims[1] * dims[2]
    bits = (total - 1).bit_length()
    carry = dims == (4, 2, 2) and fine(width, dims)
    spot = lax.axis_index(GROUP)
    place = [lax.axis_index(COLUMN), lax.axis_index("lon") % 2]
    place += [(spot >> bit) % 2 for bit in range(bits)]
    place = jnp.stack(place).astype(I32).reshape(1, 2 + bits)
    raw = [a.transpose(1, 0, 2) for a in (send_rows, incoming_rows, border_mesh_rows)]
    unit = 2 * nodes * width * width

    loads = (raw[0], grid_latent, embed_weight, target_row.reshape(1, chosen), mesh_senders.T,
             *raw[1:])
    raw_sends, grid, embed, targets, senders_raw, raw_incoming, raw_bounds, sends, *pay1 = call(
        lambda *refs: first_payload(column, len(loads), *refs), "first_payload",
        [shape(taken, 1, dtype=I32)] + [shape(capacity, width)] * peers,
        (place,), flops=unit // 2, loads=loads,
    )
    arr1 = exchange(pay1, dims)
    (mesh, merge, cot, local, slope_g, sends_row, incoming, border, border_t, back, back_t, senders_t,
     senders, place) = call(
        lambda *refs: embed_local(column, *refs), "embed_local",
        [shape(nodes, width, dtype=F32), shape(chosen, width), shape(1, taken, dtype=I32),
         shape(nodes, taken), shape(halo, nodes), shape(nodes, halo), shape(halo, nodes),
         shape(nodes, halo), shape(degree, nodes, dtype=I32), shape(nodes, 8, dtype=I32),
         shape(1, 2 + bits, dtype=I32)],
        (place, raw_sends, raw_incoming, raw_bounds, senders_raw, grid, embed, targets, sends),
        flops=3 * unit,
        loads=(mesh_latent, merge_weight, cotangent),
    )
    merged, state0, slope_a, lat_a, *pay2 = call(
        lambda *refs: merge_nodes(peers, *refs), "merge_nodes",
        [shape(nodes, width), shape(nodes, width), shape(taken, width), shape(taken, width)]
        + [shape(4 * BORDER, width)] * peers,
        (*arr1, incoming, embed, local, mesh, merge, border, back, cot),
        flops=2 * unit,
    )
    arr2 = exchange(pay2, dims)
    total0, slope0, recv_n0, sent_b0, gsum1, edges = call(
        forward_local, "forward_local",
        [shape(nodes, width, dtype=F32), shape(degree, nodes, width),
         shape(halo, width, dtype=F32), shape(halo, width), shape(nodes, width),
         shape(nodes, degree * nodes)],
        (state0, send_weight, recv_weight, update_weight, cot, senders, senders_t, border, back),
        flops=6 * unit,
    )
    summed0, state1, pre0, rows0, back0, merged_r, cot_r, *pay3 = call(
        lambda *refs: forward_halo(peers, *refs), "forward_halo",
        [shape(nodes, width), shape(nodes, width), shape(halo, width, dtype=F32)]
        + [shape(halo, width)] * 4 + [shape(2 * BORDER, width)] * peers,
        (*arr2, recv_n0, total0, state0, send_weight, update_weight, back_t, back, border),
        flops=2 * unit,
    )
    arr3 = exchange(pay3, dims)
    (total1, grecv_l, gsent_l, recv_n1, sent_b1, gsum_n1, gsum_r1, slope_k0, slope_d0,
     slope_r0) = call(
        turn_local, "turn_local",
        [shape(nodes, width, dtype=F32)] * 3 + [shape(halo, width, dtype=F32)]
        + [shape(halo, width)] * 6,
        (state1, send_weight, recv_weight, update_weight, gsum1, cot_r, pre0, recv_n0, back0,
         sent_b0, senders, edges, border, back),
        flops=10 * unit, scratch=[pltpu.VMEM((degree * nodes, width), BF)],
    )
    summed1, grecv1, gsent1, gin1, *pay4 = call(
        lambda *refs: turn_halo(peers, *refs), "turn_halo",
        [shape(nodes, width)] * 4 + [shape(BORDER, width)] * peers,
        (*arr3, recv_n1, sent_b1, gsum_n1, gsum_r1, total1, grecv_l, gsent_l, cot,
         send_weight, recv_weight, back_t, back, border_t),
        flops=3 * unit,
    )
    arr4 = exchange(pay4, dims)
    keep1, give1, mesh_out = call(
        lambda *refs: last_weights(dims, *refs), "last_weights",
        blocks_shapes(3, width, width, dims) + [shape(nodes, width)],
        (place, state1, summed1, cot, grecv1, gsent1, update_weight), flops=4 * unit,
    )
    split = fine(width, dims)
    if split:
        give1, last = lax.optimization_barrier((give1, arr4[-1]))
        arr4 = (*arr4[:-1], last)
        keep1, give1 = halve_step(1, keep1, swap(give1, 0, dims), place)
    part0, keep0, give0, keep2, give2 = call(
        lambda *refs: back_local(dims, *refs), "back_local",
        [shape(nodes, width, dtype=F32)] + blocks_shapes(2, width, width, dims) * 2,
        (place, gin1, slope0, slope_k0, slope_d0, send_weight, recv_weight, update_weight, back_t,
         back, edges, state0, rows0, summed0, merged, merged_r, keep1),
        flops=10 * unit, scratch=[pltpu.VMEM((degree * nodes, width), BF)],
    )
    if split:
        give0, give2, *arr4 = lax.optimization_barrier((give0, give2, *arr4))
        keep0, give0 = halve_step(1, keep0, swap(give0, 0, dims), place)
        keep0, *arr4 = lax.optimization_barrier((keep0, *arr4))
    shapes = blocks_shapes(1, width, width, dims)
    if carry:
        shapes[1] = shape(shapes[1].shape[0] + 2 * capacity, width)
    gpre_g, keep_e, give_e, *pay5 = call(
        lambda *refs: embed_back(peers, dims, carry, *refs), "embed_back",
        [shape(chosen, width)] + shapes + [shape(capacity, width)] * peers,
        (*arr4, place, slope_r0, part0, update_weight, send_weight, merge, border_t,
         targets, sends, incoming, slope_g, slope_a, grid, lat_a, embed),
        flops=6 * unit,
    )
    depth = width // total
    if not split:
        arr5 = exchange(pay5, dims)
        last, first, second, embed_sum = (
            scatter_plain(blocks, dims) for blocks in (keep1, keep0, keep2, keep_e)
        )
        plain = [jnp.stack([a, last[i]]) for i, a in enumerate((first[0], first[1], second[0]))]
        plain = [embed_sum[0], second[1], *plain]
    elif not carry:
        arr5 = exchange(pay5, dims)
        sums = [
            rest_of_halving(1, keep1, give1, place, dims),
            rest_of_halving(1, keep0, give0, place, dims),
            rest_of_halving(0, keep2, give2, place, dims),
            rest_of_halving(0, keep_e, give_e, place, dims),
        ]
    else:
        arr1 = swap(give1, 1, dims)
        arr0 = swap(give0, 1, dims)
        arr2 = swap(give2, 0, dims)
        (local_rows,) = call(
            grid_local, "grid_local", [shape(chosen, width)], (gpre_g, embed), flops=0, size=0
        )
        arr_e, arr1 = lax.optimization_barrier((swap(give_e, 0, dims), arr1))
        keep1, local_rows = lax.optimization_barrier((keep1, local_rows))
        keep1, give1 = halve_step(2, keep1, arr1, place)
        arr1 = swap(give1, 2, dims)
        keep_e, keep1 = lax.optimization_barrier((keep_e, keep1))
        keep_e, give_e, from_sub, on = carry_step(2, keep_e, arr_e, pay5[3:], place, capacity)
        arr_e = swap(give_e, 2, dims)
        keep2, keep_e = lax.optimization_barrier((keep2, keep_e))
        keep2, give2 = halve_step(1, keep2, arr2, place)
        arr2 = swap(give2, 1, dims)
        keep0, keep2 = lax.optimization_barrier((keep0, keep2))
        keep0, give0 = halve_step(2, keep0, arr0, place)
        arr0 = swap(give0, 2, dims)
        keep_e, keep0 = lax.optimization_barrier((keep_e, keep0))
        keep_e, give_e, from_near = carry_step(3, keep_e, arr_e, (), place, capacity)
        arr_e = swap(give_e, 3, dims)
        keep1, keep_e = lax.optimization_barrier((keep1, keep_e))
        keep1, give1 = halve_step(3, keep1, arr1, place)
        arr1 = swap(give1, 3, dims)
        keep_e, keep1 = lax.optimization_barrier((keep_e, keep1))
        keep_e, give_e, from_far = carry_step(1, keep_e, arr_e, (pay5[1], on), place, capacity)
        arr_e = swap(give_e, 1, dims)
        keep0, keep_e = lax.optimization_barrier((keep0, keep_e))
        keep0, give0 = halve_step(3, keep0, arr0, place)
        arr0 = swap(give0, 3, dims)
        keep2, keep0, arr1 = lax.optimization_barrier((keep2, keep0, arr1))
        keep2, give2 = halve_step(2, keep2, arr2, place)
        arr2 = swap(give2, 2, dims)
        keep2, give2 = halve_step(3, keep2, arr2, place)
        arr2 = swap(give2, 3, dims)
        sums = ((keep1, arr1), (keep0, arr0), (keep2, arr2), (keep_e, arr_e))
    grads = [shape(depth, width, dtype=F32)] * 2 + [shape(2, depth, width, dtype=F32)] * 3
    if carry:
        return (mesh_out, *call(
            finish_all, "finish_all", [shape(chosen, width)] + grads,
            (*(part for pair in sums for part in pair), from_sub, from_near, from_far, local_rows,
             sends_row),
            flops=unit,
        ))
    (local_rows,) = call(
        grid_local, "grid_local", [shape(chosen, width)], (gpre_g, embed), flops=2 * unit
    )
    (grid_grad,) = call(
        lambda *refs: grid_place(peers, *refs), "grid_place", [shape(chosen, width)],
        (*arr5, local_rows, sends_row), flops=unit,
    )
    if split:
        grads = call(
            finish, "finish", grads, [part for pair in sums for part in pair],
            flops=8 * depth * width,
        )
    else:
        grads = plain
    return (mesh_out, grid_grad, *grads)


def solution(mesh):
    split = ("groups", "lon", "lat", "sub")
    dims = tuple(mesh.shape[axis] for axis in GROUP)
    rows = P(split, None)
    whole = P("groups", GROUP, None)
    in_specs = (
        rows, rows, rows, P(), P(), P(), P(), P(), P(split), P(split, None, None),
        P(split, None, None), P(split, None, None), rows,
    )
    out_specs = (rows, rows, rows, rows, whole, whole, whole)
    return jax.shard_map(
        lambda *args: body(dims, *args),
        mesh=mesh, in_specs=in_specs, out_specs=out_specs, check_vma=False,
    )
```

```python
import jax
import jax.numpy as jnp
from jax import lax
from jax.experimental import pallas as pl
from jax.experimental.pallas import tpu as pltpu
from jax.sharding import PartitionSpec as P

BF = jnp.bfloat16
F32 = jnp.float32
I32 = jnp.int32
NN = (((1,), (0,)), ((), ()))
NT = (((1,), (1,)), ((), ()))
TN = (((0,), (0,)), ((), ()))
BORDER = 8
GROUP = ("lon", "lat", "sub")
COLUMN = ("lat", "sub")


def dot(a, b, dims=NN):
    return lax.dot_general(a, b, dims, preferred_element_type=F32)


def low(value):
    return value.astype(BF)


def sigmoid(value):
    return 0.5 * jnp.tanh(0.5 * value) + 0.5


def silu(value):
    return value * sigmoid(value)


def silu_both(value):
    sig = sigmoid(value)
    act = value * sig
    return act, sig + act * (1.0 - sig)


def silu_slope(value):
    return silu_both(value)[1]


def iota(rows, columns, dim):
    return lax.broadcasted_iota(I32, (rows, columns), dim)


def hot(mask):
    return jnp.where(mask, 1.0, 0.0)


def slot_rows(ref):
    return jnp.concatenate([ref[s] for s in range(ref.shape[0])], axis=0)


def slot_of(at, column, me, odd):
    far = jnp.where(at == column - 1, column + 1 - odd, column + odd)
    return jnp.where(at < column - 1, jnp.bitwise_xor(at + 1, me), far)


def as_column(values, wide, column, me, odd):
    slots = values.shape[0]
    count = (slots - 1) * wide
    row = iota(count, slots, 0)
    pick = low(hot(slot_of(row // wide, column, me, odd) == iota(count, slots, 1)))
    found = 16.0 * dot(pick, low((values // 16).astype(F32)))
    found = found + dot(pick, low((values % 16).astype(F32)))
    keep = iota(count, wide, 0) % wide == iota(count, wide, 1)
    return jnp.sum(jnp.where(keep, found, 0.0), axis=1, keepdims=True).astype(I32)


def as_row(values, wide, column, me, odd):
    slots = values.shape[0]
    count = (slots - 1) * wide
    pick = low(hot(iota(wide, count, 1) % wide == iota(wide, count, 0)))
    found = 16.0 * dot(low((values // 16).astype(F32)), pick)
    found = found + dot(low((values % 16).astype(F32)), pick)
    at = iota(slots, count, 1) // wide
    keep = slot_of(at, column, me, odd) == iota(slots, count, 0)
    return jnp.sum(jnp.where(keep, found, 0.0), axis=0, keepdims=True).astype(I32)


def split_parts(refs, starts, sizes):
    values = [ref[...].astype(F32) for ref in refs]
    return [
        jnp.concatenate([value[start : start + size] for value in values], axis=0)
        for start, size in zip(starts, sizes)
    ]


def store_parts(refs, parts):
    peers = len(refs)
    for at, ref in enumerate(refs):
        rows = []
        for part in parts:
            size = part.shape[0] // peers
            rows.append(part[at * size : (at + 1) * size])
        ref[...] = low(rows[0] if len(rows) == 1 else jnp.concatenate(rows, axis=0))


def receivers(senders_t, halo):
    degree, nodes = senders_t.shape
    found = jnp.zeros((halo, nodes), F32)
    ids = iota(halo, nodes, 0) + nodes
    for j in range(degree):
        found = found + hot(senders_t[j : j + 1, :] == ids)
    return found


def receivers_t(senders, degree, halo):
    nodes = senders.shape[0]
    found = jnp.zeros((nodes, halo), F32)
    ids = iota(nodes, halo, 1) + nodes
    for j in range(degree):
        found = found + hot(senders[:, j : j + 1] == ids)
    return found


def fine(rows, dims):
    return (rows // (dims[0] * dims[1] * dims[2])) % 16 == 0


def reverse_bits(block, bits):
    spot = 0
    for bit in range(bits):
        spot = 2 * spot + (block >> bit) % 2
    return spot


def store_blocks(keep_ref, give_ref, at, count, value, dims, bits_ref):
    value = low(value)
    rows = value.shape[0]
    total = dims[0] * dims[1] * dims[2]
    depth = rows // total
    if not fine(rows, dims):
        keep_ref[at] = value
        return
    bits = (total - 1).bit_length()
    upper = bits_ref[0:1, 2:3] == 1
    for block in range(0, total, 2):
        start = reverse_bits(block, bits) * count * depth + at * depth
        first = value[block * depth : (block + 1) * depth].astype(F32)
        second = value[(block + 1) * depth : (block + 2) * depth].astype(F32)
        keep_ref[start : start + depth, :] = low(jnp.where(upper, second, first))
        give_ref[start : start + depth, :] = low(jnp.where(upper, first, second))


def blocks_shapes(count, rows, width, dims):
    if fine(rows, dims):
        return [jax.ShapeDtypeStruct((count * rows // 2, width), BF)] * 2
    return [jax.ShapeDtypeStruct((count, rows, width), BF), jax.ShapeDtypeStruct((16, width), BF)]


def halve(bit, bits_ref, keep_ref, arr_ref, keep_out, give_out):
    half = keep_ref.shape[0] // 2
    upper = bits_ref[0:1, 2 + bit : 3 + bit] == 1
    first = keep_ref[:half, :].astype(F32) + arr_ref[:half, :].astype(F32)
    second = keep_ref[half:, :].astype(F32) + arr_ref[half:, :].astype(F32)
    keep_out[...] = low(jnp.where(upper, second, first))
    give_out[...] = low(jnp.where(upper, first, second))


def swap(block, bit, dims):
    total = dims[0] * dims[1] * dims[2]
    return lax.ppermute(block, GROUP, [(i, i ^ (1 << bit)) for i in range(total)])


def halve_step(bit, keep, arrived, place):
    rows, width = keep.shape[0] // 2, keep.shape[1]
    return call(
        lambda *refs: halve(bit, *refs), "halve", [shape(rows, width)] * 2,
        (place, keep, arrived), flops=4 * rows * width, size=0,
    )


def rest_of_halving(first, keep, give, place, dims):
    bits = (dims[0] * dims[1] * dims[2] - 1).bit_length()
    arrived = swap(give, first, dims)
    for bit in range(first + 1, bits):
        keep, give = halve_step(bit, keep, arrived, place)
        arrived = swap(give, bit, dims)
    return keep, arrived


def halve_carry(bit, count, bits_ref, keep_ref, arr_ref, *refs):
    own_refs, (keep_out, give_out, *here_refs) = refs[:count], refs[count:]
    rows = keep_ref.shape[0]
    half = rows // 2
    size = here_refs[0].shape[0]
    upper = bits_ref[0:1, 2 + bit : 3 + bit] == 1
    value = arr_ref[...].astype(F32)
    first = keep_ref[:half, :].astype(F32) + value[:half]
    second = keep_ref[half:, :].astype(F32) + value[half:rows]
    keep_out[...] = low(jnp.where(upper, second, first))
    here_refs[0][...] = low(value[rows : rows + size])
    passed = value[rows + size : rows + 2 * size]
    extra = [ref[...].astype(F32) for ref in own_refs]
    if count < 2:
        extra.append(passed)
    else:
        here_refs[1][...] = low(passed)
    give_out[...] = low(jnp.concatenate([jnp.where(upper, first, second), *extra], axis=0))


def carry_step(bit, keep, arrived, own, place, capacity):
    rows, width = keep.shape[0] // 2, keep.shape[1]
    count = len(own)
    return call(
        lambda *refs: halve_carry(bit, count, *refs), "halve_carry",
        [shape(rows, width), shape(rows + min(count + 1, 2) * capacity, width)]
        + [shape(capacity, width)] * (2 if count == 2 else 1),
        (place, keep, arrived, *own), flops=4 * rows * width, size=0,
    )


def scatter_plain(blocks, dims):
    lon, lat, sub = dims
    count, rows, width = blocks.shape
    depth = rows // (lon * lat * sub)
    blocks = blocks.reshape(count, lon, lat, sub, depth, width)
    blocks = blocks.transpose(3, 2, 1, 0, 4, 5)
    for axis in ("sub", "lat", "lon"):
        blocks = lax.psum_scatter(blocks, axis, scatter_dimension=0, tiled=False)
    return blocks.astype(F32)


def call(kernel, name, outs, args, flops, loads=(), scratch=(), size=None):
    if size is None:
        size = sum(a.size * a.dtype.itemsize for a in (*args, *outs, *loads))
    args = (*(pltpu.with_memory_space_constraint(a, pltpu.HBM) for a in loads), *args)
    scratch = list(scratch)
    if loads:
        scratch.append(pltpu.SemaphoreType.DMA((len(loads),)))
    in_specs = [pl.BlockSpec(memory_space=pltpu.HBM)] * len(loads)
    in_specs += [pl.BlockSpec(memory_space=pltpu.VMEM)] * (len(args) - len(loads))
    return pl.pallas_call(
        kernel,
        out_shape=[shape(*a.shape, dtype=a.dtype) for a in loads] + list(outs),
        in_specs=in_specs,
        out_specs=[pl.BlockSpec(memory_space=pltpu.VMEM)] * (len(outs) + len(loads)),
        scratch_shapes=scratch,
        compiler_params=pltpu.CompilerParams(vmem_limit_bytes=16 * 1024 * 1024),
        cost_estimate=pl.CostEstimate(flops=flops, bytes_accessed=size, transcendentals=0),
        name=name,
    )(*args)


def exchange(parts, dims):
    column = dims[1] * dims[2]
    count = dims[0]
    other = [(i, (i - 1 + 2 * (i % 2)) % count) for i in range(count)]
    far = lax.ppermute(parts[column], "lon", other)
    near = lax.ppermute(parts[column - 1], "lon", [(i, i ^ 1) for i in range(count)])
    arrived = [
        lax.ppermute(parts[r - 1], COLUMN, [(i, i ^ r) for i in range(column)])
        for r in range(column - 1, 0, -1)
    ]
    *others, first = arrived
    return (far, *others[::-1], near, first)


def in_order(arrived):
    far, *others, near, first = arrived
    return (first, *others, near, far)


def shape(*dims, dtype=BF):
    return jax.ShapeDtypeStruct(dims, dtype)


def start_loads(sources, targets, sems):
    copies = [
        pltpu.make_async_copy(source, target, sems.at[at])
        for at, (source, target) in enumerate(zip(sources, targets))
    ]
    for copy in copies:
        copy.start()
    return copies


def first_payload(column, count, *refs):
    sources, place_ref, targets = refs[:count], refs[count], refs[count + 1 : 2 * count + 1]
    sends_out, *pay_refs, sems = refs[2 * count + 1 :]
    sends_ref, grid_ref = targets[:2]
    sends_load, grid_load, *loads = start_loads(sources, targets, sems)
    chosen = grid_ref.shape[0]
    me, odd = place_ref[:, 0:1], place_ref[:, 1:2]
    sends_load.wait()
    sends = slot_rows(sends_ref)
    sends = as_column(sends, sends.shape[1], column, me, odd)
    sends_out[...] = sends
    pick = low(hot(sends == iota(sends.shape[0], chosen, 1)))
    grid_load.wait()
    store_parts(pay_refs, [dot(pick, grid_ref[...])])
    for load in loads:
        load.wait()


def embed_local(
    column, mesh_far, merge_far, cot_far, place_in_ref, raw_sends_ref, raw_incoming_ref,
    raw_bounds_ref, senders_ref, grid_ref, weight_ref, target_ref, sends_ref, mesh_ref, merge_ref,
    cot_ref, sum_ref, slope_ref, sends_row_ref, incoming_ref, border_ref, border_t_ref, back_ref,
    back_t_ref, senders_t_ref, senders_out_ref, place_ref, sems,
):
    loads = start_loads((mesh_far, merge_far, cot_far), (mesh_ref, merge_ref, cot_ref), sems)
    chosen = grid_ref.shape[0]
    nodes = sum_ref.shape[0]
    taken = sends_ref.shape[0]
    act, slope = silu_both(dot(grid_ref[...], weight_ref[...]))
    slope_ref[...] = low(slope)
    sent = jnp.max(hot(sends_ref[...] == iota(taken, chosen, 1)), axis=0, keepdims=True)
    label = jnp.where(sent > 0.0, nodes, target_ref[...])
    sum_ref[...] = dot(low(hot(label == iota(nodes, chosen, 0))), low(act))
    place_ref[...] = place_in_ref[...]
    me, odd = place_in_ref[:, 0:1], place_in_ref[:, 1:2]
    raw_sends, incoming = slot_rows(raw_sends_ref), slot_rows(raw_incoming_ref)
    bounds = slot_rows(raw_bounds_ref)
    capacity = incoming.shape[1]
    sends_row_ref[...] = as_row(raw_sends, capacity, column, me, odd)
    halo = border_ref.shape[0]
    incoming = as_row(incoming, capacity, column, me, odd)
    incoming_ref[...] = low(hot(incoming == iota(nodes, taken, 0)))
    border = as_column(bounds, BORDER, column, me, odd)
    border_ref[...] = low(hot(border == iota(halo, nodes, 1)))
    border = as_row(bounds, BORDER, column, me, odd)
    border_t_ref[...] = low(hot(border == iota(nodes, halo, 0)))
    senders = senders_ref[...]
    degree = senders.shape[0]
    offset = senders - nodes
    slot = offset // BORDER
    far = jnp.where(slot == column, column - odd, column - 1 + odd)
    at = jnp.where(slot < column, jnp.bitwise_xor(slot, me) - 1, far)
    senders = jnp.where(offset < 0, senders, nodes + at * BORDER + offset % BORDER)
    senders_t_ref[...] = senders
    filler = jnp.zeros((8 - degree, nodes), I32)
    back_ref[...] = low(receivers(senders, halo))
    senders_t = jnp.concatenate([senders, filler], axis=0).T
    senders_out_ref[...] = senders_t
    back_t_ref[...] = low(receivers_t(senders_t, degree, halo))
    for load in loads:
        load.wait()


def merge_nodes(peers, *refs):
    arr_refs, refs = in_order(refs[:peers]), refs[peers:]
    (incoming_ref, embed_ref, local_ref, mesh_ref, weight_ref, border_ref, back_ref, cot_ref,
     merged_ref, state_ref, slope_ref, lat_ref, *pay_refs) = refs
    lat = jnp.concatenate([ref[...] for ref in arr_refs], axis=0)
    lat_ref[...] = lat
    act, slope = silu_both(dot(lat, embed_ref[...]))
    slope_ref[...] = low(slope)
    merged = low(local_ref[...] + dot(incoming_ref[...], low(act)))
    merged_ref[...] = merged
    state = low(mesh_ref[...].astype(F32) + dot(merged, weight_ref[...]))
    state_ref[...] = state
    border, back = border_ref[...], back_ref[...]
    store_parts(
        pay_refs,
        [dot(border, state), dot(back, state), dot(border, merged), dot(back, cot_ref[...])],
    )


def local_edges(senders, degree, sent, recv, each):
    nodes = senders.shape[0]
    total = None
    ids = iota(nodes, nodes, 1)
    for j in range(degree):
        act, slope = silu_both(dot(low(hot(senders[:, j : j + 1] == ids)), sent) + recv)
        total = act if total is None else total + act
        each(j, slope)
    return total


def edge_targets(senders_t):
    degree, nodes = senders_t.shape
    ids = iota(nodes, nodes, 0)
    return jnp.concatenate(
        [low(hot(senders_t[j : j + 1, :] == ids)) for j in range(degree)], axis=1
    )


def forward_local(
    state_ref, send_ref, recv_ref, update_ref, cot_ref, senders_ref, senders_t_ref, border_ref,
    back_ref, total_ref, slope_ref, recv_n_ref, sent_b_ref, gsum_ref, targets_ref,
):
    state = state_ref[...]
    sent = low(dot(state, send_ref[0]))
    recv = dot(state, recv_ref[0])

    def keep(j, slope):
        slope_ref[j] = low(slope)

    total_ref[...] = local_edges(senders_ref[...], senders_t_ref.shape[0], sent, recv, keep)
    recv_n_ref[...] = dot(low(dot(back_ref[...], state)), recv_ref[0])
    sent_b_ref[...] = low(dot(border_ref[...], sent))
    gsum_ref[...] = low(dot(cot_ref[...], update_ref[1], NT))
    targets_ref[...] = edge_targets(senders_t_ref[...])


def forward_halo(peers, *refs):
    arr_refs, refs = in_order(refs[:peers]), refs[peers:]
    (recv_n_ref, total_ref, state_ref, send_ref, update_ref, back_t_ref, back_in_ref,
     border_ref, summed_ref, out_ref, pre_ref, rows_ref, back_ref, merged_ref, cot_ref,
     *pay_refs) = refs
    rows, back, merged, cot = split_parts(
        arr_refs, (0, BORDER, 2 * BORDER, 3 * BORDER), (BORDER,) * 4
    )
    rows_ref[...], back_ref[...] = low(rows), low(back)
    merged_ref[...], cot_ref[...] = low(merged), low(cot)
    pre = low(dot(low(rows), send_ref[0])).astype(F32) + recv_n_ref[...]
    pre_ref[...] = pre
    place = back_t_ref[...]
    extra = silu(pre) - silu(recv_n_ref[...])
    summed = low(total_ref[...] + dot(place, low(extra)))
    summed_ref[...] = summed
    state = low(state_ref[...].astype(F32) + dot(summed, update_ref[0]))
    out_ref[...] = state
    store_parts(pay_refs, [dot(border_ref[...], state), dot(back_in_ref[...], state)])


def turn_local(
    state_ref, send_ref, recv_ref, update_ref, gsum_ref, cot_r_ref, pre_ref, recv_n0_ref, back0_ref,
    sent_b0_ref, senders_ref, targets_ref, border_ref, back_ref,
    total_ref, grecv_ref, gsent_ref, recv_n_ref, sent_b_ref, gsum_n_ref, gsum_r_ref,
    slope_k_ref, slope_d_ref, slope_r_ref, gpre_ref,
):
    slope = silu_slope(pre_ref[...])
    slope_k_ref[...] = low(slope)
    slope_d_ref[...] = low(slope - silu_slope(recv_n0_ref[...]))
    pre = sent_b0_ref[...].astype(F32) + dot(back0_ref[...], recv_ref[0])
    slope_r_ref[...] = low(silu_slope(pre))
    state = state_ref[...]
    nodes = state.shape[0]
    sent = low(dot(state, send_ref[1]))
    recv = dot(state, recv_ref[1])
    gsum = gsum_ref[...]
    grad = gsum.astype(F32)
    grecv = []

    def back_edge(j, slope):
        gpre = grad * slope
        grecv.append(gpre if j == 0 else grecv[-1] + gpre)
        gpre_ref[j * nodes : (j + 1) * nodes, :] = low(gpre)

    degree = targets_ref.shape[1] // nodes
    total_ref[...] = local_edges(senders_ref[...], degree, sent, recv, back_edge)
    grecv_ref[...] = grecv[-1]
    gsent_ref[...] = dot(targets_ref[...], gpre_ref[...])
    back = back_ref[...]
    recv_n_ref[...] = dot(low(dot(back, state)), recv_ref[1])
    sent_b_ref[...] = low(dot(border_ref[...], sent))
    gsum_n_ref[...] = low(dot(back, gsum))
    gsum_r_ref[...] = low(dot(cot_r_ref[...], update_ref[1], NT))


def turn_halo(peers, *refs):
    arr_refs, refs = in_order(refs[:peers]), refs[peers:]
    (recv_n_ref, sent_b_ref, gsum_n_ref, gsum_r_ref, total_ref, grecv_ref, gsent_ref, cot_ref,
     send_ref, recv_ref, back_t_ref, back_in_ref, border_t_ref, summed_ref, grecv_out_ref,
     gsent_out_ref, gin_ref, *pay_refs) = refs
    rows, back = split_parts(arr_refs, (0, BORDER), (BORDER,) * 2)
    pre = low(dot(low(rows), send_ref[1])).astype(F32) + recv_n_ref[...]
    act, slope = silu_both(pre)
    place = back_t_ref[...]
    base, base_slope = silu_both(recv_n_ref[...])
    gpre = low(gsum_n_ref[...].astype(F32) * (slope - base_slope))
    grecv = low(grecv_ref[...] + dot(place, gpre))
    pre = sent_b_ref[...].astype(F32) + dot(low(back), recv_ref[1])
    gpre = low(gsum_r_ref[...].astype(F32) * silu_slope(pre))
    gsent = low(gsent_ref[...] + dot(border_t_ref[...], gpre))
    gin = cot_ref[...].astype(F32) + dot(grecv, recv_ref[1], NT) + dot(gsent, send_ref[1], NT)
    gin = low(gin)
    gin_ref[...] = gin
    store_parts(pay_refs, [dot(back_in_ref[...], gin)])
    summed_ref[...] = low(total_ref[...] + dot(place, low(act - base)))
    grecv_out_ref[...] = grecv
    gsent_out_ref[...] = gsent


def last_weights(
    dims, place_ref, state_ref, summed_ref, cot_ref, grecv_ref, gsent_ref, update_ref,
    keep_ref, give_ref, mesh_ref,
):
    state, summed = state_ref[...], summed_ref[...]

    def store(at, value):
        store_blocks(keep_ref, give_ref, at, 3, value, dims, place_ref)

    both = dot(state, jnp.concatenate([gsent_ref[...], grecv_ref[...]], axis=1), TN)
    store(0, both[:, : state.shape[1]])
    store(1, both[:, state.shape[1] :])
    store(2, dot(summed, cot_ref[...], TN))
    mesh_ref[...] = low(state.astype(F32) + dot(summed, update_ref[1]))


def back_local(
    dims, place_ref, gin_ref, slope_ref, slope_k_ref, slope_d_ref, send_ref, recv_ref, update_ref,
    back_t_ref, back_ref, targets_ref, state_ref, rows_ref, summed_ref, merged_ref, merged_r_ref,
    after_ref, part_ref, keep_ref, give_ref, keep2_ref, give2_ref, gpre_ref,
):
    nodes = gin_ref.shape[0]
    degree = slope_ref.shape[0]
    gin = gin_ref[...]
    gsum = low(dot(gin, update_ref[0], NT))
    place, back = back_t_ref[...], back_ref[...]
    gsum_n = low(dot(back, gsum))
    gpre_k = gsum_n * slope_k_ref[...]
    grecv = dot(place, gsum_n * slope_d_ref[...])
    for j in range(degree):
        gpre = gsum * slope_ref[j]
        grecv = grecv + gpre.astype(F32)
        gpre_ref[j * nodes : (j + 1) * nodes, :] = gpre
    gsent = dot(targets_ref[...], gpre_ref[...])
    grecv, gsent = low(grecv), low(gsent)
    part = gin.astype(F32) + dot(grecv, recv_ref[0], NT) + dot(gsent, send_ref[0], NT)
    part_ref[...] = part
    state = state_ref[...]

    def store(at, value):
        store_blocks(keep_ref, give_ref, at, 2, value, dims, place_ref)

    def store2(at, value):
        store_blocks(keep2_ref, give2_ref, at, 2, value, dims, place_ref)

    both = dot(state, jnp.concatenate([gsent, grecv], axis=1), TN)
    store(0, both[:, : state.shape[1]] + dot(rows_ref[...], gpre_k, TN))
    store(1, both[:, state.shape[1] :])
    store2(0, dot(summed_ref[...], gin, TN))
    far = low(dot(gpre_k, send_ref[0], NT))
    store2(1, dot(merged_ref[...], low(part), TN) + dot(merged_r_ref[...], far, TN))


def embed_back(peers, dims, carry, *refs):
    arr_refs, refs = in_order(refs[:peers]), refs[peers:]
    (place_ref, slope_r_ref, part_ref, update_ref, send_ref, merge_ref, border_t_ref, target_ref,
     sends_ref, incoming_ref, slope_g_ref, slope_a_ref, grid_ref, lat_ref, embed_ref,
     gpre_ref, keep_ref, give_ref, *pay_refs) = refs
    nodes = part_ref.shape[0]
    chosen = grid_ref.shape[0]
    taken = sends_ref.shape[0]
    (arrived,) = split_parts(arr_refs, (0,), (BORDER,))
    gsum = low(dot(low(arrived), update_ref[0], NT)).astype(F32)
    gpre = low(gsum * slope_r_ref[...].astype(F32))
    gsent = low(dot(border_t_ref[...], gpre))
    gin = low(part_ref[...] + dot(gsent, send_ref[0], NT))
    gmerged = low(dot(gin, merge_ref[...], NT))
    gpre_a = low(dot(incoming_ref[...], gmerged, TN) * slope_a_ref[...].astype(F32))
    sent = jnp.max(hot(sends_ref[...] == iota(taken, chosen, 1)), axis=0, keepdims=True)
    label = jnp.where(sent > 0.0, nodes, target_ref[...])
    pick = low(hot(label == iota(nodes, chosen, 0)))
    gpre_g = low(dot(pick, gmerged, TN) * slope_g_ref[...].astype(F32))
    gpre_ref[...] = gpre_g
    grad = dot(grid_ref[...], gpre_g, TN) + dot(lat_ref[...], gpre_a, TN)
    store_blocks(keep_ref, give_ref, 0, 1, grad, dims, place_ref)
    rows = dot(gpre_a, embed_ref[...], NT)
    store_parts(pay_refs, [rows])
    if carry:
        size = taken // peers
        start = keep_ref.shape[0]
        give_ref[start : start + 2 * size, :] = low(
            jnp.concatenate([rows[:size], rows[2 * size : 3 * size]], axis=0)
        )


def grid_local(gpre_ref, weight_ref, out_ref):
    out_ref[...] = low(dot(gpre_ref[...], weight_ref[...], NT))


def grid_patch(local_ref, sends_ref, arr_refs, out_ref):
    chosen = local_ref.shape[0]
    taken = sends_ref.shape[1]
    size = taken // len(arr_refs)
    place = low(hot(sends_ref[...] == iota(chosen, taken, 0)))
    rows = [ref[...].astype(F32) for ref in arr_refs]
    rows = low(jnp.concatenate([row[row.shape[0] - size :] for row in rows], axis=0))
    out_ref[...] = low(local_ref[...].astype(F32) + dot(place, rows))


def grid_place(peers, *refs):
    arr_refs, (local_ref, sends_ref, out_ref) = in_order(refs[:peers]), refs[peers:]
    grid_patch(local_ref, sends_ref, arr_refs, out_ref)


def sum_last(sums, outs):
    (keep1_ref, arr1_ref, keep0_ref, arr0_ref, keep2_ref, arr2_ref, keep_e_ref, arr_e_ref) = sums
    embed_ref, merge_ref, send_ref, recv_ref, update_ref = outs
    last = keep1_ref[...].astype(F32) + arr1_ref[...].astype(F32)
    first = keep0_ref[...].astype(F32) + arr0_ref[...].astype(F32)
    second = keep2_ref[...].astype(F32) + arr2_ref[...].astype(F32)
    depth = embed_ref.shape[0]
    embed_ref[...] = keep_e_ref[...].astype(F32) + arr_e_ref[:depth, :].astype(F32)
    for at, ref in enumerate((send_ref, recv_ref, update_ref)):
        ref[1] = last[at * depth : (at + 1) * depth]
    send_ref[0], recv_ref[0], update_ref[0] = first[:depth], first[depth:], second[:depth]
    merge_ref[...] = second[depth:]


def finish(*refs):
    sum_last(refs[:8], refs[8:])


def finish_all(*refs):
    sums, rows, (local_ref, sends_ref), outs = refs[:8], refs[8:12], refs[12:14], refs[14:]
    grid_patch(local_ref, sends_ref, (*rows, sums[7]), outs[0])
    sum_last(sums, outs[1:])


def body(
    dims,
    grid_latent, mesh_latent, cotangent, embed_weight, merge_weight, send_weight, recv_weight,
    update_weight, target_row, send_rows, incoming_rows, border_mesh_rows, mesh_senders,
):
    chosen, width = grid_latent.shape
    nodes, degree = mesh_senders.shape
    slots, capacity = send_rows.shape[1:]
    column = dims[1] * dims[2]
    peers = slots - 1
    halo = peers * BORDER
    taken = peers * capacity
    total = dims[0] * dims[1] * dims[2]
    bits = (total - 1).bit_length()
    carry = dims == (4, 2, 2) and fine(width, dims)
    spot = lax.axis_index(GROUP)
    place = [lax.axis_index(COLUMN), lax.axis_index("lon") % 2]
    place += [(spot >> bit) % 2 for bit in range(bits)]
    place = jnp.stack(place).astype(I32).reshape(1, 2 + bits)
    raw = [a.transpose(1, 0, 2) for a in (send_rows, incoming_rows, border_mesh_rows)]
    unit = 2 * nodes * width * width

    loads = (raw[0], grid_latent, embed_weight, target_row.reshape(1, chosen), mesh_senders.T,
             *raw[1:])
    raw_sends, grid, embed, targets, senders_raw, raw_incoming, raw_bounds, sends, *pay1 = call(
        lambda *refs: first_payload(column, len(loads), *refs), "first_payload",
        [shape(taken, 1, dtype=I32)] + [shape(capacity, width)] * peers,
        (place,), flops=unit // 2, loads=loads,
    )
    arr1 = exchange(pay1, dims)
    (mesh, merge, cot, local, slope_g, sends_row, incoming, border, border_t, back, back_t, senders_t,
     senders, place) = call(
        lambda *refs: embed_local(column, *refs), "embed_local",
        [shape(nodes, width, dtype=F32), shape(chosen, width), shape(1, taken, dtype=I32),
         shape(nodes, taken), shape(halo, nodes), shape(nodes, halo), shape(halo, nodes),
         shape(nodes, halo), shape(degree, nodes, dtype=I32), shape(nodes, 8, dtype=I32),
         shape(1, 2 + bits, dtype=I32)],
        (place, raw_sends, raw_incoming, raw_bounds, senders_raw, grid, embed, targets, sends),
        flops=3 * unit,
        loads=(mesh_latent, merge_weight, cotangent),
    )
    merged, state0, slope_a, lat_a, *pay2 = call(
        lambda *refs: merge_nodes(peers, *refs), "merge_nodes",
        [shape(nodes, width), shape(nodes, width), shape(taken, width), shape(taken, width)]
        + [shape(4 * BORDER, width)] * peers,
        (*arr1, incoming, embed, local, mesh, merge, border, back, cot),
        flops=2 * unit,
    )
    arr2 = exchange(pay2, dims)
    total0, slope0, recv_n0, sent_b0, gsum1, edges = call(
        forward_local, "forward_local",
        [shape(nodes, width, dtype=F32), shape(degree, nodes, width),
         shape(halo, width, dtype=F32), shape(halo, width), shape(nodes, width),
         shape(nodes, degree * nodes)],
        (state0, send_weight, recv_weight, update_weight, cot, senders, senders_t, border, back),
        flops=6 * unit,
    )
    summed0, state1, pre0, rows0, back0, merged_r, cot_r, *pay3 = call(
        lambda *refs: forward_halo(peers, *refs), "forward_halo",
        [shape(nodes, width), shape(nodes, width), shape(halo, width, dtype=F32)]
        + [shape(halo, width)] * 4 + [shape(2 * BORDER, width)] * peers,
        (*arr2, recv_n0, total0, state0, send_weight, update_weight, back_t, back, border),
        flops=2 * unit,
    )
    arr3 = exchange(pay3, dims)
    (total1, grecv_l, gsent_l, recv_n1, sent_b1, gsum_n1, gsum_r1, slope_k0, slope_d0,
     slope_r0) = call(
        turn_local, "turn_local",
        [shape(nodes, width, dtype=F32)] * 3 + [shape(halo, width, dtype=F32)]
        + [shape(halo, width)] * 6,
        (state1, send_weight, recv_weight, update_weight, gsum1, cot_r, pre0, recv_n0, back0,
         sent_b0, senders, edges, border, back),
        flops=10 * unit, scratch=[pltpu.VMEM((degree * nodes, width), BF)],
    )
    summed1, grecv1, gsent1, gin1, *pay4 = call(
        lambda *refs: turn_halo(peers, *refs), "turn_halo",
        [shape(nodes, width)] * 4 + [shape(BORDER, width)] * peers,
        (*arr3, recv_n1, sent_b1, gsum_n1, gsum_r1, total1, grecv_l, gsent_l, cot,
         send_weight, recv_weight, back_t, back, border_t),
        flops=3 * unit,
    )
    arr4 = exchange(pay4, dims)
    keep1, give1, mesh_out = call(
        lambda *refs: last_weights(dims, *refs), "last_weights",
        blocks_shapes(3, width, width, dims) + [shape(nodes, width)],
        (place, state1, summed1, cot, grecv1, gsent1, update_weight), flops=4 * unit,
    )
    split = fine(width, dims)
    if split:
        give1, last = lax.optimization_barrier((give1, arr4[-1]))
        arr4 = (*arr4[:-1], last)
        keep1, give1 = halve_step(1, keep1, swap(give1, 0, dims), place)
    part0, keep0, give0, keep2, give2 = call(
        lambda *refs: back_local(dims, *refs), "back_local",
        [shape(nodes, width, dtype=F32)] + blocks_shapes(2, width, width, dims) * 2,
        (place, gin1, slope0, slope_k0, slope_d0, send_weight, recv_weight, update_weight, back_t,
         back, edges, state0, rows0, summed0, merged, merged_r, keep1),
        flops=10 * unit, scratch=[pltpu.VMEM((degree * nodes, width), BF)],
    )
    if split:
        give0, give2, *arr4 = lax.optimization_barrier((give0, give2, *arr4))
        keep0, give0 = halve_step(1, keep0, swap(give0, 0, dims), place)
        keep0, *arr4 = lax.optimization_barrier((keep0, *arr4))
    shapes = blocks_shapes(1, width, width, dims)
    if carry:
        shapes[1] = shape(shapes[1].shape[0] + 2 * capacity, width)
    gpre_g, keep_e, give_e, *pay5 = call(
        lambda *refs: embed_back(peers, dims, carry, *refs), "embed_back",
        [shape(chosen, width)] + shapes + [shape(capacity, width)] * peers,
        (*arr4, place, slope_r0, part0, update_weight, send_weight, merge, border_t,
         targets, sends, incoming, slope_g, slope_a, grid, lat_a, embed),
        flops=6 * unit,
    )
    depth = width // total
    if not split:
        arr5 = exchange(pay5, dims)
        last, first, second, embed_sum = (
            scatter_plain(blocks, dims) for blocks in (keep1, keep0, keep2, keep_e)
        )
        plain = [jnp.stack([a, last[i]]) for i, a in enumerate((first[0], first[1], second[0]))]
        plain = [embed_sum[0], second[1], *plain]
    elif not carry:
        arr5 = exchange(pay5, dims)
        sums = [
            rest_of_halving(1, keep1, give1, place, dims),
            rest_of_halving(1, keep0, give0, place, dims),
            rest_of_halving(0, keep2, give2, place, dims),
            rest_of_halving(0, keep_e, give_e, place, dims),
        ]
    else:
        arr1 = swap(give1, 1, dims)
        arr0 = swap(give0, 1, dims)
        arr2 = swap(give2, 0, dims)
        (local_rows,) = call(
            grid_local, "grid_local", [shape(chosen, width)], (gpre_g, embed), flops=0, size=0
        )
        arr_e, arr1 = lax.optimization_barrier((swap(give_e, 0, dims), arr1))
        keep1, local_rows = lax.optimization_barrier((keep1, local_rows))
        keep1, give1 = halve_step(2, keep1, arr1, place)
        arr1 = swap(give1, 2, dims)
        keep_e, keep1 = lax.optimization_barrier((keep_e, keep1))
        keep_e, give_e, from_sub = carry_step(1, keep_e, arr_e, pay5[1:2], place, capacity)
        arr_e = swap(give_e, 1, dims)
        keep2, keep_e = lax.optimization_barrier((keep2, keep_e))
        keep2, give2 = halve_step(1, keep2, arr2, place)
        arr2 = swap(give2, 1, dims)
        keep0, keep2 = lax.optimization_barrier((keep0, keep2))
        keep0, give0 = halve_step(2, keep0, arr0, place)
        arr0 = swap(give0, 2, dims)
        keep1, keep0 = lax.optimization_barrier((keep1, keep0))
        keep1, give1 = halve_step(3, keep1, arr1, place)
        arr1 = swap(give1, 3, dims)
        keep2, keep1 = lax.optimization_barrier((keep2, keep1))
        keep2, give2 = halve_step(2, keep2, arr2, place)
        arr2 = swap(give2, 2, dims)
        keep0, keep2 = lax.optimization_barrier((keep0, keep2))
        keep0, give0 = halve_step(3, keep0, arr0, place)
        arr0 = swap(give0, 3, dims)
        keep_e, keep0, arr1 = lax.optimization_barrier((keep_e, keep0, arr1))
        keep_e, give_e, from_lat, from_diag = carry_step(
            2, keep_e, arr_e, pay5[3:], place, capacity
        )
        arr_e = swap(give_e, 2, dims)
        keep2, keep_e = lax.optimization_barrier((keep2, keep_e))
        keep2, give2 = halve_step(3, keep2, arr2, place)
        arr2 = swap(give2, 3, dims)
        keep_e, keep2 = lax.optimization_barrier((keep_e, keep2))
        keep_e, give_e, from_near = carry_step(3, keep_e, arr_e, (), place, capacity)
        arr_e = swap(give_e, 3, dims)
        sums = ((keep1, arr1), (keep0, arr0), (keep2, arr2), (keep_e, arr_e))
    grads = [shape(depth, width, dtype=F32)] * 2 + [shape(2, depth, width, dtype=F32)] * 3
    if carry:
        return (mesh_out, *call(
            finish_all, "finish_all", [shape(chosen, width)] + grads,
            (*(part for pair in sums for part in pair), from_sub, from_lat, from_diag, from_near,
             local_rows, sends_row),
            flops=unit,
        ))
    (local_rows,) = call(
        grid_local, "grid_local", [shape(chosen, width)], (gpre_g, embed), flops=2 * unit
    )
    (grid_grad,) = call(
        lambda *refs: grid_place(peers, *refs), "grid_place", [shape(chosen, width)],
        (*arr5, local_rows, sends_row), flops=unit,
    )
    if split:
        grads = call(
            finish, "finish", grads, [part for pair in sums for part in pair],
            flops=8 * depth * width,
        )
    else:
        grads = plain
    return (mesh_out, grid_grad, *grads)


def solution(mesh):
    split = ("groups", "lon", "lat", "sub")
    dims = tuple(mesh.shape[axis] for axis in GROUP)
    rows = P(split, None)
    whole = P("groups", GROUP, None)
    in_specs = (
        rows, rows, rows, P(), P(), P(), P(), P(), P(split), P(split, None, None),
        P(split, None, None), P(split, None, None), rows,
    )
    out_specs = (rows, rows, rows, rows, whole, whole, whole)
    return jax.shard_map(
        lambda *args: body(dims, *args),
        mesh=mesh, in_specs=in_specs, out_specs=out_specs, check_vma=False,
    )
```
